32 devices in a mesh: dp: 2 (over x), lon: 8 (over z, core), mp: 2 (over y).
Axes of the slice: x: 2, y: 2, z: 4, core: 2. Of those that a mesh axis runs over, the one named last changes fastest.
Arguments:
- dataset: float32 [12, 48, 128, 32], P(None, None, None, 'lon'), may hold values from -22 to 22
- indices: int32 [4], P('dp'), may hold values from 0 to 11, as said below
- run_count: float32 [48], replicated, may hold values from 4096 to 16384
- run_mean: float32 [48], replicated, may hold values from -2 to 2
- run_var: float32 [48], replicated, may hold values from 0.3 to 6
- w_embed: bfloat16 [192, 1024], replicated, may hold values from -0.4375 to 0.4375
- pos_embed: bfloat16 [1024, 1024], P('lon'), may hold values from -3 to 3
- gains: float32 [2, 1024], replicated, may hold values from 0.1 to 1.9
- w_qkv: bfloat16 [3, 1024, 1024], P(None, None, 'mp'), may hold values from -0.1875 to 0.1875
- w_out: bfloat16 [1024, 1024], P('mp'), may hold values from -1 to 1
- w_up: bfloat16 [1024, 4096], P(None, 'mp'), may hold values from -0.1875 to 0.1875
- w_down: bfloat16 [4096, 1024], P('mp'), may hold values from -0.09375 to 0.09375
- w_head: bfloat16 [1024, 192], replicated, may hold values from -0.1875 to 0.1875
- cotangent: float32 [4, 1024, 192], P('dp', 'lon'), may hold values from -6 to 6
Outputs:
- pred: float32 [4, 1024, 192], P('dp', 'lon')
- new_count: float32 [48], replicated
- new_mean: float32 [48], replicated
- new_var: float32 [48], replicated
- grad_fields: float32 [4, 48, 128, 32], P('dp', None, None, 'lon')
- grad_embed: float32 [192, 1024], P(None, ('dp', 'lon'))
- grad_pos: float32 [1024, 1024], P('lon', 'dp')
- grad_gains: float32 [2, 1024], P(None, ('dp', 'lon'))
- grad_qkv: float32 [3, 1024, 1024], P(None, ('dp', 'lon'), 'mp')
- grad_out: float32 [1024, 1024], P('mp', ('dp', 'lon'))
- grad_up: float32 [1024, 4096], P(('dp', 'lon'), 'mp')
- grad_down: float32 [4096, 1024], P('mp', ('dp', 'lon'))
- grad_head: float32 [1024, 192], P(('dp', 'lon'))
The draws below stay inside these ranges and needn't reach their ends.
Inputs may be any that keep to these rules, and one draw needn't show every extreme that they name: The 4 indices name different items.
All inputs are finite; a program needn't handle non-finite values.
Results may differ from the reference program's by a relative error of at most 0.024.
Values may be sent and summed in bfloat16 or wider, within the bound.
No kernel may reach another device: no remote copies, remote signals or barrier semaphores. Data moves between devices by JAX's collectives and lax.ppermute only.
A program may use at most 256 MiB of HBM per device.

```python
import math
import jax
import jax.numpy as jnp
from jax import lax

D = 1024
HEADS = 16
HDIM = 64
FF = 4096
VARS = 48
PATCH = 2
HGT = 128
PDIM = 192
ROWS = 64
WID = 32
PCOLS = 16
SEQ = 1024
ITEMS = 4
DSET = 12


def draw_dataset(key, part):
    key = jax.random.fold_in(key, 11)
    subkeys = jax.random.split(key, 6)
    full_shape = (DSET, VARS, HGT, WID)
    magnitude = jax.random.uniform(subkeys[0], (1, VARS, 1, 1), minval=0.5, maxval=3.0)
    polarity = jnp.where(jax.random.uniform(subkeys[1], (1, VARS, 1, 1)) < 0.5, -1.0, 1.0)
    spread = jnp.exp(jax.random.uniform(subkeys[2], (1, VARS, 1, 1), minval=math.log(0.3), maxval=math.log(3.0)))
    incline = 0.5 + jnp.arange(WID, dtype=jnp.float32) / WID
    item_shift = jax.random.uniform(subkeys[4], (DSET, VARS, 1, 1), minval=-2.5, maxval=2.5)
    item_scale = jnp.exp(jax.random.uniform(subkeys[5], (DSET, VARS, 1, 1), minval=math.log(0.6), maxval=math.log(1.6)))
    jitter = jnp.clip(jax.random.normal(subkeys[3], full_shape), -4.0, 4.0)
    values = magnitude * polarity * incline + item_shift + spread * item_scale * jitter
    return jnp.clip(values, -22.0, 22.0).astype(jnp.float32)


def draw_indices(key, part):
    key = jax.random.fold_in(key, 37)
    shuffled = jax.random.permutation(key, DSET)
    return shuffled[:ITEMS].astype(jnp.int32)


def draw_w_out(key, part):
    key = jax.random.fold_in(key, 23)
    entries = jnp.clip(jax.random.uniform(key, (D, D), minval=-1.05, maxval=1.05), -1.0, 1.0)
    return entries.astype(jnp.bfloat16)


def block_scale(rng, shape, cuts, low, largest):
    def one(position, parts):
        steps = jax.random.uniform(jax.random.fold_in(jax.random.fold_in(rng, 6), position), (parts,), jnp.float32, low / len(cuts), largest / len(cuts))
        return jnp.repeat(jnp.exp(steps), shape[position] // parts).reshape((-1,) + (1,) * (len(shape) - position - 1))

    gain = one(*cuts[0])
    for cut in cuts[1:]:
        gain = gain * one(*cut)
    return gain


def noise(key, extent, scale, reach, shards=(), held_as=jnp.bfloat16):
    drawn = scale * jax.random.normal(key, extent, jnp.float32)
    if shards:
        drawn = drawn * block_scale(key, extent, shards, -0.22, 0.18)
    return jnp.clip(drawn, -reach, reach).astype(held_as)


def setup_inputs(seed: int = 0) -> dict:
    splits = jax.random.split(jax.random.key(seed), 15)
    dataset = draw_dataset(jax.random.fold_in(splits[14], 71), 0)
    indices = draw_indices(jax.random.fold_in(splits[14], 71), 0)
    run_count = jnp.clip(jnp.exp(jax.random.uniform(splits[2], (VARS,), jnp.float32, math.log(4096.0), math.log(16384.0))), 4096.0, 16384.0)
    run_mean = jnp.clip(jax.random.uniform(splits[3], (VARS,), jnp.float32, -2.0, 2.0), -2.0, 2.0)
    run_var = jnp.clip(jnp.exp(jax.random.uniform(splits[4], (VARS,), jnp.float32, math.log(0.3), math.log(6.0))), 0.3, 6.0)
    w_embed = noise(splits[5], (PDIM, D), PDIM ** -0.5, 0.4375)
    pos_embed = noise(splits[6], (SEQ, D), 0.5, 3.0, ((0, 8),))
    gains = jnp.clip(1.0 + 0.18 * jax.random.normal(splits[7], (2, D), jnp.float32), 0.1, 1.9)
    w_qkv = noise(splits[8], (3, D, D), D ** -0.5, 0.1875, ((2, 2),))
    w_out = draw_w_out(jax.random.fold_in(splits[14], 71), 0)
    w_up = noise(splits[10], (D, FF), D ** -0.5, 0.1875, ((1, 2),))
    w_down = noise(splits[11], (FF, D), FF ** -0.5, 0.09375, ((0, 2),))
    w_head = noise(splits[12], (D, PDIM), D ** -0.5, 0.1875)
    cotangent = noise(splits[13], (ITEMS, SEQ, PDIM), 1.0, 6.0, ((0, 2), (1, 8)), jnp.float32)
    return {"dataset": dataset, "indices": indices, "run_count": run_count, "run_mean": run_mean, "run_var": run_var, "w_embed": w_embed, "pos_embed": pos_embed, "gains": gains, "w_qkv": w_qkv, "w_out": w_out, "w_up": w_up, "w_down": w_down, "w_head": w_head, "cotangent": cotangent}


@jax.custom_vjp
def low(v):
    return lax.optimization_barrier(v.astype(jnp.bfloat16)).astype(jnp.float32)

@jax.custom_vjp
def low_back(v):
    return v

def low_keep(v):
    return (low(v), None)

def low_pass(kept, grad):
    return (grad,)

def back_keep(v):
    return (v, None)

def back_low(kept, grad):
    return (low(grad),)
low.defvjp(low_keep, low_pass)
low_back.defvjp(back_keep, back_low)
NORM_EPS = 1e-06
STAT_EPS = 1e-06
HIGHEST = lax.Precision.HIGHEST

def layer_norm(hidden, scaling):
    centred = hidden - lax.optimization_barrier(jnp.mean(hidden, axis=-1, keepdims=True))
    variance = lax.optimization_barrier(jnp.mean(centred * centred, axis=-1, keepdims=True))
    return centred * lax.rsqrt(variance + NORM_EPS) * scaling

def product(former, latter):
    return jnp.dot(former, latter, precision=HIGHEST, preferred_element_type=jnp.float32)

def attend(query_block, all_keys, all_values):
    score_scale = 1.0 / math.sqrt(HDIM)
    scores = low_back(jnp.einsum('qhd,khd->qhk', query_block, all_keys, precision=HIGHEST) * score_scale)
    row_max = lax.optimization_barrier(jnp.max(scores, axis=-1, keepdims=True))
    raised = jnp.exp(scores - row_max)
    weights = raised / lax.optimization_barrier(jnp.sum(raised, axis=-1, keepdims=True))
    return jnp.einsum('qhk,khd->qhd', low(weights), all_values, precision=HIGHEST)

def item_forward(patch_rows, w_embed, pos_embed, gains, w_qkv, w_out, w_up, w_down, w_head):
    hidden_zero = low_back(product(patch_rows, w_embed)) + pos_embed
    normed_one = low(layer_norm(hidden_zero, gains[0]))
    projected = low(low_back(jnp.einsum('nd,kdc->knc', normed_one, w_qkv, precision=HIGHEST)))
    per_head = projected.reshape(3, SEQ, HEADS, HDIM)
    block_rows = 512 if SEQ % 512 == 0 else SEQ
    query_blocks = per_head[0].reshape(SEQ // block_rows, block_rows, HEADS, HDIM)
    attended = lax.map(jax.checkpoint(lambda query_block: attend(query_block, per_head[1], per_head[2])), query_blocks)
    mixed = low(low_back(attended.reshape(SEQ, HEADS * HDIM)))
    hidden_one = hidden_zero + low_back(product(mixed, w_out))
    normed_two = low(layer_norm(hidden_one, gains[1]))
    activated = low(jax.nn.gelu(low_back(product(normed_two, w_up)), approximate=False))
    hidden_two = hidden_one + low_back(product(activated, w_down))
    return low_back(product(low(hidden_two), w_head))

def forward(normed, w_embed, pos_embed, gains, w_qkv, w_out, w_up, w_down, w_head):
    rolled = jnp.roll(normed, 1, axis=3)
    layout = rolled.reshape(ITEMS, VARS, ROWS, PATCH, PCOLS, PATCH)
    patches = low(jnp.transpose(layout, (0, 4, 2, 1, 3, 5)).reshape(ITEMS, SEQ, PDIM))
    return lax.map(lambda patch_item: item_forward(patch_item, w_embed, pos_embed, gains, w_qkv, w_out, w_up, w_down, w_head), patches)

def reference(dataset, indices, run_count, run_mean, run_var, w_embed, pos_embed, gains, w_qkv, w_out, w_up, w_down, w_head, cotangent):
    fields = jnp.take(dataset, indices.astype(jnp.int32), axis=0)
    batch_count = jnp.float32(ITEMS * HGT * WID)
    batch_mean = lax.optimization_barrier(jnp.mean(fields, axis=(0, 2, 3)))
    batch_spread = lax.optimization_barrier(jnp.sum(jnp.square(fields - batch_mean[None, :, None, None]), axis=(0, 2, 3)))
    new_count = run_count + batch_count
    offset_mean = batch_mean - run_mean
    new_mean = run_mean + offset_mean * (batch_count / new_count)
    new_var = (run_var * run_count + batch_spread + offset_mean * offset_mean * (run_count * batch_count / new_count)) / new_count
    normed = (fields - new_mean[None, :, None, None]) * lax.rsqrt(new_var + STAT_EPS)[None, :, None, None]
    pred, pullback = jax.vjp(forward, normed, w_embed.astype(jnp.float32), pos_embed.astype(jnp.float32), gains.astype(jnp.float32), w_qkv.astype(jnp.float32), w_out.astype(jnp.float32), w_up.astype(jnp.float32), w_down.astype(jnp.float32), w_head.astype(jnp.float32))
    grads = pullback(cotangent)
    return (pred, new_count, new_mean, new_var, grads[0], grads[1], grads[2], grads[3], grads[4], grads[5], grads[6], grads[7], grads[8])
```

```python
import functools
import math

import jax
import jax.numpy as jnp
from jax import lax
from jax.experimental import pallas as pl
from jax.experimental.pallas import tpu as pltpu
from jax.sharding import PartitionSpec as P

HDIM = 64
PATCH = 2
NORM_EPS = 1e-06
STAT_EPS = 1e-06
BF = jnp.bfloat16
F32 = jnp.float32


def swap(block, axis, distance):
    route = [(i, i ^ distance) for i in range(lax.axis_size(axis))]
    return lax.ppermute(block, axis, route)


def from_behind(block, axis, distance):
    size = lax.axis_size(axis)
    route = [((i - distance) % size, i) for i in range(size)]
    return lax.ppermute(block, axis, route)


def layer_norm(hidden, scaling):
    centred = hidden - jnp.mean(hidden, axis=-1, keepdims=True)
    variance = jnp.mean(centred * centred, axis=-1, keepdims=True)
    return centred * lax.rsqrt(variance + NORM_EPS) * scaling


def layer_norm_back(hidden, scaling, grad):
    centred = hidden - jnp.mean(hidden, axis=-1, keepdims=True)
    variance = jnp.mean(centred * centred, axis=-1, keepdims=True)
    inverse = lax.rsqrt(variance + NORM_EPS)
    unit = centred * inverse
    scaled = grad * scaling
    back = inverse * (
        scaled
        - jnp.mean(scaled, axis=-1, keepdims=True)
        - unit * jnp.mean(scaled * unit, axis=-1, keepdims=True)
    )
    return back, jnp.sum(grad * unit, axis=0)


def nt(a, b):
    return lax.dot_general(a, b, (((1,), (1,)), ((), ())), preferred_element_type=F32)


def nn(a, b):
    return lax.dot_general(a, b, (((1,), (0,)), ((), ())), preferred_element_type=F32)


def item_mask(rows, lanes, item):
    lane = lax.broadcasted_iota(jnp.int32, (rows, lanes), 1)
    return (lane >= item * HDIM) & (lane < (item + 1) * HDIM)


def attend_kernel(items, scale, q_ref, k_ref, v_ref, o_ref, ot_ref, pt_ref, vt_ref):
    @pl.when(pl.program_id(0) == 0)
    def _():
        vt_ref[...] = v_ref[...].astype(F32).T.astype(BF)

    queries = q_ref[...] * BF(scale)
    rows, lanes = queries.shape
    for item in range(items):
        chosen = jnp.where(item_mask(rows, lanes, item), queries, BF(0))
        scores = nt(k_ref[...], chosen)
        top = jnp.max(scores, axis=0, keepdims=True)
        raised = jnp.exp(scores - top)
        total = jnp.sum(raised, axis=0, keepdims=True)
        weights = (raised * (1.0 / total)).astype(BF)
        pt_ref[item] = weights
        ot_ref[item * HDIM : (item + 1) * HDIM, :] = nn(
            vt_ref[item * HDIM : (item + 1) * HDIM, :], weights
        )
    o_ref[...] = ot_ref[...].T.astype(BF)


def attend(q, k, v, items, scale):
    rows, lanes = q.shape
    keys = k.shape[0]
    block = max(128, min(rows, 256 * 1024 // keys))
    whole = lambda j: (0, 0)
    return pl.pallas_call(
        functools.partial(attend_kernel, items, scale),
        grid=(rows // block,),
        out_shape=(
            jax.ShapeDtypeStruct((rows, lanes), BF),
            jax.ShapeDtypeStruct((lanes, rows), F32),
            jax.ShapeDtypeStruct((items, keys, rows), BF),
        ),
        in_specs=[
            pl.BlockSpec((block, lanes), lambda j: (j, 0)),
            pl.BlockSpec((keys, lanes), whole),
            pl.BlockSpec((keys, lanes), whole),
        ],
        out_specs=(
            pl.BlockSpec((block, lanes), lambda j: (j, 0)),
            pl.BlockSpec((lanes, block), lambda j: (0, j)),
            pl.BlockSpec((items, keys, block), lambda j: (0, 0, j)),
        ),
        scratch_shapes=[pltpu.VMEM((lanes, keys), BF)],
        compiler_params=pltpu.CompilerParams(vmem_limit_bytes=56 * 2**20),
        name="attend",
    )(q, k, v)


def attend_back_kernel(
    items, scale, q_ref, k_ref, v_ref, d_ref, ot_ref, pt_ref,
    dq_ref, dk_ref, dv_ref, kt_ref, dqt_ref, dk_sum, dv_sum,
):
    step = pl.program_id(0)

    @pl.when(step == 0)
    def _():
        kt_ref[...] = (k_ref[...].astype(F32) * scale).T.astype(BF)
        dk_sum[...] = jnp.zeros_like(dk_sum)
        dv_sum[...] = jnp.zeros_like(dv_sum)

    queries = q_ref[...] * BF(scale)
    grads = d_ref[...]
    rows, lanes = queries.shape
    product = grads.astype(F32).T * ot_ref[...]
    for item in range(items):
        span = slice(item * HDIM, (item + 1) * HDIM)
        mask = item_mask(rows, lanes, item)
        grad = jnp.where(mask, grads, BF(0))
        query = jnp.where(mask, queries, BF(0))
        delta = jnp.sum(product[span, :], axis=0, keepdims=True)
        weights = pt_ref[item]
        back = weights.astype(F32) * (nt(v_ref[...], grad) - delta)
        back = back.astype(BF)
        dv_sum[...] += nn(weights, grad)
        dk_sum[...] += nn(back, query)
        dqt_ref[span, :] = nn(kt_ref[span, :], back)
    dq_ref[...] = dqt_ref[...].T.astype(dq_ref.dtype)

    @pl.when(step == pl.num_programs(0) - 1)
    def _():
        dk_ref[...] = dk_sum[...].astype(dk_ref.dtype)
        dv_ref[...] = dv_sum[...].astype(dv_ref.dtype)


def attend_back(q, k, v, d, ot, pt, items, scale, kind):
    rows, lanes = q.shape
    keys = k.shape[0]
    block = max(128, min(rows, 256 * 1024 // keys))
    whole = lambda j: (0, 0)
    mine = pl.BlockSpec((block, lanes), lambda j: (j, 0))
    full = pl.BlockSpec((keys, lanes), whole)
    return pl.pallas_call(
        functools.partial(attend_back_kernel, items, scale),
        grid=(rows // block,),
        out_shape=(
            jax.ShapeDtypeStruct((rows, lanes), BF),
            jax.ShapeDtypeStruct((keys, lanes), kind),
            jax.ShapeDtypeStruct((keys, lanes), kind),
        ),
        in_specs=[
            mine,
            full,
            full,
            mine,
            pl.BlockSpec((lanes, block), lambda j: (0, j)),
            pl.BlockSpec((items, keys, block), lambda j: (0, 0, j)),
        ],
        out_specs=(mine, full, full),
        scratch_shapes=[
            pltpu.VMEM((lanes, keys), BF),
            pltpu.VMEM((lanes, block), F32),
            pltpu.VMEM((keys, lanes), F32),
            pltpu.VMEM((keys, lanes), F32),
        ],
        compiler_params=pltpu.CompilerParams(vmem_limit_bytes=56 * 2**20),
        name="attend_back",
    )(q, k, v, d, ot, pt)


def pick(x, index, axis):
    return lax.dynamic_index_in_dim(x, index, axis, keepdims=False)


def exchange(packed, me, group):
    slots = []
    for k in range(group):
        block = pick(packed, me ^ k, 0)
        slots.append(block if k == 0 else swap(block, "lon", k))
    return slots


def give_back(slots, me, group):
    got = [slots[0]] + [swap(slots[k], "lon", k) for k in range(1, group)]
    return jnp.take(jnp.stack(got), jnp.arange(group) ^ me, axis=0)


def halve(total, dims):
    dims = list(dims)
    order = sorted(range(len(dims)), key=lambda i: dims[i][2])
    left = list(range(len(dims)))
    for i in order:
        axis, bit, _ = dims[i]
        place = left.index(i)
        left.remove(i)
        side = (lax.axis_index(axis) // bit) % 2
        got = swap(pick(total, 1 - side, place), axis, bit)
        total = (pick(total, side, place).astype(F32) + got.astype(F32))
        if left:
            total = total.astype(BF)
    return total


def scatter(total):
    dp, lon = lax.axis_size("dp"), lax.axis_size("lon")
    dims = []
    bit = dp // 2
    while bit:
        dims.append(("dp", bit, 10 + bit))
        bit //= 2
    bit = lon // 2
    while bit:
        dims.append(("lon", bit, 1 if bit == 1 else 100 + bit))
        bit //= 2
    rows, columns = total.shape
    parts = dp * lon
    return halve(
        total.astype(BF).reshape((2,) * len(dims) + (rows // parts, columns)), dims
    )


def local(
    dataset,
    indices,
    run_count,
    run_mean,
    run_var,
    w_embed,
    pos_embed,
    gains,
    w_qkv,
    w_out,
    w_up,
    w_down,
    w_head,
    cotangent,
):
    item_count = indices.shape[0]
    variables, height, columns = dataset.shape[1:]
    lon_count = lax.axis_size("lon")
    everyone = lax.axis_size("dp") * lon_count
    fields = jnp.stack([pick(dataset, indices[i], 0) for i in range(item_count)])
    local_count = float(item_count * height * columns)
    raw_edge = from_behind(fields[:, :, :, columns - 1 :].astype(BF), "lon", 1).astype(F32)
    local_mean = jnp.mean(fields, axis=(0, 2, 3))
    local_spread = jnp.sum(jnp.square(fields - local_mean[None, :, None, None]), axis=(0, 2, 3))
    moments = jnp.concatenate([local_mean, local_spread])
    moments = lax.all_to_all(
        jnp.broadcast_to(moments, (everyone, 2 * variables)), ("dp", "lon"), 0, 0
    )
    batch_mean = jnp.mean(moments[:, :variables], axis=0)
    batch_spread = jnp.sum(
        moments[:, variables:] + local_count * jnp.square(moments[:, :variables] - batch_mean),
        axis=0,
    )
    batch_count = local_count * everyone
    new_count = run_count + batch_count
    shift = batch_mean - run_mean
    new_mean = run_mean + shift * (batch_count / new_count)
    new_var = (
        run_var * run_count
        + batch_spread
        + shift * shift * (run_count * batch_count / new_count)
    ) / new_count
    inv_scale = lax.rsqrt(new_var + STAT_EPS)[None, :, None, None]
    centre = new_mean[None, :, None, None]
    normed = ((fields - centre) * inv_scale).astype(BF)
    left_edge = ((raw_edge - centre) * inv_scale).astype(BF)
    extended = jnp.concatenate([left_edge, normed[:, :, :, : columns - 1]], axis=3)
    patch_rows = height // PATCH
    patch_cols = columns // PATCH
    item_tokens = patch_rows * patch_cols
    all_tokens = item_count * item_tokens
    layout = extended.reshape(item_count, variables, patch_rows, PATCH, patch_cols, PATCH)
    patches = jnp.transpose(layout, (0, 4, 2, 1, 3, 5)).reshape(
        all_tokens, variables * PATCH * PATCH
    )
    model_width = w_embed.shape[1]
    local_width = w_qkv.shape[2]
    head_count = local_width // HDIM
    scale = 1.0 / math.sqrt(HDIM)
    lanes = item_count * HDIM
    embedded = jnp.dot(patches, w_embed, preferred_element_type=F32)
    position = pos_embed.astype(F32)
    hidden_zero = (embedded.reshape(item_count, item_tokens, model_width) + position[None]).reshape(
        all_tokens, model_width
    )
    normed_one = layer_norm(hidden_zero, gains[0]).astype(BF)

    group = head_count
    far = lon_count // group
    me = lax.axis_index("lon") % group
    packed = jnp.einsum(
        "itd,kdhc->hktic",
        normed_one.reshape(item_count, item_tokens, model_width),
        w_qkv.reshape(3, model_width, head_count, HDIM),
        preferred_element_type=F32,
    ).astype(BF)
    packed = packed.reshape(head_count, 3, item_tokens, lanes)
    slots = jnp.stack(exchange(packed, me, group))
    seen = group * item_tokens
    queries, keys, values = (slots[:, c].reshape(seen, lanes) for c in range(3))
    if far > 1:
        groups = [[i + group * g for g in range(far)] for i in range(group)]
        keys = lax.all_gather(keys, "lon", axis=0, tiled=True, axis_index_groups=groups)
        values = lax.all_gather(values, "lon", axis=0, tiled=True, axis_index_groups=groups)
    attended, attended_t, weights_t = attend(queries, keys, values, item_count, scale)
    attended = attended.reshape(group, item_tokens, lanes)
    heads = give_back([attended[k] for k in range(group)], me, group)
    mixed = (
        heads.reshape(head_count, item_tokens, item_count, HDIM)
        .transpose(2, 1, 0, 3)
        .reshape(all_tokens, local_width)
    )
    branch = jnp.dot(mixed, w_out, preferred_element_type=F32).astype(BF)
    hidden_one = hidden_zero + (branch.astype(F32) + swap(branch, "mp", 1).astype(F32))
    normed_two = layer_norm(hidden_one, gains[1]).astype(BF)
    pre_act = jnp.dot(normed_two, w_up, preferred_element_type=F32)
    gelu, gelu_back = jax.vjp(lambda inner: jax.nn.gelu(inner, approximate=False), pre_act)
    activated = gelu.astype(BF)
    grad_pred = cotangent.reshape(all_tokens, cotangent.shape[2]).astype(BF)
    d_two = jnp.einsum("np,dp->nd", grad_pred, w_head, preferred_element_type=F32)
    d_two_low = d_two.astype(BF)
    d_act = jnp.einsum("nd,fd->nf", d_two_low, w_down, preferred_element_type=F32)
    d_pre = gelu_back(d_act)[0].astype(BF)
    d_norm = jnp.einsum("nf,df->nd", d_pre, w_up, preferred_element_type=F32).astype(BF)
    d_norm_two = d_norm.astype(F32) + swap(d_norm, "mp", 1).astype(F32)
    forward = jnp.dot(activated, w_down, preferred_element_type=F32).astype(BF)
    hidden_two = hidden_one + (forward.astype(F32) + swap(forward, "mp", 1).astype(F32))
    hidden_low = hidden_two.astype(BF)
    pred = jnp.dot(hidden_low, w_head, preferred_element_type=F32)

    grad_up = scatter(jnp.einsum("nd,nf->df", normed_two, d_pre, preferred_element_type=F32))
    grad_down = scatter(jnp.einsum("nd,nf->df", d_two_low, activated, preferred_element_type=F32))
    grad_head = scatter(
        jnp.einsum("nd,np->dp", hidden_low, grad_pred, preferred_element_type=F32)
    )

    d_hidden_two, gain_two = layer_norm_back(hidden_one, gains[1], d_norm_two)
    d_one = d_two + d_hidden_two
    d_one_low = d_one.astype(BF)
    d_mixed = jnp.einsum(
        "itd,hcd->htic",
        d_one_low.reshape(item_count, item_tokens, model_width),
        w_out.reshape(head_count, HDIM, model_width),
        preferred_element_type=F32,
    ).astype(BF)
    d_heads = jnp.stack(
        exchange(d_mixed.reshape(head_count, item_tokens, lanes), me, group)
    ).reshape(seen, lanes)
    grad_out = scatter(jnp.einsum("nd,nc->dc", d_one_low, mixed, preferred_element_type=F32))
    d_query, d_key, d_value = attend_back(
        queries, keys, values, d_heads, attended_t, weights_t, item_count, scale,
        BF if far == 1 else F32,
    )
    if far > 1:
        d_key, d_value = (
            lax.psum_scatter(
                d, "lon", scatter_dimension=0, tiled=True, axis_index_groups=groups
            ).astype(BF)
            for d in (d_key, d_value)
        )
    back = jnp.stack(
        [d.reshape(group, item_tokens, lanes) for d in (d_query, d_key, d_value)], axis=1
    )
    back = give_back([back[k] for k in range(group)], me, group)
    d_qkv = (
        back.reshape(head_count, 3, item_tokens, item_count, HDIM)
        .transpose(3, 2, 1, 0, 4)
        .reshape(all_tokens, 3 * local_width)
    )
    d_norm = jnp.einsum(
        "nkc,kdc->nd",
        d_qkv.reshape(all_tokens, 3, local_width),
        w_qkv,
        preferred_element_type=F32,
    ).astype(BF)
    d_norm_one = d_norm.astype(F32) + swap(d_norm, "mp", 1).astype(F32)
    grad_qkv = scatter(jnp.einsum("nd,nc->dc", normed_one, d_qkv, preferred_element_type=F32))
    d_hidden_one, gain_one = layer_norm_back(hidden_zero, gains[0], d_norm_one)
    d_zero = d_one + d_hidden_one
    d_zero_low = d_zero.astype(BF)
    pos_sum = jnp.sum(d_zero.reshape(item_count, item_tokens, model_width), axis=0).astype(BF)
    dp_count = lax.axis_size("dp")
    pos_sum = pos_sum.reshape(item_tokens, dp_count, model_width // dp_count)
    dp_index = lax.axis_index("dp")
    grad_pos = pick(pos_sum, dp_index, 1).astype(F32)
    for k in range(1, dp_count):
        grad_pos = grad_pos + swap(pick(pos_sum, dp_index ^ k, 1), "dp", k).astype(F32)
    embed = jnp.einsum("nd,np->dp", d_zero_low, patches, preferred_element_type=F32)
    pdim = patches.shape[1]
    embed = jnp.concatenate([embed, gain_one[:, None], gain_two[:, None]], axis=1)
    embed = scatter(embed)
    grad_embed, grad_gains = embed[:, :pdim], embed[:, pdim:]
    d_patches = jnp.einsum("nd,pd->np", d_zero_low, w_embed, preferred_element_type=F32)
    d_layout = jnp.transpose(
        d_patches.reshape(item_count, patch_cols, patch_rows, variables, PATCH, PATCH),
        (0, 3, 2, 4, 1, 5),
    ).reshape(item_count, variables, height, columns)
    east_grad = from_behind(d_layout[:, :, :, :1].astype(BF), "lon", -1).astype(F32)
    grad_fields = jnp.concatenate([d_layout[:, :, :, 1:], east_grad], axis=3)
    return (
        pred.reshape(item_count, item_tokens, pred.shape[1]),
        new_count,
        new_mean,
        new_var,
        grad_fields,
        grad_embed.T,
        grad_pos,
        grad_gains.T,
        grad_qkv.reshape(-1, 3, local_width).transpose(1, 0, 2),
        grad_out.T,
        grad_up,
        grad_down.T,
        grad_head,
    )


def solution(mesh):
    in_specs = (
        P(None, None, None, "lon"),
        P("dp"),
        P(),
        P(),
        P(),
        P(),
        P("lon", None),
        P(),
        P(None, None, "mp"),
        P("mp", None),
        P(None, "mp"),
        P("mp", None),
        P(),
        P("dp", "lon", None),
    )
    out_specs = (
        P("dp", "lon", None),
        P(),
        P(),
        P(),
        P("dp", None, None, "lon"),
        P(None, ("dp", "lon")),
        P("lon", "dp"),
        P(None, ("dp", "lon")),
        P(None, ("dp", "lon"), "mp"),
        P("mp", ("dp", "lon")),
        P(("dp", "lon"), "mp"),
        P("mp", ("dp", "lon")),
        P(("dp", "lon"), None),
    )
    return jax.shard_map(local, mesh=mesh, in_specs=in_specs, out_specs=out_specs, check_vma=False)
```

```python
import functools
import math

import jax
import jax.numpy as jnp
from jax import lax
from jax.experimental import pallas as pl
from jax.experimental.pallas import tpu as pltpu
from jax.sharding import PartitionSpec as P

HDIM = 64
PATCH = 2
LANES = 128
NORM_EPS = 1e-06
STAT_EPS = 1e-06
BF = jnp.bfloat16
F32 = jnp.float32
MIB = 2**20


def swap(block, axis, distance):
    route = [(i, i ^ distance) for i in range(lax.axis_size(axis))]
    return lax.ppermute(block, axis, route)


def from_behind(block, axis, distance):
    size = lax.axis_size(axis)
    route = [((i - distance) % size, i) for i in range(size)]
    return lax.ppermute(block, axis, route)


def pick(x, index, axis):
    return lax.dynamic_index_in_dim(x, index, axis, keepdims=False)


def halve(total, dims):
    for axis, bit in dims:
        side = (lax.axis_index(axis) // bit) % 2
        got = swap(pick(total, 1 - side, 0), axis, bit)
        total = (pick(total, side, 0).astype(F32) + got.astype(F32)).astype(BF)
    return total


def scatter(total):
    dp, lon = lax.axis_size("dp"), lax.axis_size("lon")
    dims = []
    for axis, size in (("dp", dp), ("lon", lon)):
        bit = size // 2
        while bit:
            dims.append((axis, bit))
            bit //= 2
    rows, columns = total.shape
    total = total.astype(BF).reshape((2,) * len(dims) + (rows // (dp * lon), columns))
    order = sorted(range(len(dims)), key=lambda i: (dims[i][1] > 1 or dims[i][0] == "dp", i))
    total = total.transpose([*order, len(dims), len(dims) + 1])
    return halve(total, [dims[i] for i in order]).astype(F32)


def nt(a, b):
    return lax.dot_general(a, b, (((1,), (1,)), ((), ())), preferred_element_type=F32)


def nn(a, b):
    return lax.dot_general(a, b, (((1,), (0,)), ((), ())), preferred_element_type=F32)


def item_mask(rows, lanes, item):
    lane = lax.broadcasted_iota(jnp.int32, (rows, lanes), 1)
    return (lane >= item * HDIM) & (lane < (item + 1) * HDIM)


def interleave(first, second):
    low = item_mask(first.shape[0], LANES, 0)
    return (
        jnp.where(low, first, pltpu.roll(second, HDIM, 1)),
        jnp.where(low, pltpu.roll(first, HDIM, 1), second),
    )


def norm_parts(hidden):
    centred = hidden - jnp.mean(hidden, axis=-1, keepdims=True)
    variance = jnp.mean(centred * centred, axis=-1, keepdims=True)
    inverse = lax.rsqrt(variance + NORM_EPS)
    return centred * inverse, inverse


def norm_back(unit, inverse, scaling, grad):
    scaled = grad * scaling
    back = inverse * (
        scaled
        - jnp.mean(scaled, axis=-1, keepdims=True)
        - unit * jnp.mean(scaled * unit, axis=-1, keepdims=True)
    )
    return back, jnp.sum(grad * unit, axis=0, keepdims=True)


def emit_turned(x, ids_ref, outs, hold):
    turned = x.T.astype(BF)
    if len(outs) == 1:
        outs[0][...] = turned
        return
    keep, send = outs
    parts, rows, tokens = keep.shape
    hold[...] = turned.reshape(parts, 2, rows, tokens)
    core = ids_ref[0]
    keep[...] = hold[:, pl.ds(core, 1)].reshape(parts, rows, tokens)
    send[...] = hold[:, pl.ds(1 - core, 1)].reshape(parts, rows, tokens)


def call(body, name, outs, *args, grid=(), in_specs=None, out_specs=None, scratch=(), limit=24, flops=0):
    vmem = pl.BlockSpec(memory_space=pltpu.VMEM)
    smem = pl.BlockSpec(memory_space=pltpu.SMEM)
    if in_specs is None:
        in_specs = [smem if a.dtype == jnp.int32 else vmem for a in args]
    if out_specs is None:
        out_specs = [vmem] * len(outs)
    nbytes = sum(math.prod(a.shape) * a.dtype.itemsize for a in [*args, *outs])
    return pl.pallas_call(
        body,
        grid=grid,
        out_shape=list(outs),
        in_specs=in_specs,
        out_specs=out_specs,
        scratch_shapes=list(scratch),
        compiler_params=pltpu.CompilerParams(vmem_limit_bytes=limit * MIB),
        cost_estimate=pl.CostEstimate(flops=int(flops), bytes_accessed=nbytes, transcendentals=0),
        name=name,
    )(*args)


def shape(dims, kind=BF):
    return jax.ShapeDtypeStruct(dims, kind)


def start_kernel(local_count, ids_ref, mom_ref, run_ref, fields_ref, edge_ref, we_ref, pos_ref, gains_ref, wq_ref,
                 stats_ref, hidden_ref, patches_ref, qkv_ref, *rest):
    turned, (column_ref, hold) = rest[:-2], rest[-2:]
    members = mom_ref.shape[0]
    items, rows, height = fields_ref.shape
    variables = edge_ref.shape[1]
    cols = rows // variables
    half = height // PATCH
    moments = mom_ref[...]
    batch_count = local_count * members
    batch_mean = jnp.sum(moments, axis=0, keepdims=True) * (1.0 / members)
    off = moments - batch_mean
    spread = jnp.sum(pltpu.roll(moments, HDIM, 1) + local_count * off * off, axis=0, keepdims=True)
    run_count, run_mean, run_var = (run_ref[k : k + 1, :] for k in range(3))
    new_count = run_count + batch_count
    shift = batch_mean - run_mean
    new_mean = run_mean + shift * (batch_count / new_count)
    new_var = (
        run_var * run_count + spread + shift * shift * (run_count * batch_count / new_count)
    ) / new_count
    stats_ref[0:1, :] = new_count
    stats_ref[1:2, :] = new_mean
    stats_ref[2:3, :] = new_var
    column_ref[...] = jnp.zeros_like(column_ref)
    column_ref[0:1, :] = new_mean
    column_ref[1:2, :] = lax.rsqrt(new_var + STAT_EPS)
    column = column_ref[...].T
    centre, inverse = column[0:variables, 0:1], column[0:variables, 1:2]

    def scaled(block):
        return ((block - centre) * inverse).astype(BF)

    row = lax.broadcasted_iota(jnp.int32, (2 * height, LANES), 0)
    lane = lax.broadcasted_iota(jnp.int32, (2 * height, LANES), 1)
    sort = [
        jnp.where(
            (row // height == lane // half) & (row % height == PATCH * (lane % half) + a), 1.0, 0.0
        ).astype(BF)
        for a in range(PATCH)
    ]
    features = PATCH * PATCH * variables
    out = lax.broadcasted_iota(jnp.int32, (features, features), 0)
    src = lax.broadcasted_iota(jnp.int32, (features, features), 1)
    natural = jnp.where(
        (out // 4 == src % variables) & (out % 4 == src // variables), 1.0, 0.0
    ).astype(BF)
    hidden = []
    for item in range(items):
        west = scaled(edge_ref[item].astype(F32))
        own = [
            scaled(fields_ref[item, pl.ds(c, variables, stride=cols), :]) for c in range(cols - 1)
        ]
        first = jnp.concatenate([west, own[0]], axis=0)
        second = jnp.concatenate([own[1], own[2]], axis=0)
        both = jnp.concatenate([first, second], axis=1)
        patches = jnp.concatenate([nn(both, sort[a]) for a in range(PATCH)], axis=0)
        patches_ref[:, item * LANES : (item + 1) * LANES] = nn(natural, patches.astype(BF)).astype(BF)
        hidden.append(nn(patches.T.astype(BF), we_ref[...]) + pos_ref[...].astype(F32))
    hidden = jnp.concatenate(hidden, axis=0)
    hidden_ref[...] = hidden
    unit, _ = norm_parts(hidden)
    normed = unit * gains_ref[0:1, :]
    low = normed.astype(BF)
    emit_turned(normed, ids_ref, turned, hold)
    for c in range(3):
        product = nn(low, wq_ref[c])
        for t in range(product.shape[1] // LANES):
            tile = product[:, t * LANES : (t + 1) * LANES]
            a, b = interleave(tile[:LANES], tile[LANES:])
            qkv_ref[2 * t, c] = a.astype(BF)
            qkv_ref[2 * t + 1, c] = b.astype(BF)


def cotangent_kernel(ids_ref, ct_ref, wh_ref, wd_ref, two_ref, act_ref, low_ref, *rest):
    turned, hold = rest[:-1], rest[-1]
    grads = []
    low_ref[...] = jnp.zeros_like(low_ref)
    for item in range(ct_ref.shape[0]):
        ct = ct_ref[item].T.astype(BF)
        low_ref[item * LANES : (item + 1) * LANES, 0 : ct.shape[1]] = ct
        grads.append(nn(ct, wh_ref[...]))
    d_two = jnp.concatenate(grads, axis=0)
    two_ref[...] = d_two
    emit_turned(d_two, ids_ref, turned, hold)
    act_ref[...] = nt(d_two.astype(BF), wd_ref[...])


def attend_kernel(items, scale, q_ref, kv_ref, o_ref, ot_ref, pt_ref, vt_ref):
    keys = kv_ref.shape[0] * kv_ref.shape[2]

    @pl.when(pl.program_id(0) == 0)
    def _():
        vt_ref[...] = kv_ref[:, 2].reshape(keys, LANES).astype(F32).T.astype(BF)

    rows = q_ref.shape[0] * q_ref.shape[2]
    queries = q_ref[:, 0].reshape(rows, LANES) * BF(scale)
    key_rows = kv_ref[:, 1].reshape(keys, LANES)
    for item in range(items):
        chosen = jnp.where(item_mask(rows, LANES, item), queries, BF(0))
        scores = nt(key_rows, chosen)
        top = jnp.max(scores, axis=0, keepdims=True)
        raised = jnp.exp(scores - top)
        total = jnp.sum(raised, axis=0, keepdims=True)
        weights = (raised * (1.0 / total)).astype(BF)
        pt_ref[item] = weights
        span = slice(item * HDIM, (item + 1) * HDIM)
        ot_ref[span, :] = nn(vt_ref[span, :], weights)
    o_ref[...] = ot_ref[...].T.astype(BF).reshape(o_ref.shape)


def attend(q, kv, items, scale):
    peers, _, tokens, lanes = q.shape
    rows, keys = peers * tokens, kv.shape[0] * tokens
    step = max(1, min(peers, 256 * 1024 // keys // tokens))
    block = step * tokens
    return call(
        functools.partial(attend_kernel, items, scale),
        "attend",
        [shape((peers, tokens, lanes)), shape((lanes, rows), F32), shape((items, keys, rows))],
        q,
        kv,
        grid=(peers // step,),
        in_specs=[
            pl.BlockSpec((step, 3, tokens, lanes), lambda j: (j, 0, 0, 0)),
            pl.BlockSpec(kv.shape, lambda j: (0, 0, 0, 0)),
        ],
        out_specs=[
            pl.BlockSpec((step, tokens, lanes), lambda j: (j, 0, 0)),
            pl.BlockSpec((lanes, block), lambda j: (0, j)),
            pl.BlockSpec((items, keys, block), lambda j: (0, 0, j)),
        ],
        scratch=[pltpu.VMEM((lanes, keys), BF)],
        limit=24 if keys <= 2048 else 56,
        flops=8 * rows * keys * lanes,
    )


def attend_back_kernel(items, scale, q_ref, kv_ref, d_ref, ot_ref, pt_ref, dq_ref, *rest):
    dkv_ref, (kt_ref, dqt_ref, dk_sum, dv_sum) = rest[:-4], rest[-4:]
    step = pl.program_id(0)
    keys = kv_ref.shape[0] * kv_ref.shape[2]

    @pl.when(step == 0)
    def _():
        kt_ref[...] = (kv_ref[:, 1].reshape(keys, LANES).astype(F32) * scale).T.astype(BF)
        dk_sum[...] = jnp.zeros_like(dk_sum)
        dv_sum[...] = jnp.zeros_like(dv_sum)

    peers, _, tokens, _ = q_ref.shape
    rows = peers * tokens
    queries = q_ref[:, 0].reshape(rows, LANES) * BF(scale)
    grads = d_ref[...].reshape(rows, LANES)
    value_rows = kv_ref[:, 2].reshape(keys, LANES)
    product = grads.astype(F32).T * ot_ref[...]
    for item in range(items):
        span = slice(item * HDIM, (item + 1) * HDIM)
        mask = item_mask(rows, LANES, item)
        grad = jnp.where(mask, grads, BF(0))
        query = jnp.where(mask, queries, BF(0))
        delta = jnp.sum(product[span, :], axis=0, keepdims=True)
        weights = pt_ref[item]
        back = (weights.astype(F32) * (nt(value_rows, grad) - delta)).astype(BF)
        dv_sum[...] += nn(weights, grad)
        dk_sum[...] += nn(back, query)
        dqt_ref[span, :] = nn(kt_ref[span, :], back)
    d_query = dqt_ref[...].T.astype(BF).reshape(peers, tokens, LANES)
    if dkv_ref:
        dq_ref[...] = d_query
    else:
        dq_ref[pl.ds(step * peers, peers), 0] = d_query

    @pl.when(step == pl.num_programs(0) - 1)
    def _():
        for c, total in ((1, dk_sum), (2, dv_sum)):
            total = total[...].reshape(kv_ref.shape[0], tokens, LANES)
            if dkv_ref:
                dkv_ref[0][:, c - 1] = total
            else:
                dq_ref[:, c] = total.astype(BF)


def attend_back(q, kv, d, ot, pt, items, scale):
    peers, _, tokens, lanes = q.shape
    rows, keys = peers * tokens, kv.shape[0] * tokens
    step = max(1, min(peers, 256 * 1024 // keys // tokens))
    block = step * tokens
    if q.shape == kv.shape:
        outs = [shape(q.shape)]
        out_specs = [pl.BlockSpec(q.shape, lambda j: (0, 0, 0, 0))]
    else:
        outs = [shape((peers, tokens, lanes)), shape((kv.shape[0], 2, tokens, lanes), F32)]
        out_specs = [
            pl.BlockSpec((step, tokens, lanes), lambda j: (j, 0, 0)),
            pl.BlockSpec(outs[1].shape, lambda j: (0, 0, 0, 0)),
        ]
    return call(
        functools.partial(attend_back_kernel, items, scale),
        "attend_back",
        outs,
        q,
        kv,
        d,
        ot,
        pt,
        grid=(peers // step,),
        in_specs=[
            pl.BlockSpec((step, 3, tokens, lanes), lambda j: (j, 0, 0, 0)),
            pl.BlockSpec(kv.shape, lambda j: (0, 0, 0, 0)),
            pl.BlockSpec((step, tokens, lanes), lambda j: (j, 0, 0)),
            pl.BlockSpec((lanes, block), lambda j: (0, j)),
            pl.BlockSpec((items, keys, block), lambda j: (0, 0, j)),
        ],
        out_specs=out_specs,
        scratch=[
            pltpu.VMEM((lanes, keys), BF),
            pltpu.VMEM((lanes, block), F32),
            pltpu.VMEM((keys, lanes), F32),
            pltpu.VMEM((keys, lanes), F32),
        ],
        limit=24 if keys <= 2048 else 60,
        flops=16 * rows * keys * lanes,
    )


def unpack(blocks_ref, index, out_ref, base):
    heads = blocks_ref.shape[0]
    for t in range(heads // 2):
        pair = [
            (blocks_ref[2 * t + s] if index is None else blocks_ref[2 * t + s, index]).astype(F32)
            for s in range(2)
        ]
        for item, tile in enumerate(interleave(*pair)):
            out_ref[item * LANES : (item + 1) * LANES, base + t * LANES : base + (t + 1) * LANES] = (
                tile.astype(BF)
            )


def pack(product, out_ref):
    for t in range(product.shape[1] // LANES):
        tile = product[:, t * LANES : (t + 1) * LANES]
        for s, block in enumerate(interleave(tile[:LANES], tile[LANES:])):
            out_ref[2 * t + s] = block.astype(BF)


def project_kernel(o_ref, wo_ref, mixed_ref, branch_ref):
    unpack(o_ref, None, mixed_ref, 0)
    branch_ref[...] = nn(mixed_ref[...], wo_ref[...]).astype(BF)


def forward_kernel(ids_ref, zero_ref, own_ref, got_ref, gains_ref, wu_ref, dact_ref,
                   one_ref, norm_ref, pre_ref, act_ref, *rest):
    turned, (normed_ref, total_ref, hold) = rest[:-3], rest[-3:]
    step = pl.program_id(0)

    @pl.when(step == 0)
    def _():
        hidden = zero_ref[...] + (own_ref[...].astype(F32) + got_ref[...].astype(F32))
        one_ref[...] = hidden
        unit, _ = norm_parts(hidden)
        normed = unit * gains_ref[1:2, :]
        normed_ref[...] = normed.astype(BF)
        emit_turned(normed, ids_ref, turned, hold)
        total_ref[...] = jnp.zeros_like(total_ref)

    pre = nn(normed_ref[...], wu_ref[...])
    chance = 0.5 * (1.0 + lax.erf(pre * (1.0 / math.sqrt(2.0))))
    slope = chance + pre * jnp.exp(-0.5 * pre * pre) * (1.0 / math.sqrt(2.0 * math.pi))
    act_ref[...] = (pre * chance).astype(BF)
    d_pre = (dact_ref[...] * slope).astype(BF)
    pre_ref[...] = d_pre
    total_ref[...] += nt(d_pre, wu_ref[...])

    @pl.when(step == pl.num_programs(0) - 1)
    def _():
        norm_ref[...] = total_ref[...].astype(BF)


def second_kernel(ids_ref, one_ref, two_ref, own_ref, got_ref, gains_ref, wo_ref,
                  d_ref, gain_ref, mixed_ref, *rest):
    turned, hold = rest[:-1], rest[-1]
    unit, inverse = norm_parts(one_ref[...])
    grad = own_ref[...].astype(F32) + got_ref[...].astype(F32)
    back, gain = norm_back(unit, inverse, gains_ref[1:2, :], grad)
    gain_ref[...] = gain
    d_one = two_ref[...] + back
    d_ref[...] = d_one
    pack(nt(d_one.astype(BF), wo_ref[...]), mixed_ref)
    emit_turned(d_one, ids_ref, turned, hold)


def head_kernel(ids_ref, one_ref, own_ref, got_ref, wh_ref, pred_ref, *rest):
    turned, hold = rest[:-1], rest[-1]
    hidden = one_ref[...] + (own_ref[...].astype(F32) + got_ref[...].astype(F32))
    low = hidden.astype(BF)
    for item in range(pred_ref.shape[0]):
        pred_ref[item] = nt(wh_ref[...], low[item * LANES : (item + 1) * LANES])
    emit_turned(hidden, ids_ref, turned, hold)


def third_kernel(back_ref, wq_ref, dqkv_ref, norm_ref):
    width = wq_ref.shape[2]
    total = None
    for c in range(3):
        unpack(back_ref, c, dqkv_ref, c * width)
        part = nt(dqkv_ref[:, c * width : (c + 1) * width], wq_ref[c])
        total = part if total is None else total + part
    norm_ref[...] = total.astype(BF)


def last_kernel(cols, zero_ref, done_ref, own_ref, got_ref, gains_ref, gain_two_ref, patches_ref, we_ref,
                pos_ref, embed_ref, fields_ref, edge_ref, rows_ref):
    unit, inverse = norm_parts(zero_ref[...])
    grad = own_ref[...].astype(F32) + got_ref[...].astype(F32)
    back, gain = norm_back(unit, inverse, gains_ref[0:1, :], grad)
    d_zero = done_ref[...] + back
    low = d_zero.astype(BF)
    items, variables, height = edge_ref.shape
    pos = d_zero[0:LANES]
    for item in range(1, items):
        pos = pos + d_zero[item * LANES : (item + 1) * LANES]
    for k in range(pos_ref.shape[0]):
        width = pos_ref.shape[2]
        pos_ref[k] = pos[:, k * width : (k + 1) * width].astype(BF)
    features = patches_ref.shape[0]
    rows_ref[...] = jnp.zeros_like(rows_ref)
    rows_ref[0:features, :] = nn(patches_ref[...], low)
    rows_ref[features : features + 1, :] = gain
    rows_ref[features + 1 : features + 2, :] = gain_two_ref[...]
    embed_ref[...] = rows_ref[...].T.astype(BF).reshape(embed_ref.shape)
    half = height // PATCH
    row = lax.broadcasted_iota(jnp.int32, (LANES, height), 0)
    lane = lax.broadcasted_iota(jnp.int32, (LANES, height), 1)
    fields_ref[...] = jnp.zeros_like(fields_ref)
    for item in range(items):
        d_patches = nt(we_ref[...], low[item * LANES : (item + 1) * LANES])
        high = d_patches.astype(BF)
        rest = (d_patches - high.astype(F32)).astype(BF)
        for j in range(2):
            total = None
            for a in range(PATCH):
                place = jnp.where(
                    (row // half == j) & (lane == PATCH * (row % half) + a), 1.0, 0.0
                ).astype(BF)
                span = slice(a * 2 * variables, (a + 1) * 2 * variables)
                part = nn(high[span], place) + nn(rest[span], place)
                total = part if total is None else total + part
            for b in range(PATCH):
                block = total[b * variables : (b + 1) * variables]
                column = 2 * j + b - 1
                if column < 0:
                    edge_ref[item] = block.astype(BF)
                else:
                    fields_ref[item, pl.ds(column, variables, stride=cols), :] = block


def grads_kernel(ids_ref, *refs):
    groups, outs, holds = (refs[0:4], refs[4:8]), (refs[8:10], refs[10:12]), refs[12:14]
    for (own, got, b_own, b_got), (send, keep), hold, axis in zip(groups, outs, holds, (1, 2)):
        parts, rows, tokens = own.shape
        product = nn(own[...].reshape(parts * rows, tokens), b_own[...])
        product = product + nn(got[...].reshape(parts * rows, tokens), b_got[...])
        hold[...] = product.astype(BF).reshape(hold.shape)
        side = ids_ref[axis]
        for out, at in ((send, 1 - side), (keep, side)):
            for k in range(parts // 2):
                place = at * (parts // 2) + k if axis == 1 else 2 * k + at
                out[k] = hold[place]


def grads(ids, first, second):
    outs, holds = [], []
    for own, _, b_own, _ in (first, second):
        parts, rows, _ = own.shape
        outs += [shape((parts // 2, rows, b_own.shape[1]))] * 2
        holds.append(pltpu.VMEM((parts, rows, b_own.shape[1]), BF))
    flops = sum(4 * a[0].size * a[2].shape[1] for a in (first, second))
    return call(grads_kernel, "grads", outs, ids, *first, *second, scratch=holds, limit=32, flops=flops)


def fold_kernel(ids_ref, keep_a, got_a, keep_b, got_b, send_a, left_a, send_b, left_b, hold_a, hold_b):
    hold_a[...] = (keep_a[...].astype(F32) + got_a[...].astype(F32)).astype(BF)
    hold_b[...] = (keep_b[...].astype(F32) + got_b[...].astype(F32)).astype(BF)
    near, dp = ids_ref[2], ids_ref[1]
    for out_a, out_b, flip in ((send_a, send_b, True), (left_a, left_b, False)):
        for k in range(2):
            out_a[k] = hold_a[2 * k + (1 - near if flip else near)]
            out_b[k] = hold_b[2 * (1 - dp if flip else dp) + k]


def merge_kernel(ids_ref, keep_a, got_a, keep_b, got_b, send, left, hold):
    width = keep_a.shape[2]
    hold[:, :, 0:width] = (keep_a[...].astype(F32) + got_a[...].astype(F32)).astype(BF)
    hold[:, :, width:] = (keep_b[...].astype(F32) + got_b[...].astype(F32)).astype(BF)
    far = ids_ref[3]
    send[...] = hold[1 - far]
    left[...] = hold[far]


def spread_sum(ids, first, second):
    send_a, keep_a, send_b, keep_b = grads(ids, first, second)
    got_a, got_b = swap(send_a, "dp", 1), swap(send_b, "lon", 2)
    halves = [shape((2, *x.shape[1:])) for x in (keep_a, keep_a, keep_b, keep_b)]
    holds = [pltpu.VMEM(x.shape, BF) for x in (keep_a, keep_b)]
    send_a, keep_a, send_b, keep_b = call(
        fold_kernel, "fold", halves, ids, keep_a, got_a, keep_b, got_b, scratch=holds
    )
    got_a, got_b = swap(send_a, "lon", 2), swap(send_b, "dp", 1)
    rows, width = keep_a.shape[1], keep_a.shape[2] + keep_b.shape[2]
    send, keep = call(
        merge_kernel, "merge", [shape((rows, width))] * 2, ids, keep_a, got_a, keep_b, got_b,
        scratch=[pltpu.VMEM((2, rows, width), BF)],
    )
    return keep.astype(F32) + swap(send, "lon", 4).astype(F32)


def local(
    dataset,
    indices,
    run_count,
    run_mean,
    run_var,
    w_embed,
    pos_embed,
    gains,
    w_qkv,
    w_out,
    w_up,
    w_down,
    w_head,
    cotangent,
):
    items = indices.shape[0]
    variables, height, columns = dataset.shape[1:]
    dp, lon = lax.axis_size("dp"), lax.axis_size("lon")
    everyone = dp * lon
    width = w_embed.shape[1]
    local_width = w_qkv.shape[2]
    heads = local_width // HDIM
    item_tokens = cotangent.shape[1]
    tokens = items * item_tokens
    features = w_embed.shape[0]
    hidden_units = w_up.shape[1]
    scale = 1.0 / math.sqrt(HDIM)
    group, far = heads, lon // heads
    groups = [[group * g + i for i in range(group)] for g in range(far)]
    across = [[i + group * g for g in range(far)] for i in range(group)]
    assert items * HDIM == LANES and item_tokens == LANES and height == LANES and columns == 4
    lon_at, dp_at = lax.axis_index("lon"), lax.axis_index("dp")
    ids = jnp.stack([lon_at % 2, dp_at, lon_at // 2 % 2, lon_at // 4 % 2]).astype(jnp.int32)
    paired = dp == 2 and lon == 8
    parts, rows = width // (2 * (width // everyone)), width // everyone
    turned_shape = (
        [shape((parts, rows, tokens))] * 2 if paired else [shape((width, tokens))]
    )
    turned_hold = pltpu.VMEM((parts, 2, rows, tokens) if paired else (8, LANES), BF)

    fields = jnp.concatenate(
        [lax.dynamic_slice_in_dim(dataset, indices[i], 1, 0) for i in range(items)]
    )
    fields = fields.transpose(0, 1, 3, 2)
    edge = from_behind(fields[:, :, columns - 1].astype(BF), "lon", 1)
    local_count = float(items * height * columns)
    local_mean = jnp.mean(fields, axis=(0, 2, 3))
    local_spread = jnp.sum(jnp.square(fields - local_mean[None, :, None, None]), axis=(0, 2, 3))
    gap = jnp.zeros((HDIM - variables,), F32)
    moments = jnp.concatenate([local_mean, gap, local_spread, gap])
    moments = lax.all_to_all(
        jnp.broadcast_to(moments, (everyone, 1, LANES)), ("dp", "lon"), 0, 0
    ).reshape(everyone, LANES)
    run = jnp.pad(jnp.stack([run_count, run_mean, run_var]), ((0, 5), (0, LANES - variables)))
    we_sorted = (
        w_embed.reshape(variables, PATCH, PATCH, width).transpose(1, 2, 0, 3).reshape(features, width)
    )
    wh_turned = w_head.T

    out = call(
        functools.partial(start_kernel, local_count),
        "start",
        [
            shape((8, LANES), F32),
            shape((tokens, width), F32),
            shape((features, tokens)),
            shape((heads, 3, item_tokens, LANES)),
            *turned_shape,
        ],
        ids, moments, run, fields.reshape(items, variables * columns, height), edge,
        we_sorted, pos_embed, gains, w_qkv,
        scratch=[pltpu.VMEM((LANES, LANES), F32), turned_hold],
        flops=2 * tokens * width * (features + 3 * local_width),
    )
    stats, hidden_zero, patches, packed = out[:4]
    normed_one = out[4:]
    sent = lax.all_to_all(packed, "lon", 0, 0, axis_index_groups=groups if far > 1 else None)
    kv = sent
    if far > 1:
        kv = lax.all_gather(sent, "lon", axis=0, tiled=True, axis_index_groups=across)

    out = call(
        cotangent_kernel,
        "cotangent",
        [
            shape((tokens, width), F32),
            shape((tokens, hidden_units), F32),
            shape((tokens, 2 * LANES)),
            *turned_shape,
        ],
        ids, cotangent.transpose(0, 2, 1), wh_turned, w_down,
        scratch=[turned_hold],
        flops=2 * tokens * width * (features + hidden_units),
    )
    d_two, d_act, grad_pred = out[:3]
    d_two_turned = out[3:]

    attended, attended_t, weights_t = attend(sent, kv, items, scale)
    attended = lax.all_to_all(attended, "lon", 0, 0, axis_index_groups=groups if far > 1 else None)
    mixed, branch = call(
        project_kernel,
        "project",
        [shape((tokens, local_width)), shape((tokens, width))],
        attended, w_out,
        flops=2 * tokens * width * local_width,
    )
    branch_got = swap(branch, "mp", 1)
    block = min(512, hidden_units)
    column = lambda j: (0, j)
    whole = lambda j: (0, 0)
    full = pl.BlockSpec((tokens, width), whole)
    turned_specs = (
        [pl.BlockSpec((parts, rows, tokens), lambda j: (0, 0, 0))] * 2
        if paired
        else [pl.BlockSpec((width, tokens), whole)]
    )
    out = call(
        forward_kernel,
        "forward",
        [
            shape((tokens, width), F32),
            shape((tokens, width)),
            shape((tokens, hidden_units)),
            shape((tokens, hidden_units)),
            *turned_shape,
        ],
        ids, hidden_zero, branch, branch_got, gains, w_up, d_act,
        grid=(hidden_units // block,),
        in_specs=[
            pl.BlockSpec(memory_space=pltpu.SMEM),
            full,
            full,
            full,
            pl.BlockSpec(gains.shape, whole),
            pl.BlockSpec((width, block), column),
            pl.BlockSpec((tokens, block), column),
        ],
        out_specs=[
            full,
            full,
            pl.BlockSpec((tokens, block), column),
            pl.BlockSpec((tokens, block), column),
            *turned_specs,
        ],
        scratch=[pltpu.VMEM((tokens, width), BF), pltpu.VMEM((tokens, width), F32), turned_hold],
        flops=4 * tokens * width * hidden_units,
    )
    hidden_one, d_norm, d_pre, activated = out[:4]
    normed_two = out[4:]
    d_norm_got = swap(d_norm, "mp", 1)

    if paired:
        up_down = spread_sum(
            ids,
            (normed_two[0], swap(normed_two[1], "lon", 1), d_pre, swap(d_pre, "lon", 1)),
            (d_two_turned[0], swap(d_two_turned[1], "lon", 1), activated, swap(activated, "lon", 1)),
        )
        grad_up, grad_down = up_down[:, :hidden_units], up_down[:, hidden_units:]
    else:
        grad_up, grad_down = scatter(nn(normed_two[0], d_pre)), scatter(nn(d_two_turned[0], activated))

    forward = nn(activated, w_down).astype(BF)
    forward_got = swap(forward, "mp", 1)

    out = call(
        second_kernel,
        "second",
        [
            shape((tokens, width), F32),
            shape((1, width), F32),
            shape((heads, item_tokens, LANES)),
            *turned_shape,
        ],
        ids, hidden_one, d_two, d_norm, d_norm_got, gains, w_out,
        scratch=[turned_hold],
        flops=2 * tokens * width * local_width,
    )
    d_one, gain_two, d_mixed = out[:3]
    d_one_turned = out[3:]
    d_heads = lax.all_to_all(d_mixed, "lon", 0, 0, axis_index_groups=groups if far > 1 else None)
    out = call(
        head_kernel,
        "head",
        [shape((items, features, item_tokens), F32), *turned_shape],
        ids, hidden_one, forward, forward_got, wh_turned,
        scratch=[turned_hold],
        flops=2 * tokens * width * features,
    )
    pred, hidden_turned = out[0].transpose(0, 2, 1), out[1:]

    back = attend_back(sent, kv, d_heads, attended_t, weights_t, items, scale)
    if far > 1:
        d_query, d_kv = back
        d_kv = lax.psum_scatter(
            d_kv, "lon", scatter_dimension=0, tiled=True, axis_index_groups=across
        ).astype(BF)
        back = [jnp.concatenate([d_query[:, None], d_kv], axis=1)]
    back = lax.all_to_all(back[0], "lon", 0, 0, axis_index_groups=groups if far > 1 else None)
    d_qkv, d_norm = call(
        third_kernel,
        "third",
        [shape((tokens, 3 * local_width)), shape((tokens, width))],
        back, w_qkv,
        flops=6 * tokens * width * local_width,
    )
    d_norm_got = swap(d_norm, "mp", 1)
    if paired:
        out_head = spread_sum(
            ids,
            (d_one_turned[0], swap(d_one_turned[1], "lon", 1), mixed, swap(mixed, "lon", 1)),
            (hidden_turned[0], swap(hidden_turned[1], "lon", 1), grad_pred, swap(grad_pred, "lon", 1)),
        )
        grad_out, grad_head = out_head[:, :local_width], out_head[:, local_width:]
        side = swap(normed_one[1], "lon", 1)
        d_qkv_got = swap(d_qkv, "lon", 1)
        cut = 3 * local_width // 2
        grad_qkv = spread_sum(
            ids,
            (normed_one[0], side, d_qkv[:, :cut], d_qkv_got[:, :cut]),
            (normed_one[0], side, d_qkv[:, cut:], d_qkv_got[:, cut:]),
        )
    else:
        grad_out, grad_head = scatter(nn(d_one_turned[0], mixed)), scatter(nn(hidden_turned[0], grad_pred))
        grad_qkv = scatter(nn(normed_one[0], d_qkv))

    pos, embed, d_fields, d_edge = call(
        functools.partial(last_kernel, columns),
        "last",
        [
            shape((dp, item_tokens, width // dp)),
            shape((everyone, rows, 2 * LANES)),
            shape((items, variables * columns, height), F32),
            shape((items, variables, height)),
        ],
        hidden_zero, d_one, d_norm, d_norm_got, gains, gain_two, patches, we_sorted,
        scratch=[pltpu.VMEM((2 * LANES, width), F32)],
        flops=4 * tokens * width * features,
    )
    east = from_behind(d_edge, "lon", -1).astype(F32)
    grad_pos = pick(pos, dp_at, 0).astype(F32)
    for k in range(1, dp):
        grad_pos = grad_pos + swap(pick(pos, dp_at ^ k, 0), "dp", k).astype(F32)
    embed = lax.all_to_all(embed, ("dp", "lon"), 0, 0)
    embed = jnp.sum(embed.astype(F32), axis=0)
    d_fields = d_fields.reshape(items, variables, columns, height)
    grad_fields = jnp.concatenate([d_fields[:, :, : columns - 1], east[:, :, None]], axis=2)
    return (
        pred,
        stats[0, :variables],
        stats[1, :variables],
        stats[2, :variables],
        grad_fields.transpose(0, 1, 3, 2),
        embed[:, :features].T,
        grad_pos,
        embed[:, features : features + 2].T,
        grad_qkv.reshape(rows, 3, local_width).transpose(1, 0, 2),
        grad_out.T,
        grad_up,
        grad_down.T,
        grad_head[:, :features],
    )


def solution(mesh):
    in_specs = (
        P(None, None, None, "lon"),
        P("dp"),
        P(),
        P(),
        P(),
        P(),
        P("lon", None),
        P(),
        P(None, None, "mp"),
        P("mp", None),
        P(None, "mp"),
        P("mp", None),
        P(),
        P("dp", "lon", None),
    )
    out_specs = (
        P("dp", "lon", None),
        P(),
        P(),
        P(),
        P("dp", None, None, "lon"),
        P(None, ("dp", "lon")),
        P("lon", "dp"),
        P(None, ("dp", "lon")),
        P(None, ("dp", "lon"), "mp"),
        P("mp", ("dp", "lon")),
        P(("dp", "lon"), "mp"),
        P("mp", ("dp", "lon")),
        P(("dp", "lon"), None),
    )
    return jax.shard_map(local, mesh=mesh, in_specs=in_specs, out_specs=out_specs, check_vma=False)
```

```python
import functools
import math

import jax
import jax.numpy as jnp
from jax import lax
from jax.experimental import pallas as pl
from jax.experimental.pallas import tpu as pltpu
from jax.sharding import PartitionSpec as P

HDIM = 64
PATCH = 2
LANES = 128
NORM_EPS = 1e-06
STAT_EPS = 1e-06
BF = jnp.bfloat16
F32 = jnp.float32
MIB = 2**20


def swap(block, axis, distance):
    route = [(i, i ^ distance) for i in range(lax.axis_size(axis))]
    return lax.ppermute(block, axis, route)


def from_behind(block, axis, distance):
    size = lax.axis_size(axis)
    route = [((i - distance) % size, i) for i in range(size)]
    return lax.ppermute(block, axis, route)


def pick(x, index, axis):
    return lax.dynamic_index_in_dim(x, index, axis, keepdims=False)


def halve(total, dims):
    for axis, bit in dims:
        side = (lax.axis_index(axis) // bit) % 2
        got = swap(pick(total, 1 - side, 0), axis, bit)
        total = (pick(total, side, 0).astype(F32) + got.astype(F32)).astype(BF)
    return total


def scatter(total):
    dp, lon = lax.axis_size("dp"), lax.axis_size("lon")
    dims = []
    for axis, size in (("dp", dp), ("lon", lon)):
        bit = size // 2
        while bit:
            dims.append((axis, bit))
            bit //= 2
    rows, columns = total.shape
    total = total.astype(BF).reshape((2,) * len(dims) + (rows // (dp * lon), columns))
    order = sorted(range(len(dims)), key=lambda i: (dims[i][1] > 1 or dims[i][0] == "dp", i))
    total = total.transpose([*order, len(dims), len(dims) + 1])
    return halve(total, [dims[i] for i in order]).astype(F32)


def nt(a, b):
    return lax.dot_general(a, b, (((1,), (1,)), ((), ())), preferred_element_type=F32)


def nn(a, b):
    return lax.dot_general(a, b, (((1,), (0,)), ((), ())), preferred_element_type=F32)


def item_mask(rows, lanes, item):
    lane = lax.broadcasted_iota(jnp.int32, (rows, lanes), 1)
    return (lane >= item * HDIM) & (lane < (item + 1) * HDIM)


def interleave(first, second):
    low = item_mask(first.shape[0], LANES, 0)
    return (
        jnp.where(low, first, pltpu.roll(second, HDIM, 1)),
        jnp.where(low, pltpu.roll(first, HDIM, 1), second),
    )


def norm_parts(hidden):
    centred = hidden - jnp.mean(hidden, axis=-1, keepdims=True)
    variance = jnp.mean(centred * centred, axis=-1, keepdims=True)
    inverse = lax.rsqrt(variance + NORM_EPS)
    return centred * inverse, inverse


def norm_back(unit, inverse, scaling, grad):
    scaled = grad * scaling
    back = inverse * (
        scaled
        - jnp.mean(scaled, axis=-1, keepdims=True)
        - unit * jnp.mean(scaled * unit, axis=-1, keepdims=True)
    )
    return back, jnp.sum(grad * unit, axis=0, keepdims=True)


def emit_turned(x, ids_ref, outs, hold):
    turned = x.T.astype(BF)
    if len(outs) == 1:
        outs[0][...] = turned
        return
    keep, send = outs
    parts, rows, tokens = keep.shape
    hold[...] = turned.reshape(parts, 2, rows, tokens)
    core = ids_ref[0]
    keep[...] = hold[:, pl.ds(core, 1)].reshape(parts, rows, tokens)
    send[...] = hold[:, pl.ds(1 - core, 1)].reshape(parts, rows, tokens)


class Warm:
    def __init__(self, value):
        self.value = value


def call(body, name, outs, *args, after=(), grid=(), in_specs=None, out_specs=None, scratch=(), limit=24, flops=0):
    vmem = pl.BlockSpec(memory_space=pltpu.VMEM)
    smem = pl.BlockSpec(memory_space=pltpu.SMEM)
    shapes = [o.value if isinstance(o, Warm) else o for o in outs]
    plain = [a.value if isinstance(a, Warm) else a for a in args]
    if in_specs is None:
        in_specs = [smem if a.dtype == jnp.int32 else vmem for a in plain]
    if out_specs is None:
        out_specs = [vmem] * len(outs)
    token = pl.BlockSpec((8, LANES), lambda *at: (0, 0)) if grid else vmem
    nbytes = sum(math.prod(a.shape) * a.dtype.itemsize for a in [*plain, *shapes])
    here, skip, there = len(args), len(after), len(outs)

    def with_token(*refs):
        refs = list(refs)
        refs[here + skip + there][...] = jnp.zeros((8, LANES), F32)
        body(*refs[:here], *refs[here + skip : here + skip + there], *refs[here + skip + there + 1 :])

    def cold(x):
        if isinstance(x, Warm):
            return x.value
        return x if x.dtype == jnp.int32 else pltpu.with_memory_space_constraint(x, pltpu.HBM)

    return pl.pallas_call(
        with_token,
        grid=grid,
        out_shape=[
            *[o.value if isinstance(o, Warm) else pltpu.HBM(o.shape, o.dtype) for o in outs],
            pltpu.HBM((8, LANES), F32),
        ],
        in_specs=[*in_specs, *[pl.BlockSpec(memory_space=pl.ANY)] * skip],
        out_specs=[*out_specs, token],
        scratch_shapes=list(scratch),
        compiler_params=pltpu.CompilerParams(vmem_limit_bytes=limit * MIB),
        cost_estimate=pl.CostEstimate(flops=int(flops), bytes_accessed=nbytes, transcendentals=0),
        name=name,
    )(*[cold(a) for a in args], *[cold(a) for a in after])


def shape(dims, kind=BF):
    return jax.ShapeDtypeStruct(dims, kind)


def warm(dims, kind=BF):
    return Warm(shape(dims, kind))


def feature_order(variables, back):
    features = PATCH * PATCH * variables
    natural = lax.broadcasted_iota(jnp.int32, (features, features), 1 if back else 0)
    sorted_ = lax.broadcasted_iota(jnp.int32, (features, features), 0 if back else 1)
    hit = (natural // 4 == sorted_ % variables) & (natural % 4 == sorted_ // variables)
    return jnp.where(hit, 1.0, 0.0).astype(BF)


def send_pairs(ids_ref, hold, messages):
    if len(messages) == 1:
        messages[0][...] = hold[...]
        return
    for k, message in enumerate(messages):
        message[...] = hold[pl.ds(2 * ids_ref[4 + k], 2)]


def moments_kernel(index_ref, data_ref, fields_ref, edge_ref, moments_ref, turn_ref, sems):
    items, variables, height = edge_ref.shape
    cols = fields_ref.shape[1] // variables
    copies = [
        pltpu.make_async_copy(data_ref.at[index_ref[i]], fields_ref.at[i], sems.at[i])
        for i in range(items)
    ]
    for copy in copies:
        copy.start()
    turn_ref[...] = jnp.zeros_like(turn_ref)
    for copy in copies:
        copy.wait()
    blocks = [
        fields_ref[i, pl.ds(c, variables, stride=cols), :] for i in range(items) for c in range(cols)
    ]
    for i in range(items):
        edge_ref[i] = blocks[i * cols + cols - 1].astype(BF)
    count = float(items * cols * height)
    mean = jnp.sum(sum(blocks), axis=1, keepdims=True) * (1.0 / count)
    spread = jnp.sum(sum(jnp.square(b - mean) for b in blocks), axis=1, keepdims=True)
    turn_ref[0:variables, 0:1] = mean
    turn_ref[HDIM : HDIM + variables, 0:1] = spread
    turned = turn_ref[...].T
    moments_ref[...] = jnp.broadcast_to(turned[0:1, :][None], moments_ref.shape)


def start_kernel(local_count, ids_ref, mom_ref, count_ref, mean_ref, var_ref, fields_ref, edge_ref, we_ref,
                 pos_ref, gains_ref, wq_ref, new_count_ref, new_mean_ref, new_var_ref, hidden_ref, patches_ref,
                 *rest):
    (*outs, column_ref, run_ref, hold, weights, sem, qkv_ref) = rest
    if len(outs) > 2:
        messages, turned = outs[:-2], outs[-2:]
    else:
        messages, turned = outs[:1], outs[1:]
    copy = pltpu.make_async_copy(wq_ref, weights, sem)
    copy.start()
    members = mom_ref.shape[0]
    items, rows, height = fields_ref.shape
    variables = edge_ref.shape[1]
    cols = rows // variables
    half = height // PATCH
    moments = mom_ref[:, 0, :]
    run_ref[...] = jnp.zeros_like(run_ref)
    for k, ref in enumerate((count_ref, mean_ref, var_ref)):
        run_ref[k : k + 1, 0:variables] = ref[...]
    batch_count = local_count * members
    batch_mean = jnp.sum(moments, axis=0, keepdims=True) * (1.0 / members)
    off = moments - batch_mean
    spread = jnp.sum(pltpu.roll(moments, HDIM, 1) + local_count * off * off, axis=0, keepdims=True)
    run_count, run_mean, run_var = (run_ref[k : k + 1, :] for k in range(3))
    new_count = run_count + batch_count
    shift = batch_mean - run_mean
    new_mean = run_mean + shift * (batch_count / new_count)
    new_var = (
        run_var * run_count + spread + shift * shift * (run_count * batch_count / new_count)
    ) / new_count
    new_count_ref[...] = new_count[:, 0:variables]
    new_mean_ref[...] = new_mean[:, 0:variables]
    new_var_ref[...] = new_var[:, 0:variables]
    column_ref[...] = jnp.zeros_like(column_ref)
    column_ref[0:1, :] = new_mean
    column_ref[1:2, :] = lax.rsqrt(new_var + STAT_EPS)
    column = column_ref[...].T
    centre, inverse = column[0:variables, 0:1], column[0:variables, 1:2]

    def scaled(block):
        return ((block - centre) * inverse).astype(BF)

    row = lax.broadcasted_iota(jnp.int32, (2 * height, LANES), 0)
    lane = lax.broadcasted_iota(jnp.int32, (2 * height, LANES), 1)
    sort = [
        jnp.where(
            (row // height == lane // half) & (row % height == PATCH * (lane % half) + a), 1.0, 0.0
        ).astype(BF)
        for a in range(PATCH)
    ]
    natural = feature_order(variables, False)
    hidden = []
    for item in range(items):
        west = scaled(edge_ref[item].astype(F32))
        own = [
            scaled(fields_ref[item, pl.ds(c, variables, stride=cols), :]) for c in range(cols - 1)
        ]
        first = jnp.concatenate([west, own[0]], axis=0)
        second = jnp.concatenate([own[1], own[2]], axis=0)
        both = jnp.concatenate([first, second], axis=1)
        patches = jnp.concatenate([nn(both, sort[a]) for a in range(PATCH)], axis=0)
        patches = nn(natural, patches.astype(BF))
        patches_ref[:, item * LANES : (item + 1) * LANES] = patches.astype(BF)
        hidden.append(nn(patches.T.astype(BF), we_ref[...]) + pos_ref[...].astype(F32))
    hidden = jnp.concatenate(hidden, axis=0)
    hidden_ref[...] = hidden
    unit, _ = norm_parts(hidden)
    normed = unit * gains_ref[0:1, :]
    low = normed.astype(BF)
    emit_turned(normed, ids_ref, turned, hold)
    copy.wait()
    for c in range(3):
        product = nn(low, weights[c])
        for t in range(product.shape[1] // LANES):
            tile = product[:, t * LANES : (t + 1) * LANES]
            a, b = interleave(tile[:LANES], tile[LANES:])
            qkv_ref[2 * t, c] = a.astype(BF)
            qkv_ref[2 * t + 1, c] = b.astype(BF)
    send_pairs(ids_ref, qkv_ref, messages)


def cotangent_kernel(ids_ref, ct_ref, wh_ref, wd_ref, two_ref, act_ref, ct_turned_ref, *rest):
    if rest:
        mine_ref, hold = rest
        hold[...] = wh_ref[...].astype(F32).T.astype(BF).reshape(hold.shape)
        mine_ref[...] = hold[ids_ref[8]]
    grads = []
    for item in range(ct_ref.shape[0]):
        ct = ct_ref[item].T.astype(BF)
        ct_turned_ref[:, item * LANES : (item + 1) * LANES] = ct_ref[item].astype(BF)
        grads.append(nn(ct, wh_ref[...]))
    d_two = jnp.concatenate(grads, axis=0)
    two_ref[...] = d_two
    act_ref[...] = nt(d_two.astype(BF), wd_ref[...])


def attend_kernel(items, scale, q_ref, kv_ref, o_ref, ot_ref, pt_ref, vt_ref):
    keys = kv_ref.shape[0] * kv_ref.shape[2]

    @pl.when(pl.program_id(0) == 0)
    def _():
        vt_ref[...] = kv_ref[:, 2].reshape(keys, LANES).astype(F32).T.astype(BF)

    rows = q_ref.shape[0] * q_ref.shape[2]
    queries = q_ref[:, 0].reshape(rows, LANES) * BF(scale)
    key_rows = kv_ref[:, 1].reshape(keys, LANES)
    for item in range(items):
        chosen = jnp.where(item_mask(rows, LANES, item), queries, BF(0))
        scores = nt(key_rows, chosen)
        top = jnp.max(scores, axis=0, keepdims=True)
        raised = jnp.exp(scores - top)
        total = jnp.sum(raised, axis=0, keepdims=True)
        weights = (raised * (1.0 / total)).astype(BF)
        pt_ref[item] = weights
        span = slice(item * HDIM, (item + 1) * HDIM)
        ot_ref[span, :] = nn(vt_ref[span, :], weights)
    o_ref[...] = ot_ref[...].T.astype(BF).reshape(o_ref.shape)


def attend(q, kv, items, scale, after):
    peers, _, tokens, lanes = q.shape
    rows, keys = peers * tokens, kv.shape[0] * tokens
    step = max(1, min(peers, 256 * 1024 // keys // tokens))
    block = step * tokens
    return call(
        functools.partial(attend_kernel, items, scale),
        "attend",
        [
            shape((peers, tokens, lanes)),
            shape((lanes, rows), F32),
            shape((items, keys, rows)),
        ],
        Warm(q),
        Warm(kv),
        after=after,
        grid=(peers // step,),
        in_specs=[
            pl.BlockSpec((step, 3, tokens, lanes), lambda j: (j, 0, 0, 0)),
            pl.BlockSpec(kv.shape, lambda j: (0, 0, 0, 0)),
        ],
        out_specs=[
            pl.BlockSpec((step, tokens, lanes), lambda j: (j, 0, 0)),
            pl.BlockSpec((lanes, block), lambda j: (0, j)),
            pl.BlockSpec((items, keys, block), lambda j: (0, 0, j)),
        ],
        scratch=[pltpu.VMEM((lanes, keys), BF)],
        limit=24 if keys <= 2048 else 56,
        flops=8 * rows * keys * lanes,
    )


def pair_attend_kernel(items, scale, *refs):
    sources, (*outs, ot_ref, pt_ref, query_rows, key_rows, vt_ref) = refs[:8], refs[8:]
    tokens = sources[0].shape[2]
    step = pl.program_id(1)

    @pl.when(step == 0)
    def _():
        for k, source in enumerate(sources):
            span = slice(k * tokens, (k + 1) * tokens)
            if k < len(outs):
                query_rows[span, :] = source[0, 0] * BF(scale)
            key_rows[span, :] = source[0, 1]
            vt_ref[:, span] = source[0, 2].astype(F32).T.astype(BF)

    block = ot_ref.shape[2]
    queries = query_rows[pl.ds(pl.multiple_of(step * block, block), block), :]
    for item in range(items):
        chosen = jnp.where(item_mask(block, LANES, item), queries, BF(0))
        scores = nt(key_rows[...], chosen)
        top = jnp.max(scores, axis=0, keepdims=True)
        raised = jnp.exp(scores - top)
        total = jnp.sum(raised, axis=0, keepdims=True)
        weights = (raised * (1.0 / total)).astype(BF)
        pt_ref[0, item] = weights
        span = slice(item * HDIM, (item + 1) * HDIM)
        ot_ref[0, span, :] = nn(vt_ref[span, :], weights)
    attended = ot_ref[0].T.astype(BF)
    per = block // tokens
    for j in range(len(outs) // per):

        @pl.when(step == j)
        def _():
            for k in range(per):
                outs[j * per + k][0] = attended[k * tokens : (k + 1) * tokens]


def pair_attend(own, other, items, scale, after):
    _, _, tokens, lanes = own[0].shape
    rows, keys = len(own) * tokens, 2 * len(own) * tokens
    block = rows // 2
    message = pl.BlockSpec((1, tokens, lanes), lambda h, j: (h, 0, 0))
    *outs, ot, pt, token = call(
        functools.partial(pair_attend_kernel, items, scale),
        "attend",
        [
            *[shape((2, tokens, lanes))] * len(own),
            shape((2, lanes, rows), F32),
            shape((2, items, keys, rows)),
        ],
        own[0],
        *[Warm(x) for x in [*own[1:], *other]],
        after=after,
        grid=(2, 2),
        in_specs=[pl.BlockSpec((1, 3, tokens, lanes), lambda h, j: (h, 0, 0, 0))] * (2 * len(own)),
        out_specs=[
            *[message] * len(own),
            pl.BlockSpec((1, lanes, block), lambda h, j: (h, 0, j)),
            pl.BlockSpec((1, items, keys, block), lambda h, j: (h, 0, 0, j)),
        ],
        scratch=[
            pltpu.VMEM((rows, lanes), BF),
            pltpu.VMEM((keys, lanes), BF),
            pltpu.VMEM((lanes, keys), BF),
        ],
        flops=16 * rows * keys * lanes,
    )
    return outs, ot, pt, token


def pair_attend_back_kernel(items, scale, ids_ref, *refs):
    sources, grads_ref, refs = refs[:8], refs[8], refs[9:]
    ot_ref, pt_ref, *outs, cross_ref, query_rows, key_rows, value_rows, kt_ref, grad_rows, dqt_ref, dk_sum, dv_sum = refs
    tokens = sources[0].shape[2]
    step = pl.program_id(1)

    @pl.when(step == 0)
    def _():
        for k, source in enumerate(sources):
            span = slice(k * tokens, (k + 1) * tokens)
            if k < len(outs):
                query_rows[span, :] = source[0, 0] * BF(scale)
                grad_rows[span, :] = grads_ref[ids_ref[4 + k], 0]
            key_rows[span, :] = source[0, 1]
            kt_ref[:, span] = (source[0, 1].astype(F32) * scale).T.astype(BF)
            value_rows[span, :] = source[0, 2]
        dk_sum[...] = jnp.zeros_like(dk_sum)
        dv_sum[...] = jnp.zeros_like(dv_sum)

    block = ot_ref.shape[2]
    at = pl.ds(pl.multiple_of(step * block, block), block)
    queries, grad_block = query_rows[at, :], grad_rows[at, :]
    product = grad_block.astype(F32).T * ot_ref[0]
    for item in range(items):
        span = slice(item * HDIM, (item + 1) * HDIM)
        mask = item_mask(block, LANES, item)
        grad = jnp.where(mask, grad_block, BF(0))
        query = jnp.where(mask, queries, BF(0))
        delta = jnp.sum(product[span, :], axis=0, keepdims=True)
        weights = pt_ref[0, item]
        back = (weights.astype(F32) * (nt(value_rows[...], grad) - delta)).astype(BF)
        dv_sum[...] += nn(weights, grad)
        dk_sum[...] += nn(back, query)
        dqt_ref[span, :] = nn(kt_ref[span, :], back)
    d_query = dqt_ref[...].T.astype(BF)
    per = block // tokens
    for j in range(len(outs) // per):

        @pl.when(step == j)
        def _():
            for k in range(per):
                outs[j * per + k][0, 0] = d_query[k * tokens : (k + 1) * tokens]

    @pl.when(step == pl.num_programs(1) - 1)
    def _():
        for k in range(2 * len(outs)):
            span = slice(k * tokens, (k + 1) * tokens)
            for c, total in ((0, dk_sum), (1, dv_sum)):
                if k < len(outs):
                    outs[k][0, 1 + c] = total[span, :].astype(BF)
                else:
                    cross_ref[k - len(outs), 0, c] = total[span, :].astype(BF)


def pair_attend_back(ids, own, other, d, ot, pt, items, scale, after):
    _, _, tokens, lanes = own[0].shape
    count = len(own)
    rows, keys = count * tokens, 2 * count * tokens
    block = rows // 2
    head = pl.BlockSpec((1, 3, tokens, lanes), lambda h, j: (h, 0, 0, 0))
    *outs, cross, token = call(
        functools.partial(pair_attend_back_kernel, items, scale),
        "attend_back",
        [*[shape((2, 3, tokens, lanes))] * count, shape((count, 2, 2, tokens, lanes))],
        ids, *own, *other, d, ot, pt,
        after=after,
        grid=(2, 2),
        in_specs=[
            pl.BlockSpec(memory_space=pltpu.SMEM),
            *[head] * (2 * count),
            pl.BlockSpec((count, 1, tokens, lanes), lambda h, j: (0, h, 0, 0)),
            pl.BlockSpec((1, lanes, block), lambda h, j: (h, 0, j)),
            pl.BlockSpec((1, items, keys, block), lambda h, j: (h, 0, 0, j)),
        ],
        out_specs=[
            *[head] * count,
            pl.BlockSpec((count, 1, 2, tokens, lanes), lambda h, j: (0, h, 0, 0, 0)),
        ],
        scratch=[
            pltpu.VMEM((rows, lanes), BF),
            pltpu.VMEM((keys, lanes), BF),
            pltpu.VMEM((keys, lanes), BF),
            pltpu.VMEM((lanes, keys), BF),
            pltpu.VMEM((rows, lanes), BF),
            pltpu.VMEM((lanes, block), F32),
            pltpu.VMEM((keys, lanes), F32),
            pltpu.VMEM((keys, lanes), F32),
        ],
        flops=32 * rows * keys * lanes,
    )
    return outs, cross, token


def combine_kernel(*refs):
    count = (len(refs) - 1) // 2
    own, cross_ref, outs = refs[:count], refs[count], refs[count + 1 :]
    for k in range(count):
        outs[k][:, 0] = own[k][:, 0]
        for c in range(2):
            outs[k][:, 1 + c] = plus(own[k].at[:, 1 + c], cross_ref.at[k, :, c])


def attend_back_kernel(items, scale, q_ref, kv_ref, d_ref, ot_ref, pt_ref, dq_ref, *rest):
    dkv_ref, (kt_ref, dqt_ref, dk_sum, dv_sum) = rest[:-4], rest[-4:]
    step = pl.program_id(0)
    keys = kv_ref.shape[0] * kv_ref.shape[2]

    @pl.when(step == 0)
    def _():
        kt_ref[...] = (kv_ref[:, 1].reshape(keys, LANES).astype(F32) * scale).T.astype(BF)
        dk_sum[...] = jnp.zeros_like(dk_sum)
        dv_sum[...] = jnp.zeros_like(dv_sum)

    peers, _, tokens, _ = q_ref.shape
    rows = peers * tokens
    queries = q_ref[:, 0].reshape(rows, LANES) * BF(scale)
    grads = d_ref[...].reshape(rows, LANES)
    value_rows = kv_ref[:, 2].reshape(keys, LANES)
    product = grads.astype(F32).T * ot_ref[...]
    for item in range(items):
        span = slice(item * HDIM, (item + 1) * HDIM)
        mask = item_mask(rows, LANES, item)
        grad = jnp.where(mask, grads, BF(0))
        query = jnp.where(mask, queries, BF(0))
        delta = jnp.sum(product[span, :], axis=0, keepdims=True)
        weights = pt_ref[item]
        back = (weights.astype(F32) * (nt(value_rows, grad) - delta)).astype(BF)
        dv_sum[...] += nn(weights, grad)
        dk_sum[...] += nn(back, query)
        dqt_ref[span, :] = nn(kt_ref[span, :], back)
    d_query = dqt_ref[...].T.astype(BF).reshape(peers, tokens, LANES)
    if dkv_ref:
        dq_ref[...] = d_query
    else:
        dq_ref[pl.ds(step * peers, peers), 0] = d_query

    @pl.when(step == pl.num_programs(0) - 1)
    def _():
        for c, total in ((1, dk_sum), (2, dv_sum)):
            total = total[...].reshape(kv_ref.shape[0], tokens, LANES)
            if dkv_ref:
                dkv_ref[0][:, c - 1] = total
            else:
                dq_ref[:, c] = total.astype(BF)


def attend_back(q, kv, d, ot, pt, items, scale, after):
    peers, _, tokens, lanes = q.shape
    rows, keys = peers * tokens, kv.shape[0] * tokens
    step = max(1, min(peers, 256 * 1024 // keys // tokens))
    block = step * tokens
    if q.shape == kv.shape:
        outs = [shape(q.shape)]
        out_specs = [pl.BlockSpec(q.shape, lambda j: (0, 0, 0, 0))]
    else:
        outs = [shape((peers, tokens, lanes)), shape((kv.shape[0], 2, tokens, lanes), F32)]
        out_specs = [
            pl.BlockSpec((step, tokens, lanes), lambda j: (j, 0, 0)),
            pl.BlockSpec(outs[1].shape, lambda j: (0, 0, 0, 0)),
        ]
    *back, token = call(
        functools.partial(attend_back_kernel, items, scale),
        "attend_back",
        outs,
        Warm(q),
        Warm(kv),
        d,
        ot,
        pt,
        after=after,
        grid=(peers // step,),
        in_specs=[
            pl.BlockSpec((step, 3, tokens, lanes), lambda j: (j, 0, 0, 0)),
            pl.BlockSpec(kv.shape, lambda j: (0, 0, 0, 0)),
            pl.BlockSpec((step, tokens, lanes), lambda j: (j, 0, 0)),
            pl.BlockSpec((lanes, block), lambda j: (0, j)),
            pl.BlockSpec((items, keys, block), lambda j: (0, 0, j)),
        ],
        out_specs=out_specs,
        scratch=[
            pltpu.VMEM((lanes, keys), BF),
            pltpu.VMEM((lanes, block), F32),
            pltpu.VMEM((keys, lanes), F32),
            pltpu.VMEM((keys, lanes), F32),
        ],
        limit=24 if keys <= 2048 else 60,
        flops=16 * rows * keys * lanes,
    )
    return back, token


def unpack(ids_ref, sources, index, out_ref, base):
    several = len(sources) > 1
    count = len(sources) if several else sources[0].shape[0] // 2
    for t in range(count):
        source, head = (sources[t], 0) if several else (sources[0], 2 * t)
        pair = [
            (source[head + s] if index is None else source[head + s, index]).astype(F32) for s in range(2)
        ]
        at = base + (pl.multiple_of(ids_ref[4 + t] * LANES, LANES) if several else t * LANES)
        for item, tile in enumerate(interleave(*pair)):
            out_ref[item * LANES : (item + 1) * LANES, pl.ds(at, LANES)] = tile.astype(BF)


def pack(product, out_ref):
    for t in range(product.shape[1] // LANES):
        tile = product[:, t * LANES : (t + 1) * LANES]
        for s, block in enumerate(interleave(tile[:LANES], tile[LANES:])):
            out_ref[2 * t + s] = block.astype(BF)


def project_kernel(ids_ref, *refs):
    *sources, wo_ref, mixed_ref, branch_ref = refs
    unpack(ids_ref, sources, None, mixed_ref, 0)
    branch_ref[...] = nn(mixed_ref[...], wo_ref[...]).astype(BF)


def forward_kernel(ids_ref, zero_ref, own_ref, got_ref, gains_ref, wu_ref, dact_ref,
                   one_ref, copy_ref, norm_ref, pre_ref, act_ref, other_ref, *rest):
    turned, (normed_ref, total_ref, hold) = rest[:-3], rest[-3:]
    step = pl.program_id(0)

    @pl.when(step == 0)
    def _():
        hidden = zero_ref[...] + (own_ref[...].astype(F32) + got_ref[...].astype(F32))
        one_ref[...] = hidden
        copy_ref[...] = hidden
        unit, _ = norm_parts(hidden)
        normed = unit * gains_ref[1:2, :]
        normed_ref[...] = normed.astype(BF)
        emit_turned(normed, ids_ref, turned, hold)
        total_ref[...] = jnp.zeros_like(total_ref)

    pre = nn(normed_ref[...], wu_ref[...])
    chance = 0.5 * (1.0 + lax.erf(pre * (1.0 / math.sqrt(2.0))))
    slope = chance + pre * jnp.exp(-0.5 * pre * pre) * (1.0 / math.sqrt(2.0 * math.pi))
    activated = (pre * chance).astype(BF)
    act_ref[0] = activated
    block = activated.shape[1]
    per_half = other_ref.shape[1] // block

    @pl.when(step // per_half == 1 - ids_ref[0])
    def _():
        at = pl.multiple_of(step % per_half * block, LANES)
        other_ref[:, pl.ds(at, block)] = activated

    d_pre = (dact_ref[...] * slope).astype(BF)
    pre_ref[...] = d_pre
    total_ref[...] += nt(d_pre, wu_ref[...])

    @pl.when(step == pl.num_programs(0) - 1)
    def _():
        norm_ref[...] = total_ref[...].astype(BF)


def second_kernel(ids_ref, one_ref, two_ref, own_ref, got_ref, gains_ref, wo_ref, d_ref, gain_ref, *rest):
    heads_ref, *turned, hold = rest
    unit, inverse = norm_parts(one_ref[...])
    grad = own_ref[...].astype(F32) + got_ref[...].astype(F32)
    back, gain = norm_back(unit, inverse, gains_ref[1:2, :], grad)
    gain_ref[...] = gain
    d_one = two_ref[...] + back
    d_ref[...] = d_one
    pack(nt(d_one.astype(BF), wo_ref[...]), heads_ref)
    emit_turned(d_one, ids_ref, turned, hold)


def head_kernel(ids_ref, one_ref, own_ref, got_ref, wh_ref, pred_ref, *rest):
    turned, hold = rest[:-1], rest[-1]
    hidden = one_ref[...] + (own_ref[...].astype(F32) + got_ref[...].astype(F32))
    low = hidden.astype(BF)
    for item in range(pred_ref.shape[0]):
        pred_ref[item] = nt(wh_ref[...], low[item * LANES : (item + 1) * LANES])
    emit_turned(hidden, ids_ref, turned, hold)


def third_kernel(count, ids_ref, *refs):
    sources, (wq_ref, dqkv_ref, norm_ref) = refs[:count], refs[count:]
    width = wq_ref.shape[2]
    total = None
    for c in range(3):
        unpack(ids_ref, sources, c, dqkv_ref, c * width)
        part = nt(dqkv_ref[:, c * width : (c + 1) * width], wq_ref[c])
        total = part if total is None else total + part
    norm_ref[...] = total.astype(BF)


def last_kernel(cols, ids_ref, zero_ref, done_ref, own_ref, got_ref, gains_ref, gain_two_ref, patches_ref, we_ref,
                pos_send, pos_keep, fields_ref, edge_ref, *rest):
    embed, (rows_ref, pos_ref, hold) = rest[:-3], rest[-3:]
    unit, inverse = norm_parts(zero_ref[...])
    grad = own_ref[...].astype(F32) + got_ref[...].astype(F32)
    back, gain = norm_back(unit, inverse, gains_ref[0:1, :], grad)
    d_zero = done_ref[...] + back
    low = d_zero.astype(BF)
    items, variables, height = edge_ref.shape
    pos = d_zero[0:LANES]
    for item in range(1, items):
        pos = pos + d_zero[item * LANES : (item + 1) * LANES]
    width = pos_ref.shape[2]
    for k in range(2):
        pos_ref[k] = pos[:, k * width : (k + 1) * width].astype(BF)
    pos_send[...] = pos_ref[1 - ids_ref[1]]
    pos_keep[...] = pos_ref[ids_ref[1]]
    features = patches_ref.shape[0]
    rows_ref[...] = jnp.zeros_like(rows_ref)
    rows_ref[0:features, :] = nn(patches_ref[...], low)
    rows_ref[features : features + 1, :] = gain
    rows_ref[features + 1 : features + 2, :] = gain_two_ref[...]
    emit_turned(rows_ref[...], ids_ref, embed, hold)
    half = height // PATCH
    row = lax.broadcasted_iota(jnp.int32, (LANES, height), 0)
    lane = lax.broadcasted_iota(jnp.int32, (LANES, height), 1)
    fields_ref[...] = jnp.zeros_like(fields_ref)
    order = feature_order(variables, True)
    for item in range(items):
        d_patches = nt(we_ref[...], low[item * LANES : (item + 1) * LANES])
        high = d_patches.astype(BF)
        rest = (d_patches - high.astype(F32)).astype(BF)
        high, rest = nn(order, high).astype(BF), nn(order, rest).astype(BF)
        for j in range(2):
            total = None
            for a in range(PATCH):
                place = jnp.where(
                    (row // half == j) & (lane == PATCH * (row % half) + a), 1.0, 0.0
                ).astype(BF)
                span = slice(a * 2 * variables, (a + 1) * 2 * variables)
                part = nn(high[span], place) + nn(rest[span], place)
                total = part if total is None else total + part
            for b in range(PATCH):
                block = total[b * variables : (b + 1) * variables]
                column = 2 * j + b - 1
                if column < 0:
                    edge_ref[item] = block.astype(BF)
                else:
                    fields_ref[item, pl.ds(column, variables, stride=cols), :] = block


def down_kernel(act_ref, wd_ref, out_ref):
    width = act_ref.shape[2]
    total = nn(act_ref[0], wd_ref[0:width, :]) + nn(act_ref[1], wd_ref[width:, :])
    out_ref[...] = total.astype(BF)


def pin(xs, after):
    def body(*refs):
        pass

    anywhere = pl.BlockSpec(memory_space=pl.ANY)
    several = isinstance(xs, (list, tuple))
    xs = list(xs) if several else [xs]
    out = pl.pallas_call(
        body,
        out_shape=[pltpu.HBM(x.shape, x.dtype) for x in xs],
        in_specs=[anywhere] * (len(xs) + len(after)),
        out_specs=[anywhere] * len(xs),
        input_output_aliases={k: k for k in range(len(xs))},
        name="pin",
    )(*[pltpu.with_memory_space_constraint(x, pltpu.HBM) for x in xs], *after)
    return out if several else out[0]


def product_of(own, got, b_own, b_got):
    parts, rows, tokens = own.shape
    total = nn(own[...].reshape(parts * rows, tokens), b_own)
    return total + nn(got[...].reshape(parts * rows, tokens), b_got)


def split_dp(ids_ref, hold, send, keep, columns):
    half = hold.shape[0] // 2
    for out, at in ((send, 1 - ids_ref[1]), (keep, ids_ref[1])):
        for k in range(half):
            out[k, :, 0:columns] = hold[at * half + k]


def split_near(ids_ref, hold, send, keep, columns):
    for out, at in ((send, 1 - ids_ref[2]), (keep, ids_ref[2])):
        for k in range(hold.shape[0] // 2):
            out[k, :, 0:columns] = hold[2 * k + at]


def plus(a, b):
    return (a[...].astype(F32) + b[...].astype(F32)).astype(BF)


def grads_ff_kernel(ids_ref, at_own, at_got, pre_own, pre_got, ct_own, ct_got, act_own, act_got,
                    send_a, keep_a, send_b, keep_b, hold, inner):
    parts, rows, total = hold.shape
    columns = total - keep_b.shape[2]
    product = product_of(at_own, at_got, pre_own[...], pre_got[...])
    hold[...] = product.astype(BF).reshape(hold.shape)
    split_dp(ids_ref, hold.at[:, :, 0:columns], send_a, keep_a, columns)
    split_near(ids_ref, hold.at[:, :, columns:], send_b, keep_b, total - columns)
    product = (nn(ct_own[...], act_own[ids_ref[0]]) + nn(ct_got[...], act_got[...])).astype(BF)
    tiles, groups = inner.shape[1], inner.shape[3] // LANES
    for k in range(2):
        for q in range(tiles):
            for g in range(groups):
                inner[k, q, :, g * LANES : (g + 1) * LANES] = product[
                    g * rows : (g + 1) * rows, (k * tiles + q) * LANES : (k * tiles + q + 1) * LANES
                ]
    for q in range(tiles):
        send_a[q, :, columns:] = inner[1 - ids_ref[1], q]
        keep_a[q, :, columns:] = inner[ids_ref[1], q]


def fold_ff_kernel(ids_ref, keep_a, got_a, keep_b, got_b, send_a, left_a, send_b, left_b, hold, hold_b):
    columns = hold.shape[2]
    extra = keep_a.shape[2] - columns
    hold[...] = plus(keep_a.at[:, :, 0:columns], got_a.at[:, :, 0:columns])
    split_near(ids_ref, hold, send_a, left_a, columns)
    for q in range(keep_a.shape[0]):
        total = plus(keep_a.at[q, :, columns:], got_a.at[q, :, columns:])
        at = columns + q % 2 * extra
        for out in (send_a, left_a):
            out[q // 2, :, at : at + extra] = total
    hold_b[...] = plus(keep_b, got_b)
    split_dp(ids_ref, hold_b, send_b, left_b, hold_b.shape[2])


def merge_ff_kernel(ids_ref, keep_a, got_a, keep_b, got_b, send, left, hold):
    columns = hold.shape[2] - keep_b.shape[2]
    extra = keep_a.shape[2] - columns
    hold[:, :, 0:columns] = plus(keep_a.at[:, :, 0:columns], got_a.at[:, :, 0:columns])
    hold[:, :, columns:] = plus(keep_b, got_b)
    far = ids_ref[3]
    width = hold.shape[2]
    send[:, 0:width] = hold[1 - far]
    left[:, 0:width] = hold[far]
    for k in range(2):
        total = plus(keep_a.at[k, :, columns:], got_a.at[k, :, columns:])
        at = width + k * extra
        for out in (send, left):
            out[:, at : at + extra] = total


def grads_oh_kernel(ids_ref, one_own, one_got, mixed_own, mixed_got, two_own, two_got, ct_own, ct_got,
                    send, keep, hold):
    width, features = mixed_own.shape[1], ct_own.shape[0]
    shape3 = hold.shape[:2]
    product = product_of(one_own, one_got, mixed_own[...], mixed_got[...])
    hold[:, :, 0:width] = product.astype(BF).reshape(*shape3, width)
    hold[:, :, width:] = jnp.zeros((*shape3, hold.shape[2] - width), BF)
    product = product_of(
        two_own, two_got, ct_own[...].astype(F32).T.astype(BF), ct_got[...].astype(F32).T.astype(BF)
    )
    hold[:, :, width : width + features] = product.astype(BF).reshape(*shape3, features)
    split_dp(ids_ref, hold, send, keep, hold.shape[2])


def grads_q_kernel(ids_ref, at_own, at_got, b_own, b_got, send_a, keep_a, send_b, keep_b, hold):
    cut, total = keep_a.shape[2], hold.shape[2]
    hold[...] = product_of(at_own, at_got, b_own[...], b_got[...]).astype(BF).reshape(hold.shape)
    split_dp(ids_ref, hold.at[:, :, 0:cut], send_a, keep_a, cut)
    split_near(ids_ref, hold.at[:, :, cut:], send_b, keep_b, total - cut)


def fold_q_kernel(ids_ref, keep_a, got_a, keep_b, got_b, up_keep, up_got, oh_keep, oh_got, embed_own, embed_got,
                  send_a, left_a, send_b, left_b, send_o, left_o, hold_a, hold_b, hold_o, hold_e):
    hold_a[...] = plus(keep_a, got_a)
    split_near(ids_ref, hold_a, send_a, left_a, hold_a.shape[2])
    hold_b[...] = plus(keep_b, got_b)
    columns = hold_b.shape[2]
    split_dp(ids_ref, hold_b, send_b, left_b, columns)
    hold_o[...] = plus(oh_keep, oh_got)
    split_near(ids_ref, hold_o, send_o, left_o, hold_o.shape[2])
    hold_e[...] = plus(embed_own, embed_got)
    width = hold_e.shape[2]
    for out, at in ((send_b, 1 - ids_ref[1]), (left_b, ids_ref[1])):
        for k in range(4):
            start = columns + k % 2 * width
            out[k // 2, :, start : start + width] = hold_e[4 * at + k]
    start = columns + 2 * width
    half = send_b.shape[2] - start
    for k in range(2):
        at = up_keep.shape[1] - (2 - k) * half
        total = plus(up_keep.at[:, at : at + half], up_got.at[:, at : at + half])
        for out in (send_b, left_b):
            out[k, :, start:] = total


def merge_q_kernel(ids_ref, keep_a, got_a, keep_b, got_b, oh_keep, oh_got, send, left, pair_ref, *rest):
    *embeds, hold, hold_e = rest
    width = embeds[0].shape[1]
    half = pair_ref.shape[2] // 2
    first = keep_a.shape[2]
    columns = keep_b.shape[2] - half - 2 * width
    hold[:, :, 0:first] = plus(keep_a, got_a)
    hold[:, :, first : first + columns] = plus(keep_b.at[:, :, 0:columns], got_b.at[:, :, 0:columns])
    hold[:, :, first + columns :] = plus(oh_keep, oh_got)
    far, near = ids_ref[3], ids_ref[2]
    send[...] = hold[1 - far]
    left[...] = hold[far]
    for k in range(2):
        span = slice(k * half, (k + 1) * half)
        pair_ref[0, :, span] = keep_b[k, :, columns + 2 * width :]
        pair_ref[1, :, span] = got_b[k, :, columns + 2 * width :]
    for k in range(4):
        span = slice(columns + k % 2 * width, columns + (k % 2 + 1) * width)
        hold_e[k] = plus(keep_b.at[k // 2, :, span], got_b.at[k // 2, :, span])
    for out, at in zip(
        embeds, (2 * far + near, 2 * far + 1 - near, 2 * (1 - far) + near, 2 * (1 - far) + 1 - near)
    ):
        out[...] = hold_e[at]


def expand(ids_ref, rows_ref, pair_own, pair_got, out_ref, block):
    rows = rows_ref.shape[0]
    groups = block.shape[0] // rows
    tiles = block.shape[1] // LANES
    for a, b in ((0, 0), (0, 1), (1, 0), (1, 1)):
        source = pair_got if a else pair_own
        for q in range(tiles):
            for g in range(groups):
                at = (q * groups + g) * LANES
                block[g * rows : (g + 1) * rows, q * LANES : (q + 1) * LANES] = source[b, :, at : at + LANES]
        core, dp = (1 - ids_ref[0] if a else ids_ref[0]), (1 - ids_ref[1] if b else ids_ref[1])
        at = pl.multiple_of((core * 2 + dp) * block.shape[1], LANES)
        out_ref[:, pl.ds(at, block.shape[1])] = nn(rows_ref[...], block[...])


def insert_east(cols, fields_ref, east_ref, out_ref):
    variables = east_ref.shape[1]
    out_ref[...] = fields_ref[...]
    for item in range(east_ref.shape[0]):
        out_ref[item, pl.ds(cols - 1, variables, stride=cols), :] = east_ref[item].astype(F32)


def close_kernel(cols, ids_ref, fields_ref, east_ref, pos_ref, pos_got_ref, *refs):
    outs = refs
    if len(refs) > 2:
        (up_ref, up_got_ref, rows_ref, pair_own, pair_got), outs, block = refs[:5], refs[5:-1], refs[-1]
        width = outs[2].shape[1]
        outs[2][...] = up_ref[:, 0:width].astype(F32) + up_got_ref[:, 0:width].astype(F32)
        expand(ids_ref, rows_ref, pair_own, pair_got, outs[3], block)
    insert_east(cols, fields_ref, east_ref, outs[0])
    outs[1][...] = pos_ref[...].astype(F32) + pos_got_ref[...].astype(F32)


def end_kernel(count, *refs):
    parts, refs = refs[:count], refs[count:]
    if len(refs) > 2:
        (keep_ref, got_ref), refs = refs[:2], refs[2:]
        out_ref, head_ref, grad_ref = refs[2:]
        both = keep_ref[...].astype(F32) + got_ref[...].astype(F32)
        width = grad_ref.shape[2]
        for c in range(3):
            grad_ref[c] = both[:, c * width : (c + 1) * width]
        out_ref[...] = both[:, 3 * width : 4 * width]
        head_ref[...] = both[:, 4 * width : 4 * width + head_ref.shape[1]]
    parts = [parts[0].at[k] for k in range(parts[0].shape[0])] if count == 1 else parts
    total = parts[0][...].astype(F32)
    for part in parts[1:]:
        total = total + part[...].astype(F32)
    features = refs[0].shape[1]
    refs[0][...] = total[:, 0:features]
    refs[1][...] = total[:, LANES:].T[features - LANES : features - LANES + 2, :]


def local(
    dataset,
    indices,
    run_count,
    run_mean,
    run_var,
    w_embed,
    pos_embed,
    gains,
    w_qkv,
    w_out,
    w_up,
    w_down,
    w_head,
    cotangent,
):
    items = indices.shape[0]
    variables, height, columns = dataset.shape[1:]
    dp, lon = lax.axis_size("dp"), lax.axis_size("lon")
    everyone = dp * lon
    width = w_embed.shape[1]
    local_width = w_qkv.shape[2]
    heads = local_width // HDIM
    item_tokens = cotangent.shape[1]
    tokens = items * item_tokens
    features = w_embed.shape[0]
    hidden_units = w_up.shape[1]
    scale = 1.0 / math.sqrt(HDIM)
    group, far = heads, lon // heads
    groups = [[group * g + i for i in range(group)] for g in range(far)]
    across = [[i + group * g for g in range(far)] for i in range(group)]
    assert items * HDIM == LANES and item_tokens == LANES and height == LANES and columns == 4
    lon_at, dp_at = lax.axis_index("lon"), lax.axis_index("dp")
    ids = [lon_at % 2, dp_at, lon_at // 2 % 2, lon_at // 4 % 2, *[lon_at // 2 ^ k for k in range(4)], dp_at * lon + lon_at]
    ids = jnp.stack(ids).astype(jnp.int32)
    paired = dp == 2 and lon == 8
    parts, rows = width // (2 * (width // everyone)), width // everyone
    turned_shape = (
        [shape((parts, rows, tokens))] * 2 if paired else [shape((width, tokens))]
    )
    turned_hold = pltpu.VMEM((parts, 2, rows, tokens) if paired else (8, LANES), BF)

    alone = dict(axis_index_groups=groups) if far > 1 else {}

    vmem, smem = pl.BlockSpec(memory_space=pltpu.VMEM), pl.BlockSpec(memory_space=pltpu.SMEM)
    assert dp == 2

    data = dataset.transpose(0, 1, 3, 2).reshape(dataset.shape[0], variables * columns, height)
    fields, edge, moments, _ = call(
        moments_kernel,
        "moments",
        [
            warm((items, variables * columns, height), F32),
            warm((items, variables, height)),
            warm((everyone, 8, LANES), F32),
        ],
        indices, data,
        in_specs=[pl.BlockSpec(memory_space=pltpu.SMEM), pl.BlockSpec(memory_space=pl.ANY)],
        scratch=[pltpu.VMEM((LANES, LANES), F32), pltpu.SemaphoreType.DMA((items,))],
    )
    edge = from_behind(edge, "lon", 1)
    moments = lax.all_to_all(moments, ("dp", "lon"), 0, 0)
    wh_turned = w_head.T

    out = call(
        functools.partial(start_kernel, float(items * height * columns)),
        "start",
        [
            *[shape((1, variables), F32)] * 3,
            shape((tokens, width), F32),
            shape((features, tokens)),
            *([shape((2, 3, item_tokens, LANES))] * 4 if paired else [shape((heads, 3, item_tokens, LANES))]),
            *turned_shape,
        ],
        ids, Warm(moments), *[r.reshape(1, variables) for r in (run_count, run_mean, run_var)],
        Warm(fields), Warm(edge), w_embed, pos_embed, gains, w_qkv,
        in_specs=[smem, *[vmem] * 9, pl.BlockSpec(memory_space=pl.ANY)],
        scratch=[
            pltpu.VMEM((LANES, LANES), F32),
            pltpu.VMEM((8, LANES), F32),
            turned_hold,
            pltpu.VMEM(w_qkv.shape, BF),
            pltpu.SemaphoreType.DMA,
            pltpu.VMEM((heads, 3, item_tokens, LANES), BF),
        ],
        flops=2 * tokens * width * (features + 3 * local_width),
    )
    count = 4 if paired else 1
    stats, (hidden_zero, patches), packed = out[:3], out[3:5], out[5 : 5 + count]
    normed_one, token = out[5 + count : -1], out[-1]

    def along(messages):
        return [messages[0], *[swap(messages[k], "lon", 2 * k) for k in range(1, count)]]

    if paired:
        own = along(packed)
    else:
        sent = lax.all_to_all(packed[0], "lon", 0, 0, **alone)
        kv = sent
        if far > 1:
            kv = lax.all_gather(sent, "lon", axis=0, tiled=True, axis_index_groups=across)

    d_two, d_act, ct_turned, *mine, token = call(
        cotangent_kernel,
        "cotangent",
        [
            shape((tokens, width), F32),
            shape((tokens, hidden_units), F32),
            shape((features, tokens)),
            *[shape((rows, features))] * paired,
        ],
        ids, cotangent.transpose(0, 2, 1), wh_turned, w_down,
        after=[token],
        scratch=[pltpu.VMEM((everyone, rows, features), BF)] * paired,
        flops=2 * tokens * width * (features + hidden_units),
    )

    if paired:
        ct_got = swap(ct_turned, "lon", 1)
        own[0] = pin(own[0], [token])
        other = [swap(x, "lon", 1) for x in own]
    if paired:
        attended, attended_t, weights_t, token = pair_attend(own, other, items, scale, [token])
        attended = along(attended)
    else:
        attended, attended_t, weights_t, token = attend(sent, kv, items, scale, [token])
        attended = [lax.all_to_all(attended, "lon", 0, 0, **alone)]
    mixed, branch, token = call(
        project_kernel,
        "project",
        [shape((tokens, local_width)), warm((tokens, width))],
        ids, attended[0], *[Warm(x) for x in attended[1:]], Warm(w_out),
        after=[token],
        flops=2 * tokens * width * local_width,
    )
    branch_got = swap(branch, "mp", 1)
    block = min(512, hidden_units // 2)
    per_half = hidden_units // 2 // block
    column = lambda j: (0, j)
    whole = lambda j: (0, 0)
    full = pl.BlockSpec((tokens, width), whole)
    turned_specs = (
        [pl.BlockSpec((parts, rows, tokens), lambda j: (0, 0, 0))] * 2
        if paired
        else [pl.BlockSpec((width, tokens), whole)]
    )
    out = call(
        forward_kernel,
        "forward",
        [
            warm((tokens, width), F32),
            shape((tokens, width), F32),
            warm((tokens, width)),
            shape((tokens, hidden_units)),
            shape((2, tokens, hidden_units // 2)),
            shape((tokens, hidden_units // 2)),
            *turned_shape,
        ],
        ids, Warm(hidden_zero), Warm(branch), Warm(branch_got), gains, Warm(w_up), Warm(d_act),
        after=[token],
        grid=(hidden_units // block,),
        in_specs=[
            pl.BlockSpec(memory_space=pltpu.SMEM),
            full,
            full,
            full,
            pl.BlockSpec(gains.shape, whole),
            pl.BlockSpec((width, block), column),
            pl.BlockSpec((tokens, block), column),
        ],
        out_specs=[
            full,
            full,
            full,
            pl.BlockSpec((tokens, block), column),
            pl.BlockSpec((1, tokens, block), lambda j: (j // per_half, 0, j % per_half)),
            pl.BlockSpec((tokens, hidden_units // 2), whole),
            *turned_specs,
        ],
        scratch=[pltpu.VMEM((tokens, width), BF), pltpu.VMEM((tokens, width), F32), turned_hold],
        flops=4 * tokens * width * hidden_units,
    )
    hidden_one, hidden_copy, d_norm, d_pre, activated, act_send = out[:6]
    normed_two, token = out[6:-1], out[-1]
    d_norm_got = swap(d_norm, "mp", 1)
    half = hidden_units // 2
    if paired:
        inner_columns = features // rows * LANES
        first = half - LANES
        out_a = shape((parts // 2, rows, first + inner_columns))
        out_b = shape((parts // 2, rows, hidden_units - first))
        send_a, keep_a, send_b, keep_b, token = call(
            grads_ff_kernel,
            "grads_ff",
            [out_a, out_a, out_b, out_b],
            ids, normed_two[0], Warm(swap(normed_two[1], "lon", 1)), d_pre, Warm(swap(d_pre, "lon", 1)),
            ct_turned, Warm(ct_got), activated, Warm(swap(act_send, "lon", 1)),
            after=[token],
            scratch=[
                pltpu.VMEM((parts, rows, hidden_units), BF),
                pltpu.VMEM((2, parts // 2, rows, inner_columns), BF),
            ],
            limit=32,
            flops=2 * tokens * (width + features) * hidden_units,
        )
        got_a, got_b = swap(send_a, "dp", 1), swap(send_b, "lon", 2)
    forward, token = call(
        down_kernel,
        "down",
        [shape((tokens, width))],
        activated, w_down,
        after=[token],
        flops=2 * tokens * width * hidden_units,
    )

    out = call(
        second_kernel,
        "second",
        [
            shape((tokens, width), F32),
            shape((1, width), F32),
            shape((heads, item_tokens, LANES)),
            *turned_shape,
        ],
        ids, Warm(hidden_one), Warm(d_two), Warm(d_norm), Warm(d_norm_got), gains, Warm(w_out),
        after=[token],
        scratch=[turned_hold],
        flops=2 * tokens * width * local_width,
    )
    d_one, gain_two, d_mixed = out[0], out[1], out[2:3]
    d_one_turned, token = out[3:-1], out[-1]
    if paired:
        chips = [[2 * k + c for k in range(lon // 2)] for c in range(2)]
        d_heads = lax.all_to_all(
            d_mixed[0].reshape(lon // 2, 2, item_tokens, LANES), "lon", 0, 0, axis_index_groups=chips
        )
    else:
        d_heads = lax.all_to_all(d_mixed[0], "lon", 0, 0, **alone)
    forward_got = swap(forward, "mp", 1)
    if paired:
        out_a = shape((2, rows, first + 2 * inner_columns))
        out_b = shape((2, rows, hidden_units - first))
        send_a, keep_a, send_b, keep_b, token = call(
            fold_ff_kernel,
            "fold_ff",
            [out_a, out_a, out_b, out_b],
            ids, keep_a, Warm(got_a), keep_b, Warm(got_b),
            after=[token],
            scratch=[
                pltpu.VMEM((parts // 2, rows, first), BF),
                pltpu.VMEM((parts // 2, rows, hidden_units - first), BF),
            ],
        )
        send_a, send_b = pin([send_a, send_b], [d_heads])
        got_a, got_b = swap(send_a, "lon", 2), swap(send_b, "dp", 1)

    if paired:
        back, cross, token = pair_attend_back(
            ids, own, other, d_heads, attended_t, weights_t, items, scale, [token]
        )
        *back, token = call(
            combine_kernel,
            "combine",
            [shape(x.shape) for x in back],
            *back, Warm(swap(pin(cross, [got_a, got_b, forward_got]), "lon", 1)),
            after=[token],
        )
        back = along(back)
    else:
        back, token = attend_back(sent, kv, d_heads, attended_t, weights_t, items, scale, [token])
        if far > 1:
            d_query, d_kv = back
            d_kv = lax.psum_scatter(
                d_kv, "lon", scatter_dimension=0, tiled=True, axis_index_groups=across
            ).astype(BF)
            back = [jnp.concatenate([d_query[:, None], d_kv], axis=1)]
        back = [lax.all_to_all(back[0], "lon", 0, 0, **alone)]
    out = call(
        head_kernel,
        "head",
        [shape((items, features, item_tokens), F32), *turned_shape],
        ids, hidden_copy, forward, Warm(forward_got), wh_turned,
        after=[token],
        scratch=[turned_hold],
        flops=2 * tokens * width * features,
    )
    pred, hidden_turned, token = out[0].transpose(0, 2, 1), list(out[1:-1]), out[-1]
    if paired:
        up_send, up_keep, token = call(
            merge_ff_kernel,
            "merge_ff",
            [shape((rows, hidden_units + 4 * inner_columns))] * 2,
            ids, keep_a, Warm(got_a), keep_b, Warm(got_b),
            after=[token],
            scratch=[pltpu.VMEM((2, rows, hidden_units), BF)],
        )
    d_qkv, d_norm, token = call(
        functools.partial(third_kernel, count),
        "third",
        [shape((tokens, 3 * local_width)), warm((tokens, width))],
        ids, back[0], *[Warm(x) for x in back[1:]], Warm(w_qkv),
        after=[token],
        flops=6 * tokens * width * local_width,
    )
    d_norm_got = swap(d_norm, "mp", 1)
    if paired:
        up_send, hidden_turned[1] = pin([up_send, hidden_turned[1]], [token])
        up_got = swap(up_send, "lon", 4)
        wide = local_width + 2 * LANES
        cut = 3 * local_width // 2 + LANES
        first, second = (shape((parts // 2, rows, c)) for c in (cut, 3 * local_width - cut))
        send_a, keep_a, send_b, keep_b, token = call(
            grads_q_kernel,
            "grads_q",
            [first, first, second, second],
            ids, normed_one[0], Warm(swap(normed_one[1], "lon", 1)), d_qkv, Warm(swap(d_qkv, "lon", 1)),
            after=[token],
            scratch=[pltpu.VMEM((parts, rows, 3 * local_width), BF)],
            flops=6 * tokens * width * local_width,
        )
        oh_send, oh_keep, token = call(
            grads_oh_kernel,
            "grads_oh",
            [shape((parts // 2, rows, wide))] * 2,
            ids, d_one_turned[0], Warm(swap(d_one_turned[1], "lon", 1)), mixed, Warm(swap(mixed, "lon", 1)),
            hidden_turned[0], Warm(swap(hidden_turned[1], "lon", 1)), ct_turned, Warm(ct_got),
            after=[token],
            scratch=[pltpu.VMEM((parts, rows, wide), BF)],
            flops=2 * tokens * width * wide,
        )
        oh_got = swap(oh_send, "dp", 1)
        got_a, got_b = swap(send_a, "dp", 1), swap(send_b, "lon", 2)

    out = call(
        functools.partial(last_kernel, columns),
        "last",
        [
            *[shape((item_tokens, width // 2))] * 2,
            shape((items, variables * columns, height), F32),
            shape((items, variables, height)),
            *([shape((parts, rows, 2 * LANES))] * 2 if paired else [shape((width, 2 * LANES))]),
        ],
        ids, Warm(hidden_zero), Warm(d_one), Warm(d_norm), Warm(d_norm_got), gains, gain_two, patches, w_embed,
        after=[token],
        scratch=[
            pltpu.VMEM((2 * LANES, width), F32),
            pltpu.VMEM((2, item_tokens, width // 2), BF),
            pltpu.VMEM((parts, 2, rows, 2 * LANES) if paired else (8, LANES), BF),
        ],
        flops=4 * tokens * width * features,
    )
    pos_send, pos, d_fields, d_edge = out[:4]
    embed, token = out[4:-1], out[-1]
    if not paired:
        east, pos_got = from_behind(d_edge, "lon", -1), swap(pos_send, "dp", 1)
    more, more_outs, more_scratch, rest, rest_outs = [], [], [], [], []
    if paired:
        embed_width = embed[0].shape[2]
        step_a, side = shape((2, rows, cut)), shape((2, rows, wide))
        step_b = shape((2, rows, 3 * local_width - cut + 2 * embed_width + 2 * inner_columns))
        send_a, keep_a, send_b, keep_b, oh_send, oh_keep, token = call(
            fold_q_kernel,
            "fold_q",
            [step_a, step_a, step_b, step_b, side, side],
            ids, keep_a, Warm(got_a), keep_b, Warm(got_b), up_keep, Warm(up_got), oh_keep, Warm(oh_got),
            embed[0], Warm(swap(embed[1], "lon", 1)),
            after=[token],
            scratch=[
                pltpu.VMEM(keep_a.shape, BF),
                pltpu.VMEM(keep_b.shape, BF),
                pltpu.VMEM(oh_keep.shape, BF),
                pltpu.VMEM(embed[0].shape, BF),
            ],
        )
        got_a, got_b, oh_got = swap(send_a, "lon", 2), swap(send_b, "dp", 1), swap(oh_send, "lon", 2)
        d_edge, pos_send = pin([d_edge, pos_send], [token])
        east, pos_got = from_behind(d_edge, "lon", -1), swap(pos_send, "dp", 1)
        final, block = shape((rows, 3 * local_width + wide)), shape((rows, embed_width))
        send, keep, pair, *embed, token = call(
            merge_q_kernel,
            "merge_q",
            [final, final, shape((2, rows, 4 * inner_columns)), *[block] * 4],
            ids, keep_a, Warm(got_a), keep_b, Warm(got_b), oh_keep, Warm(oh_got),
            after=[token, east, pos_got],
            scratch=[pltpu.VMEM((2, *final.shape), BF), pltpu.VMEM((4, *block.shape), BF)],
        )
        embed = [embed[0], *[Warm(swap(e, "lon", 2 * (k + 1))) for k, e in enumerate(embed[1:])]]
        more = [up_keep, Warm(up_got), mine[0], pair, Warm(swap(pair, "lon", 1))]
        more_outs = [shape((rows, hidden_units), F32)] * 2
        more_scratch = [pltpu.VMEM((features, hidden_units // 4), BF)]
        rest = [keep, Warm(swap(send, "lon", 4))]
        rest_outs = [
            shape((rows, local_width), F32),
            shape((rows, features), F32),
            shape((3, rows, local_width), F32),
        ]
    else:
        embed = [lax.all_to_all(embed[0].reshape(everyone, rows, 2 * LANES), ("dp", "lon"), 0, 0)]
    *closed, token = call(
        functools.partial(close_kernel, columns),
        "close",
        [shape(d_fields.shape, F32), shape(pos.shape, F32), *more_outs],
        ids, d_fields, Warm(east), pos, Warm(pos_got), *more,
        after=[token],
        scratch=more_scratch,
    )
    *ended, token = call(
        functools.partial(end_kernel, len(embed)),
        "end",
        [shape((rows, features), F32), shape((2, rows), F32), *rest_outs],
        *embed, *rest,
        after=[token],
    )
    if paired:
        grad_up, grad_down, (grad_out, grad_head, grad_qkv) = closed[2], closed[3], ended[2:]
    else:
        flat = activated.transpose(1, 0, 2).reshape(tokens, hidden_units)
        grad_up = scatter(nn(normed_two[0], d_pre))
        grad_down = scatter(nn(d_two.T.astype(BF), flat))
        grad_out = scatter(nn(d_one_turned[0], mixed))
        grad_head = scatter(nt(hidden_turned[0], ct_turned))
        grad_qkv = scatter(nn(normed_one[0], d_qkv)).reshape(rows, 3, local_width).transpose(1, 0, 2)
    return (
        pred,
        *[x.reshape(variables) for x in stats],
        closed[0].reshape(items, variables, columns, height).transpose(0, 1, 3, 2),
        ended[0].T,
        closed[1],
        ended[1],
        grad_qkv,
        grad_out.T,
        grad_up,
        grad_down.T,
        grad_head,
    )


def solution(mesh):
    in_specs = (
        P(None, None, None, "lon"),
        P("dp"),
        P(),
        P(),
        P(),
        P(),
        P("lon", None),
        P(),
        P(None, None, "mp"),
        P("mp", None),
        P(None, "mp"),
        P("mp", None),
        P(),
        P("dp", "lon", None),
    )
    out_specs = (
        P("dp", "lon", None),
        P(),
        P(),
        P(),
        P("dp", None, None, "lon"),
        P(None, ("dp", "lon")),
        P("lon", "dp"),
        P(None, ("dp", "lon")),
        P(None, ("dp", "lon"), "mp"),
        P("mp", ("dp", "lon")),
        P(("dp", "lon"), "mp"),
        P("mp", ("dp", "lon")),
        P(("dp", "lon"), None),
    )
    return jax.shard_map(local, mesh=mesh, in_specs=in_specs, out_specs=out_specs, check_vma=False)
```

```python
import functools
import math

import jax
import jax.numpy as jnp
from jax import lax
from jax.experimental import pallas as pl
from jax.experimental.pallas import tpu as pltpu
from jax.sharding import PartitionSpec as P

HDIM = 64
PATCH = 2
LANES = 128
NORM_EPS = 1e-06
STAT_EPS = 1e-06
BF = jnp.bfloat16
F32 = jnp.float32
MIB = 2**20


def swap(block, axis, distance):
    route = [(i, i ^ distance) for i in range(lax.axis_size(axis))]
    return lax.ppermute(block, axis, route)


def from_behind(block, axis, distance):
    size = lax.axis_size(axis)
    route = [((i - distance) % size, i) for i in range(size)]
    return lax.ppermute(block, axis, route)


def pick(x, index, axis):
    return lax.dynamic_index_in_dim(x, index, axis, keepdims=False)


def halve(total, dims):
    for axis, bit in dims:
        side = (lax.axis_index(axis) // bit) % 2
        got = swap(pick(total, 1 - side, 0), axis, bit)
        total = (pick(total, side, 0).astype(F32) + got.astype(F32)).astype(BF)
    return total


def scatter(total):
    dp, lon = lax.axis_size("dp"), lax.axis_size("lon")
    dims = []
    for axis, size in (("dp", dp), ("lon", lon)):
        bit = size // 2
        while bit:
            dims.append((axis, bit))
            bit //= 2
    rows, columns = total.shape
    total = total.astype(BF).reshape((2,) * len(dims) + (rows // (dp * lon), columns))
    order = sorted(range(len(dims)), key=lambda i: (dims[i][1] > 1 or dims[i][0] == "dp", i))
    total = total.transpose([*order, len(dims), len(dims) + 1])
    return halve(total, [dims[i] for i in order]).astype(F32)


def nt(a, b):
    return lax.dot_general(a, b, (((1,), (1,)), ((), ())), preferred_element_type=F32)


def nn(a, b):
    return lax.dot_general(a, b, (((1,), (0,)), ((), ())), preferred_element_type=F32)


def item_mask(rows, lanes, item):
    lane = lax.broadcasted_iota(jnp.int32, (rows, lanes), 1)
    return (lane >= item * HDIM) & (lane < (item + 1) * HDIM)


def interleave(first, second):
    low = item_mask(first.shape[0], LANES, 0)
    return (
        jnp.where(low, first, pltpu.roll(second, HDIM, 1)),
        jnp.where(low, pltpu.roll(first, HDIM, 1), second),
    )


def norm_parts(hidden):
    centred = hidden - jnp.mean(hidden, axis=-1, keepdims=True)
    variance = jnp.mean(centred * centred, axis=-1, keepdims=True)
    inverse = lax.rsqrt(variance + NORM_EPS)
    return centred * inverse, inverse


def norm_back(unit, inverse, scaling, grad):
    scaled = grad * scaling
    back = inverse * (
        scaled
        - jnp.mean(scaled, axis=-1, keepdims=True)
        - unit * jnp.mean(scaled * unit, axis=-1, keepdims=True)
    )
    return back, jnp.sum(grad * unit, axis=0, keepdims=True)


def emit_turned(x, ids_ref, outs, hold):
    turned = x.T.astype(BF)
    if len(outs) == 1:
        outs[0][...] = turned
        return
    keep, send = outs
    parts, rows, tokens = keep.shape
    hold[...] = turned.reshape(parts, 2, rows, tokens)
    core = ids_ref[0]
    keep[...] = hold[:, pl.ds(core, 1)].reshape(parts, rows, tokens)
    send[...] = hold[:, pl.ds(1 - core, 1)].reshape(parts, rows, tokens)


class Warm:
    def __init__(self, value):
        self.value = value


def call(body, name, outs, *args, after=(), grid=(), in_specs=None, out_specs=None, scratch=(), limit=24, flops=0):
    vmem = pl.BlockSpec(memory_space=pltpu.VMEM)
    smem = pl.BlockSpec(memory_space=pltpu.SMEM)
    shapes = [o.value if isinstance(o, Warm) else o for o in outs]
    plain = [a.value if isinstance(a, Warm) else a for a in args]
    if in_specs is None:
        in_specs = [smem if a.dtype == jnp.int32 else vmem for a in plain]
    if out_specs is None:
        out_specs = [vmem] * len(outs)
    token = pl.BlockSpec((8, LANES), lambda *at: (0, 0)) if grid else vmem
    nbytes = sum(math.prod(a.shape) * a.dtype.itemsize for a in [*plain, *shapes])
    here, skip, there = len(args), len(after), len(outs)

    def with_token(*refs):
        refs = list(refs)
        refs[here + skip + there][...] = jnp.zeros((8, LANES), F32)
        body(*refs[:here], *refs[here + skip : here + skip + there], *refs[here + skip + there + 1 :])

    def cold(x):
        if isinstance(x, Warm):
            return x.value
        return x if x.dtype == jnp.int32 else pltpu.with_memory_space_constraint(x, pltpu.HBM)

    return pl.pallas_call(
        with_token,
        grid=grid,
        out_shape=[
            *[o.value if isinstance(o, Warm) else pltpu.HBM(o.shape, o.dtype) for o in outs],
            pltpu.HBM((8, LANES), F32),
        ],
        in_specs=[*in_specs, *[pl.BlockSpec(memory_space=pl.ANY)] * skip],
        out_specs=[*out_specs, token],
        scratch_shapes=list(scratch),
        compiler_params=pltpu.CompilerParams(vmem_limit_bytes=limit * MIB),
        cost_estimate=pl.CostEstimate(flops=int(flops), bytes_accessed=nbytes, transcendentals=0),
        name=name,
    )(*[cold(a) for a in args], *[cold(a) for a in after])


def shape(dims, kind=BF):
    return jax.ShapeDtypeStruct(dims, kind)


def warm(dims, kind=BF):
    return Warm(shape(dims, kind))


def feature_order(variables, back):
    features = PATCH * PATCH * variables
    natural = lax.broadcasted_iota(jnp.int32, (features, features), 1 if back else 0)
    sorted_ = lax.broadcasted_iota(jnp.int32, (features, features), 0 if back else 1)
    hit = (natural // 4 == sorted_ % variables) & (natural % 4 == sorted_ // variables)
    return jnp.where(hit, 1.0, 0.0).astype(BF)


def send_pairs(ids_ref, hold, messages):
    if len(messages) == 1:
        messages[0][...] = hold[...]
        return
    for k, message in enumerate(messages):
        message[...] = hold[pl.ds(2 * ids_ref[4 + k], 2)]


def moments_kernel(index_ref, data_ref, fields_ref, edge_ref, moments_ref, turn_ref, sems):
    items, variables, height = edge_ref.shape
    cols = fields_ref.shape[1] // variables
    copies = [
        pltpu.make_async_copy(data_ref.at[index_ref[i]], fields_ref.at[i], sems.at[i])
        for i in range(items)
    ]
    for copy in copies:
        copy.start()
    turn_ref[...] = jnp.zeros_like(turn_ref)
    for copy in copies:
        copy.wait()
    blocks = [
        fields_ref[i, pl.ds(c, variables, stride=cols), :] for i in range(items) for c in range(cols)
    ]
    for i in range(items):
        edge_ref[i] = blocks[i * cols + cols - 1].astype(BF)
    count = float(items * cols * height)
    mean = jnp.sum(sum(blocks), axis=1, keepdims=True) * (1.0 / count)
    spread = jnp.sum(sum(jnp.square(b - mean) for b in blocks), axis=1, keepdims=True)
    turn_ref[0:variables, 0:1] = mean
    turn_ref[HDIM : HDIM + variables, 0:1] = spread
    turned = turn_ref[...].T
    moments_ref[...] = jnp.broadcast_to(turned[0:1, :][None], moments_ref.shape)


def start_kernel(local_count, ids_ref, mom_ref, count_ref, mean_ref, var_ref, fields_ref, edge_ref, we_ref,
                 pos_ref, gains_ref, wq_ref, new_count_ref, new_mean_ref, new_var_ref, hidden_ref, patches_ref,
                 *rest):
    (*outs, column_ref, run_ref, hold, weights, sem, qkv_ref) = rest
    if len(outs) > 2:
        messages, turned = outs[:-2], outs[-2:]
    else:
        messages, turned = outs[:1], outs[1:]
    copy = pltpu.make_async_copy(wq_ref, weights, sem)
    copy.start()
    members = mom_ref.shape[0]
    items, rows, height = fields_ref.shape
    variables = edge_ref.shape[1]
    cols = rows // variables
    half = height // PATCH
    moments = mom_ref[:, 0, :]
    run_ref[...] = jnp.zeros_like(run_ref)
    for k, ref in enumerate((count_ref, mean_ref, var_ref)):
        run_ref[k : k + 1, 0:variables] = ref[...]
    batch_count = local_count * members
    batch_mean = jnp.sum(moments, axis=0, keepdims=True) * (1.0 / members)
    off = moments - batch_mean
    spread = jnp.sum(pltpu.roll(moments, HDIM, 1) + local_count * off * off, axis=0, keepdims=True)
    run_count, run_mean, run_var = (run_ref[k : k + 1, :] for k in range(3))
    new_count = run_count + batch_count
    shift = batch_mean - run_mean
    new_mean = run_mean + shift * (batch_count / new_count)
    new_var = (
        run_var * run_count + spread + shift * shift * (run_count * batch_count / new_count)
    ) / new_count
    new_count_ref[...] = new_count[:, 0:variables]
    new_mean_ref[...] = new_mean[:, 0:variables]
    new_var_ref[...] = new_var[:, 0:variables]
    column_ref[...] = jnp.zeros_like(column_ref)
    column_ref[0:1, :] = new_mean
    column_ref[1:2, :] = lax.rsqrt(new_var + STAT_EPS)
    column = column_ref[...].T
    centre, inverse = column[0:variables, 0:1], column[0:variables, 1:2]

    def scaled(block):
        return ((block - centre) * inverse).astype(BF)

    row = lax.broadcasted_iota(jnp.int32, (2 * height, LANES), 0)
    lane = lax.broadcasted_iota(jnp.int32, (2 * height, LANES), 1)
    sort = [
        jnp.where(
            (row // height == lane // half) & (row % height == PATCH * (lane % half) + a), 1.0, 0.0
        ).astype(BF)
        for a in range(PATCH)
    ]
    natural = feature_order(variables, False)
    hidden = []
    for item in range(items):
        west = scaled(edge_ref[item].astype(F32))
        own = [
            scaled(fields_ref[item, pl.ds(c, variables, stride=cols), :]) for c in range(cols - 1)
        ]
        first = jnp.concatenate([west, own[0]], axis=0)
        second = jnp.concatenate([own[1], own[2]], axis=0)
        both = jnp.concatenate([first, second], axis=1)
        patches = jnp.concatenate([nn(both, sort[a]) for a in range(PATCH)], axis=0)
        patches = nn(natural, patches.astype(BF))
        patches_ref[:, item * LANES : (item + 1) * LANES] = patches.astype(BF)
        hidden.append(nn(patches.T.astype(BF), we_ref[...]) + pos_ref[...].astype(F32))
    hidden = jnp.concatenate(hidden, axis=0)
    hidden_ref[...] = hidden
    unit, _ = norm_parts(hidden)
    normed = unit * gains_ref[0:1, :]
    low = normed.astype(BF)
    emit_turned(normed, ids_ref, turned, hold)
    copy.wait()
    for c in range(3):
        product = nn(low, weights[c])
        for t in range(product.shape[1] // LANES):
            tile = product[:, t * LANES : (t + 1) * LANES]
            a, b = interleave(tile[:LANES], tile[LANES:])
            qkv_ref[2 * t, c] = a.astype(BF)
            qkv_ref[2 * t + 1, c] = b.astype(BF)
    send_pairs(ids_ref, qkv_ref, messages)


def cotangent_kernel(ids_ref, ct_ref, wh_ref, wd_ref, *refs):
    if len(refs) > 3:
        two_ref, act_ref, ct_turned_ref, mine_ref, hold = refs
        hold[...] = wh_ref[...].astype(F32).T.astype(BF).reshape(hold.shape)
        mine_ref[...] = hold[ids_ref[8]]
    else:
        two_ref, act_ref, ct_turned_ref = refs
    grads = []
    for item in range(ct_ref.shape[0]):
        ct = ct_ref[item].T.astype(BF)
        ct_turned_ref[:, item * LANES : (item + 1) * LANES] = ct_ref[item].astype(BF)
        grads.append(nn(ct, wh_ref[...]))
    d_two = jnp.concatenate(grads, axis=0)
    two_ref[...] = d_two
    act_ref[...] = nt(d_two.astype(BF), wd_ref[...]).astype(BF)


def attend_kernel(items, scale, q_ref, kv_ref, o_ref, ot_ref, pt_ref, vt_ref):
    keys = kv_ref.shape[0] * kv_ref.shape[2]

    @pl.when(pl.program_id(0) == 0)
    def _():
        vt_ref[...] = kv_ref[:, 2].reshape(keys, LANES).astype(F32).T.astype(BF)

    rows = q_ref.shape[0] * q_ref.shape[2]
    queries = q_ref[:, 0].reshape(rows, LANES) * BF(scale)
    key_rows = kv_ref[:, 1].reshape(keys, LANES)
    for item in range(items):
        chosen = jnp.where(item_mask(rows, LANES, item), queries, BF(0))
        scores = nt(key_rows, chosen)
        top = jnp.max(scores, axis=0, keepdims=True)
        raised = jnp.exp(scores - top)
        total = jnp.sum(raised, axis=0, keepdims=True)
        weights = (raised * (1.0 / total)).astype(BF)
        pt_ref[item] = weights
        span = slice(item * HDIM, (item + 1) * HDIM)
        ot_ref[span, :] = nn(vt_ref[span, :], weights)
    o_ref[...] = ot_ref[...].T.astype(BF).reshape(o_ref.shape)


def attend(q, kv, items, scale, after):
    peers, _, tokens, lanes = q.shape
    rows, keys = peers * tokens, kv.shape[0] * tokens
    step = max(1, min(peers, 256 * 1024 // keys // tokens))
    block = step * tokens
    return call(
        functools.partial(attend_kernel, items, scale),
        "attend",
        [
            shape((peers, tokens, lanes)),
            shape((lanes, rows), F32),
            shape((items, keys, rows)),
        ],
        Warm(q),
        Warm(kv),
        after=after,
        grid=(peers // step,),
        in_specs=[
            pl.BlockSpec((step, 3, tokens, lanes), lambda j: (j, 0, 0, 0)),
            pl.BlockSpec(kv.shape, lambda j: (0, 0, 0, 0)),
        ],
        out_specs=[
            pl.BlockSpec((step, tokens, lanes), lambda j: (j, 0, 0)),
            pl.BlockSpec((lanes, block), lambda j: (0, j)),
            pl.BlockSpec((items, keys, block), lambda j: (0, 0, j)),
        ],
        scratch=[pltpu.VMEM((lanes, keys), BF)],
        limit=24 if keys <= 2048 else 56,
        flops=8 * rows * keys * lanes,
    )


def pair_attend_kernel(items, scale, *refs):
    sources, (*outs, ot_ref, pt_ref, query_ref, key_ref, value_ref, vt_ref) = refs[:8], refs[8:]
    tokens = sources[0].shape[2]
    for k, source in enumerate(sources):
        span = slice(k * tokens, (k + 1) * tokens)
        if k < len(outs):
            query_ref[0, span, :] = source[0, 0] * BF(scale)
        key_ref[0, span, :] = source[0, 1]
        value_ref[0, span, :] = source[0, 2]
        vt_ref[:, span] = source[0, 2].astype(F32).T.astype(BF)
    queries = query_ref[0]
    for item in range(items):
        chosen = jnp.where(item_mask(queries.shape[0], LANES, item), queries, BF(0))
        scores = nt(key_ref[0], chosen)
        top = jnp.max(scores, axis=0, keepdims=True)
        raised = jnp.exp(scores - top)
        total = jnp.sum(raised, axis=0, keepdims=True)
        weights = (raised * (1.0 / total)).astype(BF)
        pt_ref[0, item] = weights
        span = slice(item * HDIM, (item + 1) * HDIM)
        ot_ref[0, span, :] = nn(vt_ref[span, :], weights)
    attended = ot_ref[0].T.astype(BF)
    for k, out in enumerate(outs):
        out[0] = attended[k * tokens : (k + 1) * tokens]


def pair_attend(own, other, items, scale, after):
    _, _, tokens, lanes = own[0].shape
    rows, keys = len(own) * tokens, 2 * len(own) * tokens
    wide = lambda *dims: pl.BlockSpec((1, *dims), lambda h: (h, *[0] * len(dims)))
    *outs, ot, pt, q, k, v, token = call(
        functools.partial(pair_attend_kernel, items, scale),
        "attend",
        [
            *[shape((2, tokens, lanes))] * len(own),
            shape((2, lanes, rows), F32),
            shape((2, items, keys, rows)),
            shape((2, rows, lanes)),
            shape((2, keys, lanes)),
            shape((2, keys, lanes)),
        ],
        own[0],
        *[Warm(x) for x in [*own[1:], *other]],
        after=after,
        grid=(2,),
        in_specs=[wide(3, tokens, lanes)] * (2 * len(own)),
        out_specs=[
            *[wide(tokens, lanes)] * len(own),
            wide(lanes, rows),
            wide(items, keys, rows),
            wide(rows, lanes),
            wide(keys, lanes),
            wide(keys, lanes),
        ],
        scratch=[pltpu.VMEM((lanes, keys), BF)],
        limit=32,
        flops=16 * rows * keys * lanes,
    )
    return outs, (q, k, v, ot, pt), token


def pair_attend_back_kernel(items, scale, ids_ref, query_ref, key_ref, value_ref, ot_ref, pt_ref, grads_ref, *refs):
    *outs, cross_ref, kt_ref, grad_rows, dqt_ref, dk_sum, dv_sum = refs
    tokens = grads_ref.shape[2]
    for k in range(len(outs)):
        grad_rows[k * tokens : (k + 1) * tokens, :] = grads_ref[ids_ref[4 + k], 0]
    kt_ref[...] = (key_ref[0].astype(F32) * scale).T.astype(BF)
    queries, grads = query_ref[0], grad_rows[...]
    product = grads.astype(F32).T * ot_ref[0]
    for item in range(items):
        span = slice(item * HDIM, (item + 1) * HDIM)
        mask = item_mask(queries.shape[0], LANES, item)
        grad = jnp.where(mask, grads, BF(0))
        query = jnp.where(mask, queries, BF(0))
        delta = jnp.sum(product[span, :], axis=0, keepdims=True)
        weights = pt_ref[0, item]
        back = (weights.astype(F32) * (nt(value_ref[0], grad) - delta)).astype(BF)
        d_value, d_key = nn(weights, grad), nn(back, query)
        if item == 0:
            dv_sum[...] = d_value
            dk_sum[...] = d_key
        else:
            dv_sum[...] += d_value
            dk_sum[...] += d_key
        dqt_ref[span, :] = nn(kt_ref[span, :], back)
    d_query = dqt_ref[...].T.astype(BF)
    for k in range(2 * len(outs)):
        span = slice(k * tokens, (k + 1) * tokens)
        if k < len(outs):
            outs[k][0, 0] = d_query[span]
        for c, total in ((0, dk_sum), (1, dv_sum)):
            if k < len(outs):
                outs[k][0, 1 + c] = total[span, :].astype(BF)
            else:
                cross_ref[k - len(outs), 0, c] = total[span, :].astype(BF)


def pair_attend_back(ids, kept, d, items, scale, after):
    count, _, tokens, lanes = d.shape
    rows, keys = count * tokens, 2 * count * tokens
    wide = lambda *dims: pl.BlockSpec((1, *dims), lambda h: (h, *[0] * len(dims)))
    *outs, cross, token = call(
        functools.partial(pair_attend_back_kernel, items, scale),
        "attend_back",
        [*[shape((2, 3, tokens, lanes))] * count, shape((count, 2, 2, tokens, lanes))],
        ids, *kept, d,
        after=after,
        grid=(2,),
        in_specs=[
            pl.BlockSpec(memory_space=pltpu.SMEM),
            wide(rows, lanes),
            wide(keys, lanes),
            wide(keys, lanes),
            wide(lanes, rows),
            wide(items, keys, rows),
            pl.BlockSpec((count, 1, tokens, lanes), lambda h: (0, h, 0, 0)),
        ],
        out_specs=[
            *[wide(3, tokens, lanes)] * count,
            pl.BlockSpec((count, 1, 2, tokens, lanes), lambda h: (0, h, 0, 0, 0)),
        ],
        scratch=[
            pltpu.VMEM((lanes, keys), BF),
            pltpu.VMEM((rows, lanes), BF),
            pltpu.VMEM((lanes, rows), F32),
            pltpu.VMEM((keys, lanes), F32),
            pltpu.VMEM((keys, lanes), F32),
        ],
        limit=32,
        flops=32 * rows * keys * lanes,
    )
    return outs, cross, token


def combine_kernel(*refs):
    count = (len(refs) - 1) // 2
    own, cross_ref, outs = refs[:count], refs[count], refs[count + 1 :]
    for k in range(count):
        outs[k][:, 0] = own[k][:, 0]
        for c in range(2):
            outs[k][:, 1 + c] = plus(own[k].at[:, 1 + c], cross_ref.at[k, :, c])


def attend_back_kernel(items, scale, q_ref, kv_ref, d_ref, ot_ref, pt_ref, dq_ref, *rest):
    dkv_ref, (kt_ref, dqt_ref, dk_sum, dv_sum) = rest[:-4], rest[-4:]
    step = pl.program_id(0)
    keys = kv_ref.shape[0] * kv_ref.shape[2]

    @pl.when(step == 0)
    def _():
        kt_ref[...] = (kv_ref[:, 1].reshape(keys, LANES).astype(F32) * scale).T.astype(BF)
        dk_sum[...] = jnp.zeros_like(dk_sum)
        dv_sum[...] = jnp.zeros_like(dv_sum)

    peers, _, tokens, _ = q_ref.shape
    rows = peers * tokens
    queries = q_ref[:, 0].reshape(rows, LANES) * BF(scale)
    grads = d_ref[...].reshape(rows, LANES)
    value_rows = kv_ref[:, 2].reshape(keys, LANES)
    product = grads.astype(F32).T * ot_ref[...]
    for item in range(items):
        span = slice(item * HDIM, (item + 1) * HDIM)
        mask = item_mask(rows, LANES, item)
        grad = jnp.where(mask, grads, BF(0))
        query = jnp.where(mask, queries, BF(0))
        delta = jnp.sum(product[span, :], axis=0, keepdims=True)
        weights = pt_ref[item]
        back = (weights.astype(F32) * (nt(value_rows, grad) - delta)).astype(BF)
        dv_sum[...] += nn(weights, grad)
        dk_sum[...] += nn(back, query)
        dqt_ref[span, :] = nn(kt_ref[span, :], back)
    d_query = dqt_ref[...].T.astype(BF).reshape(peers, tokens, LANES)
    if dkv_ref:
        dq_ref[...] = d_query
    else:
        dq_ref[pl.ds(step * peers, peers), 0] = d_query

    @pl.when(step == pl.num_programs(0) - 1)
    def _():
        for c, total in ((1, dk_sum), (2, dv_sum)):
            total = total[...].reshape(kv_ref.shape[0], tokens, LANES)
            if dkv_ref:
                dkv_ref[0][:, c - 1] = total
            else:
                dq_ref[:, c] = total.astype(BF)


def attend_back(q, kv, d, ot, pt, items, scale, after):
    peers, _, tokens, lanes = q.shape
    rows, keys = peers * tokens, kv.shape[0] * tokens
    step = max(1, min(peers, 256 * 1024 // keys // tokens))
    block = step * tokens
    if q.shape == kv.shape:
        outs = [shape(q.shape)]
        out_specs = [pl.BlockSpec(q.shape, lambda j: (0, 0, 0, 0))]
    else:
        outs = [shape((peers, tokens, lanes)), shape((kv.shape[0], 2, tokens, lanes), F32)]
        out_specs = [
            pl.BlockSpec((step, tokens, lanes), lambda j: (j, 0, 0)),
            pl.BlockSpec(outs[1].shape, lambda j: (0, 0, 0, 0)),
        ]
    *back, token = call(
        functools.partial(attend_back_kernel, items, scale),
        "attend_back",
        outs,
        Warm(q),
        Warm(kv),
        d,
        ot,
        pt,
        after=after,
        grid=(peers // step,),
        in_specs=[
            pl.BlockSpec((step, 3, tokens, lanes), lambda j: (j, 0, 0, 0)),
            pl.BlockSpec(kv.shape, lambda j: (0, 0, 0, 0)),
            pl.BlockSpec((step, tokens, lanes), lambda j: (j, 0, 0)),
            pl.BlockSpec((lanes, block), lambda j: (0, j)),
            pl.BlockSpec((items, keys, block), lambda j: (0, 0, j)),
        ],
        out_specs=out_specs,
        scratch=[
            pltpu.VMEM((lanes, keys), BF),
            pltpu.VMEM((lanes, block), F32),
            pltpu.VMEM((keys, lanes), F32),
            pltpu.VMEM((keys, lanes), F32),
        ],
        limit=24 if keys <= 2048 else 60,
        flops=16 * rows * keys * lanes,
    )
    return back, token


def unpack(ids_ref, sources, index, out_ref, base):
    several = len(sources) > 1
    count = len(sources) if several else sources[0].shape[0] // 2
    for t in range(count):
        source, head = (sources[t], 0) if several else (sources[0], 2 * t)
        pair = [
            (source[head + s] if index is None else source[head + s, index]).astype(F32) for s in range(2)
        ]
        at = base + (pl.multiple_of(ids_ref[4 + t] * LANES, LANES) if several else t * LANES)
        for item, tile in enumerate(interleave(*pair)):
            out_ref[item * LANES : (item + 1) * LANES, pl.ds(at, LANES)] = tile.astype(BF)


def pack(product, out_ref):
    for t in range(product.shape[1] // LANES):
        tile = product[:, t * LANES : (t + 1) * LANES]
        for s, block in enumerate(interleave(tile[:LANES], tile[LANES:])):
            out_ref[2 * t + s] = block.astype(BF)


def project_kernel(ids_ref, *refs):
    *sources, wo_ref, mixed_ref, branch_ref = refs
    unpack(ids_ref, sources, None, mixed_ref, 0)
    branch_ref[...] = nn(mixed_ref[...], wo_ref[...]).astype(BF)


def forward_kernel(sources, ids_ref, *refs):
    if sources:
        own, got, refs = refs[:sources], refs[sources : 2 * sources], refs[2 * sources :]
        wo_ref, wo_got_ref, zero_ref, gains_ref, wu_ref, dact_ref, norm_ref, mixed_out, *refs = refs
        *refs, wo_buf, mixed, wo_sems = refs
        me = ids_ref[9]
        wo_loads = [
            pltpu.make_async_copy(wo_ref, wo_buf.at[me], wo_sems.at[0]),
            pltpu.make_async_copy(wo_got_ref, wo_buf.at[1 - me], wo_sems.at[1]),
        ]
        for copy in wo_loads:
            copy.start()
    else:
        own_ref, got_ref, zero_ref, gains_ref, wu_ref, dact_ref, norm_ref, *refs = refs
    one_out, pre_out, act_out, other_out, *rest = refs
    count = (len(rest) - 11) // 2
    turned_out, turned = rest[:count], rest[count : 2 * count]
    zero_buf, one_ref, weights, grads, pre_ref, act_ref, normed_ref, hold, into, out_of, zero_sem = rest[2 * count :]
    zero_load = pltpu.make_async_copy(zero_ref, zero_buf, zero_sem)
    zero_load.start()
    chunks, _, block = grads.shape
    per_half = chunks // 2
    loads, stores = [], []
    for c in range(chunks):
        span = slice(c * block, (c + 1) * block)
        loads.append(
            (
                pltpu.make_async_copy(wu_ref.at[:, span], weights.at[c], into.at[2 * c]),
                pltpu.make_async_copy(dact_ref.at[:, span], grads.at[c], into.at[2 * c + 1]),
            )
        )

    def store(source, target):
        stores.append(pltpu.make_async_copy(source, target, out_of.at[len(stores)]))
        stores[-1].start()

    if sources:
        unpack(ids_ref, own, None, mixed.at[me], 0)
        unpack(ids_ref, got, None, mixed.at[1 - me], 0)
        mixed_out[...] = mixed[me]
        for copy in wo_loads:
            copy.wait()
    zero_load.wait()
    for pair in loads:
        for copy in pair:
            copy.start()
    if sources:
        branch = nn(mixed[0], wo_buf[0]) + nn(mixed[1], wo_buf[1])
    else:
        branch = own_ref[...].astype(F32) + got_ref[...].astype(F32)
    hidden = zero_buf[...] + branch
    one_ref[...] = hidden
    store(one_ref, one_out)
    unit, _ = norm_parts(hidden)
    normed = unit * gains_ref[1:2, :]
    normed_ref[...] = normed.astype(BF)
    emit_turned(normed, ids_ref, turned, hold)
    for source, target in zip(turned, turned_out):
        store(source, target)
    total = None
    for c in range(chunks):
        span = slice(c * block, (c + 1) * block)
        half, place = c // per_half, slice(c % per_half * block, (c % per_half + 1) * block)
        for copy in loads[c]:
            copy.wait()
        pre = nn(normed_ref[...], weights[c])
        chance = 0.5 * (1.0 + lax.erf(pre * (1.0 / math.sqrt(2.0))))
        slope = chance + pre * jnp.exp(-0.5 * pre * pre) * (1.0 / math.sqrt(2.0 * math.pi))
        act_ref[half, :, place] = (pre * chance).astype(BF)
        store(act_ref.at[half, :, place], act_out.at[half, :, place])
        d_pre = (grads[c].astype(F32) * slope).astype(BF)
        pre_ref[:, span] = d_pre
        store(pre_ref.at[:, span], pre_out.at[:, span])
        part = nt(d_pre, weights[c])
        total = part if total is None else total + part
    store(act_ref.at[1 - ids_ref[0]], other_out)
    norm_ref[...] = total.astype(BF)
    for copy in stores:
        copy.wait()


def second_kernel(ids_ref, one_ref, two_ref, own_ref, got_ref, gains_ref, wo_ref, d_ref, gain_ref, *rest):
    heads_ref, *turned, hold = rest
    unit, inverse = norm_parts(one_ref[...])
    grad = own_ref[...].astype(F32) + got_ref[...].astype(F32)
    back, gain = norm_back(unit, inverse, gains_ref[1:2, :], grad)
    gain_ref[...] = gain
    d_one = two_ref[...] + back
    d_ref[...] = d_one
    pack(nt(d_one.astype(BF), wo_ref[...]), heads_ref)
    emit_turned(d_one, ids_ref, turned, hold)


def head_kernel(ids_ref, one_ref, own_ref, got_ref, wh_ref, pred_ref, *rest):
    turned, hold = rest[:-1], rest[-1]
    hidden = one_ref[...] + (own_ref[...].astype(F32) + got_ref[...].astype(F32))
    low = hidden.astype(BF)
    for item in range(pred_ref.shape[0]):
        pred_ref[item] = nt(wh_ref[...], low[item * LANES : (item + 1) * LANES])
    emit_turned(hidden, ids_ref, turned, hold)


def third_kernel(count, ids_ref, *refs):
    sources, (wq_ref, dqkv_ref, norm_ref) = refs[:count], refs[count:]
    width = wq_ref.shape[2]
    total = None
    for c in range(3):
        unpack(ids_ref, sources, c, dqkv_ref, c * width)
        part = nt(dqkv_ref[:, c * width : (c + 1) * width], wq_ref[c])
        total = part if total is None else total + part
    norm_ref[...] = total.astype(BF)


def last_kernel(cols, ids_ref, zero_ref, done_ref, own_ref, got_ref, gains_ref, gain_two_ref, patches_ref, we_ref,
                pos_send, pos_keep, fields_ref, edge_ref, *rest):
    embed, (rows_ref, pos_ref, hold) = rest[:-3], rest[-3:]
    unit, inverse = norm_parts(zero_ref[...])
    grad = own_ref[...].astype(F32) + got_ref[...].astype(F32)
    back, gain = norm_back(unit, inverse, gains_ref[0:1, :], grad)
    d_zero = done_ref[...] + back
    low = d_zero.astype(BF)
    items, variables, height = edge_ref.shape
    pos = d_zero[0:LANES]
    for item in range(1, items):
        pos = pos + d_zero[item * LANES : (item + 1) * LANES]
    width = pos_ref.shape[2]
    for k in range(2):
        pos_ref[k] = pos[:, k * width : (k + 1) * width].astype(BF)
    pos_send[...] = pos_ref[1 - ids_ref[1]]
    pos_keep[...] = pos_ref[ids_ref[1]]
    features = patches_ref.shape[0]
    rows_ref[...] = jnp.zeros_like(rows_ref)
    rows_ref[0:features, :] = nn(patches_ref[...], low)
    rows_ref[features : features + 1, :] = gain
    rows_ref[features + 1 : features + 2, :] = gain_two_ref[...]
    emit_turned(rows_ref[...], ids_ref, embed, hold)
    half = height // PATCH
    row = lax.broadcasted_iota(jnp.int32, (LANES, height), 0)
    lane = lax.broadcasted_iota(jnp.int32, (LANES, height), 1)
    fields_ref[...] = jnp.zeros_like(fields_ref)
    order = feature_order(variables, True)
    for item in range(items):
        d_patches = nt(we_ref[...], low[item * LANES : (item + 1) * LANES])
        high = d_patches.astype(BF)
        rest = (d_patches - high.astype(F32)).astype(BF)
        high, rest = nn(order, high).astype(BF), nn(order, rest).astype(BF)
        for j in range(2):
            total = None
            for a in range(PATCH):
                place = jnp.where(
                    (row // half == j) & (lane == PATCH * (row % half) + a), 1.0, 0.0
                ).astype(BF)
                span = slice(a * 2 * variables, (a + 1) * 2 * variables)
                part = nn(high[span], place) + nn(rest[span], place)
                total = part if total is None else total + part
            for b in range(PATCH):
                block = total[b * variables : (b + 1) * variables]
                column = 2 * j + b - 1
                if column < 0:
                    edge_ref[item] = block.astype(BF)
                else:
                    fields_ref[item, pl.ds(column, variables, stride=cols), :] = block


def down_kernel(act_ref, wd_ref, out_ref):
    width = act_ref.shape[2]
    total = nn(act_ref[0], wd_ref[0:width, :]) + nn(act_ref[1], wd_ref[width:, :])
    out_ref[...] = total.astype(BF)


def pin(xs, after):
    def body(*refs):
        pass

    anywhere = pl.BlockSpec(memory_space=pl.ANY)
    several = isinstance(xs, (list, tuple))
    xs = list(xs) if several else [xs]
    out = pl.pallas_call(
        body,
        out_shape=[pltpu.HBM(x.shape, x.dtype) for x in xs],
        in_specs=[anywhere] * (len(xs) + len(after)),
        out_specs=[anywhere] * len(xs),
        input_output_aliases={k: k for k in range(len(xs))},
        name="pin",
    )(*[pltpu.with_memory_space_constraint(x, pltpu.HBM) for x in xs], *after)
    return out if several else out[0]


def product_of(own, got, b_own, b_got):
    parts, rows, tokens = own.shape
    total = nn(own[...].reshape(parts * rows, tokens), b_own)
    return total + nn(got[...].reshape(parts * rows, tokens), b_got)


def split_dp(ids_ref, hold, send, keep, columns):
    half = hold.shape[0] // 2
    for out, at in ((send, 1 - ids_ref[1]), (keep, ids_ref[1])):
        for k in range(half):
            out[k, :, 0:columns] = hold[at * half + k]


def split_near(ids_ref, hold, send, keep, columns):
    for out, at in ((send, 1 - ids_ref[2]), (keep, ids_ref[2])):
        for k in range(hold.shape[0] // 2):
            out[k, :, 0:columns] = hold[2 * k + at]


def plus(a, b):
    return (a[...].astype(F32) + b[...].astype(F32)).astype(BF)


def grads_ff_kernel(ids_ref, at_own, at_got, pre_own, pre_got, ct_own, ct_got, act_own, act_got,
                    send_a, keep_a, send_b, keep_b, hold, inner):
    parts, rows, total = hold.shape
    columns = total - keep_b.shape[2]
    product = product_of(at_own, at_got, pre_own[...], pre_got[...])
    hold[...] = product.astype(BF).reshape(hold.shape)
    split_dp(ids_ref, hold.at[:, :, 0:columns], send_a, keep_a, columns)
    split_near(ids_ref, hold.at[:, :, columns:], send_b, keep_b, total - columns)
    product = (nn(ct_own[...], act_own[ids_ref[0]]) + nn(ct_got[...], act_got[...])).astype(BF)
    tiles, groups = inner.shape[1], inner.shape[3] // LANES
    for k in range(2):
        for q in range(tiles):
            for g in range(groups):
                inner[k, q, :, g * LANES : (g + 1) * LANES] = product[
                    g * rows : (g + 1) * rows, (k * tiles + q) * LANES : (k * tiles + q + 1) * LANES
                ]
    for q in range(tiles):
        send_a[q, :, columns:] = inner[1 - ids_ref[1], q]
        keep_a[q, :, columns:] = inner[ids_ref[1], q]


def fold_ff_kernel(ids_ref, keep_a, got_a, keep_b, got_b, send_a, left_a, send_b, left_b, hold, hold_b):
    columns = hold.shape[2]
    extra = keep_a.shape[2] - columns
    hold[...] = plus(keep_a.at[:, :, 0:columns], got_a.at[:, :, 0:columns])
    split_near(ids_ref, hold, send_a, left_a, columns)
    for q in range(keep_a.shape[0]):
        total = plus(keep_a.at[q, :, columns:], got_a.at[q, :, columns:])
        at = columns + q % 2 * extra
        for out in (send_a, left_a):
            out[q // 2, :, at : at + extra] = total
    hold_b[...] = plus(keep_b, got_b)
    split_dp(ids_ref, hold_b, send_b, left_b, hold_b.shape[2])


def merge_ff_kernel(ids_ref, keep_a, got_a, keep_b, got_b, send, left, hold):
    columns = hold.shape[2] - keep_b.shape[2]
    extra = keep_a.shape[2] - columns
    hold[:, :, 0:columns] = plus(keep_a.at[:, :, 0:columns], got_a.at[:, :, 0:columns])
    hold[:, :, columns:] = plus(keep_b, got_b)
    far = ids_ref[3]
    width = hold.shape[2]
    send[:, 0:width] = hold[1 - far]
    left[:, 0:width] = hold[far]
    for k in range(2):
        total = plus(keep_a.at[k, :, columns:], got_a.at[k, :, columns:])
        at = width + k * extra
        for out in (send, left):
            out[:, at : at + extra] = total


def grads_oh_kernel(ids_ref, one_own, one_got, mixed_own, mixed_got, two_own, two_got, ct_own, ct_got,
                    send, keep, hold):
    width, features = mixed_own.shape[1], ct_own.shape[0]
    shape3 = hold.shape[:2]
    product = product_of(one_own, one_got, mixed_own[...], mixed_got[...])
    hold[:, :, 0:width] = product.astype(BF).reshape(*shape3, width)
    hold[:, :, width:] = jnp.zeros((*shape3, hold.shape[2] - width), BF)
    product = product_of(
        two_own, two_got, ct_own[...].astype(F32).T.astype(BF), ct_got[...].astype(F32).T.astype(BF)
    )
    hold[:, :, width : width + features] = product.astype(BF).reshape(*shape3, features)
    split_dp(ids_ref, hold, send, keep, hold.shape[2])


def grads_q_kernel(ids_ref, at_own, at_got, b_own, b_got, send_a, keep_a, send_b, keep_b, hold):
    cut, total = keep_a.shape[2], hold.shape[2]
    hold[...] = product_of(at_own, at_got, b_own[...], b_got[...]).astype(BF).reshape(hold.shape)
    split_dp(ids_ref, hold.at[:, :, 0:cut], send_a, keep_a, cut)
    split_near(ids_ref, hold.at[:, :, cut:], send_b, keep_b, total - cut)


def fold_q_kernel(ids_ref, keep_a, got_a, keep_b, got_b, up_keep, up_got, oh_keep, oh_got, embed_own, embed_got,
                  send_a, left_a, send_b, left_b, send_o, left_o, hold_a, hold_b, hold_o, hold_e):
    hold_a[...] = plus(keep_a, got_a)
    split_near(ids_ref, hold_a, send_a, left_a, hold_a.shape[2])
    hold_b[...] = plus(keep_b, got_b)
    columns = hold_b.shape[2]
    split_dp(ids_ref, hold_b, send_b, left_b, columns)
    hold_o[...] = plus(oh_keep, oh_got)
    split_near(ids_ref, hold_o, send_o, left_o, hold_o.shape[2])
    hold_e[...] = plus(embed_own, embed_got)
    width = hold_e.shape[2]
    for out, at in ((send_b, 1 - ids_ref[1]), (left_b, ids_ref[1])):
        for k in range(4):
            start = columns + k % 2 * width
            out[k // 2, :, start : start + width] = hold_e[4 * at + k]
    start = columns + 2 * width
    half = send_b.shape[2] - start
    for k in range(2):
        at = up_keep.shape[1] - (2 - k) * half
        total = plus(up_keep.at[:, at : at + half], up_got.at[:, at : at + half])
        for out in (send_b, left_b):
            out[k, :, start:] = total


def merge_q_kernel(ids_ref, keep_a, got_a, keep_b, got_b, oh_keep, oh_got,
                   send, left, pair_ref, embed_near, embed_both, hold, hold_e):
    width = embed_near.shape[1]
    half = pair_ref.shape[2] // 2
    first = keep_a.shape[2]
    columns = keep_b.shape[2] - half - 2 * width
    total = hold.shape[2]
    hold[:, :, 0:first] = plus(keep_a, got_a)
    hold[:, :, first : first + columns] = plus(keep_b.at[:, :, 0:columns], got_b.at[:, :, 0:columns])
    hold[:, :, first + columns :] = plus(oh_keep, oh_got)
    for k in range(4):
        span = slice(columns + k % 2 * width, columns + (k % 2 + 1) * width)
        hold_e[k] = plus(keep_b.at[k // 2, :, span], got_b.at[k // 2, :, span])
    far, near = ids_ref[3], ids_ref[2]
    for out, at in ((send, 1 - far), (left, far)):
        out[:, 0:total] = hold[at]
        out[:, total:] = hold_e[2 * at + near]
    embed_near[...] = hold_e[2 * far + 1 - near]
    embed_both[...] = hold_e[2 * (1 - far) + 1 - near]
    for k in range(2):
        span = slice(k * half, (k + 1) * half)
        pair_ref[0, :, span] = keep_b[k, :, columns + 2 * width :]
        pair_ref[1, :, span] = got_b[k, :, columns + 2 * width :]


def expand(ids_ref, rows_ref, pair_own, pair_got, out_ref, block):
    rows = rows_ref.shape[0]
    groups = block.shape[0] // rows
    tiles = block.shape[1] // LANES
    for a, b in ((0, 0), (0, 1), (1, 0), (1, 1)):
        source = pair_got if a else pair_own
        for q in range(tiles):
            for g in range(groups):
                at = (q * groups + g) * LANES
                block[g * rows : (g + 1) * rows, q * LANES : (q + 1) * LANES] = source[b, :, at : at + LANES]
        core, dp = (1 - ids_ref[0] if a else ids_ref[0]), (1 - ids_ref[1] if b else ids_ref[1])
        at = pl.multiple_of((core * 2 + dp) * block.shape[1], LANES)
        out_ref[:, pl.ds(at, block.shape[1])] = nn(rows_ref[...], block[...])


def insert_east(cols, fields_ref, east_ref, out_ref):
    variables = east_ref.shape[1]
    out_ref[...] = fields_ref[...]
    for item in range(east_ref.shape[0]):
        out_ref[item, pl.ds(cols - 1, variables, stride=cols), :] = east_ref[item].astype(F32)


def close_kernel(cols, ids_ref, fields_ref, east_ref, pos_ref, pos_got_ref, *refs):
    outs = refs
    if len(refs) > 2:
        (up_ref, up_got_ref, rows_ref, pair_own, pair_got), outs, block = refs[:5], refs[5:-1], refs[-1]
        width = outs[2].shape[1]
        outs[2][...] = up_ref[:, 0:width].astype(F32) + up_got_ref[:, 0:width].astype(F32)
        expand(ids_ref, rows_ref, pair_own, pair_got, outs[3], block)
    insert_east(cols, fields_ref, east_ref, outs[0])
    outs[1][...] = pos_ref[...].astype(F32) + pos_got_ref[...].astype(F32)


def end_kernel(*refs):
    if len(refs) > 3:
        (near_ref, both_ref, keep_ref, got_ref), refs = refs[:4], refs[4:]
        out_ref, head_ref, grad_ref = refs[2:]
        both = keep_ref[...].astype(F32) + got_ref[...].astype(F32)
        width = grad_ref.shape[2]
        for c in range(3):
            grad_ref[c] = both[:, c * width : (c + 1) * width]
        out_ref[...] = both[:, 3 * width : 4 * width]
        head_ref[...] = both[:, 4 * width : 4 * width + head_ref.shape[1]]
        embed = both[:, both.shape[1] - near_ref.shape[1] :]
        total = embed + near_ref[...].astype(F32) + both_ref[...].astype(F32)
    else:
        total, refs = jnp.sum(refs[0][...].astype(F32), axis=0), refs[1:]
    features = refs[0].shape[1]
    refs[0][...] = total[:, 0:features]
    refs[1][...] = total[:, LANES:].T[features - LANES : features - LANES + 2, :]


def local(
    dataset,
    indices,
    run_count,
    run_mean,
    run_var,
    w_embed,
    pos_embed,
    gains,
    w_qkv,
    w_out,
    w_up,
    w_down,
    w_head,
    cotangent,
):
    items = indices.shape[0]
    variables, height, columns = dataset.shape[1:]
    dp, lon = lax.axis_size("dp"), lax.axis_size("lon")
    everyone = dp * lon
    width = w_embed.shape[1]
    local_width = w_qkv.shape[2]
    heads = local_width // HDIM
    item_tokens = cotangent.shape[1]
    tokens = items * item_tokens
    features = w_embed.shape[0]
    hidden_units = w_up.shape[1]
    scale = 1.0 / math.sqrt(HDIM)
    group, far = heads, lon // heads
    groups = [[group * g + i for i in range(group)] for g in range(far)]
    across = [[i + group * g for g in range(far)] for i in range(group)]
    assert items * HDIM == LANES and item_tokens == LANES and height == LANES and columns == 4
    lon_at, dp_at = lax.axis_index("lon"), lax.axis_index("dp")
    ids = [lon_at % 2, dp_at, lon_at // 2 % 2, lon_at // 4 % 2, *[lon_at // 2 ^ k for k in range(4)], dp_at * lon + lon_at, lax.axis_index("mp")]
    ids = jnp.stack(ids).astype(jnp.int32)
    paired = dp == 2 and lon == 8
    parts, rows = width // (2 * (width // everyone)), width // everyone
    turned_shape = (
        [shape((parts, rows, tokens))] * 2 if paired else [shape((width, tokens))]
    )
    turned_hold = pltpu.VMEM((parts, 2, rows, tokens) if paired else (8, LANES), BF)

    alone = dict(axis_index_groups=groups) if far > 1 else {}

    vmem, smem = pl.BlockSpec(memory_space=pltpu.VMEM), pl.BlockSpec(memory_space=pltpu.SMEM)
    assert dp == 2

    data = dataset.transpose(0, 1, 3, 2).reshape(dataset.shape[0], variables * columns, height)
    fields, edge, moments, _ = call(
        moments_kernel,
        "moments",
        [
            warm((items, variables * columns, height), F32),
            warm((items, variables, height)),
            warm((everyone, 8, LANES), F32),
        ],
        indices, data,
        in_specs=[pl.BlockSpec(memory_space=pltpu.SMEM), pl.BlockSpec(memory_space=pl.ANY)],
        scratch=[pltpu.VMEM((LANES, LANES), F32), pltpu.SemaphoreType.DMA((items,))],
    )
    edge = from_behind(edge, "lon", 1)
    moments = lax.all_to_all(moments, ("dp", "lon"), 0, 0)
    wh_turned = w_head.T

    out = call(
        functools.partial(start_kernel, float(items * height * columns)),
        "start",
        [
            *[shape((1, variables), F32)] * 3,
            shape((tokens, width), F32),
            shape((features, tokens)),
            *([shape((2, 3, item_tokens, LANES))] * 4 if paired else [shape((heads, 3, item_tokens, LANES))]),
            *turned_shape,
        ],
        ids, Warm(moments), *[r.reshape(1, variables) for r in (run_count, run_mean, run_var)],
        Warm(fields), Warm(edge), w_embed, pos_embed, gains, w_qkv,
        in_specs=[smem, *[vmem] * 9, pl.BlockSpec(memory_space=pl.ANY)],
        scratch=[
            pltpu.VMEM((LANES, LANES), F32),
            pltpu.VMEM((8, LANES), F32),
            turned_hold,
            pltpu.VMEM(w_qkv.shape, BF),
            pltpu.SemaphoreType.DMA,
            pltpu.VMEM((heads, 3, item_tokens, LANES), BF),
        ],
        flops=2 * tokens * width * (features + 3 * local_width),
    )
    count = 4 if paired else 1
    stats, (hidden_zero, patches), packed = out[:3], out[3:5], out[5 : 5 + count]
    normed_one, token = out[5 + count : -1], out[-1]

    def along(messages):
        return [messages[0], *[swap(messages[k], "lon", 2 * k) for k in range(1, count)]]

    if paired:
        own = along(packed)
    else:
        sent = lax.all_to_all(packed[0], "lon", 0, 0, **alone)
        kv = sent
        if far > 1:
            kv = lax.all_gather(sent, "lon", axis=0, tiled=True, axis_index_groups=across)

    if paired:
        wo_got, normed_got = swap(w_out, "mp", 1), swap(normed_one[1], "lon", 1)
        other = [swap(x, "lon", 1) for x in own]
    if paired:
        attended, kept, token = pair_attend(own, other, items, scale, [token, normed_got, wo_got])
        attended = along(attended)
    else:
        attended, attended_t, weights_t, token = attend(sent, kv, items, scale, [token])
        attended = [lax.all_to_all(attended, "lon", 0, 0, **alone)]
    anywhere = pl.BlockSpec(memory_space=pl.ANY)
    d_two, d_act, ct_turned, *mine, token = call(
        cotangent_kernel,
        "cotangent",
        [
            shape((tokens, width), F32),
            shape((tokens, hidden_units)),
            shape((features, tokens)),
            *[shape((rows, features))] * paired,
        ],
        ids, cotangent.transpose(0, 2, 1), wh_turned, w_down,
        after=[token],
        scratch=[pltpu.VMEM((everyone, rows, features), BF)] * paired,
        flops=2 * tokens * width * (features + hidden_units),
    )

    if paired:
        ct_got = swap(ct_turned, "lon", 1)
        attended[0] = pin(attended[0], [token])
        attended += [swap(x, "mp", 1) for x in attended]
    if paired:
        branches = [attended[0], *[Warm(x) for x in attended[1:]], w_out, Warm(wo_got)]
    else:
        mixed, branch, token = call(
            project_kernel,
            "project",
            [shape((tokens, local_width)), warm((tokens, width))],
            ids, *attended, w_out,
            after=[token],
            flops=2 * tokens * width * local_width,
        )
        branches = [Warm(branch), Warm(swap(branch, "mp", 1))]
    block = min(512, hidden_units // 2)
    chunks = hidden_units // block
    out = call(
        functools.partial(forward_kernel, count if paired else 0),
        "forward",
        [
            warm((tokens, width)),
            *[shape((tokens, local_width))] * paired,
            shape((tokens, width), F32),
            shape((tokens, hidden_units)),
            shape((2, tokens, hidden_units // 2)),
            shape((tokens, hidden_units // 2)),
            *turned_shape,
        ],
        ids, *branches, hidden_zero, gains, w_up, d_act,
        after=[token],
        in_specs=[
            smem,
            *([*[vmem] * (len(branches) - 2), anywhere, anywhere] if paired else [vmem] * 2),
            anywhere,
            vmem,
            anywhere,
            anywhere,
        ],
        out_specs=[*[vmem] * (1 + paired), *[anywhere] * (4 + len(turned_shape))],
        scratch=[
            *[pltpu.VMEM(x.shape, BF) for x in turned_shape],
            pltpu.VMEM((tokens, width), F32),
            pltpu.VMEM((tokens, width), F32),
            pltpu.VMEM((chunks, width, block), BF),
            pltpu.VMEM((chunks, tokens, block), BF),
            pltpu.VMEM((tokens, hidden_units), BF),
            pltpu.VMEM((2, tokens, hidden_units // 2), BF),
            pltpu.VMEM((tokens, width), BF),
            turned_hold,
            pltpu.SemaphoreType.DMA((2 * chunks,)),
            pltpu.SemaphoreType.DMA((2 + len(turned_shape) + 2 * chunks,)),
            pltpu.SemaphoreType.DMA,
            *[
                pltpu.VMEM((2, *w_out.shape), BF),
                pltpu.VMEM((2, tokens, local_width), BF),
                pltpu.SemaphoreType.DMA((2,)),
            ] * paired,
        ],
        limit=32,
        flops=4 * tokens * width * hidden_units,
    )
    d_norm, *out, token = out
    if paired:
        mixed, out = out[0], out[1:]
        mixed_got = swap(mixed, "lon", 1)
    hidden_one, d_pre, activated, act_send = out[:4]
    normed_two = out[4:]
    d_norm_got = swap(d_norm, "mp", 1)
    half = hidden_units // 2
    if paired:
        inner_columns = features // rows * LANES
        first = half - LANES
        out_a = shape((parts // 2, rows, first + inner_columns))
        out_b = shape((parts // 2, rows, hidden_units - first))
        send_a, keep_a, send_b, keep_b, token = call(
            grads_ff_kernel,
            "grads_ff",
            [out_a, out_a, out_b, out_b],
            ids, normed_two[0], Warm(swap(normed_two[1], "lon", 1)), d_pre, Warm(swap(d_pre, "lon", 1)),
            ct_turned, Warm(ct_got), activated, Warm(swap(act_send, "lon", 1)),
            after=[token],
            scratch=[
                pltpu.VMEM((parts, rows, hidden_units), BF),
                pltpu.VMEM((2, parts // 2, rows, inner_columns), BF),
            ],
            limit=32,
            flops=2 * tokens * (width + features) * hidden_units,
        )
        got_a, got_b = swap(send_a, "dp", 1), swap(send_b, "lon", 2)
    forward, token = call(
        down_kernel,
        "down",
        [shape((tokens, width))],
        activated, w_down,
        after=[token],
        flops=2 * tokens * width * hidden_units,
    )

    out = call(
        second_kernel,
        "second",
        [
            shape((tokens, width), F32),
            shape((1, width), F32),
            shape((heads, item_tokens, LANES)),
            *turned_shape,
        ],
        ids, Warm(hidden_one), Warm(d_two), Warm(d_norm), Warm(d_norm_got), gains, Warm(w_out),
        after=[token],
        scratch=[turned_hold],
        flops=2 * tokens * width * local_width,
    )
    d_one, gain_two, d_mixed = out[0], out[1], out[2:3]
    d_one_turned, token = out[3:-1], out[-1]
    if paired:
        d_one_got = swap(d_one_turned[1], "lon", 1)
    if paired:
        chips = [[2 * k + c for k in range(lon // 2)] for c in range(2)]
        d_heads = lax.all_to_all(
            d_mixed[0].reshape(lon // 2, 2, item_tokens, LANES), "lon", 0, 0, axis_index_groups=chips
        )
    else:
        d_heads = lax.all_to_all(d_mixed[0], "lon", 0, 0, **alone)
    forward_got = swap(forward, "mp", 1)
    if paired:
        out_a = shape((2, rows, first + 2 * inner_columns))
        out_b = shape((2, rows, hidden_units - first))
        send_a, keep_a, send_b, keep_b, token = call(
            fold_ff_kernel,
            "fold_ff",
            [out_a, out_a, out_b, out_b],
            ids, keep_a, Warm(got_a), keep_b, Warm(got_b),
            after=[token],
            scratch=[
                pltpu.VMEM((parts // 2, rows, first), BF),
                pltpu.VMEM((parts // 2, rows, hidden_units - first), BF),
            ],
        )
        send_a, send_b = pin([send_a, send_b], [d_heads])
        got_a, got_b = swap(send_a, "lon", 2), swap(send_b, "dp", 1)

    if paired:
        back, cross, token = pair_attend_back(ids, kept, d_heads, items, scale, [token])
        *back, token = call(
            combine_kernel,
            "combine",
            [shape(x.shape) for x in back],
            *back, Warm(swap(pin(cross, [got_a, got_b, forward_got]), "lon", 1)),
            after=[token],
        )
        back = along(back)
    else:
        back, token = attend_back(sent, kv, d_heads, attended_t, weights_t, items, scale, [token])
        if far > 1:
            d_query, d_kv = back
            d_kv = lax.psum_scatter(
                d_kv, "lon", scatter_dimension=0, tiled=True, axis_index_groups=across
            ).astype(BF)
            back = [jnp.concatenate([d_query[:, None], d_kv], axis=1)]
        back = [lax.all_to_all(back[0], "lon", 0, 0, **alone)]
    out = call(
        head_kernel,
        "head",
        [shape((items, features, item_tokens), F32), *turned_shape],
        ids, hidden_one, forward, Warm(forward_got), wh_turned,
        after=[token],
        scratch=[turned_hold],
        flops=2 * tokens * width * features,
    )
    pred, hidden_turned, token = out[0].transpose(0, 2, 1), list(out[1:-1]), out[-1]
    if paired:
        up_send, up_keep, token = call(
            merge_ff_kernel,
            "merge_ff",
            [shape((rows, hidden_units + 4 * inner_columns))] * 2,
            ids, keep_a, Warm(got_a), keep_b, Warm(got_b),
            after=[token],
            scratch=[pltpu.VMEM((2, rows, hidden_units), BF)],
        )
    d_qkv, d_norm, token = call(
        functools.partial(third_kernel, count),
        "third",
        [shape((tokens, 3 * local_width)), warm((tokens, width))],
        ids, back[0], *[Warm(x) for x in back[1:]], Warm(w_qkv),
        after=[token],
        flops=6 * tokens * width * local_width,
    )
    d_norm_got = swap(d_norm, "mp", 1)
    if paired:
        up_send, hidden_turned[1] = pin([up_send, hidden_turned[1]], [token])
        up_got = swap(up_send, "lon", 4)
        wide = local_width + 2 * LANES
        cut = 3 * local_width // 2 + LANES
        first, second = (shape((parts // 2, rows, c)) for c in (cut, 3 * local_width - cut))
        send_a, keep_a, send_b, keep_b, token = call(
            grads_q_kernel,
            "grads_q",
            [first, first, second, second],
            ids, normed_one[0], Warm(normed_got), d_qkv, Warm(swap(d_qkv, "lon", 1)),
            after=[token],
            scratch=[pltpu.VMEM((parts, rows, 3 * local_width), BF)],
            flops=6 * tokens * width * local_width,
        )
        oh_send, oh_keep, token = call(
            grads_oh_kernel,
            "grads_oh",
            [shape((parts // 2, rows, wide))] * 2,
            ids, d_one_turned[0], Warm(d_one_got), mixed, Warm(mixed_got),
            hidden_turned[0], Warm(swap(hidden_turned[1], "lon", 1)), ct_turned, Warm(ct_got),
            after=[token],
            scratch=[pltpu.VMEM((parts, rows, wide), BF)],
            flops=2 * tokens * width * wide,
        )
        oh_got = swap(oh_send, "dp", 1)
        got_a, got_b = swap(send_a, "dp", 1), swap(send_b, "lon", 2)

    out = call(
        functools.partial(last_kernel, columns),
        "last",
        [
            *[shape((item_tokens, width // 2))] * 2,
            shape((items, variables * columns, height), F32),
            shape((items, variables, height)),
            *([shape((parts, rows, 2 * LANES))] * 2 if paired else [shape((width, 2 * LANES))]),
        ],
        ids, Warm(hidden_zero), Warm(d_one), Warm(d_norm), Warm(d_norm_got), gains, gain_two, patches, w_embed,
        after=[token],
        scratch=[
            pltpu.VMEM((2 * LANES, width), F32),
            pltpu.VMEM((2, item_tokens, width // 2), BF),
            pltpu.VMEM((parts, 2, rows, 2 * LANES) if paired else (8, LANES), BF),
        ],
        flops=4 * tokens * width * features,
    )
    pos_send, pos, d_fields, d_edge = out[:4]
    embed, token = out[4:-1], out[-1]
    if not paired:
        east, pos_got = from_behind(d_edge, "lon", -1), swap(pos_send, "dp", 1)
    more, more_outs, more_scratch, rest, rest_outs = [], [], [], [], []
    if paired:
        embed_width = embed[0].shape[2]
        step_a, side = shape((2, rows, cut)), shape((2, rows, wide))
        step_b = shape((2, rows, 3 * local_width - cut + 2 * embed_width + 2 * inner_columns))
        send_a, keep_a, send_b, keep_b, oh_send, oh_keep, token = call(
            fold_q_kernel,
            "fold_q",
            [step_a, step_a, step_b, step_b, side, side],
            ids, keep_a, Warm(got_a), keep_b, Warm(got_b), up_keep, Warm(up_got), oh_keep, Warm(oh_got),
            embed[0], Warm(swap(embed[1], "lon", 1)),
            after=[token],
            scratch=[
                pltpu.VMEM(keep_a.shape, BF),
                pltpu.VMEM(keep_b.shape, BF),
                pltpu.VMEM(oh_keep.shape, BF),
                pltpu.VMEM(embed[0].shape, BF),
            ],
        )
        got_a, got_b, oh_got = swap(send_a, "lon", 2), swap(send_b, "dp", 1), swap(oh_send, "lon", 2)
        east = from_behind(pin(d_edge, [token]), "lon", -1)
        total = 3 * local_width + wide
        final, block = shape((rows, total + embed_width)), shape((rows, embed_width))
        send, keep, pair, embed_near, embed_both, token = call(
            merge_q_kernel,
            "merge_q",
            [final, final, shape((2, rows, 4 * inner_columns)), block, block],
            ids, keep_a, Warm(got_a), keep_b, Warm(got_b), oh_keep, Warm(oh_got),
            after=[token, east],
            scratch=[pltpu.VMEM((2, rows, total), BF), pltpu.VMEM((4, *block.shape), BF)],
        )
        pos_got = swap(pin(pos_send, [token]), "dp", 1)
        more = [up_keep, Warm(up_got), mine[0], pair, Warm(swap(pair, "lon", 1))]
        more_outs = [shape((rows, hidden_units), F32)] * 2
        more_scratch = [pltpu.VMEM((features, hidden_units // 4), BF)]
        rest = [
            Warm(swap(embed_near, "lon", 2)), Warm(swap(embed_both, "lon", 6)),
            keep, Warm(swap(send, "lon", 4)),
        ]
        rest_outs = [
            shape((rows, local_width), F32),
            shape((rows, features), F32),
            shape((3, rows, local_width), F32),
        ]
    else:
        rest = [lax.all_to_all(embed[0].reshape(everyone, rows, 2 * LANES), ("dp", "lon"), 0, 0)]
    *closed, token = call(
        functools.partial(close_kernel, columns),
        "close",
        [shape(d_fields.shape, F32), shape(pos.shape, F32), *more_outs],
        ids, d_fields, Warm(east), pos, Warm(pos_got), *more,
        after=[token],
        scratch=more_scratch,
    )
    *ended, token = call(
        end_kernel,
        "end",
        [shape((rows, features), F32), shape((2, rows), F32), *rest_outs],
        *rest,
        after=[token],
    )
    if paired:
        grad_up, grad_down, (grad_out, grad_head, grad_qkv) = closed[2], closed[3], ended[2:]
    else:
        flat = activated.transpose(1, 0, 2).reshape(tokens, hidden_units)
        grad_up = scatter(nn(normed_two[0], d_pre))
        grad_down = scatter(nn(d_two.T.astype(BF), flat))
        grad_out = scatter(nn(d_one_turned[0], mixed))
        grad_head = scatter(nt(hidden_turned[0], ct_turned))
        grad_qkv = scatter(nn(normed_one[0], d_qkv)).reshape(rows, 3, local_width).transpose(1, 0, 2)
    return (
        pred,
        *[x.reshape(variables) for x in stats],
        closed[0].reshape(items, variables, columns, height).transpose(0, 1, 3, 2),
        ended[0].T,
        closed[1],
        ended[1],
        grad_qkv,
        grad_out.T,
        grad_up,
        grad_down.T,
        grad_head,
    )


def solution(mesh):
    in_specs = (
        P(None, None, None, "lon"),
        P("dp"),
        P(),
        P(),
        P(),
        P(),
        P("lon", None),
        P(),
        P(None, None, "mp"),
        P("mp", None),
        P(None, "mp"),
        P("mp", None),
        P(),
        P("dp", "lon", None),
    )
    out_specs = (
        P("dp", "lon", None),
        P(),
        P(),
        P(),
        P("dp", None, None, "lon"),
        P(None, ("dp", "lon")),
        P("lon", "dp"),
        P(None, ("dp", "lon")),
        P(None, ("dp", "lon"), "mp"),
        P("mp", ("dp", "lon")),
        P(("dp", "lon"), "mp"),
        P("mp", ("dp", "lon")),
        P(("dp", "lon"), None),
    )
    return jax.shard_map(local, mesh=mesh, in_specs=in_specs, out_specs=out_specs, check_vma=False)
```

```python
import functools
import math

import jax
import jax.numpy as jnp
from jax import lax
from jax.experimental import pallas as pl
from jax.experimental.pallas import tpu as pltpu
from jax.sharding import PartitionSpec as P

HDIM = 64
PATCH = 2
LANES = 128
NORM_EPS = 1e-06
STAT_EPS = 1e-06
BF = jnp.bfloat16
F32 = jnp.float32
MIB = 2**20


def swap(block, axis, distance):
    route = [(i, i ^ distance) for i in range(lax.axis_size(axis))]
    return lax.ppermute(block, axis, route)


def from_behind(block, axis, distance):
    size = lax.axis_size(axis)
    route = [((i - distance) % size, i) for i in range(size)]
    return lax.ppermute(block, axis, route)


def pick(x, index, axis):
    return lax.dynamic_index_in_dim(x, index, axis, keepdims=False)


def halve(total, dims):
    for axis, bit in dims:
        side = (lax.axis_index(axis) // bit) % 2
        got = swap(pick(total, 1 - side, 0), axis, bit)
        total = (pick(total, side, 0).astype(F32) + got.astype(F32)).astype(BF)
    return total


def scatter(total):
    dp, lon = lax.axis_size("dp"), lax.axis_size("lon")
    dims = []
    for axis, size in (("dp", dp), ("lon", lon)):
        bit = size // 2
        while bit:
            dims.append((axis, bit))
            bit //= 2
    rows, columns = total.shape
    total = total.astype(BF).reshape((2,) * len(dims) + (rows // (dp * lon), columns))
    order = sorted(range(len(dims)), key=lambda i: (dims[i][1] > 1 or dims[i][0] == "dp", i))
    total = total.transpose([*order, len(dims), len(dims) + 1])
    return halve(total, [dims[i] for i in order]).astype(F32)


def nt(a, b):
    return lax.dot_general(a, b, (((1,), (1,)), ((), ())), preferred_element_type=F32)


def nn(a, b):
    return lax.dot_general(a, b, (((1,), (0,)), ((), ())), preferred_element_type=F32)


def item_mask(rows, lanes, item):
    lane = lax.broadcasted_iota(jnp.int32, (rows, lanes), 1)
    return (lane >= item * HDIM) & (lane < (item + 1) * HDIM)


def interleave(first, second):
    low = item_mask(first.shape[0], LANES, 0)
    return (
        jnp.where(low, first, pltpu.roll(second, HDIM, 1)),
        jnp.where(low, pltpu.roll(first, HDIM, 1), second),
    )


def norm_parts(hidden):
    centred = hidden - jnp.mean(hidden, axis=-1, keepdims=True)
    variance = jnp.mean(centred * centred, axis=-1, keepdims=True)
    inverse = lax.rsqrt(variance + NORM_EPS)
    return centred * inverse, inverse


def norm_back(unit, inverse, scaling, grad):
    scaled = grad * scaling
    back = inverse * (
        scaled
        - jnp.mean(scaled, axis=-1, keepdims=True)
        - unit * jnp.mean(scaled * unit, axis=-1, keepdims=True)
    )
    return back, jnp.sum(grad * unit, axis=0, keepdims=True)


def emit_turned(x, ids_ref, outs, hold):
    turned = x.T.astype(BF)
    if len(outs) == 1:
        outs[0][...] = turned
        return
    keep, send = outs
    parts, rows, tokens = keep.shape
    hold[...] = turned.reshape(parts, 2, rows, tokens)
    core = ids_ref[0]
    keep[...] = hold[:, pl.ds(core, 1)].reshape(parts, rows, tokens)
    send[...] = hold[:, pl.ds(1 - core, 1)].reshape(parts, rows, tokens)


class Warm:
    def __init__(self, value):
        self.value = value


def call(body, name, outs, *args, after=(), grid=(), in_specs=None, out_specs=None, scratch=(), limit=24, flops=0):
    vmem = pl.BlockSpec(memory_space=pltpu.VMEM)
    smem = pl.BlockSpec(memory_space=pltpu.SMEM)
    shapes = [o.value if isinstance(o, Warm) else o for o in outs]
    plain = [a.value if isinstance(a, Warm) else a for a in args]
    if in_specs is None:
        in_specs = [smem if a.dtype == jnp.int32 else vmem for a in plain]
    if out_specs is None:
        out_specs = [vmem] * len(outs)
    token = pl.BlockSpec((8, LANES), lambda *at: (0, 0)) if grid else vmem
    nbytes = sum(math.prod(a.shape) * a.dtype.itemsize for a in [*plain, *shapes])
    here, skip, there = len(args), len(after), len(outs)

    def with_token(*refs):
        refs = list(refs)
        refs[here + skip + there][...] = jnp.zeros((8, LANES), F32)
        body(*refs[:here], *refs[here + skip : here + skip + there], *refs[here + skip + there + 1 :])

    def cold(x):
        if isinstance(x, Warm):
            return x.value
        return x if x.dtype == jnp.int32 else pltpu.with_memory_space_constraint(x, pltpu.HBM)

    return pl.pallas_call(
        with_token,
        grid=grid,
        out_shape=[
            *[o.value if isinstance(o, Warm) else pltpu.HBM(o.shape, o.dtype) for o in outs],
            pltpu.HBM((8, LANES), F32),
        ],
        in_specs=[*in_specs, *[pl.BlockSpec(memory_space=pl.ANY)] * skip],
        out_specs=[*out_specs, token],
        scratch_shapes=list(scratch),
        compiler_params=pltpu.CompilerParams(vmem_limit_bytes=limit * MIB),
        cost_estimate=pl.CostEstimate(flops=int(flops), bytes_accessed=nbytes, transcendentals=0),
        name=name,
    )(*[cold(a) for a in args], *[cold(a) for a in after])


def shape(dims, kind=BF):
    return jax.ShapeDtypeStruct(dims, kind)


def warm(dims, kind=BF):
    return Warm(shape(dims, kind))


def feature_order(variables, back):
    features = PATCH * PATCH * variables
    natural = lax.broadcasted_iota(jnp.int32, (features, features), 1 if back else 0)
    sorted_ = lax.broadcasted_iota(jnp.int32, (features, features), 0 if back else 1)
    hit = (natural // 4 == sorted_ % variables) & (natural % 4 == sorted_ // variables)
    return jnp.where(hit, 1.0, 0.0).astype(BF)


def send_pairs(ids_ref, hold, messages):
    if len(messages) == 1:
        messages[0][...] = hold[...]
        return
    for k, message in enumerate(messages):
        message[...] = hold[pl.ds(2 * ids_ref[4 + k], 2)]


def moments_kernel(index_ref, data_ref, fields_ref, edge_ref, moments_ref, turn_ref, sems):
    items, variables, height = edge_ref.shape
    cols = fields_ref.shape[1] // variables
    copies = [
        pltpu.make_async_copy(data_ref.at[index_ref[i]], fields_ref.at[i], sems.at[i])
        for i in range(items)
    ]
    for copy in copies:
        copy.start()
    turn_ref[...] = jnp.zeros_like(turn_ref)
    for copy in copies:
        copy.wait()
    blocks = [
        fields_ref[i, pl.ds(c, variables, stride=cols), :] for i in range(items) for c in range(cols)
    ]
    for i in range(items):
        edge_ref[i] = blocks[i * cols + cols - 1].astype(BF)
    count = float(items * cols * height)
    mean = jnp.sum(sum(blocks), axis=1, keepdims=True) * (1.0 / count)
    spread = jnp.sum(sum(jnp.square(b - mean) for b in blocks), axis=1, keepdims=True)
    turn_ref[0:variables, 0:1] = mean
    turn_ref[HDIM : HDIM + variables, 0:1] = spread
    turned = turn_ref[...].T
    moments_ref[...] = jnp.broadcast_to(turned[0:1, :][None], moments_ref.shape)


def start_kernel(local_count, ids_ref, mom_ref, count_ref, mean_ref, var_ref, fields_ref, edge_ref, we_ref,
                 pos_ref, gains_ref, wq_ref, new_count_ref, new_mean_ref, new_var_ref, hidden_ref, patches_ref,
                 *rest):
    (*outs, column_ref, run_ref, hold, weights, sem, qkv_ref) = rest
    if len(outs) > 2:
        messages, turned = outs[:-2], outs[-2:]
    else:
        messages, turned = outs[:1], outs[1:]
    copy = pltpu.make_async_copy(wq_ref, weights, sem)
    copy.start()
    members = mom_ref.shape[0]
    items, rows, height = fields_ref.shape
    variables = edge_ref.shape[1]
    cols = rows // variables
    half = height // PATCH
    moments = mom_ref[:, 0, :]
    run_ref[...] = jnp.zeros_like(run_ref)
    for k, ref in enumerate((count_ref, mean_ref, var_ref)):
        run_ref[k : k + 1, 0:variables] = ref[...]
    batch_count = local_count * members
    batch_mean = jnp.sum(moments, axis=0, keepdims=True) * (1.0 / members)
    off = moments - batch_mean
    spread = jnp.sum(pltpu.roll(moments, HDIM, 1) + local_count * off * off, axis=0, keepdims=True)
    run_count, run_mean, run_var = (run_ref[k : k + 1, :] for k in range(3))
    new_count = run_count + batch_count
    shift = batch_mean - run_mean
    new_mean = run_mean + shift * (batch_count / new_count)
    new_var = (
        run_var * run_count + spread + shift * shift * (run_count * batch_count / new_count)
    ) / new_count
    new_count_ref[...] = new_count[:, 0:variables]
    new_mean_ref[...] = new_mean[:, 0:variables]
    new_var_ref[...] = new_var[:, 0:variables]
    column_ref[...] = jnp.zeros_like(column_ref)
    column_ref[0:1, :] = new_mean
    column_ref[1:2, :] = lax.rsqrt(new_var + STAT_EPS)
    column = column_ref[...].T
    centre, inverse = column[0:variables, 0:1], column[0:variables, 1:2]

    def scaled(block):
        return ((block - centre) * inverse).astype(BF)

    row = lax.broadcasted_iota(jnp.int32, (2 * height, LANES), 0)
    lane = lax.broadcasted_iota(jnp.int32, (2 * height, LANES), 1)
    sort = [
        jnp.where(
            (row // height == lane // half) & (row % height == PATCH * (lane % half) + a), 1.0, 0.0
        ).astype(BF)
        for a in range(PATCH)
    ]
    natural = feature_order(variables, False)
    hidden = []
    for item in range(items):
        west = scaled(edge_ref[item].astype(F32))
        own = [
            scaled(fields_ref[item, pl.ds(c, variables, stride=cols), :]) for c in range(cols - 1)
        ]
        first = jnp.concatenate([west, own[0]], axis=0)
        second = jnp.concatenate([own[1], own[2]], axis=0)
        both = jnp.concatenate([first, second], axis=1)
        patches = jnp.concatenate([nn(both, sort[a]) for a in range(PATCH)], axis=0)
        patches = nn(natural, patches.astype(BF))
        patches_ref[:, item * LANES : (item + 1) * LANES] = patches.astype(BF)
        hidden.append(nn(patches.T.astype(BF), we_ref[...]) + pos_ref[...].astype(F32))
    hidden = jnp.concatenate(hidden, axis=0)
    hidden_ref[...] = hidden
    unit, _ = norm_parts(hidden)
    normed = unit * gains_ref[0:1, :]
    low = normed.astype(BF)
    emit_turned(normed, ids_ref, turned, hold)
    copy.wait()
    for c in range(3):
        product = nn(low, weights[c])
        for t in range(product.shape[1] // LANES):
            tile = product[:, t * LANES : (t + 1) * LANES]
            a, b = interleave(tile[:LANES], tile[LANES:])
            qkv_ref[2 * t, c] = a.astype(BF)
            qkv_ref[2 * t + 1, c] = b.astype(BF)
    send_pairs(ids_ref, qkv_ref, messages)


def cotangent_kernel(ids_ref, ct_ref, wh_ref, wd_ref, *refs):
    if len(refs) > 3:
        two_ref, act_ref, ct_turned_ref, mine_ref, hold = refs
        hold[...] = wh_ref[...].astype(F32).T.astype(BF).reshape(hold.shape)
        mine_ref[...] = hold[ids_ref[8]]
    else:
        two_ref, act_ref, ct_turned_ref = refs
    grads = []
    for item in range(ct_ref.shape[0]):
        ct = ct_ref[item].T.astype(BF)
        ct_turned_ref[:, item * LANES : (item + 1) * LANES] = ct_ref[item].astype(BF)
        grads.append(nn(ct, wh_ref[...]))
    d_two = jnp.concatenate(grads, axis=0)
    two_ref[...] = d_two
    act_ref[...] = nt(d_two.astype(BF), wd_ref[...]).astype(BF)


def attend_kernel(items, scale, q_ref, kv_ref, o_ref, ot_ref, pt_ref, vt_ref):
    keys = kv_ref.shape[0] * kv_ref.shape[2]

    @pl.when(pl.program_id(0) == 0)
    def _():
        vt_ref[...] = kv_ref[:, 2].reshape(keys, LANES).astype(F32).T.astype(BF)

    rows = q_ref.shape[0] * q_ref.shape[2]
    queries = q_ref[:, 0].reshape(rows, LANES) * BF(scale)
    key_rows = kv_ref[:, 1].reshape(keys, LANES)
    for item in range(items):
        chosen = jnp.where(item_mask(rows, LANES, item), queries, BF(0))
        scores = nt(key_rows, chosen)
        top = jnp.max(scores, axis=0, keepdims=True)
        raised = jnp.exp(scores - top)
        total = jnp.sum(raised, axis=0, keepdims=True)
        weights = (raised * (1.0 / total)).astype(BF)
        pt_ref[item] = weights
        span = slice(item * HDIM, (item + 1) * HDIM)
        ot_ref[span, :] = nn(vt_ref[span, :], weights)
    o_ref[...] = ot_ref[...].T.astype(BF).reshape(o_ref.shape)


def attend(q, kv, items, scale, after):
    peers, _, tokens, lanes = q.shape
    rows, keys = peers * tokens, kv.shape[0] * tokens
    step = max(1, min(peers, 256 * 1024 // keys // tokens))
    block = step * tokens
    return call(
        functools.partial(attend_kernel, items, scale),
        "attend",
        [
            shape((peers, tokens, lanes)),
            shape((lanes, rows), F32),
            shape((items, keys, rows)),
        ],
        Warm(q),
        Warm(kv),
        after=after,
        grid=(peers // step,),
        in_specs=[
            pl.BlockSpec((step, 3, tokens, lanes), lambda j: (j, 0, 0, 0)),
            pl.BlockSpec(kv.shape, lambda j: (0, 0, 0, 0)),
        ],
        out_specs=[
            pl.BlockSpec((step, tokens, lanes), lambda j: (j, 0, 0)),
            pl.BlockSpec((lanes, block), lambda j: (0, j)),
            pl.BlockSpec((items, keys, block), lambda j: (0, 0, j)),
        ],
        scratch=[pltpu.VMEM((lanes, keys), BF)],
        limit=24 if keys <= 2048 else 56,
        flops=8 * rows * keys * lanes,
    )


def pair_attend_kernel(items, scale, *refs):
    sources, (*outs, ot_ref, pt_ref, query_ref, key_ref, value_ref, vt_ref) = refs[:8], refs[8:]
    tokens = sources[0].shape[2]
    for k, source in enumerate(sources):
        span = slice(k * tokens, (k + 1) * tokens)
        if k < len(outs):
            query_ref[0, span, :] = source[0, 0] * BF(scale)
        key_ref[0, span, :] = source[0, 1]
        value_ref[0, span, :] = source[0, 2]
        vt_ref[:, span] = source[0, 2].astype(F32).T.astype(BF)
    queries = query_ref[0]
    for item in range(items):
        chosen = jnp.where(item_mask(queries.shape[0], LANES, item), queries, BF(0))
        scores = nt(key_ref[0], chosen)
        top = jnp.max(scores, axis=0, keepdims=True)
        raised = jnp.exp(scores - top)
        total = jnp.sum(raised, axis=0, keepdims=True)
        weights = (raised * (1.0 / total)).astype(BF)
        pt_ref[0, item] = weights
        span = slice(item * HDIM, (item + 1) * HDIM)
        ot_ref[0, span, :] = nn(vt_ref[span, :], weights)
    attended = ot_ref[0].T.astype(BF)
    for k, out in enumerate(outs):
        out[0] = attended[k * tokens : (k + 1) * tokens]


def pair_attend(own, other, items, scale, after):
    _, _, tokens, lanes = own[0].shape
    rows, keys = len(own) * tokens, 2 * len(own) * tokens
    wide = lambda *dims: pl.BlockSpec((1, *dims), lambda h: (h, *[0] * len(dims)))
    *outs, ot, pt, q, k, v, token = call(
        functools.partial(pair_attend_kernel, items, scale),
        "attend",
        [
            *[shape((2, tokens, lanes))] * len(own),
            shape((2, lanes, rows), F32),
            shape((2, items, keys, rows)),
            shape((2, rows, lanes)),
            shape((2, keys, lanes)),
            shape((2, keys, lanes)),
        ],
        own[0],
        *[Warm(x) for x in [*own[1:], *other]],
        after=after,
        grid=(2,),
        in_specs=[wide(3, tokens, lanes)] * (2 * len(own)),
        out_specs=[
            *[wide(tokens, lanes)] * len(own),
            wide(lanes, rows),
            wide(items, keys, rows),
            wide(rows, lanes),
            wide(keys, lanes),
            wide(keys, lanes),
        ],
        scratch=[pltpu.VMEM((lanes, keys), BF)],
        limit=32,
        flops=16 * rows * keys * lanes,
    )
    return outs, (q, k, v, ot, pt), token


def pair_attend_back_kernel(items, scale, ids_ref, query_ref, key_ref, value_ref, ot_ref, pt_ref, grads_ref, *refs):
    *outs, cross_ref, kt_ref, grad_rows, dqt_ref, dk_sum, dv_sum = refs
    tokens = grads_ref.shape[2]
    for k in range(len(outs)):
        grad_rows[k * tokens : (k + 1) * tokens, :] = grads_ref[ids_ref[4 + k], 0]
    kt_ref[...] = (key_ref[0].astype(F32) * scale).T.astype(BF)
    queries, grads = query_ref[0], grad_rows[...]
    product = grads.astype(F32).T * ot_ref[0]
    for item in range(items):
        span = slice(item * HDIM, (item + 1) * HDIM)
        mask = item_mask(queries.shape[0], LANES, item)
        grad = jnp.where(mask, grads, BF(0))
        query = jnp.where(mask, queries, BF(0))
        delta = jnp.sum(product[span, :], axis=0, keepdims=True)
        weights = pt_ref[0, item]
        back = (weights.astype(F32) * (nt(value_ref[0], grad) - delta)).astype(BF)
        d_value, d_key = nn(weights, grad), nn(back, query)
        if item == 0:
            dv_sum[...] = d_value
            dk_sum[...] = d_key
        else:
            dv_sum[...] += d_value
            dk_sum[...] += d_key
        dqt_ref[span, :] = nn(kt_ref[span, :], back)
    d_query = dqt_ref[...].T.astype(BF)
    for k in range(2 * len(outs)):
        span = slice(k * tokens, (k + 1) * tokens)
        if k < len(outs):
            outs[k][0, 0] = d_query[span]
        for c, total in ((0, dk_sum), (1, dv_sum)):
            if k < len(outs):
                outs[k][0, 1 + c] = total[span, :].astype(BF)
            else:
                cross_ref[k - len(outs), 0, c] = total[span, :].astype(BF)


def pair_attend_back(ids, kept, d, items, scale, after):
    count, _, tokens, lanes = d.shape
    rows, keys = count * tokens, 2 * count * tokens
    wide = lambda *dims: pl.BlockSpec((1, *dims), lambda h: (h, *[0] * len(dims)))
    *outs, cross, token = call(
        functools.partial(pair_attend_back_kernel, items, scale),
        "attend_back",
        [*[shape((2, 3, tokens, lanes))] * count, shape((count, 2, 2, tokens, lanes))],
        ids, *kept, d,
        after=after,
        grid=(2,),
        in_specs=[
            pl.BlockSpec(memory_space=pltpu.SMEM),
            wide(rows, lanes),
            wide(keys, lanes),
            wide(keys, lanes),
            wide(lanes, rows),
            wide(items, keys, rows),
            pl.BlockSpec((count, 1, tokens, lanes), lambda h: (0, h, 0, 0)),
        ],
        out_specs=[
            *[wide(3, tokens, lanes)] * count,
            pl.BlockSpec((count, 1, 2, tokens, lanes), lambda h: (0, h, 0, 0, 0)),
        ],
        scratch=[
            pltpu.VMEM((lanes, keys), BF),
            pltpu.VMEM((rows, lanes), BF),
            pltpu.VMEM((lanes, rows), F32),
            pltpu.VMEM((keys, lanes), F32),
            pltpu.VMEM((keys, lanes), F32),
        ],
        limit=32,
        flops=32 * rows * keys * lanes,
    )
    return outs, cross, token


def combine_kernel(*refs):
    count = (len(refs) - 1) // 2
    own, cross_ref, outs = refs[:count], refs[count], refs[count + 1 :]
    for k in range(count):
        outs[k][:, 0] = own[k][:, 0]
        for c in range(2):
            outs[k][:, 1 + c] = plus(own[k].at[:, 1 + c], cross_ref.at[k, :, c])


def attend_back_kernel(items, scale, q_ref, kv_ref, d_ref, ot_ref, pt_ref, dq_ref, *rest):
    dkv_ref, (kt_ref, dqt_ref, dk_sum, dv_sum) = rest[:-4], rest[-4:]
    step = pl.program_id(0)
    keys = kv_ref.shape[0] * kv_ref.shape[2]

    @pl.when(step == 0)
    def _():
        kt_ref[...] = (kv_ref[:, 1].reshape(keys, LANES).astype(F32) * scale).T.astype(BF)
        dk_sum[...] = jnp.zeros_like(dk_sum)
        dv_sum[...] = jnp.zeros_like(dv_sum)

    peers, _, tokens, _ = q_ref.shape
    rows = peers * tokens
    queries = q_ref[:, 0].reshape(rows, LANES) * BF(scale)
    grads = d_ref[...].reshape(rows, LANES)
    value_rows = kv_ref[:, 2].reshape(keys, LANES)
    product = grads.astype(F32).T * ot_ref[...]
    for item in range(items):
        span = slice(item * HDIM, (item + 1) * HDIM)
        mask = item_mask(rows, LANES, item)
        grad = jnp.where(mask, grads, BF(0))
        query = jnp.where(mask, queries, BF(0))
        delta = jnp.sum(product[span, :], axis=0, keepdims=True)
        weights = pt_ref[item]
        back = (weights.astype(F32) * (nt(value_rows, grad) - delta)).astype(BF)
        dv_sum[...] += nn(weights, grad)
        dk_sum[...] += nn(back, query)
        dqt_ref[span, :] = nn(kt_ref[span, :], back)
    d_query = dqt_ref[...].T.astype(BF).reshape(peers, tokens, LANES)
    if dkv_ref:
        dq_ref[...] = d_query
    else:
        dq_ref[pl.ds(step * peers, peers), 0] = d_query

    @pl.when(step == pl.num_programs(0) - 1)
    def _():
        for c, total in ((1, dk_sum), (2, dv_sum)):
            total = total[...].reshape(kv_ref.shape[0], tokens, LANES)
            if dkv_ref:
                dkv_ref[0][:, c - 1] = total
            else:
                dq_ref[:, c] = total.astype(BF)


def attend_back(q, kv, d, ot, pt, items, scale, after):
    peers, _, tokens, lanes = q.shape
    rows, keys = peers * tokens, kv.shape[0] * tokens
    step = max(1, min(peers, 256 * 1024 // keys // tokens))
    block = step * tokens
    if q.shape == kv.shape:
        outs = [shape(q.shape)]
        out_specs = [pl.BlockSpec(q.shape, lambda j: (0, 0, 0, 0))]
    else:
        outs = [shape((peers, tokens, lanes)), shape((kv.shape[0], 2, tokens, lanes), F32)]
        out_specs = [
            pl.BlockSpec((step, tokens, lanes), lambda j: (j, 0, 0)),
            pl.BlockSpec(outs[1].shape, lambda j: (0, 0, 0, 0)),
        ]
    *back, token = call(
        functools.partial(attend_back_kernel, items, scale),
        "attend_back",
        outs,
        Warm(q),
        Warm(kv),
        d,
        ot,
        pt,
        after=after,
        grid=(peers // step,),
        in_specs=[
            pl.BlockSpec((step, 3, tokens, lanes), lambda j: (j, 0, 0, 0)),
            pl.BlockSpec(kv.shape, lambda j: (0, 0, 0, 0)),
            pl.BlockSpec((step, tokens, lanes), lambda j: (j, 0, 0)),
            pl.BlockSpec((lanes, block), lambda j: (0, j)),
            pl.BlockSpec((items, keys, block), lambda j: (0, 0, j)),
        ],
        out_specs=out_specs,
        scratch=[
            pltpu.VMEM((lanes, keys), BF),
            pltpu.VMEM((lanes, block), F32),
            pltpu.VMEM((keys, lanes), F32),
            pltpu.VMEM((keys, lanes), F32),
        ],
        limit=24 if keys <= 2048 else 60,
        flops=16 * rows * keys * lanes,
    )
    return back, token


def unpack(ids_ref, sources, index, out_ref, base):
    several = len(sources) > 1
    count = len(sources) if several else sources[0].shape[0] // 2
    for t in range(count):
        source, head = (sources[t], 0) if several else (sources[0], 2 * t)
        pair = [
            (source[head + s] if index is None else source[head + s, index]).astype(F32) for s in range(2)
        ]
        at = base + (pl.multiple_of(ids_ref[4 + t] * LANES, LANES) if several else t * LANES)
        for item, tile in enumerate(interleave(*pair)):
            out_ref[item * LANES : (item + 1) * LANES, pl.ds(at, LANES)] = tile.astype(BF)


def pack(product, out_ref):
    for t in range(product.shape[1] // LANES):
        tile = product[:, t * LANES : (t + 1) * LANES]
        for s, block in enumerate(interleave(tile[:LANES], tile[LANES:])):
            out_ref[2 * t + s] = block.astype(BF)


def project_kernel(ids_ref, *refs):
    *sources, wo_ref, mixed_ref, branch_ref = refs
    unpack(ids_ref, sources, None, mixed_ref, 0)
    branch_ref[...] = nn(mixed_ref[...], wo_ref[...]).astype(BF)


def forward_kernel(sources, ids_ref, *refs):
    if sources:
        own, got, refs = refs[:sources], refs[sources : 2 * sources], refs[2 * sources :]
        wo_ref, wo_got_ref, zero_ref, gains_ref, wu_ref, dact_ref, norm_ref, mixed_out, *refs = refs
        *refs, wo_buf, mixed, wo_sems = refs
        me = ids_ref[9]
        wo_loads = [
            pltpu.make_async_copy(wo_ref, wo_buf.at[me], wo_sems.at[0]),
            pltpu.make_async_copy(wo_got_ref, wo_buf.at[1 - me], wo_sems.at[1]),
        ]
        for copy in wo_loads:
            copy.start()
    else:
        own_ref, got_ref, zero_ref, gains_ref, wu_ref, dact_ref, norm_ref, *refs = refs
    one_out, pre_out, act_out, other_out, *rest = refs
    count = (len(rest) - 9) // 2
    turned_out, turned = rest[:count], rest[count : 2 * count]
    one_ref, weights, grads, pre_ref, act_ref, normed_ref, hold, into, out_of = rest[2 * count :]
    chunks, _, block = grads.shape
    per_half = chunks // 2
    loads, stores = [], []
    for c in range(chunks):
        span = slice(c * block, (c + 1) * block)
        loads.append(
            (
                pltpu.make_async_copy(wu_ref.at[:, span], weights.at[c], into.at[2 * c]),
                pltpu.make_async_copy(dact_ref.at[:, span], grads.at[c], into.at[2 * c + 1]),
            )
        )
        for copy in loads[-1]:
            copy.start()

    def store(source, target):
        stores.append(pltpu.make_async_copy(source, target, out_of.at[len(stores)]))
        stores[-1].start()

    if sources:
        unpack(ids_ref, own, None, mixed.at[me], 0)
        unpack(ids_ref, got, None, mixed.at[1 - me], 0)
        mixed_out[...] = mixed[me]
        for copy in wo_loads:
            copy.wait()
        branch = nn(mixed[0], wo_buf[0]) + nn(mixed[1], wo_buf[1])
    else:
        branch = own_ref[...].astype(F32) + got_ref[...].astype(F32)
    hidden = zero_ref[...] + branch
    one_ref[...] = hidden
    store(one_ref, one_out)
    unit, _ = norm_parts(hidden)
    normed = unit * gains_ref[1:2, :]
    normed_ref[...] = normed.astype(BF)
    emit_turned(normed, ids_ref, turned, hold)
    for source, target in zip(turned, turned_out):
        store(source, target)
    total = None
    for c in range(chunks):
        span = slice(c * block, (c + 1) * block)
        half, place = c // per_half, slice(c % per_half * block, (c % per_half + 1) * block)
        for copy in loads[c]:
            copy.wait()
        pre = nn(normed_ref[...], weights[c])
        chance = 0.5 * (1.0 + lax.erf(pre * (1.0 / math.sqrt(2.0))))
        slope = chance + pre * jnp.exp(-0.5 * pre * pre) * (1.0 / math.sqrt(2.0 * math.pi))
        act_ref[half, :, place] = (pre * chance).astype(BF)
        store(act_ref.at[half, :, place], act_out.at[half, :, place])
        d_pre = (grads[c].astype(F32) * slope).astype(BF)
        pre_ref[:, span] = d_pre
        store(pre_ref.at[:, span], pre_out.at[:, span])
        part = nt(d_pre, weights[c])
        total = part if total is None else total + part
    store(act_ref.at[1 - ids_ref[0]], other_out)
    norm_ref[...] = total.astype(BF)
    for copy in stores:
        copy.wait()


def second_kernel(ids_ref, one_ref, two_ref, own_ref, got_ref, gains_ref, wo_ref, d_ref, gain_ref, *rest):
    heads_ref, *turned, hold = rest
    unit, inverse = norm_parts(one_ref[...])
    grad = own_ref[...].astype(F32) + got_ref[...].astype(F32)
    back, gain = norm_back(unit, inverse, gains_ref[1:2, :], grad)
    gain_ref[...] = gain
    d_one = two_ref[...] + back
    d_ref[...] = d_one
    pack(nt(d_one.astype(BF), wo_ref[...]), heads_ref)
    emit_turned(d_one, ids_ref, turned, hold)


def head_kernel(ids_ref, one_ref, own_ref, got_ref, wh_ref, pred_ref, *rest):
    turned, hold = rest[:-1], rest[-1]
    hidden = one_ref[...] + (own_ref[...].astype(F32) + got_ref[...].astype(F32))
    low = hidden.astype(BF)
    for item in range(pred_ref.shape[0]):
        pred_ref[item] = nt(wh_ref[...], low[item * LANES : (item + 1) * LANES])
    emit_turned(hidden, ids_ref, turned, hold)


def third_kernel(count, ids_ref, *refs):
    sources, (wq_ref, dqkv_ref, norm_ref) = refs[:count], refs[count:]
    width = wq_ref.shape[2]
    total = None
    for c in range(3):
        unpack(ids_ref, sources, c, dqkv_ref, c * width)
        part = nt(dqkv_ref[:, c * width : (c + 1) * width], wq_ref[c])
        total = part if total is None else total + part
    norm_ref[...] = total.astype(BF)


def last_kernel(cols, ids_ref, zero_ref, done_ref, own_ref, got_ref, gains_ref, gain_two_ref, patches_ref, we_ref,
                pos_send, pos_keep, fields_ref, edge_ref, *rest):
    embed, (rows_ref, pos_ref, hold) = rest[:-3], rest[-3:]
    unit, inverse = norm_parts(zero_ref[...])
    grad = own_ref[...].astype(F32) + got_ref[...].astype(F32)
    back, gain = norm_back(unit, inverse, gains_ref[0:1, :], grad)
    d_zero = done_ref[...] + back
    low = d_zero.astype(BF)
    items, variables, height = edge_ref.shape
    pos = d_zero[0:LANES]
    for item in range(1, items):
        pos = pos + d_zero[item * LANES : (item + 1) * LANES]
    width = pos_ref.shape[2]
    for k in range(2):
        pos_ref[k] = pos[:, k * width : (k + 1) * width].astype(BF)
    pos_send[...] = pos_ref[1 - ids_ref[1]]
    pos_keep[...] = pos_ref[ids_ref[1]]
    features = patches_ref.shape[0]
    rows_ref[...] = jnp.zeros_like(rows_ref)
    rows_ref[0:features, :] = nn(patches_ref[...], low)
    rows_ref[features : features + 1, :] = gain
    rows_ref[features + 1 : features + 2, :] = gain_two_ref[...]
    emit_turned(rows_ref[...], ids_ref, embed, hold)
    half = height // PATCH
    row = lax.broadcasted_iota(jnp.int32, (LANES, height), 0)
    lane = lax.broadcasted_iota(jnp.int32, (LANES, height), 1)
    fields_ref[...] = jnp.zeros_like(fields_ref)
    order = feature_order(variables, True)
    for item in range(items):
        d_patches = nt(we_ref[...], low[item * LANES : (item + 1) * LANES])
        high = d_patches.astype(BF)
        rest = (d_patches - high.astype(F32)).astype(BF)
        high, rest = nn(order, high).astype(BF), nn(order, rest).astype(BF)
        for j in range(2):
            total = None
            for a in range(PATCH):
                place = jnp.where(
                    (row // half == j) & (lane == PATCH * (row % half) + a), 1.0, 0.0
                ).astype(BF)
                span = slice(a * 2 * variables, (a + 1) * 2 * variables)
                part = nn(high[span], place) + nn(rest[span], place)
                total = part if total is None else total + part
            for b in range(PATCH):
                block = total[b * variables : (b + 1) * variables]
                column = 2 * j + b - 1
                if column < 0:
                    edge_ref[item] = block.astype(BF)
                else:
                    fields_ref[item, pl.ds(column, variables, stride=cols), :] = block


def down_kernel(act_ref, wd_ref, out_ref):
    width = act_ref.shape[2]
    total = nn(act_ref[0], wd_ref[0:width, :]) + nn(act_ref[1], wd_ref[width:, :])
    out_ref[...] = total.astype(BF)


def pin(xs, after):
    def body(*refs):
        pass

    anywhere = pl.BlockSpec(memory_space=pl.ANY)
    several = isinstance(xs, (list, tuple))
    xs = list(xs) if several else [xs]
    out = pl.pallas_call(
        body,
        out_shape=[pltpu.HBM(x.shape, x.dtype) for x in xs],
        in_specs=[anywhere] * (len(xs) + len(after)),
        out_specs=[anywhere] * len(xs),
        input_output_aliases={k: k for k in range(len(xs))},
        name="pin",
    )(*[pltpu.with_memory_space_constraint(x, pltpu.HBM) for x in xs], *after)
    return out if several else out[0]


def product_of(own, got, b_own, b_got):
    parts, rows, tokens = own.shape
    total = nn(own[...].reshape(parts * rows, tokens), b_own)
    return total + nn(got[...].reshape(parts * rows, tokens), b_got)


def split_dp(ids_ref, hold, send, keep, columns):
    half = hold.shape[0] // 2
    for out, at in ((send, 1 - ids_ref[1]), (keep, ids_ref[1])):
        for k in range(half):
            out[k, :, 0:columns] = hold[at * half + k]


def split_near(ids_ref, hold, send, keep, columns):
    for out, at in ((send, 1 - ids_ref[2]), (keep, ids_ref[2])):
        for k in range(hold.shape[0] // 2):
            out[k, :, 0:columns] = hold[2 * k + at]


def plus(a, b):
    return (a[...].astype(F32) + b[...].astype(F32)).astype(BF)


def grads_ff_kernel(ids_ref, at_own, at_got, pre_own, pre_got, ct_own, ct_got, act_own, act_got,
                    send_a, keep_a, send_b, keep_b, hold, inner):
    parts, rows, total = hold.shape
    columns = total - keep_b.shape[2]
    product = product_of(at_own, at_got, pre_own[...], pre_got[...])
    hold[...] = product.astype(BF).reshape(hold.shape)
    split_dp(ids_ref, hold.at[:, :, 0:columns], send_a, keep_a, columns)
    split_near(ids_ref, hold.at[:, :, columns:], send_b, keep_b, total - columns)
    product = (nn(ct_own[...], act_own[ids_ref[0]]) + nn(ct_got[...], act_got[...])).astype(BF)
    tiles, groups = inner.shape[1], inner.shape[3] // LANES
    for k in range(2):
        for q in range(tiles):
            for g in range(groups):
                inner[k, q, :, g * LANES : (g + 1) * LANES] = product[
                    g * rows : (g + 1) * rows, (k * tiles + q) * LANES : (k * tiles + q + 1) * LANES
                ]
    for q in range(tiles):
        send_a[q, :, columns:] = inner[1 - ids_ref[1], q]
        keep_a[q, :, columns:] = inner[ids_ref[1], q]


def fold_ff_kernel(ids_ref, keep_a, got_a, keep_b, got_b, send_a, left_a, send_b, left_b, hold, hold_b):
    columns = hold.shape[2]
    extra = keep_a.shape[2] - columns
    hold[...] = plus(keep_a.at[:, :, 0:columns], got_a.at[:, :, 0:columns])
    split_near(ids_ref, hold, send_a, left_a, columns)
    for q in range(keep_a.shape[0]):
        total = plus(keep_a.at[q, :, columns:], got_a.at[q, :, columns:])
        at = columns + q % 2 * extra
        for out in (send_a, left_a):
            out[q // 2, :, at : at + extra] = total
    hold_b[...] = plus(keep_b, got_b)
    split_dp(ids_ref, hold_b, send_b, left_b, hold_b.shape[2])


def merge_ff_kernel(ids_ref, keep_a, got_a, keep_b, got_b, send, left, hold):
    columns = hold.shape[2] - keep_b.shape[2]
    extra = keep_a.shape[2] - columns
    hold[:, :, 0:columns] = plus(keep_a.at[:, :, 0:columns], got_a.at[:, :, 0:columns])
    hold[:, :, columns:] = plus(keep_b, got_b)
    far = ids_ref[3]
    width = hold.shape[2]
    send[:, 0:width] = hold[1 - far]
    left[:, 0:width] = hold[far]
    for k in range(2):
        total = plus(keep_a.at[k, :, columns:], got_a.at[k, :, columns:])
        at = width + k * extra
        for out in (send, left):
            out[:, at : at + extra] = total


def grads_oh_kernel(ids_ref, one_own, one_got, mixed_own, mixed_got, two_own, two_got, ct_own, ct_got,
                    send, keep, hold):
    width, features = mixed_own.shape[1], ct_own.shape[0]
    shape3 = hold.shape[:2]
    product = product_of(one_own, one_got, mixed_own[...], mixed_got[...])
    hold[:, :, 0:width] = product.astype(BF).reshape(*shape3, width)
    hold[:, :, width:] = jnp.zeros((*shape3, hold.shape[2] - width), BF)
    product = product_of(
        two_own, two_got, ct_own[...].astype(F32).T.astype(BF), ct_got[...].astype(F32).T.astype(BF)
    )
    hold[:, :, width : width + features] = product.astype(BF).reshape(*shape3, features)
    split_dp(ids_ref, hold, send, keep, hold.shape[2])


def grads_q_kernel(ids_ref, at_own, at_got, b_own, b_got, send_a, keep_a, send_b, keep_b, hold):
    cut, total = keep_a.shape[2], hold.shape[2]
    hold[...] = product_of(at_own, at_got, b_own[...], b_got[...]).astype(BF).reshape(hold.shape)
    split_dp(ids_ref, hold.at[:, :, 0:cut], send_a, keep_a, cut)
    split_near(ids_ref, hold.at[:, :, cut:], send_b, keep_b, total - cut)


def fold_q_kernel(ids_ref, keep_a, got_a, keep_b, got_b, up_keep, up_got, oh_keep, oh_got, embed_own, embed_got,
                  send_a, left_a, send_b, left_b, send_o, left_o, hold_a, hold_b, hold_o, hold_e):
    hold_a[...] = plus(keep_a, got_a)
    split_near(ids_ref, hold_a, send_a, left_a, hold_a.shape[2])
    hold_b[...] = plus(keep_b, got_b)
    columns = hold_b.shape[2]
    split_dp(ids_ref, hold_b, send_b, left_b, columns)
    hold_o[...] = plus(oh_keep, oh_got)
    for out, at in ((send_o, 1 - ids_ref[3]), (left_o, ids_ref[3])):
        for k in range(2):
            out[k] = hold_o[2 * at + k]
    hold_e[...] = plus(embed_own, embed_got)
    width = hold_e.shape[2]
    for out, at in ((send_b, 1 - ids_ref[1]), (left_b, ids_ref[1])):
        for k in range(4):
            start = columns + k % 2 * width
            out[k // 2, :, start : start + width] = hold_e[4 * at + k]
    start = columns + 2 * width
    half = send_b.shape[2] - start
    for k in range(2):
        at = up_keep.shape[1] - (2 - k) * half
        total = plus(up_keep.at[:, at : at + half], up_got.at[:, at : at + half])
        for out in (send_b, left_b):
            out[k, :, start:] = total


def merge_q_kernel(ids_ref, keep_a, got_a, keep_b, got_b, oh_keep, oh_got,
                   send, left, pair_ref, near_ref, embed_both, oh_left, hold, hold_e, hold_o):
    width = embed_both.shape[1]
    half = pair_ref.shape[2] // 2
    first = keep_a.shape[2]
    columns = keep_b.shape[2] - half - 2 * width
    total = hold.shape[2]
    hold[:, :, 0:first] = plus(keep_a, got_a)
    hold[:, :, first:] = plus(keep_b.at[:, :, 0:columns], got_b.at[:, :, 0:columns])
    hold_o[...] = plus(oh_keep, oh_got)
    for k in range(4):
        span = slice(columns + k % 2 * width, columns + (k % 2 + 1) * width)
        hold_e[k] = plus(keep_b.at[k // 2, :, span], got_b.at[k // 2, :, span])
    far, near = ids_ref[3], ids_ref[2]
    for out, at in ((send, 1 - far), (left, far)):
        out[:, 0:total] = hold[at]
        out[:, total:] = hold_e[2 * at + near]
    near_ref[:, 0:width] = hold_e[2 * far + 1 - near]
    near_ref[:, width:] = hold_o[1 - near]
    oh_left[...] = hold_o[near]
    embed_both[...] = hold_e[2 * (1 - far) + 1 - near]
    for k in range(2):
        span = slice(k * half, (k + 1) * half)
        pair_ref[0, :, span] = keep_b[k, :, columns + 2 * width :]
        pair_ref[1, :, span] = got_b[k, :, columns + 2 * width :]


def expand(ids_ref, rows_ref, pair_own, pair_got, out_ref, block):
    rows = rows_ref.shape[0]
    groups = block.shape[0] // rows
    tiles = block.shape[1] // LANES
    for a, b in ((0, 0), (0, 1), (1, 0), (1, 1)):
        source = pair_got if a else pair_own
        for q in range(tiles):
            for g in range(groups):
                at = (q * groups + g) * LANES
                block[g * rows : (g + 1) * rows, q * LANES : (q + 1) * LANES] = source[b, :, at : at + LANES]
        core, dp = (1 - ids_ref[0] if a else ids_ref[0]), (1 - ids_ref[1] if b else ids_ref[1])
        at = pl.multiple_of((core * 2 + dp) * block.shape[1], LANES)
        out_ref[:, pl.ds(at, block.shape[1])] = nn(rows_ref[...], block[...])


def insert_east(cols, fields_ref, east_ref, out_ref):
    variables = east_ref.shape[1]
    out_ref[...] = fields_ref[...]
    for item in range(east_ref.shape[0]):
        out_ref[item, pl.ds(cols - 1, variables, stride=cols), :] = east_ref[item].astype(F32)


def close_kernel(cols, ids_ref, fields_ref, east_ref, pos_ref, pos_got_ref, *refs):
    outs = refs
    if len(refs) > 2:
        (up_ref, up_got_ref, rows_ref, pair_own, pair_got), outs, block = refs[:5], refs[5:-1], refs[-1]
        width = outs[2].shape[1]
        outs[2][...] = up_ref[:, 0:width].astype(F32) + up_got_ref[:, 0:width].astype(F32)
        expand(ids_ref, rows_ref, pair_own, pair_got, outs[3], block)
    insert_east(cols, fields_ref, east_ref, outs[0])
    outs[1][...] = pos_ref[...].astype(F32) + pos_got_ref[...].astype(F32)


def end_kernel(*refs):
    if len(refs) > 3:
        (near_ref, both_ref, oh_ref, keep_ref, got_ref), refs = refs[:5], refs[5:]
        out_ref, head_ref, grad_ref = refs[2:]
        embed_width = both_ref.shape[1]
        both = keep_ref[...].astype(F32) + got_ref[...].astype(F32)
        width = grad_ref.shape[2]
        for c in range(3):
            grad_ref[c] = both[:, c * width : (c + 1) * width]
        total = both[:, 3 * width :] + near_ref[:, 0:embed_width].astype(F32) + both_ref[...].astype(F32)
        both = oh_ref[...].astype(F32) + near_ref[:, embed_width:].astype(F32)
        out_ref[...] = both[:, 0:width]
        head_ref[...] = both[:, width : width + head_ref.shape[1]]
    else:
        total, refs = jnp.sum(refs[0][...].astype(F32), axis=0), refs[1:]
    features = refs[0].shape[1]
    refs[0][...] = total[:, 0:features]
    refs[1][...] = total[:, LANES:].T[features - LANES : features - LANES + 2, :]


def local(
    dataset,
    indices,
    run_count,
    run_mean,
    run_var,
    w_embed,
    pos_embed,
    gains,
    w_qkv,
    w_out,
    w_up,
    w_down,
    w_head,
    cotangent,
):
    items = indices.shape[0]
    variables, height, columns = dataset.shape[1:]
    dp, lon = lax.axis_size("dp"), lax.axis_size("lon")
    everyone = dp * lon
    width = w_embed.shape[1]
    local_width = w_qkv.shape[2]
    heads = local_width // HDIM
    item_tokens = cotangent.shape[1]
    tokens = items * item_tokens
    features = w_embed.shape[0]
    hidden_units = w_up.shape[1]
    scale = 1.0 / math.sqrt(HDIM)
    group, far = heads, lon // heads
    groups = [[group * g + i for i in range(group)] for g in range(far)]
    across = [[i + group * g for g in range(far)] for i in range(group)]
    assert items * HDIM == LANES and item_tokens == LANES and height == LANES and columns == 4
    lon_at, dp_at = lax.axis_index("lon"), lax.axis_index("dp")
    ids = [lon_at % 2, dp_at, lon_at // 2 % 2, lon_at // 4 % 2, *[lon_at // 2 ^ k for k in range(4)], dp_at * lon + lon_at, lax.axis_index("mp")]
    ids = jnp.stack(ids).astype(jnp.int32)
    paired = dp == 2 and lon == 8
    parts, rows = width // (2 * (width // everyone)), width // everyone
    turned_shape = (
        [shape((parts, rows, tokens))] * 2 if paired else [shape((width, tokens))]
    )
    turned_hold = pltpu.VMEM((parts, 2, rows, tokens) if paired else (8, LANES), BF)

    alone = dict(axis_index_groups=groups) if far > 1 else {}

    vmem, smem = pl.BlockSpec(memory_space=pltpu.VMEM), pl.BlockSpec(memory_space=pltpu.SMEM)
    assert dp == 2

    data = dataset.transpose(0, 1, 3, 2).reshape(dataset.shape[0], variables * columns, height)
    fields, edge, moments, _ = call(
        moments_kernel,
        "moments",
        [
            warm((items, variables * columns, height), F32),
            warm((items, variables, height)),
            warm((everyone, 8, LANES), F32),
        ],
        indices, data,
        in_specs=[pl.BlockSpec(memory_space=pltpu.SMEM), pl.BlockSpec(memory_space=pl.ANY)],
        scratch=[pltpu.VMEM((LANES, LANES), F32), pltpu.SemaphoreType.DMA((items,))],
    )
    edge = from_behind(edge, "lon", 1)
    moments = lax.all_to_all(moments, ("dp", "lon"), 0, 0)
    wh_turned = w_head.T

    out = call(
        functools.partial(start_kernel, float(items * height * columns)),
        "start",
        [
            *[shape((1, variables), F32)] * 3,
            shape((tokens, width), F32),
            shape((features, tokens)),
            *([shape((2, 3, item_tokens, LANES))] * 4 if paired else [shape((heads, 3, item_tokens, LANES))]),
            *turned_shape,
        ],
        ids, Warm(moments), *[r.reshape(1, variables) for r in (run_count, run_mean, run_var)],
        Warm(fields), Warm(edge), w_embed, pos_embed, gains, w_qkv,
        in_specs=[smem, *[vmem] * 9, pl.BlockSpec(memory_space=pl.ANY)],
        scratch=[
            pltpu.VMEM((LANES, LANES), F32),
            pltpu.VMEM((8, LANES), F32),
            turned_hold,
            pltpu.VMEM(w_qkv.shape, BF),
            pltpu.SemaphoreType.DMA,
            pltpu.VMEM((heads, 3, item_tokens, LANES), BF),
        ],
        flops=2 * tokens * width * (features + 3 * local_width),
    )
    count = 4 if paired else 1
    stats, (hidden_zero, patches), packed = out[:3], out[3:5], out[5 : 5 + count]
    normed_one, token = out[5 + count : -1], out[-1]

    def along(messages):
        return [messages[0], *[swap(messages[k], "lon", 2 * k) for k in range(1, count)]]

    if paired:
        own = along(packed)
    else:
        sent = lax.all_to_all(packed[0], "lon", 0, 0, **alone)
        kv = sent
        if far > 1:
            kv = lax.all_gather(sent, "lon", axis=0, tiled=True, axis_index_groups=across)

    if paired:
        wo_got, normed_got = swap(w_out, "mp", 1), swap(normed_one[1], "lon", 1)
        other = [swap(x, "lon", 1) for x in own]
    if paired:
        attended, kept, token = pair_attend(own, other, items, scale, [token, normed_got, wo_got])
        attended = along(attended)
    else:
        attended, attended_t, weights_t, token = attend(sent, kv, items, scale, [token])
        attended = [lax.all_to_all(attended, "lon", 0, 0, **alone)]
    anywhere = pl.BlockSpec(memory_space=pl.ANY)
    d_two, d_act, ct_turned, *mine, token = call(
        cotangent_kernel,
        "cotangent",
        [
            shape((tokens, width), F32),
            shape((tokens, hidden_units)),
            shape((features, tokens)),
            *[shape((rows, features))] * paired,
        ],
        ids, cotangent.transpose(0, 2, 1), wh_turned, w_down,
        after=[token],
        scratch=[pltpu.VMEM((everyone, rows, features), BF)] * paired,
        flops=2 * tokens * width * (features + hidden_units),
    )

    if paired:
        ct_got = swap(ct_turned, "lon", 1)
        attended[0] = pin(attended[0], [token])
        attended += [swap(x, "mp", 1) for x in attended]
    if paired:
        branches = [attended[0], *[Warm(x) for x in attended[1:]], w_out, Warm(wo_got)]
    else:
        mixed, branch, token = call(
            project_kernel,
            "project",
            [shape((tokens, local_width)), warm((tokens, width))],
            ids, *attended, w_out,
            after=[token],
            flops=2 * tokens * width * local_width,
        )
        branches = [Warm(branch), Warm(swap(branch, "mp", 1))]
    block = min(512, hidden_units // 2)
    chunks = hidden_units // block
    out = call(
        functools.partial(forward_kernel, count if paired else 0),
        "forward",
        [
            warm((tokens, width)),
            *[shape((tokens, local_width))] * paired,
            shape((tokens, width), F32),
            shape((tokens, hidden_units)),
            shape((2, tokens, hidden_units // 2)),
            shape((tokens, hidden_units // 2)),
            *turned_shape,
        ],
        ids, *branches, Warm(hidden_zero), gains, w_up, d_act,
        after=[token],
        in_specs=[
            smem,
            *([*[vmem] * (len(branches) - 2), anywhere, anywhere] if paired else [vmem] * 2),
            vmem,
            vmem,
            anywhere,
            anywhere,
        ],
        out_specs=[*[vmem] * (1 + paired), *[anywhere] * (4 + len(turned_shape))],
        scratch=[
            *[pltpu.VMEM(x.shape, BF) for x in turned_shape],
            pltpu.VMEM((tokens, width), F32),
            pltpu.VMEM((chunks, width, block), BF),
            pltpu.VMEM((chunks, tokens, block), BF),
            pltpu.VMEM((tokens, hidden_units), BF),
            pltpu.VMEM((2, tokens, hidden_units // 2), BF),
            pltpu.VMEM((tokens, width), BF),
            turned_hold,
            pltpu.SemaphoreType.DMA((2 * chunks,)),
            pltpu.SemaphoreType.DMA((2 + len(turned_shape) + 2 * chunks,)),
            *[
                pltpu.VMEM((2, *w_out.shape), BF),
                pltpu.VMEM((2, tokens, local_width), BF),
                pltpu.SemaphoreType.DMA((2,)),
            ] * paired,
        ],
        limit=32,
        flops=4 * tokens * width * hidden_units,
    )
    d_norm, *out, token = out
    if paired:
        mixed, out = out[0], out[1:]
        mixed_got = swap(mixed, "lon", 1)
    hidden_one, d_pre, activated, act_send = out[:4]
    normed_two = out[4:]
    d_norm_got = swap(d_norm, "mp", 1)
    half = hidden_units // 2
    if paired:
        inner_columns = features // rows * LANES
        first = half - LANES
        out_a = shape((parts // 2, rows, first + inner_columns))
        out_b = shape((parts // 2, rows, hidden_units - first))
        send_a, keep_a, send_b, keep_b, token = call(
            grads_ff_kernel,
            "grads_ff",
            [out_a, out_a, out_b, out_b],
            ids, normed_two[0], Warm(swap(normed_two[1], "lon", 1)), d_pre, Warm(swap(d_pre, "lon", 1)),
            ct_turned, Warm(ct_got), activated, Warm(swap(act_send, "lon", 1)),
            after=[token],
            scratch=[
                pltpu.VMEM((parts, rows, hidden_units), BF),
                pltpu.VMEM((2, parts // 2, rows, inner_columns), BF),
            ],
            limit=32,
            flops=2 * tokens * (width + features) * hidden_units,
        )
        got_a, got_b = swap(send_a, "dp", 1), swap(send_b, "lon", 2)
    forward, token = call(
        down_kernel,
        "down",
        [shape((tokens, width))],
        activated, w_down,
        after=[token, *([mixed_got] if paired else [])],
        flops=2 * tokens * width * hidden_units,
    )

    out = call(
        second_kernel,
        "second",
        [
            shape((tokens, width), F32),
            shape((1, width), F32),
            shape((heads, item_tokens, LANES)),
            *turned_shape,
        ],
        ids, Warm(hidden_one), Warm(d_two), Warm(d_norm), Warm(d_norm_got), gains, Warm(w_out),
        after=[token],
        scratch=[turned_hold],
        flops=2 * tokens * width * local_width,
    )
    d_one, gain_two, d_mixed = out[0], out[1], out[2:3]
    d_one_turned, token = out[3:-1], out[-1]
    if paired:
        d_one_got = swap(d_one_turned[1], "lon", 1)
    if paired:
        chips = [[2 * k + c for k in range(lon // 2)] for c in range(2)]
        d_heads = lax.all_to_all(
            d_mixed[0].reshape(lon // 2, 2, item_tokens, LANES), "lon", 0, 0, axis_index_groups=chips
        )
    else:
        d_heads = lax.all_to_all(d_mixed[0], "lon", 0, 0, **alone)
    forward_got = swap(forward, "mp", 1)
    if paired:
        out_a = shape((2, rows, first + 2 * inner_columns))
        out_b = shape((2, rows, hidden_units - first))
        send_a, keep_a, send_b, keep_b, token = call(
            fold_ff_kernel,
            "fold_ff",
            [out_a, out_a, out_b, out_b],
            ids, keep_a, Warm(got_a), keep_b, Warm(got_b),
            after=[token],
            scratch=[
                pltpu.VMEM((parts // 2, rows, first), BF),
                pltpu.VMEM((parts // 2, rows, hidden_units - first), BF),
            ],
        )
        send_a, send_b = pin([send_a, send_b], [d_heads])
        got_a, got_b = swap(send_a, "lon", 2), swap(send_b, "dp", 1)

    if paired:
        back, cross, token = pair_attend_back(ids, kept, d_heads, items, scale, [token])
        *back, token = call(
            combine_kernel,
            "combine",
            [shape(x.shape) for x in back],
            *back, Warm(swap(pin(cross, [got_a, got_b, forward_got]), "lon", 1)),
            after=[token],
        )
        back = along(back)
    else:
        back, token = attend_back(sent, kv, d_heads, attended_t, weights_t, items, scale, [token])
        if far > 1:
            d_query, d_kv = back
            d_kv = lax.psum_scatter(
                d_kv, "lon", scatter_dimension=0, tiled=True, axis_index_groups=across
            ).astype(BF)
            back = [jnp.concatenate([d_query[:, None], d_kv], axis=1)]
        back = [lax.all_to_all(back[0], "lon", 0, 0, **alone)]
    out = call(
        head_kernel,
        "head",
        [shape((items, features, item_tokens), F32), *turned_shape],
        ids, hidden_one, forward, Warm(forward_got), wh_turned,
        after=[token],
        scratch=[turned_hold],
        flops=2 * tokens * width * features,
    )
    pred, hidden_turned, token = out[0].transpose(0, 2, 1), list(out[1:-1]), out[-1]
    if paired:
        up_send, up_keep, token = call(
            merge_ff_kernel,
            "merge_ff",
            [shape((rows, hidden_units + 4 * inner_columns))] * 2,
            ids, keep_a, Warm(got_a), keep_b, got_b,
            after=[token],
            scratch=[pltpu.VMEM((2, rows, hidden_units), BF)],
        )
    d_qkv, d_norm, token = call(
        functools.partial(third_kernel, count),
        "third",
        [shape((tokens, 3 * local_width)), warm((tokens, width))],
        ids, back[0], *[Warm(x) for x in back[1:]], Warm(w_qkv),
        after=[token],
        flops=6 * tokens * width * local_width,
    )
    d_norm_got = swap(d_norm, "mp", 1)
    if paired:
        up_send, hidden_turned[1] = pin([up_send, hidden_turned[1]], [token])
        up_got = swap(up_send, "lon", 4)
        wide = local_width + 2 * LANES
        cut = 3 * local_width // 2 + LANES
        first, second = (shape((parts // 2, rows, c)) for c in (cut, 3 * local_width - cut))
        send_a, keep_a, send_b, keep_b, token = call(
            grads_q_kernel,
            "grads_q",
            [first, first, second, second],
            ids, normed_one[0], normed_got, d_qkv, Warm(swap(d_qkv, "lon", 1)),
            after=[token],
            scratch=[pltpu.VMEM((parts, rows, 3 * local_width), BF)],
            flops=6 * tokens * width * local_width,
        )
        oh_send, oh_keep, token = call(
            grads_oh_kernel,
            "grads_oh",
            [shape((parts // 2, rows, wide))] * 2,
            ids, d_one_turned[0], Warm(d_one_got), mixed, Warm(mixed_got),
            hidden_turned[0], Warm(swap(hidden_turned[1], "lon", 1)), ct_turned, Warm(ct_got),
            after=[token],
            scratch=[pltpu.VMEM((parts, rows, wide), BF)],
            flops=2 * tokens * width * wide,
        )
        oh_got = swap(oh_send, "dp", 1)
        got_a, got_b = swap(send_a, "dp", 1), swap(send_b, "lon", 2)

    out = call(
        functools.partial(last_kernel, columns),
        "last",
        [
            *[shape((item_tokens, width // 2))] * 2,
            shape((items, variables * columns, height), F32),
            shape((items, variables, height)),
            *([shape((parts, rows, 2 * LANES))] * 2 if paired else [shape((width, 2 * LANES))]),
        ],
        ids, Warm(hidden_zero), Warm(d_one), Warm(d_norm), Warm(d_norm_got), gains, gain_two, patches, w_embed,
        after=[token],
        scratch=[
            pltpu.VMEM((2 * LANES, width), F32),
            pltpu.VMEM((2, item_tokens, width // 2), BF),
            pltpu.VMEM((parts, 2, rows, 2 * LANES) if paired else (8, LANES), BF),
        ],
        flops=4 * tokens * width * features,
    )
    pos_send, pos, d_fields, d_edge = out[:4]
    embed, token = out[4:-1], out[-1]
    if not paired:
        east, pos_got = from_behind(d_edge, "lon", -1), swap(pos_send, "dp", 1)
    more, more_outs, more_scratch, rest, rest_outs = [], [], [], [], []
    if paired:
        embed_width = embed[0].shape[2]
        step_a, side = shape((2, rows, cut)), shape((2, rows, wide))
        step_b = shape((2, rows, 3 * local_width - cut + 2 * embed_width + 2 * inner_columns))
        send_a, keep_a, send_b, keep_b, oh_send, oh_keep, token = call(
            fold_q_kernel,
            "fold_q",
            [step_a, step_a, step_b, step_b, side, side],
            ids, keep_a, Warm(got_a), keep_b, Warm(got_b), up_keep, Warm(up_got), oh_keep, Warm(oh_got),
            embed[0], Warm(swap(embed[1], "lon", 1)),
            after=[token],
            scratch=[
                pltpu.VMEM(keep_a.shape, BF),
                pltpu.VMEM(keep_b.shape, BF),
                pltpu.VMEM(oh_keep.shape, BF),
                pltpu.VMEM(embed[0].shape, BF),
            ],
        )
        got_a, got_b, oh_got = swap(send_a, "lon", 2), swap(send_b, "dp", 1), swap(oh_send, "lon", 4)
        east = from_behind(pin(d_edge, [token]), "lon", -1)
        final, block = shape((rows, 3 * local_width + embed_width)), shape((rows, embed_width))
        send, keep, pair, near_send, embed_both, oh_keep, token = call(
            merge_q_kernel,
            "merge_q",
            [
                final,
                final,
                shape((2, rows, 4 * inner_columns)),
                shape((rows, embed_width + wide)),
                block,
                shape((rows, wide)),
            ],
            ids, keep_a, Warm(got_a), keep_b, Warm(got_b), oh_keep, Warm(oh_got),
            after=[token, east],
            scratch=[
                pltpu.VMEM((2, rows, 3 * local_width), BF),
                pltpu.VMEM((4, *block.shape), BF),
                pltpu.VMEM((2, rows, wide), BF),
            ],
        )
        pos_got = swap(pin(pos_send, [token]), "dp", 1)
        more = [up_keep, Warm(up_got), mine[0], pair, Warm(swap(pair, "lon", 1))]
        more_outs = [shape((rows, hidden_units), F32)] * 2
        more_scratch = [pltpu.VMEM((features, hidden_units // 4), BF)]
        rest = [
            Warm(swap(near_send, "lon", 2)), Warm(swap(embed_both, "lon", 6)), oh_keep,
            keep, Warm(swap(send, "lon", 4)),
        ]
        rest_outs = [
            shape((rows, local_width), F32),
            shape((rows, features), F32),
            shape((3, rows, local_width), F32),
        ]
    else:
        rest = [lax.all_to_all(embed[0].reshape(everyone, rows, 2 * LANES), ("dp", "lon"), 0, 0)]
    *closed, token = call(
        functools.partial(close_kernel, columns),
        "close",
        [shape(d_fields.shape, F32), shape(pos.shape, F32), *more_outs],
        ids, d_fields, east, pos, Warm(pos_got), *more,
        after=[token],
        scratch=more_scratch,
    )
    *ended, token = call(
        end_kernel,
        "end",
        [shape((rows, features), F32), shape((2, rows), F32), *rest_outs],
        *rest,
        after=[token],
    )
    if paired:
        grad_up, grad_down, (grad_out, grad_head, grad_qkv) = closed[2], closed[3], ended[2:]
    else:
        flat = activated.transpose(1, 0, 2).reshape(tokens, hidden_units)
        grad_up = scatter(nn(normed_two[0], d_pre))
        grad_down = scatter(nn(d_two.T.astype(BF), flat))
        grad_out = scatter(nn(d_one_turned[0], mixed))
        grad_head = scatter(nt(hidden_turned[0], ct_turned))
        grad_qkv = scatter(nn(normed_one[0], d_qkv)).reshape(rows, 3, local_width).transpose(1, 0, 2)
    return (
        pred,
        *[x.reshape(variables) for x in stats],
        closed[0].reshape(items, variables, columns, height).transpose(0, 1, 3, 2),
        ended[0].T,
        closed[1],
        ended[1],
        grad_qkv,
        grad_out.T,
        grad_up,
        grad_down.T,
        grad_head,
    )


def solution(mesh):
    in_specs = (
        P(None, None, None, "lon"),
        P("dp"),
        P(),
        P(),
        P(),
        P(),
        P("lon", None),
        P(),
        P(None, None, "mp"),
        P("mp", None),
        P(None, "mp"),
        P("mp", None),
        P(),
        P("dp", "lon", None),
    )
    out_specs = (
        P("dp", "lon", None),
        P(),
        P(),
        P(),
        P("dp", None, None, "lon"),
        P(None, ("dp", "lon")),
        P("lon", "dp"),
        P(None, ("dp", "lon")),
        P(None, ("dp", "lon"), "mp"),
        P("mp", ("dp", "lon")),
        P(("dp", "lon"), "mp"),
        P("mp", ("dp", "lon")),
        P(("dp", "lon"), None),
    )
    return jax.shard_map(local, mesh=mesh, in_specs=in_specs, out_specs=out_specs, check_vma=False)
```

```python
import functools
import math

import jax
import jax.numpy as jnp
from jax import lax
from jax.experimental import pallas as pl
from jax.experimental.pallas import tpu as pltpu
from jax.sharding import PartitionSpec as P

HDIM = 64
PATCH = 2
LANES = 128
NORM_EPS = 1e-06
STAT_EPS = 1e-06
BF = jnp.bfloat16
F32 = jnp.float32
MIB = 2**20


def swap(block, axis, distance):
    route = [(i, i ^ distance) for i in range(lax.axis_size(axis))]
    return lax.ppermute(block, axis, route)


def from_behind(block, axis, distance):
    size = lax.axis_size(axis)
    route = [((i - distance) % size, i) for i in range(size)]
    return lax.ppermute(block, axis, route)


def pick(x, index, axis):
    return lax.dynamic_index_in_dim(x, index, axis, keepdims=False)


def halve(total, dims):
    for axis, bit in dims:
        side = (lax.axis_index(axis) // bit) % 2
        got = swap(pick(total, 1 - side, 0), axis, bit)
        total = (pick(total, side, 0).astype(F32) + got.astype(F32)).astype(BF)
    return total


def scatter(total):
    dp, lon = lax.axis_size("dp"), lax.axis_size("lon")
    dims = []
    for axis, size in (("dp", dp), ("lon", lon)):
        bit = size // 2
        while bit:
            dims.append((axis, bit))
            bit //= 2
    rows, columns = total.shape
    total = total.astype(BF).reshape((2,) * len(dims) + (rows // (dp * lon), columns))
    order = sorted(range(len(dims)), key=lambda i: (dims[i][1] > 1 or dims[i][0] == "dp", i))
    total = total.transpose([*order, len(dims), len(dims) + 1])
    return halve(total, [dims[i] for i in order]).astype(F32)


def nt(a, b):
    return lax.dot_general(a, b, (((1,), (1,)), ((), ())), preferred_element_type=F32)


def nn(a, b):
    return lax.dot_general(a, b, (((1,), (0,)), ((), ())), preferred_element_type=F32)


def item_mask(rows, lanes, item):
    lane = lax.broadcasted_iota(jnp.int32, (rows, lanes), 1)
    return (lane >= item * HDIM) & (lane < (item + 1) * HDIM)


def interleave(first, second):
    low = item_mask(first.shape[0], LANES, 0)
    return (
        jnp.where(low, first, pltpu.roll(second, HDIM, 1)),
        jnp.where(low, pltpu.roll(first, HDIM, 1), second),
    )


def norm_parts(hidden):
    centred = hidden - jnp.mean(hidden, axis=-1, keepdims=True)
    variance = jnp.mean(centred * centred, axis=-1, keepdims=True)
    inverse = lax.rsqrt(variance + NORM_EPS)
    return centred * inverse, inverse


def norm_back(unit, inverse, scaling, grad):
    scaled = grad * scaling
    back = inverse * (
        scaled
        - jnp.mean(scaled, axis=-1, keepdims=True)
        - unit * jnp.mean(scaled * unit, axis=-1, keepdims=True)
    )
    return back, jnp.sum(grad * unit, axis=0, keepdims=True)


def emit_turned(x, ids_ref, outs, hold):
    turned = x.T.astype(BF)
    if len(outs) == 1:
        outs[0][...] = turned
        return
    keep, send = outs
    parts, rows, tokens = keep.shape
    hold[...] = turned.reshape(parts, 2, rows, tokens)
    core = ids_ref[0]
    keep[...] = hold[:, pl.ds(core, 1)].reshape(parts, rows, tokens)
    send[...] = hold[:, pl.ds(1 - core, 1)].reshape(parts, rows, tokens)


class Warm:
    def __init__(self, value):
        self.value = value


def call(body, name, outs, *args, after=(), grid=(), in_specs=None, out_specs=None, scratch=(), limit=24, flops=0):
    vmem = pl.BlockSpec(memory_space=pltpu.VMEM)
    smem = pl.BlockSpec(memory_space=pltpu.SMEM)
    shapes = [o.value if isinstance(o, Warm) else o for o in outs]
    plain = [a.value if isinstance(a, Warm) else a for a in args]
    if in_specs is None:
        in_specs = [smem if a.dtype == jnp.int32 else vmem for a in plain]
    if out_specs is None:
        out_specs = [vmem] * len(outs)
    token = pl.BlockSpec((8, LANES), lambda *at: (0, 0)) if grid else vmem
    nbytes = sum(math.prod(a.shape) * a.dtype.itemsize for a in [*plain, *shapes])
    here, skip, there = len(args), len(after), len(outs)

    def with_token(*refs):
        refs = list(refs)
        refs[here + skip + there][...] = jnp.zeros((8, LANES), F32)
        body(*refs[:here], *refs[here + skip : here + skip + there], *refs[here + skip + there + 1 :])

    def cold(x):
        if isinstance(x, Warm):
            return x.value
        return x if x.dtype == jnp.int32 else pltpu.with_memory_space_constraint(x, pltpu.HBM)

    return pl.pallas_call(
        with_token,
        grid=grid,
        out_shape=[
            *[o.value if isinstance(o, Warm) else pltpu.HBM(o.shape, o.dtype) for o in outs],
            pltpu.HBM((8, LANES), F32),
        ],
        in_specs=[*in_specs, *[pl.BlockSpec(memory_space=pl.ANY)] * skip],
        out_specs=[*out_specs, token],
        scratch_shapes=list(scratch),
        compiler_params=pltpu.CompilerParams(vmem_limit_bytes=limit * MIB),
        cost_estimate=pl.CostEstimate(flops=int(flops), bytes_accessed=nbytes, transcendentals=0),
        name=name,
    )(*[cold(a) for a in args], *[cold(a) for a in after])


def shape(dims, kind=BF):
    return jax.ShapeDtypeStruct(dims, kind)


def warm(dims, kind=BF):
    return Warm(shape(dims, kind))


def feature_order(variables, back):
    features = PATCH * PATCH * variables
    natural = lax.broadcasted_iota(jnp.int32, (features, features), 1 if back else 0)
    sorted_ = lax.broadcasted_iota(jnp.int32, (features, features), 0 if back else 1)
    hit = (natural // 4 == sorted_ % variables) & (natural % 4 == sorted_ // variables)
    return jnp.where(hit, 1.0, 0.0).astype(BF)


def send_pairs(ids_ref, hold, messages):
    if len(messages) == 1:
        messages[0][...] = hold[...]
        return
    for k, message in enumerate(messages):
        message[...] = hold[pl.ds(2 * ids_ref[4 + k], 2)]


def moments_kernel(index_ref, data_ref, fields_ref, edge_ref, moments_ref, turn_ref, sems):
    items, variables, height = edge_ref.shape
    cols = fields_ref.shape[1] // variables
    copies = [
        pltpu.make_async_copy(data_ref.at[index_ref[i]], fields_ref.at[i], sems.at[i])
        for i in range(items)
    ]
    for copy in copies:
        copy.start()
    turn_ref[...] = jnp.zeros_like(turn_ref)
    for copy in copies:
        copy.wait()
    blocks = [
        fields_ref[i, pl.ds(c, variables, stride=cols), :] for i in range(items) for c in range(cols)
    ]
    for i in range(items):
        edge_ref[i] = blocks[i * cols + cols - 1].astype(BF)
    count = float(items * cols * height)
    mean = jnp.sum(sum(blocks), axis=1, keepdims=True) * (1.0 / count)
    spread = jnp.sum(sum(jnp.square(b - mean) for b in blocks), axis=1, keepdims=True)
    turn_ref[0:variables, 0:1] = mean
    turn_ref[HDIM : HDIM + variables, 0:1] = spread
    turn_ref[0:variables, 1:2] = spread
    turned = turn_ref[...].T
    if len(moments_ref.shape) == 2:
        moments_ref[...] = turned[0 : moments_ref.shape[0], :]
    else:
        moments_ref[...] = jnp.broadcast_to(turned[0:1, :][None], moments_ref.shape)


def start_kernel(local_count, members, ids_ref, mom_ref, count_ref, mean_ref, var_ref, fields_ref, edge_ref, we_ref,
                 pos_ref, gains_ref, wq_ref, new_count_ref, new_mean_ref, new_var_ref, hidden_ref, patches_ref,
                 *rest):
    (*outs, column_ref, run_ref, hold, weights, sem, qkv_ref) = rest
    if len(outs) > 2:
        messages, turned = outs[:-2], outs[-2:]
    else:
        messages, turned = outs[:1], outs[1:]
    copy = pltpu.make_async_copy(wq_ref, weights, sem)
    copy.start()
    items, rows, height = fields_ref.shape
    variables = edge_ref.shape[1]
    cols = rows // variables
    half = height // PATCH
    run_ref[...] = jnp.zeros_like(run_ref)
    for k, ref in enumerate((count_ref, mean_ref, var_ref)):
        run_ref[k : k + 1, 0:variables] = ref[...]
    batch_count = local_count * members
    if len(mom_ref.shape) == 2:
        batch_mean, spread = mom_ref[0:1, :], mom_ref[1:2, :]
    else:
        moments = mom_ref[:, 0, :]
        batch_mean = jnp.sum(moments, axis=0, keepdims=True) * (1.0 / members)
        off = moments - batch_mean
        spread = jnp.sum(pltpu.roll(moments, HDIM, 1) + local_count * off * off, axis=0, keepdims=True)
    run_count, run_mean, run_var = (run_ref[k : k + 1, :] for k in range(3))
    new_count = run_count + batch_count
    shift = batch_mean - run_mean
    new_mean = run_mean + shift * (batch_count / new_count)
    new_var = (
        run_var * run_count + spread + shift * shift * (run_count * batch_count / new_count)
    ) / new_count
    new_count_ref[...] = new_count[:, 0:variables]
    new_mean_ref[...] = new_mean[:, 0:variables]
    new_var_ref[...] = new_var[:, 0:variables]
    column_ref[...] = jnp.zeros_like(column_ref)
    column_ref[0:1, :] = new_mean
    column_ref[1:2, :] = lax.rsqrt(new_var + STAT_EPS)
    column = column_ref[...].T
    centre, inverse = column[0:variables, 0:1], column[0:variables, 1:2]

    def scaled(block):
        return ((block - centre) * inverse).astype(BF)

    row = lax.broadcasted_iota(jnp.int32, (2 * height, LANES), 0)
    lane = lax.broadcasted_iota(jnp.int32, (2 * height, LANES), 1)
    sort = [
        jnp.where(
            (row // height == lane // half) & (row % height == PATCH * (lane % half) + a), 1.0, 0.0
        ).astype(BF)
        for a in range(PATCH)
    ]
    natural = feature_order(variables, False)
    hidden = []
    for item in range(items):
        west = scaled(edge_ref[item].astype(F32))
        own = [
            scaled(fields_ref[item, pl.ds(c, variables, stride=cols), :]) for c in range(cols - 1)
        ]
        first = jnp.concatenate([west, own[0]], axis=0)
        second = jnp.concatenate([own[1], own[2]], axis=0)
        both = jnp.concatenate([first, second], axis=1)
        patches = jnp.concatenate([nn(both, sort[a]) for a in range(PATCH)], axis=0)
        patches = nn(natural, patches.astype(BF))
        patches_ref[:, item * LANES : (item + 1) * LANES] = patches.astype(BF)
        hidden.append(nn(patches.T.astype(BF), we_ref[...]) + pos_ref[...].astype(F32))
    hidden = jnp.concatenate(hidden, axis=0)
    hidden_ref[...] = hidden
    unit, _ = norm_parts(hidden)
    normed = unit * gains_ref[0:1, :]
    low = normed.astype(BF)
    emit_turned(normed, ids_ref, turned, hold)
    copy.wait()
    for c in range(3):
        product = nn(low, weights[c])
        for t in range(product.shape[1] // LANES):
            tile = product[:, t * LANES : (t + 1) * LANES]
            a, b = interleave(tile[:LANES], tile[LANES:])
            qkv_ref[2 * t, c] = a.astype(BF)
            qkv_ref[2 * t + 1, c] = b.astype(BF)
    send_pairs(ids_ref, qkv_ref, messages)


def cotangent_kernel(ids_ref, ct_ref, wh_ref, wd_ref, *refs):
    if len(refs) > 3:
        two_ref, act_ref, ct_turned_ref, mine_ref, hold = refs
        hold[...] = wh_ref[...].astype(F32).T.astype(BF).reshape(hold.shape)
        mine_ref[...] = hold[ids_ref[8]]
    else:
        two_ref, act_ref, ct_turned_ref = refs
    grads = []
    for item in range(ct_ref.shape[0]):
        ct = ct_ref[item].T.astype(BF)
        ct_turned_ref[:, item * LANES : (item + 1) * LANES] = ct_ref[item].astype(BF)
        grads.append(nn(ct, wh_ref[...]))
    d_two = jnp.concatenate(grads, axis=0)
    two_ref[...] = d_two
    act_ref[...] = nt(d_two.astype(BF), wd_ref[...]).astype(BF)


def attend_kernel(items, scale, q_ref, kv_ref, o_ref, ot_ref, pt_ref, vt_ref):
    keys = kv_ref.shape[0] * kv_ref.shape[2]

    @pl.when(pl.program_id(0) == 0)
    def _():
        vt_ref[...] = kv_ref[:, 2].reshape(keys, LANES).astype(F32).T.astype(BF)

    rows = q_ref.shape[0] * q_ref.shape[2]
    queries = q_ref[:, 0].reshape(rows, LANES) * BF(scale)
    key_rows = kv_ref[:, 1].reshape(keys, LANES)
    for item in range(items):
        chosen = jnp.where(item_mask(rows, LANES, item), queries, BF(0))
        scores = nt(key_rows, chosen)
        top = jnp.max(scores, axis=0, keepdims=True)
        raised = jnp.exp(scores - top)
        total = jnp.sum(raised, axis=0, keepdims=True)
        weights = (raised * (1.0 / total)).astype(BF)
        pt_ref[item] = weights
        span = slice(item * HDIM, (item + 1) * HDIM)
        ot_ref[span, :] = nn(vt_ref[span, :], weights)
    o_ref[...] = ot_ref[...].T.astype(BF).reshape(o_ref.shape)


def attend(q, kv, items, scale, after):
    peers, _, tokens, lanes = q.shape
    rows, keys = peers * tokens, kv.shape[0] * tokens
    step = max(1, min(peers, 256 * 1024 // keys // tokens))
    block = step * tokens
    return call(
        functools.partial(attend_kernel, items, scale),
        "attend",
        [
            shape((peers, tokens, lanes)),
            shape((lanes, rows), F32),
            shape((items, keys, rows)),
        ],
        Warm(q),
        Warm(kv),
        after=after,
        grid=(peers // step,),
        in_specs=[
            pl.BlockSpec((step, 3, tokens, lanes), lambda j: (j, 0, 0, 0)),
            pl.BlockSpec(kv.shape, lambda j: (0, 0, 0, 0)),
        ],
        out_specs=[
            pl.BlockSpec((step, tokens, lanes), lambda j: (j, 0, 0)),
            pl.BlockSpec((lanes, block), lambda j: (0, j)),
            pl.BlockSpec((items, keys, block), lambda j: (0, 0, j)),
        ],
        scratch=[pltpu.VMEM((lanes, keys), BF)],
        limit=24 if keys <= 2048 else 56,
        flops=8 * rows * keys * lanes,
    )


def pair_attend_kernel(items, scale, *refs):
    sources, (*outs, ot_ref, pt_ref, query_ref, key_ref, value_ref, vt_ref) = refs[:8], refs[8:]
    tokens = sources[0].shape[2]
    for k, source in enumerate(sources):
        span = slice(k * tokens, (k + 1) * tokens)
        if k < len(outs):
            query_ref[0, span, :] = source[0, 0] * BF(scale)
        key_ref[0, span, :] = source[0, 1]
        value_ref[0, span, :] = source[0, 2]
        vt_ref[:, span] = source[0, 2].astype(F32).T.astype(BF)
    queries = query_ref[0]
    for item in range(items):
        chosen = jnp.where(item_mask(queries.shape[0], LANES, item), queries, BF(0))
        scores = nt(key_ref[0], chosen)
        top = jnp.max(scores, axis=0, keepdims=True)
        raised = jnp.exp(scores - top)
        total = jnp.sum(raised, axis=0, keepdims=True)
        weights = (raised * (1.0 / total)).astype(BF)
        pt_ref[0, item] = weights
        span = slice(item * HDIM, (item + 1) * HDIM)
        ot_ref[0, span, :] = nn(vt_ref[span, :], weights)
    attended = ot_ref[0].T.astype(BF)
    for k, out in enumerate(outs):
        out[0] = attended[k * tokens : (k + 1) * tokens]


def pair_attend(own, other, items, scale, after):
    _, _, tokens, lanes = own[0].shape
    rows, keys = len(own) * tokens, 2 * len(own) * tokens
    wide = lambda *dims: pl.BlockSpec((1, *dims), lambda h: (h, *[0] * len(dims)))
    *outs, ot, pt, q, k, v, token = call(
        functools.partial(pair_attend_kernel, items, scale),
        "attend",
        [
            *[shape((2, tokens, lanes))] * len(own),
            shape((2, lanes, rows), F32),
            shape((2, items, keys, rows)),
            shape((2, rows, lanes)),
            shape((2, keys, lanes)),
            shape((2, keys, lanes)),
        ],
        own[0],
        *[Warm(x) for x in [*own[1:], *other]],
        after=after,
        grid=(2,),
        in_specs=[wide(3, tokens, lanes)] * (2 * len(own)),
        out_specs=[
            *[wide(tokens, lanes)] * len(own),
            wide(lanes, rows),
            wide(items, keys, rows),
            wide(rows, lanes),
            wide(keys, lanes),
            wide(keys, lanes),
        ],
        scratch=[pltpu.VMEM((lanes, keys), BF)],
        limit=32,
        flops=16 * rows * keys * lanes,
    )
    return outs, (q, k, v, ot, pt), token


def pair_attend_back_kernel(items, scale, ids_ref, query_ref, key_ref, value_ref, ot_ref, pt_ref, grads_ref, *refs):
    *outs, cross_ref, kt_ref, grad_rows, dqt_ref, dk_sum, dv_sum = refs
    tokens = grads_ref.shape[2]
    for k in range(len(outs)):
        grad_rows[k * tokens : (k + 1) * tokens, :] = grads_ref[ids_ref[4 + k], 0]
    kt_ref[...] = (key_ref[0].astype(F32) * scale).T.astype(BF)
    queries, grads = query_ref[0], grad_rows[...]
    product = grads.astype(F32).T * ot_ref[0]
    for item in range(items):
        span = slice(item * HDIM, (item + 1) * HDIM)
        mask = item_mask(queries.shape[0], LANES, item)
        grad = jnp.where(mask, grads, BF(0))
        query = jnp.where(mask, queries, BF(0))
        delta = jnp.sum(product[span, :], axis=0, keepdims=True)
        weights = pt_ref[0, item]
        back = (weights.astype(F32) * (nt(value_ref[0], grad) - delta)).astype(BF)
        d_value, d_key = nn(weights, grad), nn(back, query)
        if item == 0:
            dv_sum[...] = d_value
            dk_sum[...] = d_key
        else:
            dv_sum[...] += d_value
            dk_sum[...] += d_key
        dqt_ref[span, :] = nn(kt_ref[span, :], back)
    d_query = dqt_ref[...].T.astype(BF)
    for k in range(2 * len(outs)):
        span = slice(k * tokens, (k + 1) * tokens)
        if k < len(outs):
            outs[k][0, 0] = d_query[span]
        for c, total in ((0, dk_sum), (1, dv_sum)):
            if k < len(outs):
                outs[k][0, 1 + c] = total[span, :].astype(BF)
            else:
                cross_ref[k - len(outs), 0, c] = total[span, :].astype(BF)


def pair_attend_back(ids, kept, d, items, scale, after):
    count, _, tokens, lanes = d.shape
    rows, keys = count * tokens, 2 * count * tokens
    wide = lambda *dims: pl.BlockSpec((1, *dims), lambda h: (h, *[0] * len(dims)))
    *outs, cross, token = call(
        functools.partial(pair_attend_back_kernel, items, scale),
        "attend_back",
        [*[shape((2, 3, tokens, lanes))] * count, shape((count, 2, 2, tokens, lanes))],
        ids, *kept, d,
        after=after,
        grid=(2,),
        in_specs=[
            pl.BlockSpec(memory_space=pltpu.SMEM),
            wide(rows, lanes),
            wide(keys, lanes),
            wide(keys, lanes),
            wide(lanes, rows),
            wide(items, keys, rows),
            pl.BlockSpec((count, 1, tokens, lanes), lambda h: (0, h, 0, 0)),
        ],
        out_specs=[
            *[wide(3, tokens, lanes)] * count,
            pl.BlockSpec((count, 1, 2, tokens, lanes), lambda h: (0, h, 0, 0, 0)),
        ],
        scratch=[
            pltpu.VMEM((lanes, keys), BF),
            pltpu.VMEM((rows, lanes), BF),
            pltpu.VMEM((lanes, rows), F32),
            pltpu.VMEM((keys, lanes), F32),
            pltpu.VMEM((keys, lanes), F32),
        ],
        limit=32,
        flops=32 * rows * keys * lanes,
    )
    return outs, cross, token


def combine_kernel(*refs):
    count = (len(refs) - 1) // 2
    own, cross_ref, outs = refs[:count], refs[count], refs[count + 1 :]
    for k in range(count):
        outs[k][:, 0] = own[k][:, 0]
        for c in range(2):
            outs[k][:, 1 + c] = plus(own[k].at[:, 1 + c], cross_ref.at[k, :, c])


def attend_back_kernel(items, scale, q_ref, kv_ref, d_ref, ot_ref, pt_ref, dq_ref, *rest):
    dkv_ref, (kt_ref, dqt_ref, dk_sum, dv_sum) = rest[:-4], rest[-4:]
    step = pl.program_id(0)
    keys = kv_ref.shape[0] * kv_ref.shape[2]

    @pl.when(step == 0)
    def _():
        kt_ref[...] = (kv_ref[:, 1].reshape(keys, LANES).astype(F32) * scale).T.astype(BF)
        dk_sum[...] = jnp.zeros_like(dk_sum)
        dv_sum[...] = jnp.zeros_like(dv_sum)

    peers, _, tokens, _ = q_ref.shape
    rows = peers * tokens
    queries = q_ref[:, 0].reshape(rows, LANES) * BF(scale)
    grads = d_ref[...].reshape(rows, LANES)
    value_rows = kv_ref[:, 2].reshape(keys, LANES)
    product = grads.astype(F32).T * ot_ref[...]
    for item in range(items):
        span = slice(item * HDIM, (item + 1) * HDIM)
        mask = item_mask(rows, LANES, item)
        grad = jnp.where(mask, grads, BF(0))
        query = jnp.where(mask, queries, BF(0))
        delta = jnp.sum(product[span, :], axis=0, keepdims=True)
        weights = pt_ref[item]
        back = (weights.astype(F32) * (nt(value_rows, grad) - delta)).astype(BF)
        dv_sum[...] += nn(weights, grad)
        dk_sum[...] += nn(back, query)
        dqt_ref[span, :] = nn(kt_ref[span, :], back)
    d_query = dqt_ref[...].T.astype(BF).reshape(peers, tokens, LANES)
    if dkv_ref:
        dq_ref[...] = d_query
    else:
        dq_ref[pl.ds(step * peers, peers), 0] = d_query

    @pl.when(step == pl.num_programs(0) - 1)
    def _():
        for c, total in ((1, dk_sum), (2, dv_sum)):
            total = total[...].reshape(kv_ref.shape[0], tokens, LANES)
            if dkv_ref:
                dkv_ref[0][:, c - 1] = total
            else:
                dq_ref[:, c] = total.astype(BF)


def attend_back(q, kv, d, ot, pt, items, scale, after):
    peers, _, tokens, lanes = q.shape
    rows, keys = peers * tokens, kv.shape[0] * tokens
    step = max(1, min(peers, 256 * 1024 // keys // tokens))
    block = step * tokens
    if q.shape == kv.shape:
        outs = [shape(q.shape)]
        out_specs = [pl.BlockSpec(q.shape, lambda j: (0, 0, 0, 0))]
    else:
        outs = [shape((peers, tokens, lanes)), shape((kv.shape[0], 2, tokens, lanes), F32)]
        out_specs = [
            pl.BlockSpec((step, tokens, lanes), lambda j: (j, 0, 0)),
            pl.BlockSpec(outs[1].shape, lambda j: (0, 0, 0, 0)),
        ]
    *back, token = call(
        functools.partial(attend_back_kernel, items, scale),
        "attend_back",
        outs,
        Warm(q),
        Warm(kv),
        d,
        ot,
        pt,
        after=after,
        grid=(peers // step,),
        in_specs=[
            pl.BlockSpec((step, 3, tokens, lanes), lambda j: (j, 0, 0, 0)),
            pl.BlockSpec(kv.shape, lambda j: (0, 0, 0, 0)),
            pl.BlockSpec((step, tokens, lanes), lambda j: (j, 0, 0)),
            pl.BlockSpec((lanes, block), lambda j: (0, j)),
            pl.BlockSpec((items, keys, block), lambda j: (0, 0, j)),
        ],
        out_specs=out_specs,
        scratch=[
            pltpu.VMEM((lanes, keys), BF),
            pltpu.VMEM((lanes, block), F32),
            pltpu.VMEM((keys, lanes), F32),
            pltpu.VMEM((keys, lanes), F32),
        ],
        limit=24 if keys <= 2048 else 60,
        flops=16 * rows * keys * lanes,
    )
    return back, token


def unpack(ids_ref, sources, index, out_ref, base):
    several = len(sources) > 1
    count = len(sources) if several else sources[0].shape[0] // 2
    for t in range(count):
        source, head = (sources[t], 0) if several else (sources[0], 2 * t)
        pair = [
            (source[head + s] if index is None else source[head + s, index]).astype(F32) for s in range(2)
        ]
        at = base + (pl.multiple_of(ids_ref[4 + t] * LANES, LANES) if several else t * LANES)
        for item, tile in enumerate(interleave(*pair)):
            out_ref[item * LANES : (item + 1) * LANES, pl.ds(at, LANES)] = tile.astype(BF)


def pack(product, out_ref):
    for t in range(product.shape[1] // LANES):
        tile = product[:, t * LANES : (t + 1) * LANES]
        for s, block in enumerate(interleave(tile[:LANES], tile[LANES:])):
            out_ref[2 * t + s] = block.astype(BF)


def project_kernel(ids_ref, *refs):
    *sources, wo_ref, mixed_ref, branch_ref = refs
    unpack(ids_ref, sources, None, mixed_ref, 0)
    branch_ref[...] = nn(mixed_ref[...], wo_ref[...]).astype(BF)


def forward_kernel(sources, ids_ref, *refs):
    if sources:
        own, got, refs = refs[:sources], refs[sources : 2 * sources], refs[2 * sources :]
        wo_ref, wo_got_ref, zero_ref, gains_ref, wu_ref, dact_ref, norm_ref, mixed_out, *refs = refs
        *refs, wo_buf, mixed, wo_sems = refs
        me = ids_ref[9]
        wo_loads = [
            pltpu.make_async_copy(wo_ref, wo_buf.at[me], wo_sems.at[0]),
            pltpu.make_async_copy(wo_got_ref, wo_buf.at[1 - me], wo_sems.at[1]),
        ]
        for copy in wo_loads:
            copy.start()
    else:
        own_ref, got_ref, zero_ref, gains_ref, wu_ref, dact_ref, norm_ref, *refs = refs
    one_out, pre_out, act_out, other_out, *rest = refs
    count = (len(rest) - 9) // 2
    turned_out, turned = rest[:count], rest[count : 2 * count]
    one_ref, weights, grads, pre_ref, act_ref, normed_ref, hold, into, out_of = rest[2 * count :]
    chunks, _, block = grads.shape
    per_half = chunks // 2
    loads, stores = [], []
    for c in range(chunks):
        span = slice(c * block, (c + 1) * block)
        loads.append(
            (
                pltpu.make_async_copy(wu_ref.at[:, span], weights.at[c], into.at[2 * c]),
                pltpu.make_async_copy(dact_ref.at[:, span], grads.at[c], into.at[2 * c + 1]),
            )
        )
        for copy in loads[-1]:
            copy.start()

    def store(source, target):
        stores.append(pltpu.make_async_copy(source, target, out_of.at[len(stores)]))
        stores[-1].start()

    if sources:
        unpack(ids_ref, own, None, mixed.at[me], 0)
        unpack(ids_ref, got, None, mixed.at[1 - me], 0)
        mixed_out[...] = mixed[me]
        for copy in wo_loads:
            copy.wait()
        branch = nn(mixed[0], wo_buf[0]) + nn(mixed[1], wo_buf[1])
    else:
        branch = own_ref[...].astype(F32) + got_ref[...].astype(F32)
    hidden = zero_ref[...] + branch
    one_ref[...] = hidden
    store(one_ref, one_out)
    unit, _ = norm_parts(hidden)
    normed = unit * gains_ref[1:2, :]
    normed_ref[...] = normed.astype(BF)
    emit_turned(normed, ids_ref, turned, hold)
    for source, target in zip(turned, turned_out):
        store(source, target)
    total = None
    for c in range(chunks):
        span = slice(c * block, (c + 1) * block)
        half, place = c // per_half, slice(c % per_half * block, (c % per_half + 1) * block)
        for copy in loads[c]:
            copy.wait()
        pre = nn(normed_ref[...], weights[c])
        chance = 0.5 * (1.0 + lax.erf(pre * (1.0 / math.sqrt(2.0))))
        slope = chance + pre * jnp.exp(-0.5 * pre * pre) * (1.0 / math.sqrt(2.0 * math.pi))
        act_ref[half, :, place] = (pre * chance).astype(BF)
        store(act_ref.at[half, :, place], act_out.at[half, :, place])
        d_pre = (grads[c].astype(F32) * slope).astype(BF)
        pre_ref[:, span] = d_pre
        store(pre_ref.at[:, span], pre_out.at[:, span])
        part = nt(d_pre, weights[c])
        total = part if total is None else total + part
    store(act_ref.at[1 - ids_ref[0]], other_out)
    norm_ref[...] = total.astype(BF)
    for copy in stores:
        copy.wait()


def second_kernel(ids_ref, one_ref, two_ref, own_ref, got_ref, gains_ref, wo_ref, d_ref, gain_ref, *rest):
    heads_ref, *turned, hold = rest
    unit, inverse = norm_parts(one_ref[...])
    grad = own_ref[...].astype(F32) + got_ref[...].astype(F32)
    back, gain = norm_back(unit, inverse, gains_ref[1:2, :], grad)
    gain_ref[...] = gain
    d_one = two_ref[...] + back
    d_ref[...] = d_one
    pack(nt(d_one.astype(BF), wo_ref[...]), heads_ref)
    emit_turned(d_one, ids_ref, turned, hold)


def head_kernel(ids_ref, one_ref, own_ref, got_ref, wh_ref, pred_ref, *rest):
    turned, hold = rest[:-1], rest[-1]
    hidden = one_ref[...] + (own_ref[...].astype(F32) + got_ref[...].astype(F32))
    low = hidden.astype(BF)
    for item in range(pred_ref.shape[0]):
        pred_ref[item] = nt(wh_ref[...], low[item * LANES : (item + 1) * LANES])
    emit_turned(hidden, ids_ref, turned, hold)


def third_kernel(count, ids_ref, *refs):
    sources, (wq_ref, dqkv_ref, norm_ref) = refs[:count], refs[count:]
    width = wq_ref.shape[2]
    total = None
    for c in range(3):
        unpack(ids_ref, sources, c, dqkv_ref, c * width)
        part = nt(dqkv_ref[:, c * width : (c + 1) * width], wq_ref[c])
        total = part if total is None else total + part
    norm_ref[...] = total.astype(BF)


def last_kernel(cols, ids_ref, zero_ref, done_ref, own_ref, got_ref, gains_ref, gain_two_ref, patches_ref, we_ref,
                pos_send, pos_keep, fields_ref, edge_ref, *rest):
    embed, (rows_ref, pos_ref, hold) = rest[:-3], rest[-3:]
    unit, inverse = norm_parts(zero_ref[...])
    grad = own_ref[...].astype(F32) + got_ref[...].astype(F32)
    back, gain = norm_back(unit, inverse, gains_ref[0:1, :], grad)
    d_zero = done_ref[...] + back
    low = d_zero.astype(BF)
    items, variables, height = edge_ref.shape
    pos = d_zero[0:LANES]
    for item in range(1, items):
        pos = pos + d_zero[item * LANES : (item + 1) * LANES]
    width = pos_ref.shape[2]
    for k in range(2):
        pos_ref[k] = pos[:, k * width : (k + 1) * width].astype(BF)
    pos_send[...] = pos_ref[1 - ids_ref[1]]
    pos_keep[...] = pos_ref[ids_ref[1]]
    features = patches_ref.shape[0]
    rows_ref[...] = jnp.zeros_like(rows_ref)
    rows_ref[0:features, :] = nn(patches_ref[...], low)
    rows_ref[features : features + 1, :] = gain
    rows_ref[features + 1 : features + 2, :] = gain_two_ref[...]
    emit_turned(rows_ref[...], ids_ref, embed, hold)
    half = height // PATCH
    row = lax.broadcasted_iota(jnp.int32, (LANES, height), 0)
    lane = lax.broadcasted_iota(jnp.int32, (LANES, height), 1)
    fields_ref[...] = jnp.zeros_like(fields_ref)
    order = feature_order(variables, True)
    for item in range(items):
        d_patches = nt(we_ref[...], low[item * LANES : (item + 1) * LANES])
        high = d_patches.astype(BF)
        rest = (d_patches - high.astype(F32)).astype(BF)
        high, rest = nn(order, high).astype(BF), nn(order, rest).astype(BF)
        for j in range(2):
            total = None
            for a in range(PATCH):
                place = jnp.where(
                    (row // half == j) & (lane == PATCH * (row % half) + a), 1.0, 0.0
                ).astype(BF)
                span = slice(a * 2 * variables, (a + 1) * 2 * variables)
                part = nn(high[span], place) + nn(rest[span], place)
                total = part if total is None else total + part
            for b in range(PATCH):
                block = total[b * variables : (b + 1) * variables]
                column = 2 * j + b - 1
                if column < 0:
                    edge_ref[item] = block.astype(BF)
                else:
                    fields_ref[item, pl.ds(column, variables, stride=cols), :] = block


def down_kernel(act_ref, wd_ref, out_ref):
    width = act_ref.shape[2]
    total = nn(act_ref[0], wd_ref[0:width, :]) + nn(act_ref[1], wd_ref[width:, :])
    out_ref[...] = total.astype(BF)


def pin(xs, after):
    def body(*refs):
        pass

    anywhere = pl.BlockSpec(memory_space=pl.ANY)
    several = isinstance(xs, (list, tuple))
    xs = list(xs) if several else [xs]
    out = pl.pallas_call(
        body,
        out_shape=[pltpu.HBM(x.shape, x.dtype) for x in xs],
        in_specs=[anywhere] * (len(xs) + len(after)),
        out_specs=[anywhere] * len(xs),
        input_output_aliases={k: k for k in range(len(xs))},
        name="pin",
    )(*[pltpu.with_memory_space_constraint(x, pltpu.HBM) for x in xs], *after)
    return out if several else out[0]


def product_of(own, got, b_own, b_got):
    parts, rows, tokens = own.shape
    total = nn(own[...].reshape(parts * rows, tokens), b_own)
    return total + nn(got[...].reshape(parts * rows, tokens), b_got)


def split_dp(ids_ref, hold, send, keep, columns):
    half = hold.shape[0] // 2
    for out, at in ((send, 1 - ids_ref[1]), (keep, ids_ref[1])):
        for k in range(half):
            out[k, :, 0:columns] = hold[at * half + k]


def split_near(ids_ref, hold, send, keep, columns):
    for out, at in ((send, 1 - ids_ref[2]), (keep, ids_ref[2])):
        for k in range(hold.shape[0] // 2):
            out[k, :, 0:columns] = hold[2 * k + at]


def plus(a, b):
    return (a[...].astype(F32) + b[...].astype(F32)).astype(BF)


def grads_ff_kernel(ids_ref, at_own, at_got, pre_own, pre_got, ct_own, ct_got, act_own, act_got,
                    send_a, keep_a, send_b, keep_b, hold, inner):
    parts, rows, total = hold.shape
    columns = total - keep_b.shape[2]
    product = product_of(at_own, at_got, pre_own[...], pre_got[...])
    hold[...] = product.astype(BF).reshape(hold.shape)
    split_dp(ids_ref, hold.at[:, :, 0:columns], send_a, keep_a, columns)
    split_near(ids_ref, hold.at[:, :, columns:], send_b, keep_b, total - columns)
    product = (nn(ct_own[...], act_own[ids_ref[0]]) + nn(ct_got[...], act_got[...])).astype(BF)
    tiles, groups = inner.shape[1], inner.shape[3] // LANES
    for k in range(2):
        for q in range(tiles):
            for g in range(groups):
                inner[k, q, :, g * LANES : (g + 1) * LANES] = product[
                    g * rows : (g + 1) * rows, (k * tiles + q) * LANES : (k * tiles + q + 1) * LANES
                ]
    for q in range(tiles):
        send_a[q, :, columns:] = inner[1 - ids_ref[1], q]
        keep_a[q, :, columns:] = inner[ids_ref[1], q]


def fold_ff_kernel(ids_ref, keep_a, got_a, keep_b, got_b, send_a, left_a, send_b, left_b, hold, hold_b):
    columns = hold.shape[2]
    extra = keep_a.shape[2] - columns
    hold[...] = plus(keep_a.at[:, :, 0:columns], got_a.at[:, :, 0:columns])
    split_near(ids_ref, hold, send_a, left_a, columns)
    for q in range(keep_a.shape[0]):
        total = plus(keep_a.at[q, :, columns:], got_a.at[q, :, columns:])
        at = columns + q % 2 * extra
        for out in (send_a, left_a):
            out[q // 2, :, at : at + extra] = total
    hold_b[...] = plus(keep_b, got_b)
    split_dp(ids_ref, hold_b, send_b, left_b, hold_b.shape[2])


def merge_ff_kernel(ids_ref, keep_a, got_a, keep_b, got_b, send, left, hold):
    columns = hold.shape[2] - keep_b.shape[2]
    extra = keep_a.shape[2] - columns
    hold[:, :, 0:columns] = plus(keep_a.at[:, :, 0:columns], got_a.at[:, :, 0:columns])
    hold[:, :, columns:] = plus(keep_b, got_b)
    far = ids_ref[3]
    width = hold.shape[2]
    send[:, 0:width] = hold[1 - far]
    left[:, 0:width] = hold[far]
    for k in range(2):
        total = plus(keep_a.at[k, :, columns:], got_a.at[k, :, columns:])
        at = width + k * extra
        for out in (send, left):
            out[:, at : at + extra] = total


def grads_oh_kernel(ids_ref, one_own, one_got, mixed_own, mixed_got, two_own, two_got, ct_own, ct_got,
                    send, keep, hold):
    width, features = mixed_own.shape[1], ct_own.shape[0]
    shape3 = hold.shape[:2]
    product = product_of(one_own, one_got, mixed_own[...], mixed_got[...])
    hold[:, :, 0:width] = product.astype(BF).reshape(*shape3, width)
    hold[:, :, width:] = jnp.zeros((*shape3, hold.shape[2] - width), BF)
    product = product_of(
        two_own, two_got, ct_own[...].astype(F32).T.astype(BF), ct_got[...].astype(F32).T.astype(BF)
    )
    hold[:, :, width : width + features] = product.astype(BF).reshape(*shape3, features)
    split_dp(ids_ref, hold, send, keep, hold.shape[2])


def grads_q_kernel(ids_ref, at_own, at_got, b_own, b_got, send_a, keep_a, send_b, keep_b, hold):
    cut, total = keep_a.shape[2], hold.shape[2]
    hold[...] = product_of(at_own, at_got, b_own[...], b_got[...]).astype(BF).reshape(hold.shape)
    split_dp(ids_ref, hold.at[:, :, 0:cut], send_a, keep_a, cut)
    split_near(ids_ref, hold.at[:, :, cut:], send_b, keep_b, total - cut)


def fold_q_kernel(ids_ref, keep_a, got_a, keep_b, got_b, up_keep, up_got, oh_keep, oh_got, embed_own, embed_got,
                  send_a, left_a, send_b, left_b, send_o, left_o, hold_a, hold_b, hold_o, hold_e):
    hold_a[...] = plus(keep_a, got_a)
    split_near(ids_ref, hold_a, send_a, left_a, hold_a.shape[2])
    hold_b[...] = plus(keep_b, got_b)
    columns = hold_b.shape[2]
    split_dp(ids_ref, hold_b, send_b, left_b, columns)
    hold_o[...] = plus(oh_keep, oh_got)
    for out, at in ((send_o, 1 - ids_ref[3]), (left_o, ids_ref[3])):
        for k in range(2):
            out[k] = hold_o[2 * at + k]
    hold_e[...] = plus(embed_own, embed_got)
    width = hold_e.shape[2]
    for out, at in ((send_b, 1 - ids_ref[1]), (left_b, ids_ref[1])):
        for k in range(4):
            start = columns + k % 2 * width
            out[k // 2, :, start : start + width] = hold_e[4 * at + k]
    start = columns + 2 * width
    half = send_b.shape[2] - start
    for k in range(2):
        at = up_keep.shape[1] - (2 - k) * half
        total = plus(up_keep.at[:, at : at + half], up_got.at[:, at : at + half])
        for out in (send_b, left_b):
            out[k, :, start:] = total


def merge_q_kernel(ids_ref, keep_a, got_a, keep_b, got_b, oh_keep, oh_got,
                   send, left, pair_ref, near_ref, embed_both, oh_left, hold, hold_e, hold_o):
    width = embed_both.shape[1]
    half = pair_ref.shape[2] // 2
    first = keep_a.shape[2]
    columns = keep_b.shape[2] - half - 2 * width
    total = hold.shape[2]
    hold[:, :, 0:first] = plus(keep_a, got_a)
    hold[:, :, first:] = plus(keep_b.at[:, :, 0:columns], got_b.at[:, :, 0:columns])
    hold_o[...] = plus(oh_keep, oh_got)
    for k in range(4):
        span = slice(columns + k % 2 * width, columns + (k % 2 + 1) * width)
        hold_e[k] = plus(keep_b.at[k // 2, :, span], got_b.at[k // 2, :, span])
    far, near = ids_ref[3], ids_ref[2]
    for out, at in ((send, 1 - far), (left, far)):
        out[:, 0:total] = hold[at]
        out[:, total:] = hold_e[2 * at + near]
    near_ref[:, 0:width] = hold_e[2 * far + 1 - near]
    near_ref[:, width:] = hold_o[1 - near]
    oh_left[...] = hold_o[near]
    embed_both[...] = hold_e[2 * (1 - far) + 1 - near]
    for k in range(2):
        span = slice(k * half, (k + 1) * half)
        pair_ref[0, :, span] = keep_b[k, :, columns + 2 * width :]
        pair_ref[1, :, span] = got_b[k, :, columns + 2 * width :]


def expand(ids_ref, rows_ref, pair_own, pair_got, out_ref, block):
    rows = rows_ref.shape[0]
    groups = block.shape[0] // rows
    tiles = block.shape[1] // LANES
    for a, b in ((0, 0), (0, 1), (1, 0), (1, 1)):
        source = pair_got if a else pair_own
        for q in range(tiles):
            for g in range(groups):
                at = (q * groups + g) * LANES
                block[g * rows : (g + 1) * rows, q * LANES : (q + 1) * LANES] = source[b, :, at : at + LANES]
        core, dp = (1 - ids_ref[0] if a else ids_ref[0]), (1 - ids_ref[1] if b else ids_ref[1])
        at = pl.multiple_of((core * 2 + dp) * block.shape[1], LANES)
        out_ref[:, pl.ds(at, block.shape[1])] = nn(rows_ref[...], block[...])


def insert_east(cols, fields_ref, east_ref, out_ref):
    variables = east_ref.shape[1]
    out_ref[...] = fields_ref[...]
    for item in range(east_ref.shape[0]):
        out_ref[item, pl.ds(cols - 1, variables, stride=cols), :] = east_ref[item].astype(F32)


def close_kernel(cols, ids_ref, fields_ref, east_ref, pos_ref, pos_got_ref, *refs):
    outs = refs
    if len(refs) > 2:
        (up_ref, up_got_ref, rows_ref, pair_own, pair_got), outs, block = refs[:5], refs[5:-1], refs[-1]
        width = outs[2].shape[1]
        outs[2][...] = up_ref[:, 0:width].astype(F32) + up_got_ref[:, 0:width].astype(F32)
        expand(ids_ref, rows_ref, pair_own, pair_got, outs[3], block)
    insert_east(cols, fields_ref, east_ref, outs[0])
    outs[1][...] = pos_ref[...].astype(F32) + pos_got_ref[...].astype(F32)


def end_kernel(*refs):
    if len(refs) > 3:
        (near_ref, both_ref, oh_ref, keep_ref, got_ref), refs = refs[:5], refs[5:]
        out_ref, head_ref, grad_ref = refs[2:]
        embed_width = both_ref.shape[1]
        both = keep_ref[...].astype(F32) + got_ref[...].astype(F32)
        width = grad_ref.shape[2]
        for c in range(3):
            grad_ref[c] = both[:, c * width : (c + 1) * width]
        total = both[:, 3 * width :] + near_ref[:, 0:embed_width].astype(F32) + both_ref[...].astype(F32)
        both = oh_ref[...].astype(F32) + near_ref[:, embed_width:].astype(F32)
        out_ref[...] = both[:, 0:width]
        head_ref[...] = both[:, width : width + head_ref.shape[1]]
    else:
        total, refs = jnp.sum(refs[0][...].astype(F32), axis=0), refs[1:]
    features = refs[0].shape[1]
    refs[0][...] = total[:, 0:features]
    refs[1][...] = total[:, LANES:].T[features - LANES : features - LANES + 2, :]


def local(
    dataset,
    indices,
    run_count,
    run_mean,
    run_var,
    w_embed,
    pos_embed,
    gains,
    w_qkv,
    w_out,
    w_up,
    w_down,
    w_head,
    cotangent,
):
    items = indices.shape[0]
    variables, height, columns = dataset.shape[1:]
    dp, lon = lax.axis_size("dp"), lax.axis_size("lon")
    everyone = dp * lon
    width = w_embed.shape[1]
    local_width = w_qkv.shape[2]
    heads = local_width // HDIM
    item_tokens = cotangent.shape[1]
    tokens = items * item_tokens
    features = w_embed.shape[0]
    hidden_units = w_up.shape[1]
    scale = 1.0 / math.sqrt(HDIM)
    group, far = heads, lon // heads
    groups = [[group * g + i for i in range(group)] for g in range(far)]
    across = [[i + group * g for g in range(far)] for i in range(group)]
    assert items * HDIM == LANES and item_tokens == LANES and height == LANES and columns == 4
    lon_at, dp_at = lax.axis_index("lon"), lax.axis_index("dp")
    ids = [lon_at % 2, dp_at, lon_at // 2 % 2, lon_at // 4 % 2, *[lon_at // 2 ^ k for k in range(4)], dp_at * lon + lon_at, lax.axis_index("mp")]
    ids = jnp.stack(ids).astype(jnp.int32)
    paired = dp == 2 and lon == 8
    parts, rows = width // (2 * (width // everyone)), width // everyone
    turned_shape = (
        [shape((parts, rows, tokens))] * 2 if paired else [shape((width, tokens))]
    )
    turned_hold = pltpu.VMEM((parts, 2, rows, tokens) if paired else (8, LANES), BF)

    alone = dict(axis_index_groups=groups) if far > 1 else {}

    vmem, smem = pl.BlockSpec(memory_space=pltpu.VMEM), pl.BlockSpec(memory_space=pltpu.SMEM)
    assert dp == 2

    data = dataset.transpose(0, 1, 3, 2).reshape(dataset.shape[0], variables * columns, height)
    fields, edge, moments, _ = call(
        moments_kernel,
        "moments",
        [
            warm((items, variables * columns, height), F32),
            warm((items, variables, height)),
            warm((8, LANES) if paired else (everyone, 8, LANES), F32),
        ],
        indices, data,
        in_specs=[pl.BlockSpec(memory_space=pltpu.SMEM), pl.BlockSpec(memory_space=pl.ANY)],
        scratch=[pltpu.VMEM((LANES, LANES), F32), pltpu.SemaphoreType.DMA((items,))],
    )
    edge = from_behind(edge, "lon", 1)
    if paired:
        row = lax.broadcasted_iota(jnp.int32, moments.shape, 0)
        held = float(items * height * columns)
        for axis, distance in (("lon", 1), ("lon", 2), ("lon", 4), ("dp", 1)):
            got = swap(moments, axis, distance)
            apart = jnp.square(moments[0:1] - got[0:1]) * (0.5 * held)
            moments = jnp.where(row == 0, 0.5 * (moments + got), moments + got + apart)
            held = 2.0 * held
    else:
        moments = lax.all_to_all(moments, ("dp", "lon"), 0, 0)
    wh_turned = w_head.T

    out = call(
        functools.partial(start_kernel, float(items * height * columns), everyone),
        "start",
        [
            *[shape((1, variables), F32)] * 3,
            shape((tokens, width), F32),
            shape((features, tokens)),
            *([shape((2, 3, item_tokens, LANES))] * 4 if paired else [shape((heads, 3, item_tokens, LANES))]),
            *turned_shape,
        ],
        ids, Warm(moments), *[r.reshape(1, variables) for r in (run_count, run_mean, run_var)],
        Warm(fields), Warm(edge), w_embed, pos_embed, gains, w_qkv,
        in_specs=[smem, *[vmem] * 9, pl.BlockSpec(memory_space=pl.ANY)],
        scratch=[
            pltpu.VMEM((LANES, LANES), F32),
            pltpu.VMEM((8, LANES), F32),
            turned_hold,
            pltpu.VMEM(w_qkv.shape, BF),
            pltpu.SemaphoreType.DMA,
            pltpu.VMEM((heads, 3, item_tokens, LANES), BF),
        ],
        flops=2 * tokens * width * (features + 3 * local_width),
    )
    count = 4 if paired else 1
    stats, (hidden_zero, patches), packed = out[:3], out[3:5], out[5 : 5 + count]
    normed_one, token = out[5 + count : -1], out[-1]

    def along(messages):
        return [messages[0], *[swap(messages[k], "lon", 2 * k) for k in range(1, count)]]

    if paired:
        own = along(packed)
    else:
        sent = lax.all_to_all(packed[0], "lon", 0, 0, **alone)
        kv = sent
        if far > 1:
            kv = lax.all_gather(sent, "lon", axis=0, tiled=True, axis_index_groups=across)

    if paired:
        wo_got, normed_got = swap(w_out, "mp", 1), swap(normed_one[1], "lon", 1)
        other = [swap(x, "lon", 1) for x in own]
    if paired:
        attended, kept, token = pair_attend(own, other, items, scale, [token, normed_got])
        attended = along(attended)
    else:
        attended, attended_t, weights_t, token = attend(sent, kv, items, scale, [token])
        attended = [lax.all_to_all(attended, "lon", 0, 0, **alone)]
    anywhere = pl.BlockSpec(memory_space=pl.ANY)
    d_two, d_act, ct_turned, *mine, token = call(
        cotangent_kernel,
        "cotangent",
        [
            shape((tokens, width), F32),
            shape((tokens, hidden_units)),
            shape((features, tokens)),
            *[shape((rows, features))] * paired,
        ],
        ids, cotangent.transpose(0, 2, 1), wh_turned, w_down,
        after=[token],
        scratch=[pltpu.VMEM((everyone, rows, features), BF)] * paired,
        flops=2 * tokens * width * (features + hidden_units),
    )

    if paired:
        ct_got = swap(ct_turned, "lon", 1)
        attended[0] = pin(attended[0], [token])
        attended += [swap(x, "mp", 1) for x in attended]
    if paired:
        branches = [attended[0], *[Warm(x) for x in attended[1:]], w_out, Warm(wo_got)]
    else:
        mixed, branch, token = call(
            project_kernel,
            "project",
            [shape((tokens, local_width)), warm((tokens, width))],
            ids, *attended, w_out,
            after=[token],
            flops=2 * tokens * width * local_width,
        )
        branches = [Warm(branch), Warm(swap(branch, "mp", 1))]
    block = min(512, hidden_units // 2)
    chunks = hidden_units // block
    out = call(
        functools.partial(forward_kernel, count if paired else 0),
        "forward",
        [
            warm((tokens, width)),
            *[shape((tokens, local_width))] * paired,
            shape((tokens, width), F32),
            shape((tokens, hidden_units)),
            shape((2, tokens, hidden_units // 2)),
            shape((tokens, hidden_units // 2)),
            *turned_shape,
        ],
        ids, *branches, Warm(hidden_zero), gains, w_up, d_act,
        after=[token],
        in_specs=[
            smem,
            *([*[vmem] * (len(branches) - 2), anywhere, anywhere] if paired else [vmem] * 2),
            vmem,
            vmem,
            anywhere,
            anywhere,
        ],
        out_specs=[*[vmem] * (1 + paired), *[anywhere] * (4 + len(turned_shape))],
        scratch=[
            *[pltpu.VMEM(x.shape, BF) for x in turned_shape],
            pltpu.VMEM((tokens, width), F32),
            pltpu.VMEM((chunks, width, block), BF),
            pltpu.VMEM((chunks, tokens, block), BF),
            pltpu.VMEM((tokens, hidden_units), BF),
            pltpu.VMEM((2, tokens, hidden_units // 2), BF),
            pltpu.VMEM((tokens, width), BF),
            turned_hold,
            pltpu.SemaphoreType.DMA((2 * chunks,)),
            pltpu.SemaphoreType.DMA((2 + len(turned_shape) + 2 * chunks,)),
            *[
                pltpu.VMEM((2, *w_out.shape), BF),
                pltpu.VMEM((2, tokens, local_width), BF),
                pltpu.SemaphoreType.DMA((2,)),
            ] * paired,
        ],
        limit=32,
        flops=4 * tokens * width * hidden_units,
    )
    d_norm, *out, token = out
    if paired:
        mixed, out = out[0], out[1:]
        mixed_got = swap(mixed, "lon", 1)
    hidden_one, d_pre, activated, act_send = out[:4]
    normed_two = out[4:]
    d_norm_got = swap(d_norm, "mp", 1)
    half = hidden_units // 2
    if paired:
        inner_columns = features // rows * LANES
        first = half - LANES
        out_a = shape((parts // 2, rows, first + inner_columns))
        out_b = shape((parts // 2, rows, hidden_units - first))
        send_a, keep_a, send_b, keep_b, token = call(
            grads_ff_kernel,
            "grads_ff",
            [out_a, out_a, out_b, out_b],
            ids, normed_two[0], Warm(swap(normed_two[1], "lon", 1)), d_pre, Warm(swap(d_pre, "lon", 1)),
            ct_turned, Warm(ct_got), activated, Warm(swap(act_send, "lon", 1)),
            after=[token],
            scratch=[
                pltpu.VMEM((parts, rows, hidden_units), BF),
                pltpu.VMEM((2, parts // 2, rows, inner_columns), BF),
            ],
            limit=32,
            flops=2 * tokens * (width + features) * hidden_units,
        )
        got_a, got_b = swap(send_a, "dp", 1), swap(send_b, "lon", 2)
    forward, token = call(
        down_kernel,
        "down",
        [shape((tokens, width))],
        activated, w_down,
        after=[token, *([mixed_got] if paired else [])],
        flops=2 * tokens * width * hidden_units,
    )

    out = call(
        second_kernel,
        "second",
        [
            shape((tokens, width), F32),
            shape((1, width), F32),
            shape((heads, item_tokens, LANES)),
            *turned_shape,
        ],
        ids, Warm(hidden_one), Warm(d_two), Warm(d_norm), Warm(d_norm_got), gains, Warm(w_out),
        after=[token],
        scratch=[turned_hold],
        flops=2 * tokens * width * local_width,
    )
    d_one, gain_two, d_mixed = out[0], out[1], out[2:3]
    d_one_turned, token = out[3:-1], out[-1]
    if paired:
        d_one_got = swap(d_one_turned[1], "lon", 1)
    if paired:
        chips = [[2 * k + c for k in range(lon // 2)] for c in range(2)]
        d_heads = lax.all_to_all(
            d_mixed[0].reshape(lon // 2, 2, item_tokens, LANES), "lon", 0, 0, axis_index_groups=chips
        )
    else:
        d_heads = lax.all_to_all(d_mixed[0], "lon", 0, 0, **alone)
    forward_got = swap(forward, "mp", 1)
    if paired:
        out_a = shape((2, rows, first + 2 * inner_columns))
        out_b = shape((2, rows, hidden_units - first))
        send_a, keep_a, send_b, keep_b, token = call(
            fold_ff_kernel,
            "fold_ff",
            [out_a, out_a, out_b, out_b],
            ids, keep_a, Warm(got_a), keep_b, Warm(got_b),
            after=[token],
            scratch=[
                pltpu.VMEM((parts // 2, rows, first), BF),
                pltpu.VMEM((parts // 2, rows, hidden_units - first), BF),
            ],
        )
        send_a, send_b = pin([send_a, send_b], [d_heads])
        got_a, got_b = swap(send_a, "lon", 2), swap(send_b, "dp", 1)

    if paired:
        back, cross, token = pair_attend_back(ids, kept, d_heads, items, scale, [token])
        *back, token = call(
            combine_kernel,
            "combine",
            [shape(x.shape) for x in back],
            *back, Warm(swap(pin(cross, [got_a, got_b, forward_got]), "lon", 1)),
            after=[token],
        )
        back = along(back)
    else:
        back, token = attend_back(sent, kv, d_heads, attended_t, weights_t, items, scale, [token])
        if far > 1:
            d_query, d_kv = back
            d_kv = lax.psum_scatter(
                d_kv, "lon", scatter_dimension=0, tiled=True, axis_index_groups=across
            ).astype(BF)
            back = [jnp.concatenate([d_query[:, None], d_kv], axis=1)]
        back = [lax.all_to_all(back[0], "lon", 0, 0, **alone)]
    out = call(
        head_kernel,
        "head",
        [shape((items, features, item_tokens), F32), *turned_shape],
        ids, hidden_one, forward, Warm(forward_got), wh_turned,
        after=[token],
        scratch=[turned_hold],
        flops=2 * tokens * width * features,
    )
    pred, hidden_turned, token = out[0].transpose(0, 2, 1), list(out[1:-1]), out[-1]
    if paired:
        up_send, up_keep, token = call(
            merge_ff_kernel,
            "merge_ff",
            [shape((rows, hidden_units + 4 * inner_columns))] * 2,
            ids, keep_a, Warm(got_a), keep_b, got_b,
            after=[token],
            scratch=[pltpu.VMEM((2, rows, hidden_units), BF)],
        )
    d_qkv, d_norm, token = call(
        functools.partial(third_kernel, count),
        "third",
        [shape((tokens, 3 * local_width)), warm((tokens, width))],
        ids, back[0], *[Warm(x) for x in back[1:]], Warm(w_qkv),
        after=[token],
        flops=6 * tokens * width * local_width,
    )
    d_norm_got = swap(d_norm, "mp", 1)
    if paired:
        up_send, hidden_turned[1] = pin([up_send, hidden_turned[1]], [token])
        up_got = swap(up_send, "lon", 4)
        wide = local_width + 2 * LANES
        cut = 3 * local_width // 2 + LANES
        first, second = (shape((parts // 2, rows, c)) for c in (cut, 3 * local_width - cut))
        send_a, keep_a, send_b, keep_b, token = call(
            grads_q_kernel,
            "grads_q",
            [first, first, second, second],
            ids, normed_one[0], normed_got, d_qkv, Warm(swap(d_qkv, "lon", 1)),
            after=[token],
            scratch=[pltpu.VMEM((parts, rows, 3 * local_width), BF)],
            flops=6 * tokens * width * local_width,
        )
        oh_send, oh_keep, token = call(
            grads_oh_kernel,
            "grads_oh",
            [shape((parts // 2, rows, wide))] * 2,
            ids, d_one_turned[0], Warm(d_one_got), mixed, Warm(mixed_got),
            hidden_turned[0], Warm(swap(hidden_turned[1], "lon", 1)), ct_turned, Warm(ct_got),
            after=[token],
            scratch=[pltpu.VMEM((parts, rows, wide), BF)],
            flops=2 * tokens * width * wide,
        )
        oh_got = swap(oh_send, "dp", 1)
        got_a, got_b = swap(send_a, "dp", 1), swap(send_b, "lon", 2)

    out = call(
        functools.partial(last_kernel, columns),
        "last",
        [
            *[shape((item_tokens, width // 2))] * 2,
            shape((items, variables * columns, height), F32),
            shape((items, variables, height)),
            *([shape((parts, rows, 2 * LANES))] * 2 if paired else [shape((width, 2 * LANES))]),
        ],
        ids, Warm(hidden_zero), Warm(d_one), Warm(d_norm), Warm(d_norm_got), gains, gain_two, patches, w_embed,
        after=[token],
        scratch=[
            pltpu.VMEM((2 * LANES, width), F32),
            pltpu.VMEM((2, item_tokens, width // 2), BF),
            pltpu.VMEM((parts, 2, rows, 2 * LANES) if paired else (8, LANES), BF),
        ],
        flops=4 * tokens * width * features,
    )
    pos_send, pos, d_fields, d_edge = out[:4]
    embed, token = out[4:-1], out[-1]
    if not paired:
        east, pos_got = from_behind(d_edge, "lon", -1), swap(pos_send, "dp", 1)
    more, more_outs, more_scratch, rest, rest_outs = [], [], [], [], []
    if paired:
        embed_width = embed[0].shape[2]
        step_a, side = shape((2, rows, cut)), shape((2, rows, wide))
        step_b = shape((2, rows, 3 * local_width - cut + 2 * embed_width + 2 * inner_columns))
        send_a, keep_a, send_b, keep_b, oh_send, oh_keep, token = call(
            fold_q_kernel,
            "fold_q",
            [step_a, step_a, step_b, step_b, side, side],
            ids, keep_a, Warm(got_a), keep_b, Warm(got_b), up_keep, Warm(up_got), oh_keep, Warm(oh_got),
            embed[0], Warm(swap(embed[1], "lon", 1)),
            after=[token],
            scratch=[
                pltpu.VMEM(keep_a.shape, BF),
                pltpu.VMEM(keep_b.shape, BF),
                pltpu.VMEM(oh_keep.shape, BF),
                pltpu.VMEM(embed[0].shape, BF),
            ],
        )
        got_a, got_b, oh_got = swap(send_a, "lon", 2), swap(send_b, "dp", 1), swap(oh_send, "lon", 4)
        east = from_behind(pin(d_edge, [token]), "lon", -1)
        final, block = shape((rows, 3 * local_width + embed_width)), shape((rows, embed_width))
        send, keep, pair, near_send, embed_both, oh_keep, token = call(
            merge_q_kernel,
            "merge_q",
            [
                final,
                final,
                shape((2, rows, 4 * inner_columns)),
                shape((rows, embed_width + wide)),
                block,
                shape((rows, wide)),
            ],
            ids, keep_a, Warm(got_a), keep_b, Warm(got_b), oh_keep, Warm(oh_got),
            after=[token, east],
            scratch=[
                pltpu.VMEM((2, rows, 3 * local_width), BF),
                pltpu.VMEM((4, *block.shape), BF),
                pltpu.VMEM((2, rows, wide), BF),
            ],
        )
        pos_got = swap(pin(pos_send, [token]), "dp", 1)
        more = [up_keep, Warm(up_got), mine[0], pair, Warm(swap(pair, "lon", 1))]
        more_outs = [shape((rows, hidden_units), F32)] * 2
        more_scratch = [pltpu.VMEM((features, hidden_units // 4), BF)]
        rest = [
            Warm(swap(near_send, "lon", 2)), Warm(swap(embed_both, "lon", 6)), oh_keep,
            keep, Warm(swap(send, "lon", 4)),
        ]
        rest_outs = [
            shape((rows, local_width), F32),
            shape((rows, features), F32),
            shape((3, rows, local_width), F32),
        ]
    else:
        rest = [lax.all_to_all(embed[0].reshape(everyone, rows, 2 * LANES), ("dp", "lon"), 0, 0)]
    *closed, token = call(
        functools.partial(close_kernel, columns),
        "close",
        [shape(d_fields.shape, F32), shape(pos.shape, F32), *more_outs],
        ids, d_fields, east, pos, Warm(pos_got), *more,
        after=[token],
        scratch=more_scratch,
    )
    *ended, token = call(
        end_kernel,
        "end",
        [shape((rows, features), F32), shape((2, rows), F32), *rest_outs],
        *rest,
        after=[token],
    )
    if paired:
        grad_up, grad_down, (grad_out, grad_head, grad_qkv) = closed[2], closed[3], ended[2:]
    else:
        flat = activated.transpose(1, 0, 2).reshape(tokens, hidden_units)
        grad_up = scatter(nn(normed_two[0], d_pre))
        grad_down = scatter(nn(d_two.T.astype(BF), flat))
        grad_out = scatter(nn(d_one_turned[0], mixed))
        grad_head = scatter(nt(hidden_turned[0], ct_turned))
        grad_qkv = scatter(nn(normed_one[0], d_qkv)).reshape(rows, 3, local_width).transpose(1, 0, 2)
    return (
        pred,
        *[x.reshape(variables) for x in stats],
        closed[0].reshape(items, variables, columns, height).transpose(0, 1, 3, 2),
        ended[0].T,
        closed[1],
        ended[1],
        grad_qkv,
        grad_out.T,
        grad_up,
        grad_down.T,
        grad_head,
    )


def solution(mesh):
    in_specs = (
        P(None, None, None, "lon"),
        P("dp"),
        P(),
        P(),
        P(),
        P(),
        P("lon", None),
        P(),
        P(None, None, "mp"),
        P("mp", None),
        P(None, "mp"),
        P("mp", None),
        P(),
        P("dp", "lon", None),
    )
    out_specs = (
        P("dp", "lon", None),
        P(),
        P(),
        P(),
        P("dp", None, None, "lon"),
        P(None, ("dp", "lon")),
        P("lon", "dp"),
        P(None, ("dp", "lon")),
        P(None, ("dp", "lon"), "mp"),
        P("mp", ("dp", "lon")),
        P(("dp", "lon"), "mp"),
        P("mp", ("dp", "lon")),
        P(("dp", "lon"), None),
    )
    return jax.shard_map(local, mesh=mesh, in_specs=in_specs, out_specs=out_specs, check_vma=False)
```

```python
import functools
import math

import jax
import jax.numpy as jnp
from jax import lax
from jax.experimental import pallas as pl
from jax.experimental.pallas import tpu as pltpu
from jax.sharding import PartitionSpec as P

HDIM = 64
PATCH = 2
LANES = 128
NORM_EPS = 1e-06
STAT_EPS = 1e-06
BF = jnp.bfloat16
F32 = jnp.float32
MIB = 2**20


def swap(block, axis, distance):
    route = [(i, i ^ distance) for i in range(lax.axis_size(axis))]
    return lax.ppermute(block, axis, route)


def from_behind(block, axis, distance):
    size = lax.axis_size(axis)
    route = [((i - distance) % size, i) for i in range(size)]
    return lax.ppermute(block, axis, route)


def pick(x, index, axis):
    return lax.dynamic_index_in_dim(x, index, axis, keepdims=False)


def halve(total, dims):
    for axis, bit in dims:
        side = (lax.axis_index(axis) // bit) % 2
        got = swap(pick(total, 1 - side, 0), axis, bit)
        total = (pick(total, side, 0).astype(F32) + got.astype(F32)).astype(BF)
    return total


def scatter(total):
    dp, lon = lax.axis_size("dp"), lax.axis_size("lon")
    dims = []
    for axis, size in (("dp", dp), ("lon", lon)):
        bit = size // 2
        while bit:
            dims.append((axis, bit))
            bit //= 2
    rows, columns = total.shape
    total = total.astype(BF).reshape((2,) * len(dims) + (rows // (dp * lon), columns))
    order = sorted(range(len(dims)), key=lambda i: (dims[i][1] > 1 or dims[i][0] == "dp", i))
    total = total.transpose([*order, len(dims), len(dims) + 1])
    return halve(total, [dims[i] for i in order]).astype(F32)


def nt(a, b):
    return lax.dot_general(a, b, (((1,), (1,)), ((), ())), preferred_element_type=F32)


def nn(a, b):
    return lax.dot_general(a, b, (((1,), (0,)), ((), ())), preferred_element_type=F32)


def item_mask(rows, lanes, item):
    lane = lax.broadcasted_iota(jnp.int32, (rows, lanes), 1)
    return (lane >= item * HDIM) & (lane < (item + 1) * HDIM)


def interleave(first, second):
    low = item_mask(first.shape[0], LANES, 0)
    return (
        jnp.where(low, first, pltpu.roll(second, HDIM, 1)),
        jnp.where(low, pltpu.roll(first, HDIM, 1), second),
    )


def norm_parts(hidden):
    centred = hidden - jnp.mean(hidden, axis=-1, keepdims=True)
    variance = jnp.mean(centred * centred, axis=-1, keepdims=True)
    inverse = lax.rsqrt(variance + NORM_EPS)
    return centred * inverse, inverse


def norm_back(unit, inverse, scaling, grad):
    scaled = grad * scaling
    back = inverse * (
        scaled
        - jnp.mean(scaled, axis=-1, keepdims=True)
        - unit * jnp.mean(scaled * unit, axis=-1, keepdims=True)
    )
    return back, jnp.sum(grad * unit, axis=0, keepdims=True)


def emit_turned(x, ids_ref, outs, hold):
    turned = x.T.astype(BF)
    if len(outs) == 1:
        outs[0][...] = turned
        return
    keep, send = outs
    parts, rows, tokens = keep.shape
    hold[...] = turned.reshape(parts, 2, rows, tokens)
    core = ids_ref[0]
    keep[...] = hold[:, pl.ds(core, 1)].reshape(parts, rows, tokens)
    send[...] = hold[:, pl.ds(1 - core, 1)].reshape(parts, rows, tokens)


class Warm:
    def __init__(self, value):
        self.value = value


def call(body, name, outs, *args, after=(), grid=(), in_specs=None, out_specs=None, scratch=(), limit=24, flops=0):
    vmem = pl.BlockSpec(memory_space=pltpu.VMEM)
    smem = pl.BlockSpec(memory_space=pltpu.SMEM)
    shapes = [o.value if isinstance(o, Warm) else o for o in outs]
    plain = [a.value if isinstance(a, Warm) else a for a in args]
    if in_specs is None:
        in_specs = [smem if a.dtype == jnp.int32 else vmem for a in plain]
    if out_specs is None:
        out_specs = [vmem] * len(outs)
    token = pl.BlockSpec((8, LANES), lambda *at: (0, 0)) if grid else vmem
    nbytes = sum(math.prod(a.shape) * a.dtype.itemsize for a in [*plain, *shapes])
    here, skip, there = len(args), len(after), len(outs)

    def with_token(*refs):
        refs = list(refs)
        refs[here + skip + there][...] = jnp.zeros((8, LANES), F32)
        body(*refs[:here], *refs[here + skip : here + skip + there], *refs[here + skip + there + 1 :])

    def cold(x):
        if isinstance(x, Warm):
            return x.value
        return x if x.dtype == jnp.int32 else pltpu.with_memory_space_constraint(x, pltpu.HBM)

    return pl.pallas_call(
        with_token,
        grid=grid,
        out_shape=[
            *[o.value if isinstance(o, Warm) else pltpu.HBM(o.shape, o.dtype) for o in outs],
            pltpu.HBM((8, LANES), F32),
        ],
        in_specs=[*in_specs, *[pl.BlockSpec(memory_space=pl.ANY)] * skip],
        out_specs=[*out_specs, token],
        scratch_shapes=list(scratch),
        compiler_params=pltpu.CompilerParams(vmem_limit_bytes=limit * MIB),
        cost_estimate=pl.CostEstimate(flops=int(flops), bytes_accessed=nbytes, transcendentals=0),
        name=name,
    )(*[cold(a) for a in args], *[cold(a) for a in after])


def shape(dims, kind=BF):
    return jax.ShapeDtypeStruct(dims, kind)


def warm(dims, kind=BF):
    return Warm(shape(dims, kind))


def feature_order(variables, back):
    features = PATCH * PATCH * variables
    natural = lax.broadcasted_iota(jnp.int32, (features, features), 1 if back else 0)
    sorted_ = lax.broadcasted_iota(jnp.int32, (features, features), 0 if back else 1)
    hit = (natural // 4 == sorted_ % variables) & (natural % 4 == sorted_ // variables)
    return jnp.where(hit, 1.0, 0.0).astype(BF)


def send_pairs(ids_ref, hold, messages):
    if len(messages) == 1:
        messages[0][...] = hold[...]
        return
    for k, message in enumerate(messages):
        message[...] = hold[pl.ds(2 * ids_ref[4 + k], 2)]


def moments_kernel(index_ref, data_ref, fields_ref, edge_ref, moments_ref, turn_ref, sems):
    items, variables, height = edge_ref.shape
    cols = fields_ref.shape[1] // variables
    copies = [
        pltpu.make_async_copy(data_ref.at[index_ref[i]], fields_ref.at[i], sems.at[i])
        for i in range(items)
    ]
    for copy in copies:
        copy.start()
    turn_ref[...] = jnp.zeros_like(turn_ref)
    for copy in copies:
        copy.wait()
    blocks = [
        fields_ref[i, pl.ds(c, variables, stride=cols), :] for i in range(items) for c in range(cols)
    ]
    for i in range(items):
        edge_ref[i] = blocks[i * cols + cols - 1].astype(BF)
    count = float(items * cols * height)
    mean = jnp.sum(sum(blocks), axis=1, keepdims=True) * (1.0 / count)
    spread = jnp.sum(sum(jnp.square(b - mean) for b in blocks), axis=1, keepdims=True)
    turn_ref[0:variables, 0:1] = mean
    turn_ref[HDIM : HDIM + variables, 0:1] = spread
    turn_ref[0:variables, 1:2] = spread
    turned = turn_ref[...].T
    if len(moments_ref.shape) == 2:
        moments_ref[...] = turned[0 : moments_ref.shape[0], :]
    else:
        moments_ref[...] = jnp.broadcast_to(turned[0:1, :][None], moments_ref.shape)


def start_kernel(local_count, members, ids_ref, mom_ref, count_ref, mean_ref, var_ref, fields_ref, edge_ref, we_ref,
                 pos_ref, gains_ref, wq_ref, new_count_ref, new_mean_ref, new_var_ref, hidden_ref, patches_ref,
                 *rest):
    (*outs, column_ref, run_ref, hold, weights, sem, qkv_ref) = rest
    if len(outs) > 2:
        messages, turned = outs[:-2], outs[-2:]
    else:
        messages, turned = outs[:1], outs[1:]
    copy = pltpu.make_async_copy(wq_ref, weights, sem)
    copy.start()
    items, rows, height = fields_ref.shape
    variables = edge_ref.shape[1]
    cols = rows // variables
    half = height // PATCH
    run_ref[...] = jnp.zeros_like(run_ref)
    for k, ref in enumerate((count_ref, mean_ref, var_ref)):
        run_ref[k : k + 1, 0:variables] = ref[...]
    batch_count = local_count * members
    if len(mom_ref.shape) == 2:
        batch_mean, spread = mom_ref[0:1, :], mom_ref[1:2, :]
    else:
        moments = mom_ref[:, 0, :]
        batch_mean = jnp.sum(moments, axis=0, keepdims=True) * (1.0 / members)
        off = moments - batch_mean
        spread = jnp.sum(pltpu.roll(moments, HDIM, 1) + local_count * off * off, axis=0, keepdims=True)
    run_count, run_mean, run_var = (run_ref[k : k + 1, :] for k in range(3))
    new_count = run_count + batch_count
    shift = batch_mean - run_mean
    new_mean = run_mean + shift * (batch_count / new_count)
    new_var = (
        run_var * run_count + spread + shift * shift * (run_count * batch_count / new_count)
    ) / new_count
    new_count_ref[...] = new_count[:, 0:variables]
    new_mean_ref[...] = new_mean[:, 0:variables]
    new_var_ref[...] = new_var[:, 0:variables]
    column_ref[...] = jnp.zeros_like(column_ref)
    column_ref[0:1, :] = new_mean
    column_ref[1:2, :] = lax.rsqrt(new_var + STAT_EPS)
    column = column_ref[...].T
    centre, inverse = column[0:variables, 0:1], column[0:variables, 1:2]

    def scaled(block):
        return ((block - centre) * inverse).astype(BF)

    row = lax.broadcasted_iota(jnp.int32, (2 * height, LANES), 0)
    lane = lax.broadcasted_iota(jnp.int32, (2 * height, LANES), 1)
    sort = [
        jnp.where(
            (row // height == lane // half) & (row % height == PATCH * (lane % half) + a), 1.0, 0.0
        ).astype(BF)
        for a in range(PATCH)
    ]
    natural = feature_order(variables, False)
    hidden = []
    for item in range(items):
        west = scaled(edge_ref[item].astype(F32))
        own = [
            scaled(fields_ref[item, pl.ds(c, variables, stride=cols), :]) for c in range(cols - 1)
        ]
        first = jnp.concatenate([west, own[0]], axis=0)
        second = jnp.concatenate([own[1], own[2]], axis=0)
        both = jnp.concatenate([first, second], axis=1)
        patches = jnp.concatenate([nn(both, sort[a]) for a in range(PATCH)], axis=0)
        patches = nn(natural, patches.astype(BF))
        patches_ref[:, item * LANES : (item + 1) * LANES] = patches.astype(BF)
        hidden.append(nn(patches.T.astype(BF), we_ref[...]) + pos_ref[...].astype(F32))
    hidden = jnp.concatenate(hidden, axis=0)
    hidden_ref[...] = hidden
    unit, _ = norm_parts(hidden)
    normed = unit * gains_ref[0:1, :]
    low = normed.astype(BF)
    emit_turned(normed, ids_ref, turned, hold)
    copy.wait()
    for c in range(3):
        product = nn(low, weights[c])
        for t in range(product.shape[1] // LANES):
            tile = product[:, t * LANES : (t + 1) * LANES]
            a, b = interleave(tile[:LANES], tile[LANES:])
            qkv_ref[2 * t, c] = a.astype(BF)
            qkv_ref[2 * t + 1, c] = b.astype(BF)
    send_pairs(ids_ref, qkv_ref, messages)


def cotangent_kernel(ids_ref, ct_ref, wh_ref, wd_ref, *refs):
    if len(refs) > 3:
        two_ref, act_ref, ct_turned_ref, mine_ref, hold = refs
        hold[...] = wh_ref[...].astype(F32).T.astype(BF).reshape(hold.shape)
        mine_ref[...] = hold[ids_ref[8]]
    else:
        two_ref, act_ref, ct_turned_ref = refs
    grads = []
    for item in range(ct_ref.shape[0]):
        ct = ct_ref[item].T.astype(BF)
        ct_turned_ref[:, item * LANES : (item + 1) * LANES] = ct_ref[item].astype(BF)
        grads.append(nn(ct, wh_ref[...]))
    d_two = jnp.concatenate(grads, axis=0)
    two_ref[...] = d_two
    act_ref[...] = nt(d_two.astype(BF), wd_ref[...]).astype(BF)


def attend_kernel(items, scale, q_ref, kv_ref, o_ref, ot_ref, pt_ref, vt_ref):
    keys = kv_ref.shape[0] * kv_ref.shape[2]

    @pl.when(pl.program_id(0) == 0)
    def _():
        vt_ref[...] = kv_ref[:, 2].reshape(keys, LANES).astype(F32).T.astype(BF)

    rows = q_ref.shape[0] * q_ref.shape[2]
    queries = q_ref[:, 0].reshape(rows, LANES) * BF(scale)
    key_rows = kv_ref[:, 1].reshape(keys, LANES)
    for item in range(items):
        chosen = jnp.where(item_mask(rows, LANES, item), queries, BF(0))
        scores = nt(key_rows, chosen)
        top = jnp.max(scores, axis=0, keepdims=True)
        raised = jnp.exp(scores - top)
        total = jnp.sum(raised, axis=0, keepdims=True)
        weights = (raised * (1.0 / total)).astype(BF)
        pt_ref[item] = weights
        span = slice(item * HDIM, (item + 1) * HDIM)
        ot_ref[span, :] = nn(vt_ref[span, :], weights)
    o_ref[...] = ot_ref[...].T.astype(BF).reshape(o_ref.shape)


def attend(q, kv, items, scale, after):
    peers, _, tokens, lanes = q.shape
    rows, keys = peers * tokens, kv.shape[0] * tokens
    step = max(1, min(peers, 256 * 1024 // keys // tokens))
    block = step * tokens
    return call(
        functools.partial(attend_kernel, items, scale),
        "attend",
        [
            shape((peers, tokens, lanes)),
            shape((lanes, rows), F32),
            shape((items, keys, rows)),
        ],
        Warm(q),
        Warm(kv),
        after=after,
        grid=(peers // step,),
        in_specs=[
            pl.BlockSpec((step, 3, tokens, lanes), lambda j: (j, 0, 0, 0)),
            pl.BlockSpec(kv.shape, lambda j: (0, 0, 0, 0)),
        ],
        out_specs=[
            pl.BlockSpec((step, tokens, lanes), lambda j: (j, 0, 0)),
            pl.BlockSpec((lanes, block), lambda j: (0, j)),
            pl.BlockSpec((items, keys, block), lambda j: (0, 0, j)),
        ],
        scratch=[pltpu.VMEM((lanes, keys), BF)],
        limit=24 if keys <= 2048 else 56,
        flops=8 * rows * keys * lanes,
    )


def pair_attend_kernel(items, scale, *refs):
    sources, (*outs, ot_ref, pt_ref, query_ref, key_ref, value_ref, vt_ref) = refs[:8], refs[8:]
    tokens = sources[0].shape[2]
    for k, source in enumerate(sources):
        span = slice(k * tokens, (k + 1) * tokens)
        if k < len(outs):
            query_ref[0, span, :] = source[0, 0] * BF(scale)
        key_ref[0, span, :] = source[0, 1]
        value_ref[0, span, :] = source[0, 2]
        vt_ref[:, span] = source[0, 2].astype(F32).T.astype(BF)
    queries = query_ref[0]
    for item in range(items):
        chosen = jnp.where(item_mask(queries.shape[0], LANES, item), queries, BF(0))
        scores = nt(key_ref[0], chosen)
        top = jnp.max(scores, axis=0, keepdims=True)
        raised = jnp.exp(scores - top)
        total = jnp.sum(raised, axis=0, keepdims=True)
        weights = (raised * (1.0 / total)).astype(BF)
        pt_ref[0, item] = weights
        span = slice(item * HDIM, (item + 1) * HDIM)
        ot_ref[0, span, :] = nn(vt_ref[span, :], weights)
    attended = ot_ref[0].T.astype(BF)
    for k, out in enumerate(outs):
        out[0] = attended[k * tokens : (k + 1) * tokens]


def pair_attend(own, other, items, scale, after):
    _, _, tokens, lanes = own[0].shape
    rows, keys = len(own) * tokens, 2 * len(own) * tokens
    wide = lambda *dims: pl.BlockSpec((1, *dims), lambda h: (h, *[0] * len(dims)))
    *outs, ot, pt, q, k, v, token = call(
        functools.partial(pair_attend_kernel, items, scale),
        "attend",
        [
            shape((2, tokens, lanes)),
            *[warm((2, tokens, lanes))] * (len(own) - 1),
            shape((2, lanes, rows), F32),
            shape((2, items, keys, rows)),
            shape((2, rows, lanes)),
            shape((2, keys, lanes)),
            shape((2, keys, lanes)),
        ],
        *[Warm(x) for x in [*own, *other]],
        after=after,
        grid=(2,),
        in_specs=[wide(3, tokens, lanes)] * (2 * len(own)),
        out_specs=[
            *[wide(tokens, lanes)] * len(own),
            wide(lanes, rows),
            wide(items, keys, rows),
            wide(rows, lanes),
            wide(keys, lanes),
            wide(keys, lanes),
        ],
        scratch=[pltpu.VMEM((lanes, keys), BF)],
        limit=32,
        flops=16 * rows * keys * lanes,
    )
    return outs, (q, k, v, ot, pt), token


def pair_attend_back_kernel(items, scale, ids_ref, query_ref, key_ref, value_ref, ot_ref, pt_ref, grads_ref, *refs):
    *outs, cross_ref, kt_ref, grad_rows, dqt_ref, dk_sum, dv_sum = refs
    tokens = grads_ref.shape[2]
    for k in range(len(outs)):
        grad_rows[k * tokens : (k + 1) * tokens, :] = grads_ref[ids_ref[4 + k], 0]
    kt_ref[...] = (key_ref[0].astype(F32) * scale).T.astype(BF)
    queries, grads = query_ref[0], grad_rows[...]
    product = grads.astype(F32).T * ot_ref[0]
    for item in range(items):
        span = slice(item * HDIM, (item + 1) * HDIM)
        mask = item_mask(queries.shape[0], LANES, item)
        grad = jnp.where(mask, grads, BF(0))
        query = jnp.where(mask, queries, BF(0))
        delta = jnp.sum(product[span, :], axis=0, keepdims=True)
        weights = pt_ref[0, item]
        back = (weights.astype(F32) * (nt(value_ref[0], grad) - delta)).astype(BF)
        d_value, d_key = nn(weights, grad), nn(back, query)
        if item == 0:
            dv_sum[...] = d_value
            dk_sum[...] = d_key
        else:
            dv_sum[...] += d_value
            dk_sum[...] += d_key
        dqt_ref[span, :] = nn(kt_ref[span, :], back)
    d_query = dqt_ref[...].T.astype(BF)
    for k in range(2 * len(outs)):
        span = slice(k * tokens, (k + 1) * tokens)
        if k < len(outs):
            outs[k][0, 0] = d_query[span]
        for c, total in ((0, dk_sum), (1, dv_sum)):
            if k < len(outs):
                outs[k][0, 1 + c] = total[span, :].astype(BF)
            else:
                cross_ref[k - len(outs), 0, c] = total[span, :].astype(BF)


def pair_attend_back(ids, kept, d, items, scale, after):
    count, _, tokens, lanes = d.shape
    rows, keys = count * tokens, 2 * count * tokens
    wide = lambda *dims: pl.BlockSpec((1, *dims), lambda h: (h, *[0] * len(dims)))
    *outs, cross, token = call(
        functools.partial(pair_attend_back_kernel, items, scale),
        "attend_back",
        [*[shape((2, 3, tokens, lanes))] * count, shape((count, 2, 2, tokens, lanes))],
        ids, *kept, d,
        after=after,
        grid=(2,),
        in_specs=[
            pl.BlockSpec(memory_space=pltpu.SMEM),
            wide(rows, lanes),
            wide(keys, lanes),
            wide(keys, lanes),
            wide(lanes, rows),
            wide(items, keys, rows),
            pl.BlockSpec((count, 1, tokens, lanes), lambda h: (0, h, 0, 0)),
        ],
        out_specs=[
            *[wide(3, tokens, lanes)] * count,
            pl.BlockSpec((count, 1, 2, tokens, lanes), lambda h: (0, h, 0, 0, 0)),
        ],
        scratch=[
            pltpu.VMEM((lanes, keys), BF),
            pltpu.VMEM((rows, lanes), BF),
            pltpu.VMEM((lanes, rows), F32),
            pltpu.VMEM((keys, lanes), F32),
            pltpu.VMEM((keys, lanes), F32),
        ],
        limit=32,
        flops=32 * rows * keys * lanes,
    )
    return outs, cross, token


def combine_kernel(*refs):
    count = (len(refs) - 1) // 2
    own, cross_ref, outs = refs[:count], refs[count], refs[count + 1 :]
    for k in range(count):
        outs[k][:, 0] = own[k][:, 0]
        for c in range(2):
            outs[k][:, 1 + c] = plus(own[k].at[:, 1 + c], cross_ref.at[k, :, c])


def attend_back_kernel(items, scale, q_ref, kv_ref, d_ref, ot_ref, pt_ref, dq_ref, *rest):
    dkv_ref, (kt_ref, dqt_ref, dk_sum, dv_sum) = rest[:-4], rest[-4:]
    step = pl.program_id(0)
    keys = kv_ref.shape[0] * kv_ref.shape[2]

    @pl.when(step == 0)
    def _():
        kt_ref[...] = (kv_ref[:, 1].reshape(keys, LANES).astype(F32) * scale).T.astype(BF)
        dk_sum[...] = jnp.zeros_like(dk_sum)
        dv_sum[...] = jnp.zeros_like(dv_sum)

    peers, _, tokens, _ = q_ref.shape
    rows = peers * tokens
    queries = q_ref[:, 0].reshape(rows, LANES) * BF(scale)
    grads = d_ref[...].reshape(rows, LANES)
    value_rows = kv_ref[:, 2].reshape(keys, LANES)
    product = grads.astype(F32).T * ot_ref[...]
    for item in range(items):
        span = slice(item * HDIM, (item + 1) * HDIM)
        mask = item_mask(rows, LANES, item)
        grad = jnp.where(mask, grads, BF(0))
        query = jnp.where(mask, queries, BF(0))
        delta = jnp.sum(product[span, :], axis=0, keepdims=True)
        weights = pt_ref[item]
        back = (weights.astype(F32) * (nt(value_rows, grad) - delta)).astype(BF)
        dv_sum[...] += nn(weights, grad)
        dk_sum[...] += nn(back, query)
        dqt_ref[span, :] = nn(kt_ref[span, :], back)
    d_query = dqt_ref[...].T.astype(BF).reshape(peers, tokens, LANES)
    if dkv_ref:
        dq_ref[...] = d_query
    else:
        dq_ref[pl.ds(step * peers, peers), 0] = d_query

    @pl.when(step == pl.num_programs(0) - 1)
    def _():
        for c, total in ((1, dk_sum), (2, dv_sum)):
            total = total[...].reshape(kv_ref.shape[0], tokens, LANES)
            if dkv_ref:
                dkv_ref[0][:, c - 1] = total
            else:
                dq_ref[:, c] = total.astype(BF)


def attend_back(q, kv, d, ot, pt, items, scale, after):
    peers, _, tokens, lanes = q.shape
    rows, keys = peers * tokens, kv.shape[0] * tokens
    step = max(1, min(peers, 256 * 1024 // keys // tokens))
    block = step * tokens
    if q.shape == kv.shape:
        outs = [shape(q.shape)]
        out_specs = [pl.BlockSpec(q.shape, lambda j: (0, 0, 0, 0))]
    else:
        outs = [shape((peers, tokens, lanes)), shape((kv.shape[0], 2, tokens, lanes), F32)]
        out_specs = [
            pl.BlockSpec((step, tokens, lanes), lambda j: (j, 0, 0)),
            pl.BlockSpec(outs[1].shape, lambda j: (0, 0, 0, 0)),
        ]
    *back, token = call(
        functools.partial(attend_back_kernel, items, scale),
        "attend_back",
        outs,
        Warm(q),
        Warm(kv),
        d,
        ot,
        pt,
        after=after,
        grid=(peers // step,),
        in_specs=[
            pl.BlockSpec((step, 3, tokens, lanes), lambda j: (j, 0, 0, 0)),
            pl.BlockSpec(kv.shape, lambda j: (0, 0, 0, 0)),
            pl.BlockSpec((step, tokens, lanes), lambda j: (j, 0, 0)),
            pl.BlockSpec((lanes, block), lambda j: (0, j)),
            pl.BlockSpec((items, keys, block), lambda j: (0, 0, j)),
        ],
        out_specs=out_specs,
        scratch=[
            pltpu.VMEM((lanes, keys), BF),
            pltpu.VMEM((lanes, block), F32),
            pltpu.VMEM((keys, lanes), F32),
            pltpu.VMEM((keys, lanes), F32),
        ],
        limit=24 if keys <= 2048 else 60,
        flops=16 * rows * keys * lanes,
    )
    return back, token


def unpack(ids_ref, sources, index, out_ref, base):
    several = len(sources) > 1
    count = len(sources) if several else sources[0].shape[0] // 2
    for t in range(count):
        source, head = (sources[t], 0) if several else (sources[0], 2 * t)
        pair = [
            (source[head + s] if index is None else source[head + s, index]).astype(F32) for s in range(2)
        ]
        at = base + (pl.multiple_of(ids_ref[4 + t] * LANES, LANES) if several else t * LANES)
        for item, tile in enumerate(interleave(*pair)):
            out_ref[item * LANES : (item + 1) * LANES, pl.ds(at, LANES)] = tile.astype(BF)


def pack(product, out_ref):
    for t in range(product.shape[1] // LANES):
        tile = product[:, t * LANES : (t + 1) * LANES]
        for s, block in enumerate(interleave(tile[:LANES], tile[LANES:])):
            out_ref[2 * t + s] = block.astype(BF)


def project_kernel(ids_ref, *refs):
    *sources, wo_ref, mixed_ref, branch_ref = refs
    unpack(ids_ref, sources, None, mixed_ref, 0)
    branch_ref[...] = nn(mixed_ref[...], wo_ref[...]).astype(BF)


def forward_kernel(sources, ids_ref, *refs):
    if sources:
        own, got, refs = refs[:sources], refs[sources : 2 * sources], refs[2 * sources :]
        wo_ref, wo_got_ref, zero_ref, gains_ref, wu_ref, dact_ref, norm_ref, mixed_out, *refs = refs
        *refs, wo_buf, mixed, wo_sems = refs
        me = ids_ref[9]
        wo_loads = [
            pltpu.make_async_copy(wo_ref, wo_buf.at[me], wo_sems.at[0]),
            pltpu.make_async_copy(wo_got_ref, wo_buf.at[1 - me], wo_sems.at[1]),
        ]
        for copy in wo_loads:
            copy.start()
    else:
        own_ref, got_ref, zero_ref, gains_ref, wu_ref, dact_ref, norm_ref, *refs = refs
    one_out, pre_out, act_out, other_out, *rest = refs
    count = (len(rest) - 9) // 2
    turned_out, turned = rest[:count], rest[count : 2 * count]
    one_ref, weights, grads, pre_ref, act_ref, normed_ref, hold, into, out_of = rest[2 * count :]
    chunks, _, block = grads.shape
    per_half = chunks // 2
    loads, stores = [], []
    for c in range(chunks):
        span = slice(c * block, (c + 1) * block)
        loads.append(
            (
                pltpu.make_async_copy(wu_ref.at[:, span], weights.at[c], into.at[2 * c]),
                pltpu.make_async_copy(dact_ref.at[:, span], grads.at[c], into.at[2 * c + 1]),
            )
        )
        for copy in loads[-1]:
            copy.start()

    def store(source, target):
        stores.append(pltpu.make_async_copy(source, target, out_of.at[len(stores)]))
        stores[-1].start()

    if sources:
        unpack(ids_ref, own, None, mixed.at[me], 0)
        unpack(ids_ref, got, None, mixed.at[1 - me], 0)
        mixed_out[...] = mixed[me]
        for copy in wo_loads:
            copy.wait()
        branch = nn(mixed[0], wo_buf[0]) + nn(mixed[1], wo_buf[1])
    else:
        branch = own_ref[...].astype(F32) + got_ref[...].astype(F32)
    hidden = zero_ref[...] + branch
    one_ref[...] = hidden
    store(one_ref, one_out)
    unit, _ = norm_parts(hidden)
    normed = unit * gains_ref[1:2, :]
    normed_ref[...] = normed.astype(BF)
    emit_turned(normed, ids_ref, turned, hold)
    for source, target in zip(turned, turned_out):
        store(source, target)
    total = None
    for c in range(chunks):
        span = slice(c * block, (c + 1) * block)
        half, place = c // per_half, slice(c % per_half * block, (c % per_half + 1) * block)
        for copy in loads[c]:
            copy.wait()
        pre = nn(normed_ref[...], weights[c])
        chance = 0.5 * (1.0 + lax.erf(pre * (1.0 / math.sqrt(2.0))))
        slope = chance + pre * jnp.exp(-0.5 * pre * pre) * (1.0 / math.sqrt(2.0 * math.pi))
        act_ref[half, :, place] = (pre * chance).astype(BF)
        store(act_ref.at[half, :, place], act_out.at[half, :, place])
        d_pre = (grads[c].astype(F32) * slope).astype(BF)
        pre_ref[:, span] = d_pre
        store(pre_ref.at[:, span], pre_out.at[:, span])
        part = nt(d_pre, weights[c])
        total = part if total is None else total + part
    store(act_ref.at[1 - ids_ref[0]], other_out)
    norm_ref[...] = total.astype(BF)
    for copy in stores:
        copy.wait()


def second_kernel(ids_ref, one_ref, two_ref, own_ref, got_ref, gains_ref, wo_ref, d_ref, gain_ref, *rest):
    heads_ref, *turned, hold = rest
    unit, inverse = norm_parts(one_ref[...])
    grad = own_ref[...].astype(F32) + got_ref[...].astype(F32)
    back, gain = norm_back(unit, inverse, gains_ref[1:2, :], grad)
    gain_ref[...] = gain
    d_one = two_ref[...] + back
    d_ref[...] = d_one
    pack(nt(d_one.astype(BF), wo_ref[...]), heads_ref)
    emit_turned(d_one, ids_ref, turned, hold)


def head_kernel(ids_ref, one_ref, own_ref, got_ref, wh_ref, pred_ref, *rest):
    turned, hold = rest[:-1], rest[-1]
    hidden = one_ref[...] + (own_ref[...].astype(F32) + got_ref[...].astype(F32))
    low = hidden.astype(BF)
    for item in range(pred_ref.shape[0]):
        pred_ref[item] = nt(wh_ref[...], low[item * LANES : (item + 1) * LANES])
    emit_turned(hidden, ids_ref, turned, hold)


def third_kernel(count, ids_ref, *refs):
    sources, (wq_ref, dqkv_ref, norm_ref) = refs[:count], refs[count:]
    width = wq_ref.shape[2]
    total = None
    for c in range(3):
        unpack(ids_ref, sources, c, dqkv_ref, c * width)
        part = nt(dqkv_ref[:, c * width : (c + 1) * width], wq_ref[c])
        total = part if total is None else total + part
    norm_ref[...] = total.astype(BF)


def last_kernel(cols, ids_ref, zero_ref, done_ref, own_ref, got_ref, gains_ref, gain_two_ref, patches_ref, we_ref,
                pos_send, pos_keep, fields_ref, edge_ref, *rest):
    embed, (rows_ref, pos_ref, hold) = rest[:-3], rest[-3:]
    unit, inverse = norm_parts(zero_ref[...])
    grad = own_ref[...].astype(F32) + got_ref[...].astype(F32)
    back, gain = norm_back(unit, inverse, gains_ref[0:1, :], grad)
    d_zero = done_ref[...] + back
    low = d_zero.astype(BF)
    items, variables, height = edge_ref.shape
    pos = d_zero[0:LANES]
    for item in range(1, items):
        pos = pos + d_zero[item * LANES : (item + 1) * LANES]
    width = pos_ref.shape[2]
    for k in range(2):
        pos_ref[k] = pos[:, k * width : (k + 1) * width].astype(BF)
    pos_send[...] = pos_ref[1 - ids_ref[1]]
    pos_keep[...] = pos_ref[ids_ref[1]]
    features = patches_ref.shape[0]
    rows_ref[...] = jnp.zeros_like(rows_ref)
    rows_ref[0:features, :] = nn(patches_ref[...], low)
    rows_ref[features : features + 1, :] = gain
    rows_ref[features + 1 : features + 2, :] = gain_two_ref[...]
    emit_turned(rows_ref[...], ids_ref, embed, hold)
    half = height // PATCH
    row = lax.broadcasted_iota(jnp.int32, (LANES, height), 0)
    lane = lax.broadcasted_iota(jnp.int32, (LANES, height), 1)
    fields_ref[...] = jnp.zeros_like(fields_ref)
    order = feature_order(variables, True)
    for item in range(items):
        d_patches = nt(we_ref[...], low[item * LANES : (item + 1) * LANES])
        high = d_patches.astype(BF)
        rest = (d_patches - high.astype(F32)).astype(BF)
        high, rest = nn(order, high).astype(BF), nn(order, rest).astype(BF)
        for j in range(2):
            total = None
            for a in range(PATCH):
                place = jnp.where(
                    (row // half == j) & (lane == PATCH * (row % half) + a), 1.0, 0.0
                ).astype(BF)
                span = slice(a * 2 * variables, (a + 1) * 2 * variables)
                part = nn(high[span], place) + nn(rest[span], place)
                total = part if total is None else total + part
            for b in range(PATCH):
                block = total[b * variables : (b + 1) * variables]
                column = 2 * j + b - 1
                if column < 0:
                    edge_ref[item] = block.astype(BF)
                else:
                    fields_ref[item, pl.ds(column, variables, stride=cols), :] = block


def down_kernel(act_ref, wd_ref, out_ref):
    width = act_ref.shape[2]
    total = nn(act_ref[0], wd_ref[0:width, :]) + nn(act_ref[1], wd_ref[width:, :])
    out_ref[...] = total.astype(BF)


def pin(xs, after):
    def body(*refs):
        pass

    anywhere = pl.BlockSpec(memory_space=pl.ANY)
    several = isinstance(xs, (list, tuple))
    xs = list(xs) if several else [xs]
    out = pl.pallas_call(
        body,
        out_shape=[pltpu.HBM(x.shape, x.dtype) for x in xs],
        in_specs=[anywhere] * (len(xs) + len(after)),
        out_specs=[anywhere] * len(xs),
        input_output_aliases={k: k for k in range(len(xs))},
        name="pin",
    )(*[pltpu.with_memory_space_constraint(x, pltpu.HBM) for x in xs], *after)
    return out if several else out[0]


def product_of(own, got, b_own, b_got):
    parts, rows, tokens = own.shape
    total = nn(own[...].reshape(parts * rows, tokens), b_own)
    return total + nn(got[...].reshape(parts * rows, tokens), b_got)


def split_dp(ids_ref, hold, send, keep, columns):
    half = hold.shape[0] // 2
    for out, at in ((send, 1 - ids_ref[1]), (keep, ids_ref[1])):
        for k in range(half):
            out[k, :, 0:columns] = hold[at * half + k]


def split_near(ids_ref, hold, send, keep, columns):
    for out, at in ((send, 1 - ids_ref[2]), (keep, ids_ref[2])):
        for k in range(hold.shape[0] // 2):
            out[k, :, 0:columns] = hold[2 * k + at]


def plus(a, b):
    return (a[...].astype(F32) + b[...].astype(F32)).astype(BF)


def grads_ff_kernel(ids_ref, at_own, at_got, pre_own, pre_got, ct_own, ct_got, act_own, act_got,
                    send_a, keep_a, send_b, keep_b, hold, inner):
    parts, rows, total = hold.shape
    columns = total - keep_b.shape[2]
    product = product_of(at_own, at_got, pre_own[...], pre_got[...])
    hold[...] = product.astype(BF).reshape(hold.shape)
    split_dp(ids_ref, hold.at[:, :, 0:columns], send_a, keep_a, columns)
    split_near(ids_ref, hold.at[:, :, columns:], send_b, keep_b, total - columns)
    product = (nn(ct_own[...], act_own[ids_ref[0]]) + nn(ct_got[...], act_got[...])).astype(BF)
    tiles, groups = inner.shape[1], inner.shape[3] // LANES
    for k in range(2):
        for q in range(tiles):
            for g in range(groups):
                inner[k, q, :, g * LANES : (g + 1) * LANES] = product[
                    g * rows : (g + 1) * rows, (k * tiles + q) * LANES : (k * tiles + q + 1) * LANES
                ]
    for q in range(tiles):
        send_a[q, :, columns:] = inner[1 - ids_ref[1], q]
        keep_a[q, :, columns:] = inner[ids_ref[1], q]


def fold_ff_kernel(ids_ref, keep_a, got_a, keep_b, got_b, send_a, left_a, send_b, left_b, hold, hold_b):
    columns = hold.shape[2]
    extra = keep_a.shape[2] - columns
    hold[...] = plus(keep_a.at[:, :, 0:columns], got_a.at[:, :, 0:columns])
    split_near(ids_ref, hold, send_a, left_a, columns)
    for q in range(keep_a.shape[0]):
        total = plus(keep_a.at[q, :, columns:], got_a.at[q, :, columns:])
        at = columns + q % 2 * extra
        for out in (send_a, left_a):
            out[q // 2, :, at : at + extra] = total
    hold_b[...] = plus(keep_b, got_b)
    split_dp(ids_ref, hold_b, send_b, left_b, hold_b.shape[2])


def merge_ff_kernel(ids_ref, keep_a, got_a, keep_b, got_b, send, left, hold):
    columns = hold.shape[2] - keep_b.shape[2]
    extra = keep_a.shape[2] - columns
    hold[:, :, 0:columns] = plus(keep_a.at[:, :, 0:columns], got_a.at[:, :, 0:columns])
    hold[:, :, columns:] = plus(keep_b, got_b)
    far = ids_ref[3]
    width = hold.shape[2]
    send[:, 0:width] = hold[1 - far]
    left[:, 0:width] = hold[far]
    for k in range(2):
        total = plus(keep_a.at[k, :, columns:], got_a.at[k, :, columns:])
        at = width + k * extra
        for out in (send, left):
            out[:, at : at + extra] = total


def grads_oh_kernel(ids_ref, one_own, one_got, mixed_own, mixed_got, two_own, two_got, ct_own, ct_got,
                    send, keep, hold):
    width, features = mixed_own.shape[1], ct_own.shape[0]
    shape3 = hold.shape[:2]
    product = product_of(one_own, one_got, mixed_own[...], mixed_got[...])
    hold[:, :, 0:width] = product.astype(BF).reshape(*shape3, width)
    hold[:, :, width:] = jnp.zeros((*shape3, hold.shape[2] - width), BF)
    product = product_of(
        two_own, two_got, ct_own[...].astype(F32).T.astype(BF), ct_got[...].astype(F32).T.astype(BF)
    )
    hold[:, :, width : width + features] = product.astype(BF).reshape(*shape3, features)
    split_dp(ids_ref, hold, send, keep, hold.shape[2])


def grads_q_kernel(ids_ref, at_own, at_got, b_own, b_got, send_a, keep_a, send_b, keep_b, hold):
    cut, total = keep_a.shape[2], hold.shape[2]
    hold[...] = product_of(at_own, at_got, b_own[...], b_got[...]).astype(BF).reshape(hold.shape)
    split_dp(ids_ref, hold.at[:, :, 0:cut], send_a, keep_a, cut)
    split_near(ids_ref, hold.at[:, :, cut:], send_b, keep_b, total - cut)


def fold_q_kernel(ids_ref, keep_a, got_a, keep_b, got_b, up_keep, up_got, oh_keep, oh_got, embed_own, embed_got,
                  send_a, left_a, send_b, left_b, send_o, left_o, hold_a, hold_b, hold_o, hold_e):
    hold_a[...] = plus(keep_a, got_a)
    split_near(ids_ref, hold_a, send_a, left_a, hold_a.shape[2])
    hold_b[...] = plus(keep_b, got_b)
    columns = hold_b.shape[2]
    split_dp(ids_ref, hold_b, send_b, left_b, columns)
    hold_o[...] = plus(oh_keep, oh_got)
    for out, at in ((send_o, 1 - ids_ref[3]), (left_o, ids_ref[3])):
        for k in range(2):
            out[k] = hold_o[2 * at + k]
    hold_e[...] = plus(embed_own, embed_got)
    width = hold_e.shape[2]
    for out, at in ((send_b, 1 - ids_ref[1]), (left_b, ids_ref[1])):
        for k in range(4):
            start = columns + k % 2 * width
            out[k // 2, :, start : start + width] = hold_e[4 * at + k]
    start = columns + 2 * width
    half = send_b.shape[2] - start
    for k in range(2):
        at = up_keep.shape[1] - (2 - k) * half
        total = plus(up_keep.at[:, at : at + half], up_got.at[:, at : at + half])
        for out in (send_b, left_b):
            out[k, :, start:] = total


def merge_q_kernel(ids_ref, keep_a, got_a, keep_b, got_b, oh_keep, oh_got,
                   send, left, pair_ref, near_ref, embed_both, oh_left, hold, hold_e, hold_o):
    width = embed_both.shape[1]
    half = pair_ref.shape[2] // 2
    first = keep_a.shape[2]
    columns = keep_b.shape[2] - half - 2 * width
    total = hold.shape[2]
    hold[:, :, 0:first] = plus(keep_a, got_a)
    hold[:, :, first:] = plus(keep_b.at[:, :, 0:columns], got_b.at[:, :, 0:columns])
    hold_o[...] = plus(oh_keep, oh_got)
    for k in range(4):
        span = slice(columns + k % 2 * width, columns + (k % 2 + 1) * width)
        hold_e[k] = plus(keep_b.at[k // 2, :, span], got_b.at[k // 2, :, span])
    far, near = ids_ref[3], ids_ref[2]
    for out, at in ((send, 1 - far), (left, far)):
        out[:, 0:total] = hold[at]
        out[:, total:] = hold_e[2 * at + near]
    near_ref[:, 0:width] = hold_e[2 * far + 1 - near]
    near_ref[:, width:] = hold_o[1 - near]
    oh_left[...] = hold_o[near]
    embed_both[...] = hold_e[2 * (1 - far) + 1 - near]
    for k in range(2):
        span = slice(k * half, (k + 1) * half)
        pair_ref[0, :, span] = keep_b[k, :, columns + 2 * width :]
        pair_ref[1, :, span] = got_b[k, :, columns + 2 * width :]


def expand(ids_ref, rows_ref, pair_own, pair_got, out_ref, block):
    rows = rows_ref.shape[0]
    groups = block.shape[0] // rows
    tiles = block.shape[1] // LANES
    for a, b in ((0, 0), (0, 1), (1, 0), (1, 1)):
        source = pair_got if a else pair_own
        for q in range(tiles):
            for g in range(groups):
                at = (q * groups + g) * LANES
                block[g * rows : (g + 1) * rows, q * LANES : (q + 1) * LANES] = source[b, :, at : at + LANES]
        core, dp = (1 - ids_ref[0] if a else ids_ref[0]), (1 - ids_ref[1] if b else ids_ref[1])
        at = pl.multiple_of((core * 2 + dp) * block.shape[1], LANES)
        out_ref[:, pl.ds(at, block.shape[1])] = nn(rows_ref[...], block[...])


def insert_east(cols, fields_ref, east_ref, out_ref):
    variables = east_ref.shape[1]
    out_ref[...] = fields_ref[...]
    for item in range(east_ref.shape[0]):
        out_ref[item, pl.ds(cols - 1, variables, stride=cols), :] = east_ref[item].astype(F32)


def close_kernel(cols, ids_ref, fields_ref, east_ref, pos_ref, pos_got_ref, *refs):
    outs = refs
    if len(refs) > 2:
        (up_ref, up_got_ref, rows_ref, pair_own, pair_got), outs, block = refs[:5], refs[5:-1], refs[-1]
        width = outs[2].shape[1]
        outs[2][...] = up_ref[:, 0:width].astype(F32) + up_got_ref[:, 0:width].astype(F32)
        expand(ids_ref, rows_ref, pair_own, pair_got, outs[3], block)
    insert_east(cols, fields_ref, east_ref, outs[0])
    outs[1][...] = pos_ref[...].astype(F32) + pos_got_ref[...].astype(F32)


def end_kernel(*refs):
    if len(refs) > 3:
        (near_ref, both_ref, oh_ref, keep_ref, got_ref), refs = refs[:5], refs[5:]
        out_ref, head_ref, grad_ref = refs[2:]
        embed_width = both_ref.shape[1]
        both = keep_ref[...].astype(F32) + got_ref[...].astype(F32)
        width = grad_ref.shape[2]
        for c in range(3):
            grad_ref[c] = both[:, c * width : (c + 1) * width]
        total = both[:, 3 * width :] + near_ref[:, 0:embed_width].astype(F32) + both_ref[...].astype(F32)
        both = oh_ref[...].astype(F32) + near_ref[:, embed_width:].astype(F32)
        out_ref[...] = both[:, 0:width]
        head_ref[...] = both[:, width : width + head_ref.shape[1]]
    else:
        total, refs = jnp.sum(refs[0][...].astype(F32), axis=0), refs[1:]
    features = refs[0].shape[1]
    refs[0][...] = total[:, 0:features]
    refs[1][...] = total[:, LANES:].T[features - LANES : features - LANES + 2, :]


def local(
    dataset,
    indices,
    run_count,
    run_mean,
    run_var,
    w_embed,
    pos_embed,
    gains,
    w_qkv,
    w_out,
    w_up,
    w_down,
    w_head,
    cotangent,
):
    items = indices.shape[0]
    variables, height, columns = dataset.shape[1:]
    dp, lon = lax.axis_size("dp"), lax.axis_size("lon")
    everyone = dp * lon
    width = w_embed.shape[1]
    local_width = w_qkv.shape[2]
    heads = local_width // HDIM
    item_tokens = cotangent.shape[1]
    tokens = items * item_tokens
    features = w_embed.shape[0]
    hidden_units = w_up.shape[1]
    scale = 1.0 / math.sqrt(HDIM)
    group, far = heads, lon // heads
    groups = [[group * g + i for i in range(group)] for g in range(far)]
    across = [[i + group * g for g in range(far)] for i in range(group)]
    assert items * HDIM == LANES and item_tokens == LANES and height == LANES and columns == 4
    lon_at, dp_at = lax.axis_index("lon"), lax.axis_index("dp")
    ids = [lon_at % 2, dp_at, lon_at // 2 % 2, lon_at // 4 % 2, *[lon_at // 2 ^ k for k in range(4)], dp_at * lon + lon_at, lax.axis_index("mp")]
    ids = jnp.stack(ids).astype(jnp.int32)
    paired = dp == 2 and lon == 8
    parts, rows = width // (2 * (width // everyone)), width // everyone
    turned_shape = (
        [shape((parts, rows, tokens))] * 2 if paired else [shape((width, tokens))]
    )
    turned_hold = pltpu.VMEM((parts, 2, rows, tokens) if paired else (8, LANES), BF)

    alone = dict(axis_index_groups=groups) if far > 1 else {}

    vmem, smem = pl.BlockSpec(memory_space=pltpu.VMEM), pl.BlockSpec(memory_space=pltpu.SMEM)
    assert dp == 2

    data = dataset.transpose(0, 1, 3, 2).reshape(dataset.shape[0], variables * columns, height)
    fields, edge, moments, _ = call(
        moments_kernel,
        "moments",
        [
            warm((items, variables * columns, height), F32),
            warm((items, variables, height)),
            warm((8, LANES) if paired else (everyone, 8, LANES), F32),
        ],
        indices, data,
        in_specs=[pl.BlockSpec(memory_space=pltpu.SMEM), pl.BlockSpec(memory_space=pl.ANY)],
        scratch=[pltpu.VMEM((LANES, LANES), F32), pltpu.SemaphoreType.DMA((items,))],
    )
    edge = from_behind(edge, "lon", 1)
    if paired:
        row = lax.broadcasted_iota(jnp.int32, moments.shape, 0)
        held = float(items * height * columns)
        for axis, distance in (("lon", 1), ("lon", 2), ("lon", 4), ("dp", 1)):
            got = swap(moments, axis, distance)
            apart = jnp.square(moments[0:1] - got[0:1]) * (0.5 * held)
            moments = jnp.where(row == 0, 0.5 * (moments + got), moments + got + apart)
            held = 2.0 * held
    else:
        moments = lax.all_to_all(moments, ("dp", "lon"), 0, 0)
    wh_turned = w_head.T

    out = call(
        functools.partial(start_kernel, float(items * height * columns), everyone),
        "start",
        [
            *[shape((1, variables), F32)] * 3,
            shape((tokens, width), F32),
            shape((features, tokens)),
            *([warm((2, 3, item_tokens, LANES))] * 4 if paired else [shape((heads, 3, item_tokens, LANES))]),
            *turned_shape,
        ],
        ids, Warm(moments), *[r.reshape(1, variables) for r in (run_count, run_mean, run_var)],
        Warm(fields), Warm(edge), w_embed, pos_embed, gains, w_qkv,
        in_specs=[smem, *[vmem] * 9, pl.BlockSpec(memory_space=pl.ANY)],
        scratch=[
            pltpu.VMEM((LANES, LANES), F32),
            pltpu.VMEM((8, LANES), F32),
            turned_hold,
            pltpu.VMEM(w_qkv.shape, BF),
            pltpu.SemaphoreType.DMA,
            pltpu.VMEM((heads, 3, item_tokens, LANES), BF),
        ],
        flops=2 * tokens * width * (features + 3 * local_width),
    )
    count = 4 if paired else 1
    stats, (hidden_zero, patches), packed = out[:3], out[3:5], out[5 : 5 + count]
    normed_one, token = out[5 + count : -1], out[-1]

    def along(messages):
        return [messages[0], *[swap(messages[k], "lon", 2 * k) for k in range(1, count)]]

    if paired:
        own = along(packed)
    else:
        sent = lax.all_to_all(packed[0], "lon", 0, 0, **alone)
        kv = sent
        if far > 1:
            kv = lax.all_gather(sent, "lon", axis=0, tiled=True, axis_index_groups=across)

    if paired:
        wo_got, normed_got = swap(w_out, "mp", 1), swap(normed_one[1], "lon", 1)
        other = [swap(x, "lon", 1) for x in own]
    if paired:
        attended, kept, token = pair_attend(own, other, items, scale, [token, normed_got])
        attended = along(attended)
    else:
        attended, attended_t, weights_t, token = attend(sent, kv, items, scale, [token])
        attended = [lax.all_to_all(attended, "lon", 0, 0, **alone)]
    anywhere = pl.BlockSpec(memory_space=pl.ANY)
    d_two, d_act, ct_turned, *mine, token = call(
        cotangent_kernel,
        "cotangent",
        [
            shape((tokens, width), F32),
            shape((tokens, hidden_units)),
            shape((features, tokens)),
            *[shape((rows, features))] * paired,
        ],
        ids, cotangent.transpose(0, 2, 1), wh_turned, w_down,
        after=[token],
        scratch=[pltpu.VMEM((everyone, rows, features), BF)] * paired,
        flops=2 * tokens * width * (features + hidden_units),
    )

    if paired:
        ct_got = swap(ct_turned, "lon", 1)
        attended[0] = pin(attended[0], [token])
        attended += [swap(x, "mp", 1) for x in attended]
    if paired:
        branches = [attended[0], *[Warm(x) for x in attended[1:]], w_out, Warm(wo_got)]
    else:
        mixed, branch, token = call(
            project_kernel,
            "project",
            [shape((tokens, local_width)), warm((tokens, width))],
            ids, *attended, w_out,
            after=[token],
            flops=2 * tokens * width * local_width,
        )
        branches = [Warm(branch), Warm(swap(branch, "mp", 1))]
    block = min(512, hidden_units // 2)
    chunks = hidden_units // block
    out = call(
        functools.partial(forward_kernel, count if paired else 0),
        "forward",
        [
            warm((tokens, width)),
            *[shape((tokens, local_width))] * paired,
            shape((tokens, width), F32),
            shape((tokens, hidden_units)),
            shape((2, tokens, hidden_units // 2)),
            shape((tokens, hidden_units // 2)),
            *turned_shape,
        ],
        ids, *branches, Warm(hidden_zero), gains, w_up, d_act,
        after=[token],
        in_specs=[
            smem,
            *([*[vmem] * (len(branches) - 2), anywhere, anywhere] if paired else [vmem] * 2),
            vmem,
            vmem,
            anywhere,
            anywhere,
        ],
        out_specs=[*[vmem] * (1 + paired), *[anywhere] * (4 + len(turned_shape))],
        scratch=[
            *[pltpu.VMEM(x.shape, BF) for x in turned_shape],
            pltpu.VMEM((tokens, width), F32),
            pltpu.VMEM((chunks, width, block), BF),
            pltpu.VMEM((chunks, tokens, block), BF),
            pltpu.VMEM((tokens, hidden_units), BF),
            pltpu.VMEM((2, tokens, hidden_units // 2), BF),
            pltpu.VMEM((tokens, width), BF),
            turned_hold,
            pltpu.SemaphoreType.DMA((2 * chunks,)),
            pltpu.SemaphoreType.DMA((2 + len(turned_shape) + 2 * chunks,)),
            *[
                pltpu.VMEM((2, *w_out.shape), BF),
                pltpu.VMEM((2, tokens, local_width), BF),
                pltpu.SemaphoreType.DMA((2,)),
            ] * paired,
        ],
        limit=32,
        flops=4 * tokens * width * hidden_units,
    )
    d_norm, *out, token = out
    if paired:
        mixed, out = out[0], out[1:]
        mixed_got = swap(mixed, "lon", 1)
    hidden_one, d_pre, activated, act_send = out[:4]
    normed_two = out[4:]
    d_norm_got = swap(d_norm, "mp", 1)
    half = hidden_units // 2
    if paired:
        inner_columns = features // rows * LANES
        first = half - LANES
        out_a = shape((parts // 2, rows, first + inner_columns))
        out_b = shape((parts // 2, rows, hidden_units - first))
        send_a, keep_a, send_b, keep_b, token = call(
            grads_ff_kernel,
            "grads_ff",
            [out_a, out_a, out_b, out_b],
            ids, normed_two[0], Warm(swap(normed_two[1], "lon", 1)), d_pre, Warm(swap(d_pre, "lon", 1)),
            ct_turned, Warm(ct_got), activated, Warm(swap(act_send, "lon", 1)),
            after=[token],
            scratch=[
                pltpu.VMEM((parts, rows, hidden_units), BF),
                pltpu.VMEM((2, parts // 2, rows, inner_columns), BF),
            ],
            limit=32,
            flops=2 * tokens * (width + features) * hidden_units,
        )
        got_a, got_b = swap(send_a, "dp", 1), swap(send_b, "lon", 2)
    forward, token = call(
        down_kernel,
        "down",
        [shape((tokens, width))],
        activated, Warm(w_down),
        after=[token, *([mixed_got] if paired else [])],
        flops=2 * tokens * width * hidden_units,
    )

    out = call(
        second_kernel,
        "second",
        [
            shape((tokens, width), F32),
            shape((1, width), F32),
            warm((heads, item_tokens, LANES)),
            *turned_shape,
        ],
        ids, Warm(hidden_one), Warm(d_two), Warm(d_norm), Warm(d_norm_got), gains, Warm(w_out),
        after=[token],
        scratch=[turned_hold],
        flops=2 * tokens * width * local_width,
    )
    d_one, gain_two, d_mixed = out[0], out[1], out[2:3]
    d_one_turned, token = out[3:-1], out[-1]
    if paired:
        d_one_got = swap(d_one_turned[1], "lon", 1)
    if paired:
        chips = [[2 * k + c for k in range(lon // 2)] for c in range(2)]
        d_heads = lax.all_to_all(
            d_mixed[0].reshape(lon // 2, 2, item_tokens, LANES), "lon", 0, 0, axis_index_groups=chips
        )
    else:
        d_heads = lax.all_to_all(d_mixed[0], "lon", 0, 0, **alone)
    forward_got = swap(forward, "mp", 1)
    if paired:
        out_a = shape((2, rows, first + 2 * inner_columns))
        out_b = shape((2, rows, hidden_units - first))
        send_a, keep_a, send_b, keep_b, token = call(
            fold_ff_kernel,
            "fold_ff",
            [out_a, out_a, out_b, out_b],
            ids, keep_a, Warm(got_a), keep_b, Warm(got_b),
            after=[token],
            scratch=[
                pltpu.VMEM((parts // 2, rows, first), BF),
                pltpu.VMEM((parts // 2, rows, hidden_units - first), BF),
            ],
        )
        send_a, send_b = pin([send_a, send_b], [d_heads])
        got_a, got_b = swap(send_a, "lon", 2), swap(send_b, "dp", 1)

    if paired:
        back, cross, token = pair_attend_back(ids, kept, d_heads, items, scale, [token])
        *back, token = call(
            combine_kernel,
            "combine",
            [warm(x.shape) for x in back],
            *back, Warm(swap(pin(cross, [got_a, got_b, forward_got]), "lon", 1)),
            after=[token],
        )
        back = along(back)
    else:
        back, token = attend_back(sent, kv, d_heads, attended_t, weights_t, items, scale, [token])
        if far > 1:
            d_query, d_kv = back
            d_kv = lax.psum_scatter(
                d_kv, "lon", scatter_dimension=0, tiled=True, axis_index_groups=across
            ).astype(BF)
            back = [jnp.concatenate([d_query[:, None], d_kv], axis=1)]
        back = [lax.all_to_all(back[0], "lon", 0, 0, **alone)]
    out = call(
        head_kernel,
        "head",
        [shape((items, features, item_tokens), F32), *turned_shape],
        ids, hidden_one, forward, Warm(forward_got), wh_turned,
        after=[token],
        scratch=[turned_hold],
        flops=2 * tokens * width * features,
    )
    pred, hidden_turned, token = out[0].transpose(0, 2, 1), list(out[1:-1]), out[-1]
    if paired:
        up_send, up_keep, token = call(
            merge_ff_kernel,
            "merge_ff",
            [shape((rows, hidden_units + 4 * inner_columns))] * 2,
            ids, keep_a, Warm(got_a), keep_b, got_b,
            after=[token],
            scratch=[pltpu.VMEM((2, rows, hidden_units), BF)],
        )
    d_qkv, d_norm, token = call(
        functools.partial(third_kernel, count),
        "third",
        [shape((tokens, 3 * local_width)), warm((tokens, width))],
        ids, *[Warm(x) for x in back], Warm(w_qkv),
        after=[token],
        flops=6 * tokens * width * local_width,
    )
    d_norm_got = swap(d_norm, "mp", 1)
    if paired:
        up_send, hidden_turned[1] = pin([up_send, hidden_turned[1]], [token])
        up_got = swap(up_send, "lon", 4)
        wide = local_width + 2 * LANES
        cut = 3 * local_width // 2 + LANES
        first, second = (shape((parts // 2, rows, c)) for c in (cut, 3 * local_width - cut))
        send_a, keep_a, send_b, keep_b, token = call(
            grads_q_kernel,
            "grads_q",
            [first, first, second, second],
            ids, normed_one[0], normed_got, d_qkv, Warm(swap(d_qkv, "lon", 1)),
            after=[token],
            scratch=[pltpu.VMEM((parts, rows, 3 * local_width), BF)],
            flops=6 * tokens * width * local_width,
        )
        oh_send, oh_keep, token = call(
            grads_oh_kernel,
            "grads_oh",
            [shape((parts // 2, rows, wide))] * 2,
            ids, d_one_turned[0], Warm(d_one_got), mixed, Warm(mixed_got),
            hidden_turned[0], Warm(swap(hidden_turned[1], "lon", 1)), ct_turned, Warm(ct_got),
            after=[token],
            scratch=[pltpu.VMEM((parts, rows, wide), BF)],
            flops=2 * tokens * width * wide,
        )
        oh_got = swap(oh_send, "dp", 1)
        got_a, got_b = swap(send_a, "dp", 1), swap(send_b, "lon", 2)

    out = call(
        functools.partial(last_kernel, columns),
        "last",
        [
            *[shape((item_tokens, width // 2))] * 2,
            shape((items, variables * columns, height), F32),
            shape((items, variables, height)),
            *([shape((parts, rows, 2 * LANES))] * 2 if paired else [shape((width, 2 * LANES))]),
        ],
        ids, Warm(hidden_zero), Warm(d_one), Warm(d_norm), Warm(d_norm_got), gains, gain_two, patches, w_embed,
        after=[token],
        scratch=[
            pltpu.VMEM((2 * LANES, width), F32),
            pltpu.VMEM((2, item_tokens, width // 2), BF),
            pltpu.VMEM((parts, 2, rows, 2 * LANES) if paired else (8, LANES), BF),
        ],
        flops=4 * tokens * width * features,
    )
    pos_send, pos, d_fields, d_edge = out[:4]
    embed, token = out[4:-1], out[-1]
    if not paired:
        east, pos_got = from_behind(d_edge, "lon", -1), swap(pos_send, "dp", 1)
    more, more_outs, more_scratch, rest, rest_outs = [], [], [], [], []
    if paired:
        embed_width = embed[0].shape[2]
        step_a, side = shape((2, rows, cut)), shape((2, rows, wide))
        step_b = shape((2, rows, 3 * local_width - cut + 2 * embed_width + 2 * inner_columns))
        send_a, keep_a, send_b, keep_b, oh_send, oh_keep, token = call(
            fold_q_kernel,
            "fold_q",
            [step_a, step_a, step_b, step_b, side, side],
            ids, keep_a, Warm(got_a), keep_b, Warm(got_b), up_keep, Warm(up_got), oh_keep, Warm(oh_got),
            embed[0], Warm(swap(embed[1], "lon", 1)),
            after=[token],
            scratch=[
                pltpu.VMEM(keep_a.shape, BF),
                pltpu.VMEM(keep_b.shape, BF),
                pltpu.VMEM(oh_keep.shape, BF),
                pltpu.VMEM(embed[0].shape, BF),
            ],
        )
        got_a, got_b, oh_got = swap(send_a, "lon", 2), swap(send_b, "dp", 1), swap(oh_send, "lon", 4)
        east = from_behind(pin(d_edge, [token]), "lon", -1)
        final, block = shape((rows, 3 * local_width + embed_width)), shape((rows, embed_width))
        send, keep, pair, near_send, embed_both, oh_keep, token = call(
            merge_q_kernel,
            "merge_q",
            [
                final,
                final,
                shape((2, rows, 4 * inner_columns)),
                shape((rows, embed_width + wide)),
                block,
                shape((rows, wide)),
            ],
            ids, keep_a, Warm(got_a), keep_b, Warm(got_b), oh_keep, Warm(oh_got),
            after=[token, east],
            scratch=[
                pltpu.VMEM((2, rows, 3 * local_width), BF),
                pltpu.VMEM((4, *block.shape), BF),
                pltpu.VMEM((2, rows, wide), BF),
            ],
        )
        pos_got = swap(pin(pos_send, [token]), "dp", 1)
        more = [up_keep, Warm(up_got), mine[0], pair, Warm(swap(pair, "lon", 1))]
        more_outs = [shape((rows, hidden_units), F32)] * 2
        more_scratch = [pltpu.VMEM((features, hidden_units // 4), BF)]
        rest = [
            Warm(swap(near_send, "lon", 2)), Warm(swap(embed_both, "lon", 6)), oh_keep,
            keep, Warm(swap(send, "lon", 4)),
        ]
        rest_outs = [
            shape((rows, local_width), F32),
            shape((rows, features), F32),
            shape((3, rows, local_width), F32),
        ]
    else:
        rest = [lax.all_to_all(embed[0].reshape(everyone, rows, 2 * LANES), ("dp", "lon"), 0, 0)]
    *closed, token = call(
        functools.partial(close_kernel, columns),
        "close",
        [shape(d_fields.shape, F32), shape(pos.shape, F32), *more_outs],
        ids, d_fields, east, pos, Warm(pos_got), *more,
        after=[token],
        scratch=more_scratch,
    )
    *ended, token = call(
        end_kernel,
        "end",
        [shape((rows, features), F32), shape((2, rows), F32), *rest_outs],
        *rest,
        after=[token],
    )
    if paired:
        grad_up, grad_down, (grad_out, grad_head, grad_qkv) = closed[2], closed[3], ended[2:]
    else:
        flat = activated.transpose(1, 0, 2).reshape(tokens, hidden_units)
        grad_up = scatter(nn(normed_two[0], d_pre))
        grad_down = scatter(nn(d_two.T.astype(BF), flat))
        grad_out = scatter(nn(d_one_turned[0], mixed))
        grad_head = scatter(nt(hidden_turned[0], ct_turned))
        grad_qkv = scatter(nn(normed_one[0], d_qkv)).reshape(rows, 3, local_width).transpose(1, 0, 2)
    return (
        pred,
        *[x.reshape(variables) for x in stats],
        closed[0].reshape(items, variables, columns, height).transpose(0, 1, 3, 2),
        ended[0].T,
        closed[1],
        ended[1],
        grad_qkv,
        grad_out.T,
        grad_up,
        grad_down.T,
        grad_head,
    )


def solution(mesh):
    in_specs = (
        P(None, None, None, "lon"),
        P("dp"),
        P(),
        P(),
        P(),
        P(),
        P("lon", None),
        P(),
        P(None, None, "mp"),
        P("mp", None),
        P(None, "mp"),
        P("mp", None),
        P(),
        P("dp", "lon", None),
    )
    out_specs = (
        P("dp", "lon", None),
        P(),
        P(),
        P(),
        P("dp", None, None, "lon"),
        P(None, ("dp", "lon")),
        P("lon", "dp"),
        P(None, ("dp", "lon")),
        P(None, ("dp", "lon"), "mp"),
        P("mp", ("dp", "lon")),
        P(("dp", "lon"), "mp"),
        P("mp", ("dp", "lon")),
        P(("dp", "lon"), None),
    )
    return jax.shard_map(local, mesh=mesh, in_specs=in_specs, out_specs=out_specs, check_vma=False)
```

```python
import functools
import math

import jax
import jax.numpy as jnp
from jax import lax
from jax.experimental import pallas as pl
from jax.experimental.pallas import tpu as pltpu
from jax.sharding import PartitionSpec as P

HDIM = 64
PATCH = 2
LANES = 128
NORM_EPS = 1e-06
STAT_EPS = 1e-06
BF = jnp.bfloat16
F32 = jnp.float32
MIB = 2**20


def swap(block, axis, distance):
    route = [(i, i ^ distance) for i in range(lax.axis_size(axis))]
    return lax.ppermute(block, axis, route)


def from_behind(block, axis, distance):
    size = lax.axis_size(axis)
    route = [((i - distance) % size, i) for i in range(size)]
    return lax.ppermute(block, axis, route)


def pick(x, index, axis):
    return lax.dynamic_index_in_dim(x, index, axis, keepdims=False)


def halve(total, dims):
    for axis, bit in dims:
        side = (lax.axis_index(axis) // bit) % 2
        got = swap(pick(total, 1 - side, 0), axis, bit)
        total = (pick(total, side, 0).astype(F32) + got.astype(F32)).astype(BF)
    return total


def scatter(total):
    dp, lon = lax.axis_size("dp"), lax.axis_size("lon")
    dims = []
    for axis, size in (("dp", dp), ("lon", lon)):
        bit = size // 2
        while bit:
            dims.append((axis, bit))
            bit //= 2
    rows, columns = total.shape
    total = total.astype(BF).reshape((2,) * len(dims) + (rows // (dp * lon), columns))
    order = sorted(range(len(dims)), key=lambda i: (dims[i][1] > 1 or dims[i][0] == "dp", i))
    total = total.transpose([*order, len(dims), len(dims) + 1])
    return halve(total, [dims[i] for i in order]).astype(F32)


def nt(a, b):
    return lax.dot_general(a, b, (((1,), (1,)), ((), ())), preferred_element_type=F32)


def nn(a, b):
    return lax.dot_general(a, b, (((1,), (0,)), ((), ())), preferred_element_type=F32)


def item_mask(rows, lanes, item):
    lane = lax.broadcasted_iota(jnp.int32, (rows, lanes), 1)
    return (lane >= item * HDIM) & (lane < (item + 1) * HDIM)


def interleave(first, second):
    low = item_mask(first.shape[0], LANES, 0)
    return (
        jnp.where(low, first, pltpu.roll(second, HDIM, 1)),
        jnp.where(low, pltpu.roll(first, HDIM, 1), second),
    )


def norm_parts(hidden):
    centred = hidden - jnp.mean(hidden, axis=-1, keepdims=True)
    variance = jnp.mean(centred * centred, axis=-1, keepdims=True)
    inverse = lax.rsqrt(variance + NORM_EPS)
    return centred * inverse, inverse


def norm_back(unit, inverse, scaling, grad):
    scaled = grad * scaling
    back = inverse * (
        scaled
        - jnp.mean(scaled, axis=-1, keepdims=True)
        - unit * jnp.mean(scaled * unit, axis=-1, keepdims=True)
    )
    return back, jnp.sum(grad * unit, axis=0, keepdims=True)


def emit_turned(x, ids_ref, outs, hold):
    turned = x.T.astype(BF)
    if len(outs) == 1:
        outs[0][...] = turned
        return
    keep, send = outs
    parts, rows, tokens = keep.shape
    hold[...] = turned.reshape(parts, 2, rows, tokens)
    core = ids_ref[0]
    keep[...] = hold[:, pl.ds(core, 1)].reshape(parts, rows, tokens)
    send[...] = hold[:, pl.ds(1 - core, 1)].reshape(parts, rows, tokens)


class Warm:
    def __init__(self, value):
        self.value = value


def call(body, name, outs, *args, after=(), grid=(), in_specs=None, out_specs=None, scratch=(), limit=24, flops=0):
    vmem = pl.BlockSpec(memory_space=pltpu.VMEM)
    smem = pl.BlockSpec(memory_space=pltpu.SMEM)
    shapes = [o.value if isinstance(o, Warm) else o for o in outs]
    plain = [a.value if isinstance(a, Warm) else a for a in args]
    if in_specs is None:
        in_specs = [smem if a.dtype == jnp.int32 else vmem for a in plain]
    if out_specs is None:
        out_specs = [vmem] * len(outs)
    token = pl.BlockSpec((8, LANES), lambda *at: (0, 0)) if grid else vmem
    nbytes = sum(math.prod(a.shape) * a.dtype.itemsize for a in [*plain, *shapes])
    here, skip, there = len(args), len(after), len(outs)

    def with_token(*refs):
        refs = list(refs)
        refs[here + skip + there][...] = jnp.zeros((8, LANES), F32)
        body(*refs[:here], *refs[here + skip : here + skip + there], *refs[here + skip + there + 1 :])

    def cold(x):
        if isinstance(x, Warm):
            return x.value
        return x if x.dtype == jnp.int32 else pltpu.with_memory_space_constraint(x, pltpu.HBM)

    return pl.pallas_call(
        with_token,
        grid=grid,
        out_shape=[
            *[o.value if isinstance(o, Warm) else pltpu.HBM(o.shape, o.dtype) for o in outs],
            pltpu.HBM((8, LANES), F32),
        ],
        in_specs=[*in_specs, *[pl.BlockSpec(memory_space=pl.ANY)] * skip],
        out_specs=[*out_specs, token],
        scratch_shapes=list(scratch),
        compiler_params=pltpu.CompilerParams(vmem_limit_bytes=limit * MIB),
        cost_estimate=pl.CostEstimate(flops=int(flops), bytes_accessed=nbytes, transcendentals=0),
        name=name,
    )(*[cold(a) for a in args], *[cold(a) for a in after])


def shape(dims, kind=BF):
    return jax.ShapeDtypeStruct(dims, kind)


def warm(dims, kind=BF):
    return Warm(shape(dims, kind))


def feature_order(variables, back):
    features = PATCH * PATCH * variables
    natural = lax.broadcasted_iota(jnp.int32, (features, features), 1 if back else 0)
    sorted_ = lax.broadcasted_iota(jnp.int32, (features, features), 0 if back else 1)
    hit = (natural // 4 == sorted_ % variables) & (natural % 4 == sorted_ // variables)
    return jnp.where(hit, 1.0, 0.0).astype(BF)


def send_pairs(ids_ref, hold, messages):
    if len(messages) == 1:
        messages[0][...] = hold[...]
        return
    for k, message in enumerate(messages):
        message[...] = hold[pl.ds(2 * ids_ref[4 + k], 2)]


def moments_kernel(index_ref, data_ref, fields_ref, edge_ref, moments_ref, turn_ref, sems):
    items, variables, height = edge_ref.shape
    cols = fields_ref.shape[1] // variables
    copies = [
        pltpu.make_async_copy(data_ref.at[index_ref[i]], fields_ref.at[i], sems.at[i])
        for i in range(items)
    ]
    for copy in copies:
        copy.start()
    turn_ref[...] = jnp.zeros_like(turn_ref)
    for copy in copies:
        copy.wait()
    blocks = [
        fields_ref[i, pl.ds(c, variables, stride=cols), :] for i in range(items) for c in range(cols)
    ]
    for i in range(items):
        edge_ref[i] = blocks[i * cols + cols - 1].astype(BF)
    count = float(items * cols * height)
    mean = jnp.sum(sum(blocks), axis=1, keepdims=True) * (1.0 / count)
    spread = jnp.sum(sum(jnp.square(b - mean) for b in blocks), axis=1, keepdims=True)
    turn_ref[0:variables, 0:1] = mean
    turn_ref[HDIM : HDIM + variables, 0:1] = spread
    turn_ref[0:variables, 1:2] = spread
    turned = turn_ref[...].T
    if len(moments_ref.shape) == 2:
        moments_ref[...] = turned[0 : moments_ref.shape[0], :]
    else:
        moments_ref[...] = jnp.broadcast_to(turned[0:1, :][None], moments_ref.shape)


def start_kernel(local_count, members, ids_ref, mom_ref, count_ref, mean_ref, var_ref, fields_ref, edge_ref, we_ref,
                 pos_ref, gains_ref, wq_ref, new_count_ref, new_mean_ref, new_var_ref, hidden_ref, patches_ref,
                 *rest):
    (*outs, column_ref, run_ref, hold, weights, sem, qkv_ref) = rest
    if len(outs) > 2:
        messages, turned = outs[:-2], outs[-2:]
    else:
        messages, turned = outs[:1], outs[1:]
    copy = pltpu.make_async_copy(wq_ref, weights, sem)
    copy.start()
    items, rows, height = fields_ref.shape
    variables = edge_ref.shape[1]
    cols = rows // variables
    half = height // PATCH
    run_ref[...] = jnp.zeros_like(run_ref)
    for k, ref in enumerate((count_ref, mean_ref, var_ref)):
        run_ref[k : k + 1, 0:variables] = ref[...]
    batch_count = local_count * members
    if len(mom_ref.shape) == 2:
        batch_mean, spread = mom_ref[0:1, :], mom_ref[1:2, :]
    else:
        moments = mom_ref[:, 0, :]
        batch_mean = jnp.sum(moments, axis=0, keepdims=True) * (1.0 / members)
        off = moments - batch_mean
        spread = jnp.sum(pltpu.roll(moments, HDIM, 1) + local_count * off * off, axis=0, keepdims=True)
    run_count, run_mean, run_var = (run_ref[k : k + 1, :] for k in range(3))
    new_count = run_count + batch_count
    shift = batch_mean - run_mean
    new_mean = run_mean + shift * (batch_count / new_count)
    new_var = (
        run_var * run_count + spread + shift * shift * (run_count * batch_count / new_count)
    ) / new_count
    new_count_ref[...] = new_count[:, 0:variables]
    new_mean_ref[...] = new_mean[:, 0:variables]
    new_var_ref[...] = new_var[:, 0:variables]
    column_ref[...] = jnp.zeros_like(column_ref)
    column_ref[0:1, :] = new_mean
    column_ref[1:2, :] = lax.rsqrt(new_var + STAT_EPS)
    column = column_ref[...].T
    centre, inverse = column[0:variables, 0:1], column[0:variables, 1:2]

    def scaled(block):
        return ((block - centre) * inverse).astype(BF)

    row = lax.broadcasted_iota(jnp.int32, (2 * height, LANES), 0)
    lane = lax.broadcasted_iota(jnp.int32, (2 * height, LANES), 1)
    sort = [
        jnp.where(
            (row // height == lane // half) & (row % height == PATCH * (lane % half) + a), 1.0, 0.0
        ).astype(BF)
        for a in range(PATCH)
    ]
    natural = feature_order(variables, False)
    hidden = []
    for item in range(items):
        west = scaled(edge_ref[item].astype(F32))
        own = [
            scaled(fields_ref[item, pl.ds(c, variables, stride=cols), :]) for c in range(cols - 1)
        ]
        first = jnp.concatenate([west, own[0]], axis=0)
        second = jnp.concatenate([own[1], own[2]], axis=0)
        both = jnp.concatenate([first, second], axis=1)
        patches = jnp.concatenate([nn(both, sort[a]) for a in range(PATCH)], axis=0)
        patches = nn(natural, patches.astype(BF))
        patches_ref[:, item * LANES : (item + 1) * LANES] = patches.astype(BF)
        hidden.append(nn(patches.T.astype(BF), we_ref[...]) + pos_ref[...].astype(F32))
    hidden = jnp.concatenate(hidden, axis=0)
    hidden_ref[...] = hidden
    unit, _ = norm_parts(hidden)
    normed = unit * gains_ref[0:1, :]
    low = normed.astype(BF)
    emit_turned(normed, ids_ref, turned, hold)
    copy.wait()
    for c in range(3):
        product = nn(low, weights[c])
        for t in range(product.shape[1] // LANES):
            tile = product[:, t * LANES : (t + 1) * LANES]
            a, b = interleave(tile[:LANES], tile[LANES:])
            qkv_ref[2 * t, c] = a.astype(BF)
            qkv_ref[2 * t + 1, c] = b.astype(BF)
    send_pairs(ids_ref, qkv_ref, messages)


def cotangent_kernel(ids_ref, ct_ref, wh_ref, wd_ref, *refs):
    if len(refs) > 3:
        two_ref, act_ref, ct_turned_ref, mine_ref, hold = refs
        hold[...] = wh_ref[...].astype(F32).T.astype(BF).reshape(hold.shape)
        mine_ref[...] = hold[ids_ref[8]]
    else:
        two_ref, act_ref, ct_turned_ref = refs
    grads = []
    for item in range(ct_ref.shape[0]):
        ct = ct_ref[item].T.astype(BF)
        ct_turned_ref[:, item * LANES : (item + 1) * LANES] = ct_ref[item].astype(BF)
        grads.append(nn(ct, wh_ref[...]))
    d_two = jnp.concatenate(grads, axis=0)
    two_ref[...] = d_two
    act_ref[...] = nt(d_two.astype(BF), wd_ref[...]).astype(BF)


def attend_kernel(items, scale, q_ref, kv_ref, o_ref, ot_ref, pt_ref, vt_ref):
    keys = kv_ref.shape[0] * kv_ref.shape[2]

    @pl.when(pl.program_id(0) == 0)
    def _():
        vt_ref[...] = kv_ref[:, 2].reshape(keys, LANES).astype(F32).T.astype(BF)

    rows = q_ref.shape[0] * q_ref.shape[2]
    queries = q_ref[:, 0].reshape(rows, LANES) * BF(scale)
    key_rows = kv_ref[:, 1].reshape(keys, LANES)
    for item in range(items):
        chosen = jnp.where(item_mask(rows, LANES, item), queries, BF(0))
        scores = nt(key_rows, chosen)
        top = jnp.max(scores, axis=0, keepdims=True)
        raised = jnp.exp(scores - top)
        total = jnp.sum(raised, axis=0, keepdims=True)
        weights = (raised * (1.0 / total)).astype(BF)
        pt_ref[item] = weights
        span = slice(item * HDIM, (item + 1) * HDIM)
        ot_ref[span, :] = nn(vt_ref[span, :], weights)
    o_ref[...] = ot_ref[...].T.astype(BF).reshape(o_ref.shape)


def attend(q, kv, items, scale, after):
    peers, _, tokens, lanes = q.shape
    rows, keys = peers * tokens, kv.shape[0] * tokens
    step = max(1, min(peers, 256 * 1024 // keys // tokens))
    block = step * tokens
    return call(
        functools.partial(attend_kernel, items, scale),
        "attend",
        [
            shape((peers, tokens, lanes)),
            shape((lanes, rows), F32),
            shape((items, keys, rows)),
        ],
        Warm(q),
        Warm(kv),
        after=after,
        grid=(peers // step,),
        in_specs=[
            pl.BlockSpec((step, 3, tokens, lanes), lambda j: (j, 0, 0, 0)),
            pl.BlockSpec(kv.shape, lambda j: (0, 0, 0, 0)),
        ],
        out_specs=[
            pl.BlockSpec((step, tokens, lanes), lambda j: (j, 0, 0)),
            pl.BlockSpec((lanes, block), lambda j: (0, j)),
            pl.BlockSpec((items, keys, block), lambda j: (0, 0, j)),
        ],
        scratch=[pltpu.VMEM((lanes, keys), BF)],
        limit=24 if keys <= 2048 else 56,
        flops=8 * rows * keys * lanes,
    )


def pair_attend_kernel(items, scale, *refs):
    sources, (*outs, ot_ref, pt_ref, query_ref, key_ref, value_ref, vt_ref) = refs[:8], refs[8:]
    tokens = sources[0].shape[2]
    for k, source in enumerate(sources):
        span = slice(k * tokens, (k + 1) * tokens)
        if k < len(outs):
            query_ref[0, span, :] = source[0, 0] * BF(scale)
        key_ref[0, span, :] = source[0, 1]
        value_ref[0, span, :] = source[0, 2]
        vt_ref[:, span] = source[0, 2].astype(F32).T.astype(BF)
    queries = query_ref[0]
    for item in range(items):
        chosen = jnp.where(item_mask(queries.shape[0], LANES, item), queries, BF(0))
        scores = nt(key_ref[0], chosen)
        top = jnp.max(scores, axis=0, keepdims=True)
        raised = jnp.exp(scores - top)
        total = jnp.sum(raised, axis=0, keepdims=True)
        weights = (raised * (1.0 / total)).astype(BF)
        pt_ref[0, item] = weights
        span = slice(item * HDIM, (item + 1) * HDIM)
        ot_ref[0, span, :] = nn(vt_ref[span, :], weights)
    attended = ot_ref[0].T.astype(BF)
    for k, out in enumerate(outs):
        out[0] = attended[k * tokens : (k + 1) * tokens]


def pair_attend(own, other, items, scale, after):
    _, _, tokens, lanes = own[0].shape
    rows, keys = len(own) * tokens, 2 * len(own) * tokens
    wide = lambda *dims: pl.BlockSpec((1, *dims), lambda h: (h, *[0] * len(dims)))
    *outs, ot, pt, q, k, v, token = call(
        functools.partial(pair_attend_kernel, items, scale),
        "attend",
        [
            shape((2, tokens, lanes)),
            *[warm((2, tokens, lanes))] * (len(own) - 1),
            shape((2, lanes, rows), F32),
            shape((2, items, keys, rows)),
            shape((2, rows, lanes)),
            shape((2, keys, lanes)),
            shape((2, keys, lanes)),
        ],
        *[Warm(x) for x in [*own, *other]],
        after=after,
        grid=(2,),
        in_specs=[wide(3, tokens, lanes)] * (2 * len(own)),
        out_specs=[
            *[wide(tokens, lanes)] * len(own),
            wide(lanes, rows),
            wide(items, keys, rows),
            wide(rows, lanes),
            wide(keys, lanes),
            wide(keys, lanes),
        ],
        scratch=[pltpu.VMEM((lanes, keys), BF)],
        limit=32,
        flops=16 * rows * keys * lanes,
    )
    return outs, (q, k, v, ot, pt), token


def pair_attend_back_kernel(items, scale, ids_ref, query_ref, key_ref, value_ref, ot_ref, pt_ref, grads_ref, *refs):
    *outs, cross_ref, kt_ref, grad_rows, dqt_ref, dk_sum, dv_sum = refs
    tokens = grads_ref.shape[2]
    for k in range(len(outs)):
        grad_rows[k * tokens : (k + 1) * tokens, :] = grads_ref[ids_ref[4 + k], 0]
    kt_ref[...] = (key_ref[0].astype(F32) * scale).T.astype(BF)
    queries, grads = query_ref[0], grad_rows[...]
    product = grads.astype(F32).T * ot_ref[0]
    for item in range(items):
        span = slice(item * HDIM, (item + 1) * HDIM)
        mask = item_mask(queries.shape[0], LANES, item)
        grad = jnp.where(mask, grads, BF(0))
        query = jnp.where(mask, queries, BF(0))
        delta = jnp.sum(product[span, :], axis=0, keepdims=True)
        weights = pt_ref[0, item]
        back = (weights.astype(F32) * (nt(value_ref[0], grad) - delta)).astype(BF)
        d_value, d_key = nn(weights, grad), nn(back, query)
        if item == 0:
            dv_sum[...] = d_value
            dk_sum[...] = d_key
        else:
            dv_sum[...] += d_value
            dk_sum[...] += d_key
        dqt_ref[span, :] = nn(kt_ref[span, :], back)
    d_query = dqt_ref[...].T.astype(BF)
    for k in range(2 * len(outs)):
        span = slice(k * tokens, (k + 1) * tokens)
        if k < len(outs):
            outs[k][0, 0] = d_query[span]
        for c, total in ((0, dk_sum), (1, dv_sum)):
            if k < len(outs):
                outs[k][0, 1 + c] = total[span, :].astype(BF)
            else:
                cross_ref[k - len(outs), 0, c] = total[span, :].astype(BF)


def pair_attend_back(ids, kept, d, items, scale, after):
    count, _, tokens, lanes = d.shape
    rows, keys = count * tokens, 2 * count * tokens
    wide = lambda *dims: pl.BlockSpec((1, *dims), lambda h: (h, *[0] * len(dims)))
    *outs, cross, token = call(
        functools.partial(pair_attend_back_kernel, items, scale),
        "attend_back",
        [*[shape((2, 3, tokens, lanes))] * count, shape((count, 2, 2, tokens, lanes))],
        ids, *kept, d,
        after=after,
        grid=(2,),
        in_specs=[
            pl.BlockSpec(memory_space=pltpu.SMEM),
            wide(rows, lanes),
            wide(keys, lanes),
            wide(keys, lanes),
            wide(lanes, rows),
            wide(items, keys, rows),
            pl.BlockSpec((count, 1, tokens, lanes), lambda h: (0, h, 0, 0)),
        ],
        out_specs=[
            *[wide(3, tokens, lanes)] * count,
            pl.BlockSpec((count, 1, 2, tokens, lanes), lambda h: (0, h, 0, 0, 0)),
        ],
        scratch=[
            pltpu.VMEM((lanes, keys), BF),
            pltpu.VMEM((rows, lanes), BF),
            pltpu.VMEM((lanes, rows), F32),
            pltpu.VMEM((keys, lanes), F32),
            pltpu.VMEM((keys, lanes), F32),
        ],
        limit=32,
        flops=32 * rows * keys * lanes,
    )
    return outs, cross, token


def combine_kernel(*refs):
    count = (len(refs) - 1) // 2
    own, cross_ref, outs = refs[:count], refs[count], refs[count + 1 :]
    for k in range(count):
        outs[k][:, 0] = own[k][:, 0]
        for c in range(2):
            outs[k][:, 1 + c] = plus(own[k].at[:, 1 + c], cross_ref.at[k, :, c])


def attend_back_kernel(items, scale, q_ref, kv_ref, d_ref, ot_ref, pt_ref, dq_ref, *rest):
    dkv_ref, (kt_ref, dqt_ref, dk_sum, dv_sum) = rest[:-4], rest[-4:]
    step = pl.program_id(0)
    keys = kv_ref.shape[0] * kv_ref.shape[2]

    @pl.when(step == 0)
    def _():
        kt_ref[...] = (kv_ref[:, 1].reshape(keys, LANES).astype(F32) * scale).T.astype(BF)
        dk_sum[...] = jnp.zeros_like(dk_sum)
        dv_sum[...] = jnp.zeros_like(dv_sum)

    peers, _, tokens, _ = q_ref.shape
    rows = peers * tokens
    queries = q_ref[:, 0].reshape(rows, LANES) * BF(scale)
    grads = d_ref[...].reshape(rows, LANES)
    value_rows = kv_ref[:, 2].reshape(keys, LANES)
    product = grads.astype(F32).T * ot_ref[...]
    for item in range(items):
        span = slice(item * HDIM, (item + 1) * HDIM)
        mask = item_mask(rows, LANES, item)
        grad = jnp.where(mask, grads, BF(0))
        query = jnp.where(mask, queries, BF(0))
        delta = jnp.sum(product[span, :], axis=0, keepdims=True)
        weights = pt_ref[item]
        back = (weights.astype(F32) * (nt(value_rows, grad) - delta)).astype(BF)
        dv_sum[...] += nn(weights, grad)
        dk_sum[...] += nn(back, query)
        dqt_ref[span, :] = nn(kt_ref[span, :], back)
    d_query = dqt_ref[...].T.astype(BF).reshape(peers, tokens, LANES)
    if dkv_ref:
        dq_ref[...] = d_query
    else:
        dq_ref[pl.ds(step * peers, peers), 0] = d_query

    @pl.when(step == pl.num_programs(0) - 1)
    def _():
        for c, total in ((1, dk_sum), (2, dv_sum)):
            total = total[...].reshape(kv_ref.shape[0], tokens, LANES)
            if dkv_ref:
                dkv_ref[0][:, c - 1] = total
            else:
                dq_ref[:, c] = total.astype(BF)


def attend_back(q, kv, d, ot, pt, items, scale, after):
    peers, _, tokens, lanes = q.shape
    rows, keys = peers * tokens, kv.shape[0] * tokens
    step = max(1, min(peers, 256 * 1024 // keys // tokens))
    block = step * tokens
    if q.shape == kv.shape:
        outs = [shape(q.shape)]
        out_specs = [pl.BlockSpec(q.shape, lambda j: (0, 0, 0, 0))]
    else:
        outs = [shape((peers, tokens, lanes)), shape((kv.shape[0], 2, tokens, lanes), F32)]
        out_specs = [
            pl.BlockSpec((step, tokens, lanes), lambda j: (j, 0, 0)),
            pl.BlockSpec(outs[1].shape, lambda j: (0, 0, 0, 0)),
        ]
    *back, token = call(
        functools.partial(attend_back_kernel, items, scale),
        "attend_back",
        outs,
        Warm(q),
        Warm(kv),
        d,
        ot,
        pt,
        after=after,
        grid=(peers // step,),
        in_specs=[
            pl.BlockSpec((step, 3, tokens, lanes), lambda j: (j, 0, 0, 0)),
            pl.BlockSpec(kv.shape, lambda j: (0, 0, 0, 0)),
            pl.BlockSpec((step, tokens, lanes), lambda j: (j, 0, 0)),
            pl.BlockSpec((lanes, block), lambda j: (0, j)),
            pl.BlockSpec((items, keys, block), lambda j: (0, 0, j)),
        ],
        out_specs=out_specs,
        scratch=[
            pltpu.VMEM((lanes, keys), BF),
            pltpu.VMEM((lanes, block), F32),
            pltpu.VMEM((keys, lanes), F32),
            pltpu.VMEM((keys, lanes), F32),
        ],
        limit=24 if keys <= 2048 else 60,
        flops=16 * rows * keys * lanes,
    )
    return back, token


def unpack(ids_ref, sources, index, out_ref, base):
    several = len(sources) > 1
    count = len(sources) if several else sources[0].shape[0] // 2
    for t in range(count):
        source, head = (sources[t], 0) if several else (sources[0], 2 * t)
        pair = [
            (source[head + s] if index is None else source[head + s, index]).astype(F32) for s in range(2)
        ]
        at = base + (pl.multiple_of(ids_ref[4 + t] * LANES, LANES) if several else t * LANES)
        for item, tile in enumerate(interleave(*pair)):
            out_ref[item * LANES : (item + 1) * LANES, pl.ds(at, LANES)] = tile.astype(BF)


def pack(product, out_ref):
    for t in range(product.shape[1] // LANES):
        tile = product[:, t * LANES : (t + 1) * LANES]
        for s, block in enumerate(interleave(tile[:LANES], tile[LANES:])):
            out_ref[2 * t + s] = block.astype(BF)


def project_kernel(ids_ref, *refs):
    *sources, wo_ref, mixed_ref, branch_ref = refs
    unpack(ids_ref, sources, None, mixed_ref, 0)
    branch_ref[...] = nn(mixed_ref[...], wo_ref[...]).astype(BF)


def forward_kernel(sources, ids_ref, *refs):
    if sources:
        own, got, refs = refs[:sources], refs[sources : 2 * sources], refs[2 * sources :]
        wo_ref, wo_got_ref, zero_ref, gains_ref, wu_ref, dact_ref, norm_ref, mixed_out, *refs = refs
        *refs, wo_buf, mixed, wo_sems = refs
        me = ids_ref[9]
        wo_loads = [
            pltpu.make_async_copy(wo_ref, wo_buf.at[me], wo_sems.at[0]),
            pltpu.make_async_copy(wo_got_ref, wo_buf.at[1 - me], wo_sems.at[1]),
        ]
        for copy in wo_loads:
            copy.start()
    else:
        own_ref, got_ref, zero_ref, gains_ref, wu_ref, dact_ref, norm_ref, *refs = refs
    one_out, pre_out, act_out, other_out, *rest = refs
    count = (len(rest) - 9) // 2
    turned_out, turned = rest[:count], rest[count : 2 * count]
    one_ref, weights, grads, pre_ref, act_ref, normed_ref, hold, into, out_of = rest[2 * count :]
    chunks, _, block = grads.shape
    per_half = chunks // 2
    loads, stores = [], []
    for c in range(chunks):
        span = slice(c * block, (c + 1) * block)
        loads.append(
            (
                pltpu.make_async_copy(wu_ref.at[:, span], weights.at[c], into.at[2 * c]),
                pltpu.make_async_copy(dact_ref.at[:, span], grads.at[c], into.at[2 * c + 1]),
            )
        )
        for copy in loads[-1]:
            copy.start()

    def store(source, target):
        stores.append(pltpu.make_async_copy(source, target, out_of.at[len(stores)]))
        stores[-1].start()

    if sources:
        unpack(ids_ref, own, None, mixed.at[me], 0)
        unpack(ids_ref, got, None, mixed.at[1 - me], 0)
        mixed_out[...] = mixed[me]
        for copy in wo_loads:
            copy.wait()
        branch = nn(mixed[0], wo_buf[0]) + nn(mixed[1], wo_buf[1])
    else:
        branch = own_ref[...].astype(F32) + got_ref[...].astype(F32)
    hidden = zero_ref[...] + branch
    one_ref[...] = hidden
    store(one_ref, one_out)
    unit, _ = norm_parts(hidden)
    normed = unit * gains_ref[1:2, :]
    normed_ref[...] = normed.astype(BF)
    emit_turned(normed, ids_ref, turned, hold)
    for source, target in zip(turned, turned_out):
        store(source, target)
    total = None
    for c in range(chunks):
        span = slice(c * block, (c + 1) * block)
        half, place = c // per_half, slice(c % per_half * block, (c % per_half + 1) * block)
        for copy in loads[c]:
            copy.wait()
        pre = nn(normed_ref[...], weights[c])
        chance = 0.5 * (1.0 + lax.erf(pre * (1.0 / math.sqrt(2.0))))
        slope = chance + pre * jnp.exp(-0.5 * pre * pre) * (1.0 / math.sqrt(2.0 * math.pi))
        act_ref[half, :, place] = (pre * chance).astype(BF)
        store(act_ref.at[half, :, place], act_out.at[half, :, place])
        d_pre = (grads[c].astype(F32) * slope).astype(BF)
        pre_ref[:, span] = d_pre
        store(pre_ref.at[:, span], pre_out.at[:, span])
        part = nt(d_pre, weights[c])
        total = part if total is None else total + part
    store(act_ref.at[1 - ids_ref[0]], other_out)
    norm_ref[...] = total.astype(BF)
    for copy in stores:
        copy.wait()


def second_kernel(ids_ref, one_ref, two_ref, own_ref, got_ref, gains_ref, wo_ref, d_ref, gain_ref, *rest):
    heads_ref, *turned, hold = rest
    unit, inverse = norm_parts(one_ref[...])
    grad = own_ref[...].astype(F32) + got_ref[...].astype(F32)
    back, gain = norm_back(unit, inverse, gains_ref[1:2, :], grad)
    gain_ref[...] = gain
    d_one = two_ref[...] + back
    d_ref[...] = d_one
    pack(nt(d_one.astype(BF), wo_ref[...]), heads_ref)
    emit_turned(d_one, ids_ref, turned, hold)


def head_kernel(ids_ref, one_ref, own_ref, got_ref, wh_ref, pred_ref, *rest):
    turned, hold = rest[:-1], rest[-1]
    hidden = one_ref[...] + (own_ref[...].astype(F32) + got_ref[...].astype(F32))
    low = hidden.astype(BF)
    for item in range(pred_ref.shape[0]):
        pred_ref[item] = nt(wh_ref[...], low[item * LANES : (item + 1) * LANES])
    emit_turned(hidden, ids_ref, turned, hold)


def third_kernel(count, ids_ref, *refs):
    sources, (wq_ref, dqkv_ref, norm_ref) = refs[:count], refs[count:]
    width = wq_ref.shape[2]
    total = None
    for c in range(3):
        unpack(ids_ref, sources, c, dqkv_ref, c * width)
        part = nt(dqkv_ref[:, c * width : (c + 1) * width], wq_ref[c])
        total = part if total is None else total + part
    norm_ref[...] = total.astype(BF)


def last_kernel(cols, ids_ref, zero_ref, done_ref, own_ref, got_ref, gains_ref, gain_two_ref, patches_ref, we_ref,
                pos_send, pos_keep, fields_ref, edge_ref, *rest):
    embed, (rows_ref, pos_ref, hold) = rest[:-3], rest[-3:]
    unit, inverse = norm_parts(zero_ref[...])
    grad = own_ref[...].astype(F32) + got_ref[...].astype(F32)
    back, gain = norm_back(unit, inverse, gains_ref[0:1, :], grad)
    d_zero = done_ref[...] + back
    low = d_zero.astype(BF)
    items, variables, height = edge_ref.shape
    pos = d_zero[0:LANES]
    for item in range(1, items):
        pos = pos + d_zero[item * LANES : (item + 1) * LANES]
    width = pos_ref.shape[2]
    for k in range(2):
        pos_ref[k] = pos[:, k * width : (k + 1) * width].astype(BF)
    pos_send[...] = pos_ref[1 - ids_ref[1]]
    pos_keep[...] = pos_ref[ids_ref[1]]
    features = patches_ref.shape[0]
    rows_ref[...] = jnp.zeros_like(rows_ref)
    rows_ref[0:features, :] = nn(patches_ref[...], low)
    rows_ref[features : features + 1, :] = gain
    rows_ref[features + 1 : features + 2, :] = gain_two_ref[...]
    emit_turned(rows_ref[...], ids_ref, embed, hold)
    half = height // PATCH
    row = lax.broadcasted_iota(jnp.int32, (LANES, height), 0)
    lane = lax.broadcasted_iota(jnp.int32, (LANES, height), 1)
    fields_ref[...] = jnp.zeros_like(fields_ref)
    order = feature_order(variables, True)
    for item in range(items):
        d_patches = nt(we_ref[...], low[item * LANES : (item + 1) * LANES])
        high = d_patches.astype(BF)
        rest = (d_patches - high.astype(F32)).astype(BF)
        high, rest = nn(order, high).astype(BF), nn(order, rest).astype(BF)
        for j in range(2):
            total = None
            for a in range(PATCH):
                place = jnp.where(
                    (row // half == j) & (lane == PATCH * (row % half) + a), 1.0, 0.0
                ).astype(BF)
                span = slice(a * 2 * variables, (a + 1) * 2 * variables)
                part = nn(high[span], place) + nn(rest[span], place)
                total = part if total is None else total + part
            for b in range(PATCH):
                block = total[b * variables : (b + 1) * variables]
                column = 2 * j + b - 1
                if column < 0:
                    edge_ref[item] = block.astype(BF)
                else:
                    fields_ref[item, pl.ds(column, variables, stride=cols), :] = block


def down_kernel(act_ref, wd_ref, out_ref):
    width = act_ref.shape[2]
    total = nn(act_ref[0], wd_ref[0:width, :]) + nn(act_ref[1], wd_ref[width:, :])
    out_ref[...] = total.astype(BF)


def pin(xs, after):
    def body(*refs):
        pass

    anywhere = pl.BlockSpec(memory_space=pl.ANY)
    several = isinstance(xs, (list, tuple))
    xs = list(xs) if several else [xs]
    out = pl.pallas_call(
        body,
        out_shape=[pltpu.HBM(x.shape, x.dtype) for x in xs],
        in_specs=[anywhere] * (len(xs) + len(after)),
        out_specs=[anywhere] * len(xs),
        input_output_aliases={k: k for k in range(len(xs))},
        name="pin",
    )(*[pltpu.with_memory_space_constraint(x, pltpu.HBM) for x in xs], *after)
    return out if several else out[0]


def product_of(own, got, b_own, b_got):
    parts, rows, tokens = own.shape
    total = nn(own[...].reshape(parts * rows, tokens), b_own)
    return total + nn(got[...].reshape(parts * rows, tokens), b_got)


def split_dp(ids_ref, hold, send, keep, columns):
    half = hold.shape[0] // 2
    for out, at in ((send, 1 - ids_ref[1]), (keep, ids_ref[1])):
        for k in range(half):
            out[k, :, 0:columns] = hold[at * half + k]


def split_near(ids_ref, hold, send, keep, columns):
    for out, at in ((send, 1 - ids_ref[2]), (keep, ids_ref[2])):
        for k in range(hold.shape[0] // 2):
            out[k, :, 0:columns] = hold[2 * k + at]


def plus(a, b):
    return (a[...].astype(F32) + b[...].astype(F32)).astype(BF)


def grads_ff_kernel(ids_ref, at_own, at_got, pre_own, pre_got, ct_own, ct_got, act_own, act_got,
                    send_a, keep_a, send_b, keep_b, hold, inner):
    parts, rows, total = hold.shape
    columns = total - keep_b.shape[2]
    product = product_of(at_own, at_got, pre_own[...], pre_got[...])
    hold[...] = product.astype(BF).reshape(hold.shape)
    split_dp(ids_ref, hold.at[:, :, 0:columns], send_a, keep_a, columns)
    split_near(ids_ref, hold.at[:, :, columns:], send_b, keep_b, total - columns)
    product = (nn(ct_own[...], act_own[ids_ref[0]]) + nn(ct_got[...], act_got[...])).astype(BF)
    tiles, groups = inner.shape[1], inner.shape[3] // LANES
    for k in range(2):
        for q in range(tiles):
            for g in range(groups):
                inner[k, q, :, g * LANES : (g + 1) * LANES] = product[
                    g * rows : (g + 1) * rows, (k * tiles + q) * LANES : (k * tiles + q + 1) * LANES
                ]
    for q in range(tiles):
        send_a[q, :, columns:] = inner[1 - ids_ref[1], q]
        keep_a[q, :, columns:] = inner[ids_ref[1], q]


def fold_ff_kernel(ids_ref, keep_a, got_a, keep_b, got_b, send_a, left_a, send_b, left_b, hold, hold_b):
    columns = hold.shape[2]
    extra = keep_a.shape[2] - columns
    hold[...] = plus(keep_a.at[:, :, 0:columns], got_a.at[:, :, 0:columns])
    split_near(ids_ref, hold, send_a, left_a, columns)
    for q in range(keep_a.shape[0]):
        total = plus(keep_a.at[q, :, columns:], got_a.at[q, :, columns:])
        at = columns + q % 2 * extra
        for out in (send_a, left_a):
            out[q // 2, :, at : at + extra] = total
    hold_b[...] = plus(keep_b, got_b)
    split_dp(ids_ref, hold_b, send_b, left_b, hold_b.shape[2])


def merge_ff_kernel(ids_ref, keep_a, got_a, keep_b, got_b, send, left, hold):
    columns = hold.shape[2] - keep_b.shape[2]
    extra = keep_a.shape[2] - columns
    hold[:, :, 0:columns] = plus(keep_a.at[:, :, 0:columns], got_a.at[:, :, 0:columns])
    hold[:, :, columns:] = plus(keep_b, got_b)
    far = ids_ref[3]
    width = hold.shape[2]
    send[:, 0:width] = hold[1 - far]
    left[:, 0:width] = hold[far]
    for k in range(2):
        total = plus(keep_a.at[k, :, columns:], got_a.at[k, :, columns:])
        at = width + k * extra
        for out in (send, left):
            out[:, at : at + extra] = total


def grads_oh_kernel(ids_ref, one_own, one_got, mixed_own, mixed_got, two_own, two_got, ct_own, ct_got,
                    send, keep, hold):
    width, features = mixed_own.shape[1], ct_own.shape[0]
    shape3 = hold.shape[:2]
    product = product_of(one_own, one_got, mixed_own[...], mixed_got[...])
    hold[:, :, 0:width] = product.astype(BF).reshape(*shape3, width)
    hold[:, :, width:] = jnp.zeros((*shape3, hold.shape[2] - width), BF)
    product = product_of(
        two_own, two_got, ct_own[...].astype(F32).T.astype(BF), ct_got[...].astype(F32).T.astype(BF)
    )
    hold[:, :, width : width + features] = product.astype(BF).reshape(*shape3, features)
    split_dp(ids_ref, hold, send, keep, hold.shape[2])


def grads_q_kernel(ids_ref, at_own, at_got, b_own, b_got, send_a, keep_a, send_b, keep_b, hold):
    cut, total = keep_a.shape[2], hold.shape[2]
    hold[...] = product_of(at_own, at_got, b_own[...], b_got[...]).astype(BF).reshape(hold.shape)
    split_dp(ids_ref, hold.at[:, :, 0:cut], send_a, keep_a, cut)
    split_near(ids_ref, hold.at[:, :, cut:], send_b, keep_b, total - cut)


def fold_q_kernel(ids_ref, keep_a, got_a, keep_b, got_b, up_keep, up_got, oh_keep, oh_got, embed_own, embed_got,
                  send_a, left_a, send_b, left_b, send_o, left_o, hold_a, hold_b, hold_o, hold_e):
    hold_a[...] = plus(keep_a, got_a)
    split_near(ids_ref, hold_a, send_a, left_a, hold_a.shape[2])
    hold_b[...] = plus(keep_b, got_b)
    columns = hold_b.shape[2]
    split_dp(ids_ref, hold_b, send_b, left_b, columns)
    hold_o[...] = plus(oh_keep, oh_got)
    for out, at in ((send_o, 1 - ids_ref[3]), (left_o, ids_ref[3])):
        for k in range(2):
            out[k] = hold_o[2 * at + k]
    hold_e[...] = plus(embed_own, embed_got)
    width = hold_e.shape[2]
    for out, at in ((send_b, 1 - ids_ref[1]), (left_b, ids_ref[1])):
        for k in range(4):
            start = columns + k % 2 * width
            out[k // 2, :, start : start + width] = hold_e[4 * at + k]
    start = columns + 2 * width
    half = send_b.shape[2] - start
    for k in range(2):
        at = up_keep.shape[1] - (2 - k) * half
        total = plus(up_keep.at[:, at : at + half], up_got.at[:, at : at + half])
        for out in (send_b, left_b):
            out[k, :, start:] = total


def merge_q_kernel(ids_ref, keep_a, got_a, keep_b, got_b, oh_keep, oh_got,
                   send, left, pair_ref, near_ref, embed_both, oh_left, hold, hold_e, hold_o):
    width = embed_both.shape[1]
    half = pair_ref.shape[2] // 2
    first = keep_a.shape[2]
    columns = keep_b.shape[2] - half - 2 * width
    total = hold.shape[2]
    hold[:, :, 0:first] = plus(keep_a, got_a)
    hold[:, :, first:] = plus(keep_b.at[:, :, 0:columns], got_b.at[:, :, 0:columns])
    hold_o[...] = plus(oh_keep, oh_got)
    for k in range(4):
        span = slice(columns + k % 2 * width, columns + (k % 2 + 1) * width)
        hold_e[k] = plus(keep_b.at[k // 2, :, span], got_b.at[k // 2, :, span])
    far, near = ids_ref[3], ids_ref[2]
    for out, at in ((send, 1 - far), (left, far)):
        out[:, 0:total] = hold[at]
        out[:, total:] = hold_e[2 * at + near]
    near_ref[:, 0:width] = hold_e[2 * far + 1 - near]
    near_ref[:, width:] = hold_o[1 - near]
    oh_left[...] = hold_o[near]
    embed_both[...] = hold_e[2 * (1 - far) + 1 - near]
    for k in range(2):
        span = slice(k * half, (k + 1) * half)
        pair_ref[0, :, span] = keep_b[k, :, columns + 2 * width :]
        pair_ref[1, :, span] = got_b[k, :, columns + 2 * width :]


def expand(ids_ref, rows_ref, pair_own, pair_got, out_ref, block):
    rows = rows_ref.shape[0]
    groups = block.shape[0] // rows
    tiles = block.shape[1] // LANES
    for a, b in ((0, 0), (0, 1), (1, 0), (1, 1)):
        source = pair_got if a else pair_own
        for q in range(tiles):
            for g in range(groups):
                at = (q * groups + g) * LANES
                block[g * rows : (g + 1) * rows, q * LANES : (q + 1) * LANES] = source[b, :, at : at + LANES]
        core, dp = (1 - ids_ref[0] if a else ids_ref[0]), (1 - ids_ref[1] if b else ids_ref[1])
        at = pl.multiple_of((core * 2 + dp) * block.shape[1], LANES)
        out_ref[:, pl.ds(at, block.shape[1])] = nn(rows_ref[...], block[...])


def insert_east(cols, fields_ref, east_ref, out_ref):
    variables = east_ref.shape[1]
    out_ref[...] = fields_ref[...]
    for item in range(east_ref.shape[0]):
        out_ref[item, pl.ds(cols - 1, variables, stride=cols), :] = east_ref[item].astype(F32)


def close_kernel(cols, ids_ref, fields_ref, east_ref, pos_ref, pos_got_ref, *refs):
    outs = refs
    if len(refs) > 2:
        (up_ref, up_got_ref, rows_ref, pair_own, pair_got), outs, block = refs[:5], refs[5:-1], refs[-1]
        width = outs[2].shape[1]
        outs[2][...] = up_ref[:, 0:width].astype(F32) + up_got_ref[:, 0:width].astype(F32)
        expand(ids_ref, rows_ref, pair_own, pair_got, outs[3], block)
    insert_east(cols, fields_ref, east_ref, outs[0])
    outs[1][...] = pos_ref[...].astype(F32) + pos_got_ref[...].astype(F32)


def end_kernel(*refs):
    if len(refs) > 3:
        (near_ref, both_ref, oh_ref, keep_ref, got_ref), refs = refs[:5], refs[5:]
        out_ref, head_ref, grad_ref = refs[2:]
        embed_width = both_ref.shape[1]
        both = keep_ref[...].astype(F32) + got_ref[...].astype(F32)
        width = grad_ref.shape[2]
        for c in range(3):
            grad_ref[c] = both[:, c * width : (c + 1) * width]
        total = both[:, 3 * width :] + near_ref[:, 0:embed_width].astype(F32) + both_ref[...].astype(F32)
        both = oh_ref[...].astype(F32) + near_ref[:, embed_width:].astype(F32)
        out_ref[...] = both[:, 0:width]
        head_ref[...] = both[:, width : width + head_ref.shape[1]]
    else:
        total, refs = jnp.sum(refs[0][...].astype(F32), axis=0), refs[1:]
    features = refs[0].shape[1]
    refs[0][...] = total[:, 0:features]
    refs[1][...] = total[:, LANES:].T[features - LANES : features - LANES + 2, :]


def local(
    dataset,
    indices,
    run_count,
    run_mean,
    run_var,
    w_embed,
    pos_embed,
    gains,
    w_qkv,
    w_out,
    w_up,
    w_down,
    w_head,
    cotangent,
):
    items = indices.shape[0]
    variables, height, columns = dataset.shape[1:]
    dp, lon = lax.axis_size("dp"), lax.axis_size("lon")
    everyone = dp * lon
    width = w_embed.shape[1]
    local_width = w_qkv.shape[2]
    heads = local_width // HDIM
    item_tokens = cotangent.shape[1]
    tokens = items * item_tokens
    features = w_embed.shape[0]
    hidden_units = w_up.shape[1]
    scale = 1.0 / math.sqrt(HDIM)
    group, far = heads, lon // heads
    groups = [[group * g + i for i in range(group)] for g in range(far)]
    across = [[i + group * g for g in range(far)] for i in range(group)]
    assert items * HDIM == LANES and item_tokens == LANES and height == LANES and columns == 4
    lon_at, dp_at = lax.axis_index("lon"), lax.axis_index("dp")
    ids = [lon_at % 2, dp_at, lon_at // 2 % 2, lon_at // 4 % 2, *[lon_at // 2 ^ k for k in range(4)], dp_at * lon + lon_at, lax.axis_index("mp")]
    ids = jnp.stack(ids).astype(jnp.int32)
    paired = dp == 2 and lon == 8
    parts, rows = width // (2 * (width // everyone)), width // everyone
    turned_shape = (
        [shape((parts, rows, tokens))] * 2 if paired else [shape((width, tokens))]
    )
    turned_hold = pltpu.VMEM((parts, 2, rows, tokens) if paired else (8, LANES), BF)

    alone = dict(axis_index_groups=groups) if far > 1 else {}

    vmem, smem = pl.BlockSpec(memory_space=pltpu.VMEM), pl.BlockSpec(memory_space=pltpu.SMEM)
    assert dp == 2

    data = dataset.transpose(0, 1, 3, 2).reshape(dataset.shape[0], variables * columns, height)
    fields, edge, moments, _ = call(
        moments_kernel,
        "moments",
        [
            warm((items, variables * columns, height), F32),
            warm((items, variables, height)),
            warm((8, LANES) if paired else (everyone, 8, LANES), F32),
        ],
        indices, data,
        in_specs=[pl.BlockSpec(memory_space=pltpu.SMEM), pl.BlockSpec(memory_space=pl.ANY)],
        scratch=[pltpu.VMEM((LANES, LANES), F32), pltpu.SemaphoreType.DMA((items,))],
    )
    edge = from_behind(edge, "lon", 1)
    if paired:
        row = lax.broadcasted_iota(jnp.int32, moments.shape, 0)
        held = float(items * height * columns)
        for axis, distance in (("lon", 1), ("lon", 2), ("lon", 4), ("dp", 1)):
            got = swap(moments, axis, distance)
            apart = jnp.square(moments[0:1] - got[0:1]) * (0.5 * held)
            moments = jnp.where(row == 0, 0.5 * (moments + got), moments + got + apart)
            held = 2.0 * held
    else:
        moments = lax.all_to_all(moments, ("dp", "lon"), 0, 0)
    wh_turned = w_head.T

    out = call(
        functools.partial(start_kernel, float(items * height * columns), everyone),
        "start",
        [
            *[shape((1, variables), F32)] * 3,
            shape((tokens, width), F32),
            shape((features, tokens)),
            *([warm((2, 3, item_tokens, LANES))] * 4 if paired else [shape((heads, 3, item_tokens, LANES))]),
            *turned_shape,
        ],
        ids, Warm(moments), *[r.reshape(1, variables) for r in (run_count, run_mean, run_var)],
        Warm(fields), Warm(edge), w_embed, pos_embed, gains, w_qkv,
        in_specs=[smem, *[vmem] * 9, pl.BlockSpec(memory_space=pl.ANY)],
        scratch=[
            pltpu.VMEM((LANES, LANES), F32),
            pltpu.VMEM((8, LANES), F32),
            turned_hold,
            pltpu.VMEM(w_qkv.shape, BF),
            pltpu.SemaphoreType.DMA,
            pltpu.VMEM((heads, 3, item_tokens, LANES), BF),
        ],
        flops=2 * tokens * width * (features + 3 * local_width),
    )
    count = 4 if paired else 1
    stats, (hidden_zero, patches), packed = out[:3], out[3:5], out[5 : 5 + count]
    normed_one, token = out[5 + count : -1], out[-1]

    def along(messages):
        return [messages[0], *[swap(messages[k], "lon", 2 * k) for k in range(1, count)]]

    if paired:
        own = along(packed)
    else:
        sent = lax.all_to_all(packed[0], "lon", 0, 0, **alone)
        kv = sent
        if far > 1:
            kv = lax.all_gather(sent, "lon", axis=0, tiled=True, axis_index_groups=across)

    if paired:
        wo_got, normed_got = swap(w_out, "mp", 1), swap(normed_one[1], "lon", 1)
        other = [swap(x, "lon", 1) for x in own]
    if paired:
        attended, kept, token = pair_attend(own, other, items, scale, [token, normed_got])
        attended = along(attended)
    else:
        attended, attended_t, weights_t, token = attend(sent, kv, items, scale, [token])
        attended = [lax.all_to_all(attended, "lon", 0, 0, **alone)]
    anywhere = pl.BlockSpec(memory_space=pl.ANY)
    d_two, d_act, ct_turned, *mine, token = call(
        cotangent_kernel,
        "cotangent",
        [
            shape((tokens, width), F32),
            shape((tokens, hidden_units)),
            shape((features, tokens)),
            *[shape((rows, features))] * paired,
        ],
        ids, cotangent.transpose(0, 2, 1), wh_turned, w_down,
        after=[token],
        scratch=[pltpu.VMEM((everyone, rows, features), BF)] * paired,
        flops=2 * tokens * width * (features + hidden_units),
    )

    if paired:
        ct_got = swap(ct_turned, "lon", 1)
        attended[0] = pin(attended[0], [token])
        attended += [swap(x, "mp", 1) for x in attended]
    if paired:
        branches = [attended[0], *[Warm(x) for x in attended[1:]], w_out, Warm(wo_got)]
    else:
        mixed, branch, token = call(
            project_kernel,
            "project",
            [shape((tokens, local_width)), warm((tokens, width))],
            ids, *attended, w_out,
            after=[token],
            flops=2 * tokens * width * local_width,
        )
        branches = [Warm(branch), Warm(swap(branch, "mp", 1))]
    block = min(512, hidden_units // 2)
    chunks = hidden_units // block
    out = call(
        functools.partial(forward_kernel, count if paired else 0),
        "forward",
        [
            warm((tokens, width)),
            *[shape((tokens, local_width))] * paired,
            shape((tokens, width), F32),
            shape((tokens, hidden_units)),
            shape((2, tokens, hidden_units // 2)),
            shape((tokens, hidden_units // 2)),
            *turned_shape,
        ],
        ids, *branches, Warm(hidden_zero), gains, w_up, d_act,
        after=[token],
        in_specs=[
            smem,
            *([*[vmem] * (len(branches) - 2), anywhere, anywhere] if paired else [vmem] * 2),
            vmem,
            vmem,
            anywhere,
            anywhere,
        ],
        out_specs=[*[vmem] * (1 + paired), *[anywhere] * (4 + len(turned_shape))],
        scratch=[
            *[pltpu.VMEM(x.shape, BF) for x in turned_shape],
            pltpu.VMEM((tokens, width), F32),
            pltpu.VMEM((chunks, width, block), BF),
            pltpu.VMEM((chunks, tokens, block), BF),
            pltpu.VMEM((tokens, hidden_units), BF),
            pltpu.VMEM((2, tokens, hidden_units // 2), BF),
            pltpu.VMEM((tokens, width), BF),
            turned_hold,
            pltpu.SemaphoreType.DMA((2 * chunks,)),
            pltpu.SemaphoreType.DMA((2 + len(turned_shape) + 2 * chunks,)),
            *[
                pltpu.VMEM((2, *w_out.shape), BF),
                pltpu.VMEM((2, tokens, local_width), BF),
                pltpu.SemaphoreType.DMA((2,)),
            ] * paired,
        ],
        limit=32,
        flops=4 * tokens * width * hidden_units,
    )
    d_norm, *out, token = out
    if paired:
        mixed, out = out[0], out[1:]
        mixed_got = swap(mixed, "lon", 1)
    hidden_one, d_pre, activated, act_send = out[:4]
    normed_two = out[4:]
    d_norm_got = swap(d_norm, "mp", 1)
    half = hidden_units // 2
    if paired:
        inner_columns = features // rows * LANES
        first = half - LANES
        out_a = shape((parts // 2, rows, first + inner_columns))
        out_b = shape((parts // 2, rows, hidden_units - first))
        send_a, keep_a, send_b, keep_b, token = call(
            grads_ff_kernel,
            "grads_ff",
            [Warm(out_a), out_a, Warm(out_b), out_b],
            ids, normed_two[0], Warm(swap(normed_two[1], "lon", 1)), d_pre, Warm(swap(d_pre, "lon", 1)),
            ct_turned, Warm(ct_got), activated, Warm(swap(act_send, "lon", 1)),
            after=[token],
            scratch=[
                pltpu.VMEM((parts, rows, hidden_units), BF),
                pltpu.VMEM((2, parts // 2, rows, inner_columns), BF),
            ],
            limit=32,
            flops=2 * tokens * (width + features) * hidden_units,
        )
        got_a, got_b = swap(send_a, "dp", 1), swap(send_b, "lon", 2)
    forward, token = call(
        down_kernel,
        "down",
        [shape((tokens, width))],
        activated, Warm(w_down),
        after=[token, *([mixed_got] if paired else [])],
        flops=2 * tokens * width * hidden_units,
    )

    out = call(
        second_kernel,
        "second",
        [
            shape((tokens, width), F32),
            shape((1, width), F32),
            warm((heads, item_tokens, LANES)),
            *turned_shape,
        ],
        ids, Warm(hidden_one), Warm(d_two), Warm(d_norm), Warm(d_norm_got), gains, Warm(w_out),
        after=[token],
        scratch=[turned_hold],
        flops=2 * tokens * width * local_width,
    )
    d_one, gain_two, d_mixed = out[0], out[1], out[2:3]
    d_one_turned, token = out[3:-1], out[-1]
    if paired:
        d_one_got = swap(d_one_turned[1], "lon", 1)
    if paired:
        chips = [[2 * k + c for k in range(lon // 2)] for c in range(2)]
        d_heads = lax.all_to_all(
            d_mixed[0].reshape(lon // 2, 2, item_tokens, LANES), "lon", 0, 0, axis_index_groups=chips
        )
    else:
        d_heads = lax.all_to_all(d_mixed[0], "lon", 0, 0, **alone)
    forward_got = swap(forward, "mp", 1)
    if paired:
        out_a = shape((2, rows, first + 2 * inner_columns))
        out_b = shape((2, rows, hidden_units - first))
        send_a, keep_a, send_b, keep_b, token = call(
            fold_ff_kernel,
            "fold_ff",
            [out_a, out_a, out_b, out_b],
            ids, keep_a, Warm(got_a), keep_b, Warm(got_b),
            after=[token],
            scratch=[
                pltpu.VMEM((parts // 2, rows, first), BF),
                pltpu.VMEM((parts // 2, rows, hidden_units - first), BF),
            ],
        )
        send_a, send_b = pin([send_a, send_b], [d_heads])
        got_a, got_b = swap(send_a, "lon", 2), swap(send_b, "dp", 1)

    if paired:
        back, cross, token = pair_attend_back(ids, kept, d_heads, items, scale, [token])
        *back, token = call(
            combine_kernel,
            "combine",
            [warm(x.shape) for x in back],
            *back, Warm(swap(pin(cross, [got_a, got_b, forward_got]), "lon", 1)),
            after=[token],
        )
        back = along(back)
    else:
        back, token = attend_back(sent, kv, d_heads, attended_t, weights_t, items, scale, [token])
        if far > 1:
            d_query, d_kv = back
            d_kv = lax.psum_scatter(
                d_kv, "lon", scatter_dimension=0, tiled=True, axis_index_groups=across
            ).astype(BF)
            back = [jnp.concatenate([d_query[:, None], d_kv], axis=1)]
        back = [lax.all_to_all(back[0], "lon", 0, 0, **alone)]
    out = call(
        head_kernel,
        "head",
        [shape((items, features, item_tokens), F32), *turned_shape],
        ids, hidden_one, forward, Warm(forward_got), wh_turned,
        after=[token],
        scratch=[turned_hold],
        flops=2 * tokens * width * features,
    )
    pred, hidden_turned, token = out[0].transpose(0, 2, 1), list(out[1:-1]), out[-1]
    if paired:
        up_send, up_keep, token = call(
            merge_ff_kernel,
            "merge_ff",
            [shape((rows, hidden_units + 4 * inner_columns))] * 2,
            ids, keep_a, Warm(got_a), keep_b, got_b,
            after=[token],
            scratch=[pltpu.VMEM((2, rows, hidden_units), BF)],
        )
    d_qkv, d_norm, token = call(
        functools.partial(third_kernel, count),
        "third",
        [shape((tokens, 3 * local_width)), warm((tokens, width))],
        ids, *[Warm(x) for x in back], Warm(w_qkv),
        after=[token],
        flops=6 * tokens * width * local_width,
    )
    d_norm_got = swap(d_norm, "mp", 1)
    if paired:
        up_send, hidden_turned[1] = pin([up_send, hidden_turned[1]], [token])
        up_got = swap(up_send, "lon", 4)
        wide = local_width + 2 * LANES
        cut = 3 * local_width // 2 + LANES
        first, second = (shape((parts // 2, rows, c)) for c in (cut, 3 * local_width - cut))
        send_a, keep_a, send_b, keep_b, token = call(
            grads_q_kernel,
            "grads_q",
            [first, first, second, second],
            ids, normed_one[0], normed_got, d_qkv, Warm(swap(d_qkv, "lon", 1)),
            after=[token],
            scratch=[pltpu.VMEM((parts, rows, 3 * local_width), BF)],
            flops=6 * tokens * width * local_width,
        )
        oh_send, oh_keep, token = call(
            grads_oh_kernel,
            "grads_oh",
            [shape((parts // 2, rows, wide))] * 2,
            ids, d_one_turned[0], Warm(d_one_got), mixed, Warm(mixed_got),
            hidden_turned[0], Warm(swap(hidden_turned[1], "lon", 1)), ct_turned, Warm(ct_got),
            after=[token],
            scratch=[pltpu.VMEM((parts, rows, wide), BF)],
            flops=2 * tokens * width * wide,
        )
        oh_got = swap(oh_send, "dp", 1)
        got_a, got_b = swap(send_a, "dp", 1), swap(send_b, "lon", 2)

    out = call(
        functools.partial(last_kernel, columns),
        "last",
        [
            *[shape((item_tokens, width // 2))] * 2,
            shape((items, variables * columns, height), F32),
            shape((items, variables, height)),
            *([shape((parts, rows, 2 * LANES))] * 2 if paired else [shape((width, 2 * LANES))]),
        ],
        ids, Warm(hidden_zero), Warm(d_one), Warm(d_norm), Warm(d_norm_got), gains, gain_two, patches, w_embed,
        after=[token],
        scratch=[
            pltpu.VMEM((2 * LANES, width), F32),
            pltpu.VMEM((2, item_tokens, width // 2), BF),
            pltpu.VMEM((parts, 2, rows, 2 * LANES) if paired else (8, LANES), BF),
        ],
        flops=4 * tokens * width * features,
    )
    pos_send, pos, d_fields, d_edge = out[:4]
    embed, token = out[4:-1], out[-1]
    if not paired:
        east, pos_got = from_behind(d_edge, "lon", -1), swap(pos_send, "dp", 1)
    more, more_outs, more_scratch, rest, rest_outs = [], [], [], [], []
    if paired:
        embed_width = embed[0].shape[2]
        step_a, side = shape((2, rows, cut)), shape((2, rows, wide))
        step_b = shape((2, rows, 3 * local_width - cut + 2 * embed_width + 2 * inner_columns))
        send_a, keep_a, send_b, keep_b, oh_send, oh_keep, token = call(
            fold_q_kernel,
            "fold_q",
            [Warm(step_a), step_a, Warm(step_b), step_b, Warm(side), side],
            ids, keep_a, Warm(got_a), keep_b, Warm(got_b), up_keep, Warm(up_got), oh_keep, Warm(oh_got),
            embed[0], Warm(swap(embed[1], "lon", 1)),
            after=[token],
            scratch=[
                pltpu.VMEM(keep_a.shape, BF),
                pltpu.VMEM(keep_b.shape, BF),
                pltpu.VMEM(oh_keep.shape, BF),
                pltpu.VMEM(embed[0].shape, BF),
            ],
        )
        got_a, got_b, oh_got = swap(send_a, "lon", 2), swap(send_b, "dp", 1), swap(oh_send, "lon", 4)
        east = from_behind(pin(d_edge, [token]), "lon", -1)
        final, block = shape((rows, 3 * local_width + embed_width)), shape((rows, embed_width))
        send, keep, pair, near_send, embed_both, oh_keep, token = call(
            merge_q_kernel,
            "merge_q",
            [
                Warm(final),
                final,
                shape((2, rows, 4 * inner_columns)),
                warm((rows, embed_width + wide)),
                Warm(block),
                shape((rows, wide)),
            ],
            ids, keep_a, Warm(got_a), keep_b, Warm(got_b), oh_keep, Warm(oh_got),
            after=[token, east],
            scratch=[
                pltpu.VMEM((2, rows, 3 * local_width), BF),
                pltpu.VMEM((4, *block.shape), BF),
                pltpu.VMEM((2, rows, wide), BF),
            ],
        )
        pos_got = swap(pin(pos_send, [token]), "dp", 1)
        more = [up_keep, Warm(up_got), mine[0], pair, Warm(swap(pair, "lon", 1))]
        more_outs = [shape((rows, hidden_units), F32)] * 2
        more_scratch = [pltpu.VMEM((features, hidden_units // 4), BF)]
        rest = [
            Warm(swap(near_send, "lon", 2)), Warm(swap(embed_both, "lon", 6)), oh_keep,
            keep, Warm(swap(send, "lon", 4)),
        ]
        rest_outs = [
            shape((rows, local_width), F32),
            shape((rows, features), F32),
            shape((3, rows, local_width), F32),
        ]
    else:
        rest = [lax.all_to_all(embed[0].reshape(everyone, rows, 2 * LANES), ("dp", "lon"), 0, 0)]
    *closed, token = call(
        functools.partial(close_kernel, columns),
        "close",
        [shape(d_fields.shape, F32), shape(pos.shape, F32), *more_outs],
        ids, d_fields, east, pos, Warm(pos_got), *more,
        after=[token],
        scratch=more_scratch,
    )
    *ended, token = call(
        end_kernel,
        "end",
        [shape((rows, features), F32), shape((2, rows), F32), *rest_outs],
        *rest,
        after=[token],
    )
    if paired:
        grad_up, grad_down, (grad_out, grad_head, grad_qkv) = closed[2], closed[3], ended[2:]
    else:
        flat = activated.transpose(1, 0, 2).reshape(tokens, hidden_units)
        grad_up = scatter(nn(normed_two[0], d_pre))
        grad_down = scatter(nn(d_two.T.astype(BF), flat))
        grad_out = scatter(nn(d_one_turned[0], mixed))
        grad_head = scatter(nt(hidden_turned[0], ct_turned))
        grad_qkv = scatter(nn(normed_one[0], d_qkv)).reshape(rows, 3, local_width).transpose(1, 0, 2)
    return (
        pred,
        *[x.reshape(variables) for x in stats],
        closed[0].reshape(items, variables, columns, height).transpose(0, 1, 3, 2),
        ended[0].T,
        closed[1],
        ended[1],
        grad_qkv,
        grad_out.T,
        grad_up,
        grad_down.T,
        grad_head,
    )


def solution(mesh):
    in_specs = (
        P(None, None, None, "lon"),
        P("dp"),
        P(),
        P(),
        P(),
        P(),
        P("lon", None),
        P(),
        P(None, None, "mp"),
        P("mp", None),
        P(None, "mp"),
        P("mp", None),
        P(),
        P("dp", "lon", None),
    )
    out_specs = (
        P("dp", "lon", None),
        P(),
        P(),
        P(),
        P("dp", None, None, "lon"),
        P(None, ("dp", "lon")),
        P("lon", "dp"),
        P(None, ("dp", "lon")),
        P(None, ("dp", "lon"), "mp"),
        P("mp", ("dp", "lon")),
        P(("dp", "lon"), "mp"),
        P("mp", ("dp", "lon")),
        P(("dp", "lon"), None),
    )
    return jax.shard_map(local, mesh=mesh, in_specs=in_specs, out_specs=out_specs, check_vma=False)
```

```python
import functools
import math

import jax
import jax.numpy as jnp
from jax import lax
from jax.experimental import pallas as pl
from jax.experimental.pallas import tpu as pltpu
from jax.sharding import PartitionSpec as P

HDIM = 64
PATCH = 2
LANES = 128
NORM_EPS = 1e-06
STAT_EPS = 1e-06
BF = jnp.bfloat16
F32 = jnp.float32
MIB = 2**20


def swap(block, axis, distance):
    route = [(i, i ^ distance) for i in range(lax.axis_size(axis))]
    return lax.ppermute(block, axis, route)


def from_behind(block, axis, distance):
    size = lax.axis_size(axis)
    route = [((i - distance) % size, i) for i in range(size)]
    return lax.ppermute(block, axis, route)


def pick(x, index, axis):
    return lax.dynamic_index_in_dim(x, index, axis, keepdims=False)


def halve(total, dims):
    for axis, bit in dims:
        side = (lax.axis_index(axis) // bit) % 2
        got = swap(pick(total, 1 - side, 0), axis, bit)
        total = (pick(total, side, 0).astype(F32) + got.astype(F32)).astype(BF)
    return total


def scatter(total):
    dp, lon = lax.axis_size("dp"), lax.axis_size("lon")
    dims = []
    for axis, size in (("dp", dp), ("lon", lon)):
        bit = size // 2
        while bit:
            dims.append((axis, bit))
            bit //= 2
    rows, columns = total.shape
    total = total.astype(BF).reshape((2,) * len(dims) + (rows // (dp * lon), columns))
    order = sorted(range(len(dims)), key=lambda i: (dims[i][1] > 1 or dims[i][0] == "dp", i))
    total = total.transpose([*order, len(dims), len(dims) + 1])
    return halve(total, [dims[i] for i in order]).astype(F32)


def nt(a, b):
    return lax.dot_general(a, b, (((1,), (1,)), ((), ())), preferred_element_type=F32)


def nn(a, b):
    return lax.dot_general(a, b, (((1,), (0,)), ((), ())), preferred_element_type=F32)


def item_mask(rows, lanes, item):
    lane = lax.broadcasted_iota(jnp.int32, (rows, lanes), 1)
    return (lane >= item * HDIM) & (lane < (item + 1) * HDIM)


def interleave(first, second):
    low = item_mask(first.shape[0], LANES, 0)
    return (
        jnp.where(low, first, pltpu.roll(second, HDIM, 1)),
        jnp.where(low, pltpu.roll(first, HDIM, 1), second),
    )


def norm_parts(hidden):
    centred = hidden - jnp.mean(hidden, axis=-1, keepdims=True)
    variance = jnp.mean(centred * centred, axis=-1, keepdims=True)
    inverse = lax.rsqrt(variance + NORM_EPS)
    return centred * inverse, inverse


def norm_back(unit, inverse, scaling, grad):
    scaled = grad * scaling
    back = inverse * (
        scaled
        - jnp.mean(scaled, axis=-1, keepdims=True)
        - unit * jnp.mean(scaled * unit, axis=-1, keepdims=True)
    )
    return back, jnp.sum(grad * unit, axis=0, keepdims=True)


def emit_turned(x, ids_ref, outs, hold):
    turned = x.T.astype(BF)
    if len(outs) == 1:
        outs[0][...] = turned
        return
    keep, send = outs
    parts, rows, tokens = keep.shape
    hold[...] = turned.reshape(parts, 2, rows, tokens)
    core = ids_ref[0]
    keep[...] = hold[:, pl.ds(core, 1)].reshape(parts, rows, tokens)
    send[...] = hold[:, pl.ds(1 - core, 1)].reshape(parts, rows, tokens)


class Warm:
    def __init__(self, value):
        self.value = value


def call(body, name, outs, *args, after=(), grid=(), in_specs=None, out_specs=None, scratch=(), limit=24, flops=0):
    vmem = pl.BlockSpec(memory_space=pltpu.VMEM)
    smem = pl.BlockSpec(memory_space=pltpu.SMEM)
    shapes = [o.value if isinstance(o, Warm) else o for o in outs]
    plain = [a.value if isinstance(a, Warm) else a for a in args]
    if in_specs is None:
        in_specs = [smem if a.dtype == jnp.int32 else vmem for a in plain]
    if out_specs is None:
        out_specs = [vmem] * len(outs)
    token = pl.BlockSpec((8, LANES), lambda *at: (0, 0)) if grid else vmem
    nbytes = sum(math.prod(a.shape) * a.dtype.itemsize for a in [*plain, *shapes])
    here, skip, there = len(args), len(after), len(outs)

    def with_token(*refs):
        refs = list(refs)
        refs[here + skip + there][...] = jnp.zeros((8, LANES), F32)
        body(*refs[:here], *refs[here + skip : here + skip + there], *refs[here + skip + there + 1 :])

    def cold(x):
        if isinstance(x, Warm):
            return x.value
        return x if x.dtype == jnp.int32 else pltpu.with_memory_space_constraint(x, pltpu.HBM)

    return pl.pallas_call(
        with_token,
        grid=grid,
        out_shape=[
            *[o.value if isinstance(o, Warm) else pltpu.HBM(o.shape, o.dtype) for o in outs],
            pltpu.HBM((8, LANES), F32),
        ],
        in_specs=[*in_specs, *[pl.BlockSpec(memory_space=pl.ANY)] * skip],
        out_specs=[*out_specs, token],
        scratch_shapes=list(scratch),
        compiler_params=pltpu.CompilerParams(vmem_limit_bytes=limit * MIB),
        cost_estimate=pl.CostEstimate(flops=int(flops), bytes_accessed=nbytes, transcendentals=0),
        name=name,
    )(*[cold(a) for a in args], *[cold(a) for a in after])


def shape(dims, kind=BF):
    return jax.ShapeDtypeStruct(dims, kind)


def warm(dims, kind=BF):
    return Warm(shape(dims, kind))


def feature_order(variables, back):
    features = PATCH * PATCH * variables
    natural = lax.broadcasted_iota(jnp.int32, (features, features), 1 if back else 0)
    sorted_ = lax.broadcasted_iota(jnp.int32, (features, features), 0 if back else 1)
    hit = (natural // 4 == sorted_ % variables) & (natural % 4 == sorted_ // variables)
    return jnp.where(hit, 1.0, 0.0).astype(BF)


def send_pairs(ids_ref, hold, messages):
    if len(messages) == 1:
        messages[0][...] = hold[...]
        return
    for k, message in enumerate(messages):
        message[...] = hold[pl.ds(2 * ids_ref[4 + k], 2)]


def moments_kernel(index_ref, data_ref, fields_ref, edge_ref, moments_ref, turn_ref, sems):
    items, variables, height = edge_ref.shape
    cols = fields_ref.shape[1] // variables
    copies = [
        pltpu.make_async_copy(data_ref.at[index_ref[i]], fields_ref.at[i], sems.at[i])
        for i in range(items)
    ]
    for copy in copies:
        copy.start()
    turn_ref[...] = jnp.zeros_like(turn_ref)
    for copy in copies:
        copy.wait()
    blocks = [
        fields_ref[i, pl.ds(c, variables, stride=cols), :] for i in range(items) for c in range(cols)
    ]
    for i in range(items):
        edge_ref[i] = blocks[i * cols + cols - 1].astype(BF)
    count = float(items * cols * height)
    mean = jnp.sum(sum(blocks), axis=1, keepdims=True) * (1.0 / count)
    spread = jnp.sum(sum(jnp.square(b - mean) for b in blocks), axis=1, keepdims=True)
    turn_ref[0:variables, 0:1] = mean
    turn_ref[HDIM : HDIM + variables, 0:1] = spread
    turn_ref[0:variables, 1:2] = spread
    turned = turn_ref[...].T
    if len(moments_ref.shape) == 2:
        moments_ref[...] = turned[0 : moments_ref.shape[0], :]
    else:
        moments_ref[...] = jnp.broadcast_to(turned[0:1, :][None], moments_ref.shape)


def start_kernel(local_count, members, ids_ref, mom_ref, count_ref, mean_ref, var_ref, fields_ref, edge_ref, we_ref,
                 pos_ref, gains_ref, wq_ref, new_count_ref, new_mean_ref, new_var_ref, hidden_ref, patches_ref,
                 *rest):
    (*outs, column_ref, run_ref, hold, weights, sem, qkv_ref) = rest
    if len(outs) > 2:
        messages, turned = outs[:-2], outs[-2:]
    else:
        messages, turned = outs[:1], outs[1:]
    copy = pltpu.make_async_copy(wq_ref, weights, sem)
    copy.start()
    items, rows, height = fields_ref.shape
    variables = edge_ref.shape[1]
    cols = rows // variables
    half = height // PATCH
    run_ref[...] = jnp.zeros_like(run_ref)
    for k, ref in enumerate((count_ref, mean_ref, var_ref)):
        run_ref[k : k + 1, 0:variables] = ref[...]
    batch_count = local_count * members
    if len(mom_ref.shape) == 2:
        batch_mean, spread = mom_ref[0:1, :], mom_ref[1:2, :]
    else:
        moments = mom_ref[:, 0, :]
        batch_mean = jnp.sum(moments, axis=0, keepdims=True) * (1.0 / members)
        off = moments - batch_mean
        spread = jnp.sum(pltpu.roll(moments, HDIM, 1) + local_count * off * off, axis=0, keepdims=True)
    run_count, run_mean, run_var = (run_ref[k : k + 1, :] for k in range(3))
    new_count = run_count + batch_count
    shift = batch_mean - run_mean
    new_mean = run_mean + shift * (batch_count / new_count)
    new_var = (
        run_var * run_count + spread + shift * shift * (run_count * batch_count / new_count)
    ) / new_count
    new_count_ref[...] = new_count[:, 0:variables]
    new_mean_ref[...] = new_mean[:, 0:variables]
    new_var_ref[...] = new_var[:, 0:variables]
    column_ref[...] = jnp.zeros_like(column_ref)
    column_ref[0:1, :] = new_mean
    column_ref[1:2, :] = lax.rsqrt(new_var + STAT_EPS)
    column = column_ref[...].T
    centre, inverse = column[0:variables, 0:1], column[0:variables, 1:2]

    def scaled(block):
        return ((block - centre) * inverse).astype(BF)

    row = lax.broadcasted_iota(jnp.int32, (2 * height, LANES), 0)
    lane = lax.broadcasted_iota(jnp.int32, (2 * height, LANES), 1)
    sort = [
        jnp.where(
            (row // height == lane // half) & (row % height == PATCH * (lane % half) + a), 1.0, 0.0
        ).astype(BF)
        for a in range(PATCH)
    ]
    natural = feature_order(variables, False)
    hidden = []
    for item in range(items):
        west = scaled(edge_ref[item].astype(F32))
        own = [
            scaled(fields_ref[item, pl.ds(c, variables, stride=cols), :]) for c in range(cols - 1)
        ]
        first = jnp.concatenate([west, own[0]], axis=0)
        second = jnp.concatenate([own[1], own[2]], axis=0)
        both = jnp.concatenate([first, second], axis=1)
        patches = jnp.concatenate([nn(both, sort[a]) for a in range(PATCH)], axis=0)
        patches = nn(natural, patches.astype(BF))
        patches_ref[:, item * LANES : (item + 1) * LANES] = patches.astype(BF)
        hidden.append(nn(patches.T.astype(BF), we_ref[...]) + pos_ref[...].astype(F32))
    hidden = jnp.concatenate(hidden, axis=0)
    hidden_ref[...] = hidden
    unit, _ = norm_parts(hidden)
    normed = unit * gains_ref[0:1, :]
    low = normed.astype(BF)
    emit_turned(normed, ids_ref, turned, hold)
    copy.wait()
    for c in range(3):
        product = nn(low, weights[c])
        for t in range(product.shape[1] // LANES):
            tile = product[:, t * LANES : (t + 1) * LANES]
            a, b = interleave(tile[:LANES], tile[LANES:])
            qkv_ref[2 * t, c] = a.astype(BF)
            qkv_ref[2 * t + 1, c] = b.astype(BF)
    send_pairs(ids_ref, qkv_ref, messages)


def cotangent_kernel(ids_ref, ct_ref, wh_ref, wd_ref, *refs):
    if len(refs) > 3:
        two_ref, act_ref, ct_turned_ref, mine_ref, hold = refs
        hold[...] = wh_ref[...].astype(F32).T.astype(BF).reshape(hold.shape)
        mine_ref[...] = hold[ids_ref[8]]
    else:
        two_ref, act_ref, ct_turned_ref = refs
    grads = []
    for item in range(ct_ref.shape[0]):
        ct = ct_ref[item].T.astype(BF)
        ct_turned_ref[:, item * LANES : (item + 1) * LANES] = ct_ref[item].astype(BF)
        grads.append(nn(ct, wh_ref[...]))
    d_two = jnp.concatenate(grads, axis=0)
    two_ref[...] = d_two
    act_ref[...] = nt(d_two.astype(BF), wd_ref[...]).astype(BF)


def attend_kernel(items, scale, q_ref, kv_ref, o_ref, ot_ref, pt_ref, vt_ref):
    keys = kv_ref.shape[0] * kv_ref.shape[2]

    @pl.when(pl.program_id(0) == 0)
    def _():
        vt_ref[...] = kv_ref[:, 2].reshape(keys, LANES).astype(F32).T.astype(BF)

    rows = q_ref.shape[0] * q_ref.shape[2]
    queries = q_ref[:, 0].reshape(rows, LANES) * BF(scale)
    key_rows = kv_ref[:, 1].reshape(keys, LANES)
    for item in range(items):
        chosen = jnp.where(item_mask(rows, LANES, item), queries, BF(0))
        scores = nt(key_rows, chosen)
        top = jnp.max(scores, axis=0, keepdims=True)
        raised = jnp.exp(scores - top)
        total = jnp.sum(raised, axis=0, keepdims=True)
        weights = (raised * (1.0 / total)).astype(BF)
        pt_ref[item] = weights
        span = slice(item * HDIM, (item + 1) * HDIM)
        ot_ref[span, :] = nn(vt_ref[span, :], weights)
    o_ref[...] = ot_ref[...].T.astype(BF).reshape(o_ref.shape)


def attend(q, kv, items, scale, after):
    peers, _, tokens, lanes = q.shape
    rows, keys = peers * tokens, kv.shape[0] * tokens
    step = max(1, min(peers, 256 * 1024 // keys // tokens))
    block = step * tokens
    return call(
        functools.partial(attend_kernel, items, scale),
        "attend",
        [
            shape((peers, tokens, lanes)),
            shape((lanes, rows), F32),
            shape((items, keys, rows)),
        ],
        Warm(q),
        Warm(kv),
        after=after,
        grid=(peers // step,),
        in_specs=[
            pl.BlockSpec((step, 3, tokens, lanes), lambda j: (j, 0, 0, 0)),
            pl.BlockSpec(kv.shape, lambda j: (0, 0, 0, 0)),
        ],
        out_specs=[
            pl.BlockSpec((step, tokens, lanes), lambda j: (j, 0, 0)),
            pl.BlockSpec((lanes, block), lambda j: (0, j)),
            pl.BlockSpec((items, keys, block), lambda j: (0, 0, j)),
        ],
        scratch=[pltpu.VMEM((lanes, keys), BF)],
        limit=24 if keys <= 2048 else 56,
        flops=8 * rows * keys * lanes,
    )


def pair_attend_kernel(items, scale, *refs):
    sources, (*outs, ot_ref, pt_ref, query_ref, key_ref, value_ref, vt_ref) = refs[:8], refs[8:]
    tokens = sources[0].shape[2]
    for k, source in enumerate(sources):
        span = slice(k * tokens, (k + 1) * tokens)
        if k < len(outs):
            query_ref[0, span, :] = source[0, 0] * BF(scale)
        key_ref[0, span, :] = source[0, 1]
        value_ref[0, span, :] = source[0, 2]
        vt_ref[:, span] = source[0, 2].astype(F32).T.astype(BF)
    queries = query_ref[0]
    for item in range(items):
        chosen = jnp.where(item_mask(queries.shape[0], LANES, item), queries, BF(0))
        scores = nt(key_ref[0], chosen)
        top = jnp.max(scores, axis=0, keepdims=True)
        raised = jnp.exp(scores - top)
        total = jnp.sum(raised, axis=0, keepdims=True)
        weights = (raised * (1.0 / total)).astype(BF)
        pt_ref[0, item] = weights
        span = slice(item * HDIM, (item + 1) * HDIM)
        ot_ref[0, span, :] = nn(vt_ref[span, :], weights)
    attended = ot_ref[0].T.astype(BF)
    for k, out in enumerate(outs):
        out[0] = attended[k * tokens : (k + 1) * tokens]


def pair_attend(own, other, items, scale, after):
    _, _, tokens, lanes = own[0].shape
    rows, keys = len(own) * tokens, 2 * len(own) * tokens
    wide = lambda *dims: pl.BlockSpec((1, *dims), lambda h: (h, *[0] * len(dims)))
    *outs, ot, pt, q, k, v, token = call(
        functools.partial(pair_attend_kernel, items, scale),
        "attend",
        [
            shape((2, tokens, lanes)),
            *[warm((2, tokens, lanes))] * (len(own) - 1),
            shape((2, lanes, rows), F32),
            shape((2, items, keys, rows)),
            shape((2, rows, lanes)),
            shape((2, keys, lanes)),
            shape((2, keys, lanes)),
        ],
        *[Warm(x) for x in [*own, *other]],
        after=after,
        grid=(2,),
        in_specs=[wide(3, tokens, lanes)] * (2 * len(own)),
        out_specs=[
            *[wide(tokens, lanes)] * len(own),
            wide(lanes, rows),
            wide(items, keys, rows),
            wide(rows, lanes),
            wide(keys, lanes),
            wide(keys, lanes),
        ],
        scratch=[pltpu.VMEM((lanes, keys), BF)],
        limit=32,
        flops=16 * rows * keys * lanes,
    )
    return outs, (q, k, v, ot, pt), token


def pair_attend_back_kernel(items, scale, ids_ref, query_ref, key_ref, value_ref, ot_ref, pt_ref, grads_ref, *refs):
    *outs, cross_ref, kt_ref, grad_rows, dqt_ref, dk_sum, dv_sum = refs
    tokens = grads_ref.shape[2]
    for k in range(len(outs)):
        grad_rows[k * tokens : (k + 1) * tokens, :] = grads_ref[ids_ref[4 + k], 0]
    kt_ref[...] = (key_ref[0].astype(F32) * scale).T.astype(BF)
    queries, grads = query_ref[0], grad_rows[...]
    product = grads.astype(F32).T * ot_ref[0]
    for item in range(items):
        span = slice(item * HDIM, (item + 1) * HDIM)
        mask = item_mask(queries.shape[0], LANES, item)
        grad = jnp.where(mask, grads, BF(0))
        query = jnp.where(mask, queries, BF(0))
        delta = jnp.sum(product[span, :], axis=0, keepdims=True)
        weights = pt_ref[0, item]
        back = (weights.astype(F32) * (nt(value_ref[0], grad) - delta)).astype(BF)
        d_value, d_key = nn(weights, grad), nn(back, query)
        if item == 0:
            dv_sum[...] = d_value
            dk_sum[...] = d_key
        else:
            dv_sum[...] += d_value
            dk_sum[...] += d_key
        dqt_ref[span, :] = nn(kt_ref[span, :], back)
    d_query = dqt_ref[...].T.astype(BF)
    for k in range(2 * len(outs)):
        span = slice(k * tokens, (k + 1) * tokens)
        if k < len(outs):
            outs[k][0, 0] = d_query[span]
        for c, total in ((0, dk_sum), (1, dv_sum)):
            if k < len(outs):
                outs[k][0, 1 + c] = total[span, :].astype(BF)
            else:
                cross_ref[k - len(outs), 0, c] = total[span, :].astype(BF)


def pair_attend_back(ids, kept, d, items, scale, after):
    count, _, tokens, lanes = d.shape
    rows, keys = count * tokens, 2 * count * tokens
    wide = lambda *dims: pl.BlockSpec((1, *dims), lambda h: (h, *[0] * len(dims)))
    *outs, cross, token = call(
        functools.partial(pair_attend_back_kernel, items, scale),
        "attend_back",
        [*[shape((2, 3, tokens, lanes))] * count, shape((count, 2, 2, tokens, lanes))],
        ids, *kept, d,
        after=after,
        grid=(2,),
        in_specs=[
            pl.BlockSpec(memory_space=pltpu.SMEM),
            wide(rows, lanes),
            wide(keys, lanes),
            wide(keys, lanes),
            wide(lanes, rows),
            wide(items, keys, rows),
            pl.BlockSpec((count, 1, tokens, lanes), lambda h: (0, h, 0, 0)),
        ],
        out_specs=[
            *[wide(3, tokens, lanes)] * count,
            pl.BlockSpec((count, 1, 2, tokens, lanes), lambda h: (0, h, 0, 0, 0)),
        ],
        scratch=[
            pltpu.VMEM((lanes, keys), BF),
            pltpu.VMEM((rows, lanes), BF),
            pltpu.VMEM((lanes, rows), F32),
            pltpu.VMEM((keys, lanes), F32),
            pltpu.VMEM((keys, lanes), F32),
        ],
        limit=32,
        flops=32 * rows * keys * lanes,
    )
    return outs, cross, token


def combine_kernel(*refs):
    count = (len(refs) - 1) // 2
    own, cross_ref, outs = refs[:count], refs[count], refs[count + 1 :]
    for k in range(count):
        outs[k][:, 0] = own[k][:, 0]
        for c in range(2):
            outs[k][:, 1 + c] = plus(own[k].at[:, 1 + c], cross_ref.at[k, :, c])


def attend_back_kernel(items, scale, q_ref, kv_ref, d_ref, ot_ref, pt_ref, dq_ref, *rest):
    dkv_ref, (kt_ref, dqt_ref, dk_sum, dv_sum) = rest[:-4], rest[-4:]
    step = pl.program_id(0)
    keys = kv_ref.shape[0] * kv_ref.shape[2]

    @pl.when(step == 0)
    def _():
        kt_ref[...] = (kv_ref[:, 1].reshape(keys, LANES).astype(F32) * scale).T.astype(BF)
        dk_sum[...] = jnp.zeros_like(dk_sum)
        dv_sum[...] = jnp.zeros_like(dv_sum)

    peers, _, tokens, _ = q_ref.shape
    rows = peers * tokens
    queries = q_ref[:, 0].reshape(rows, LANES) * BF(scale)
    grads = d_ref[...].reshape(rows, LANES)
    value_rows = kv_ref[:, 2].reshape(keys, LANES)
    product = grads.astype(F32).T * ot_ref[...]
    for item in range(items):
        span = slice(item * HDIM, (item + 1) * HDIM)
        mask = item_mask(rows, LANES, item)
        grad = jnp.where(mask, grads, BF(0))
        query = jnp.where(mask, queries, BF(0))
        delta = jnp.sum(product[span, :], axis=0, keepdims=True)
        weights = pt_ref[item]
        back = (weights.astype(F32) * (nt(value_rows, grad) - delta)).astype(BF)
        dv_sum[...] += nn(weights, grad)
        dk_sum[...] += nn(back, query)
        dqt_ref[span, :] = nn(kt_ref[span, :], back)
    d_query = dqt_ref[...].T.astype(BF).reshape(peers, tokens, LANES)
    if dkv_ref:
        dq_ref[...] = d_query
    else:
        dq_ref[pl.ds(step * peers, peers), 0] = d_query

    @pl.when(step == pl.num_programs(0) - 1)
    def _():
        for c, total in ((1, dk_sum), (2, dv_sum)):
            total = total[...].reshape(kv_ref.shape[0], tokens, LANES)
            if dkv_ref:
                dkv_ref[0][:, c - 1] = total
            else:
                dq_ref[:, c] = total.astype(BF)


def attend_back(q, kv, d, ot, pt, items, scale, after):
    peers, _, tokens, lanes = q.shape
    rows, keys = peers * tokens, kv.shape[0] * tokens
    step = max(1, min(peers, 256 * 1024 // keys // tokens))
    block = step * tokens
    if q.shape == kv.shape:
        outs = [shape(q.shape)]
        out_specs = [pl.BlockSpec(q.shape, lambda j: (0, 0, 0, 0))]
    else:
        outs = [shape((peers, tokens, lanes)), shape((kv.shape[0], 2, tokens, lanes), F32)]
        out_specs = [
            pl.BlockSpec((step, tokens, lanes), lambda j: (j, 0, 0)),
            pl.BlockSpec(outs[1].shape, lambda j: (0, 0, 0, 0)),
        ]
    *back, token = call(
        functools.partial(attend_back_kernel, items, scale),
        "attend_back",
        outs,
        Warm(q),
        Warm(kv),
        d,
        ot,
        pt,
        after=after,
        grid=(peers // step,),
        in_specs=[
            pl.BlockSpec((step, 3, tokens, lanes), lambda j: (j, 0, 0, 0)),
            pl.BlockSpec(kv.shape, lambda j: (0, 0, 0, 0)),
            pl.BlockSpec((step, tokens, lanes), lambda j: (j, 0, 0)),
            pl.BlockSpec((lanes, block), lambda j: (0, j)),
            pl.BlockSpec((items, keys, block), lambda j: (0, 0, j)),
        ],
        out_specs=out_specs,
        scratch=[
            pltpu.VMEM((lanes, keys), BF),
            pltpu.VMEM((lanes, block), F32),
            pltpu.VMEM((keys, lanes), F32),
            pltpu.VMEM((keys, lanes), F32),
        ],
        limit=24 if keys <= 2048 else 60,
        flops=16 * rows * keys * lanes,
    )
    return back, token


def unpack(ids_ref, sources, index, out_ref, base):
    several = len(sources) > 1
    count = len(sources) if several else sources[0].shape[0] // 2
    for t in range(count):
        source, head = (sources[t], 0) if several else (sources[0], 2 * t)
        pair = [
            (source[head + s] if index is None else source[head + s, index]).astype(F32) for s in range(2)
        ]
        at = base + (pl.multiple_of(ids_ref[4 + t] * LANES, LANES) if several else t * LANES)
        for item, tile in enumerate(interleave(*pair)):
            out_ref[item * LANES : (item + 1) * LANES, pl.ds(at, LANES)] = tile.astype(BF)


def pack(product, out_ref):
    for t in range(product.shape[1] // LANES):
        tile = product[:, t * LANES : (t + 1) * LANES]
        for s, block in enumerate(interleave(tile[:LANES], tile[LANES:])):
            out_ref[2 * t + s] = block.astype(BF)


def project_kernel(ids_ref, *refs):
    *sources, wo_ref, mixed_ref, branch_ref = refs
    unpack(ids_ref, sources, None, mixed_ref, 0)
    branch_ref[...] = nn(mixed_ref[...], wo_ref[...]).astype(BF)


def forward_kernel(sources, ids_ref, *refs):
    if sources:
        own, got, refs = refs[:sources], refs[sources : 2 * sources], refs[2 * sources :]
        wo_ref, wo_got_ref, zero_ref, gains_ref, wu_ref, dact_ref, norm_ref, mixed_out, *refs = refs
        *refs, wo_buf, mixed, wo_sems = refs
        me = ids_ref[9]
        wo_loads = [
            pltpu.make_async_copy(wo_ref, wo_buf.at[me], wo_sems.at[0]),
            pltpu.make_async_copy(wo_got_ref, wo_buf.at[1 - me], wo_sems.at[1]),
        ]
        for copy in wo_loads:
            copy.start()
    else:
        own_ref, got_ref, zero_ref, gains_ref, wu_ref, dact_ref, norm_ref, *refs = refs
    one_out, pre_out, act_out, other_out, *rest = refs
    count = (len(rest) - 9) // 2
    turned_out, turned = rest[:count], rest[count : 2 * count]
    one_ref, weights, grads, pre_ref, act_ref, normed_ref, hold, into, out_of = rest[2 * count :]
    chunks, _, block = grads.shape
    per_half = chunks // 2
    loads, stores = [], []
    for c in range(chunks):
        span = slice(c * block, (c + 1) * block)
        loads.append(
            (
                pltpu.make_async_copy(wu_ref.at[:, span], weights.at[c], into.at[2 * c]),
                pltpu.make_async_copy(dact_ref.at[:, span], grads.at[c], into.at[2 * c + 1]),
            )
        )
        for copy in loads[-1]:
            copy.start()

    def store(source, target):
        stores.append(pltpu.make_async_copy(source, target, out_of.at[len(stores)]))
        stores[-1].start()

    if sources:
        unpack(ids_ref, own, None, mixed.at[me], 0)
        unpack(ids_ref, got, None, mixed.at[1 - me], 0)
        mixed_out[...] = mixed[me]
        for copy in wo_loads:
            copy.wait()
        branch = nn(mixed[0], wo_buf[0]) + nn(mixed[1], wo_buf[1])
    else:
        branch = own_ref[...].astype(F32) + got_ref[...].astype(F32)
    hidden = zero_ref[...] + branch
    one_ref[...] = hidden
    store(one_ref, one_out)
    unit, _ = norm_parts(hidden)
    normed = unit * gains_ref[1:2, :]
    normed_ref[...] = normed.astype(BF)
    emit_turned(normed, ids_ref, turned, hold)
    for source, target in zip(turned, turned_out):
        store(source, target)
    total = None
    for c in range(chunks):
        span = slice(c * block, (c + 1) * block)
        half, place = c // per_half, slice(c % per_half * block, (c % per_half + 1) * block)
        for copy in loads[c]:
            copy.wait()
        pre = nn(normed_ref[...], weights[c])
        chance = 0.5 * (1.0 + lax.erf(pre * (1.0 / math.sqrt(2.0))))
        slope = chance + pre * jnp.exp(-0.5 * pre * pre) * (1.0 / math.sqrt(2.0 * math.pi))
        act_ref[half, :, place] = (pre * chance).astype(BF)
        store(act_ref.at[half, :, place], act_out.at[half, :, place])
        d_pre = (grads[c].astype(F32) * slope).astype(BF)
        pre_ref[:, span] = d_pre
        store(pre_ref.at[:, span], pre_out.at[:, span])
        part = nt(d_pre, weights[c])
        total = part if total is None else total + part
    store(act_ref.at[1 - ids_ref[0]], other_out)
    norm_ref[...] = total.astype(BF)
    for copy in stores:
        copy.wait()


def second_kernel(ids_ref, one_ref, two_ref, own_ref, got_ref, gains_ref, wo_ref, d_ref, gain_ref, *rest):
    heads_ref, *turned, hold = rest
    unit, inverse = norm_parts(one_ref[...])
    grad = own_ref[...].astype(F32) + got_ref[...].astype(F32)
    back, gain = norm_back(unit, inverse, gains_ref[1:2, :], grad)
    gain_ref[...] = gain
    d_one = two_ref[...] + back
    d_ref[...] = d_one
    pack(nt(d_one.astype(BF), wo_ref[...]), heads_ref)
    emit_turned(d_one, ids_ref, turned, hold)


def head_kernel(ids_ref, one_ref, own_ref, got_ref, wh_ref, pred_ref, *rest):
    turned, hold = rest[:-1], rest[-1]
    hidden = one_ref[...] + (own_ref[...].astype(F32) + got_ref[...].astype(F32))
    low = hidden.astype(BF)
    for item in range(pred_ref.shape[0]):
        pred_ref[item] = nt(wh_ref[...], low[item * LANES : (item + 1) * LANES])
    emit_turned(hidden, ids_ref, turned, hold)


def third_kernel(count, ids_ref, *refs):
    sources, (wq_ref, dqkv_ref, norm_ref) = refs[:count], refs[count:]
    width = wq_ref.shape[2]
    total = None
    for c in range(3):
        unpack(ids_ref, sources, c, dqkv_ref, c * width)
        part = nt(dqkv_ref[:, c * width : (c + 1) * width], wq_ref[c])
        total = part if total is None else total + part
    norm_ref[...] = total.astype(BF)


def last_kernel(cols, ids_ref, zero_ref, done_ref, own_ref, got_ref, gains_ref, gain_two_ref, patches_ref, we_ref,
                pos_send, pos_keep, fields_ref, edge_ref, *rest):
    embed, (rows_ref, pos_ref, hold) = rest[:-3], rest[-3:]
    unit, inverse = norm_parts(zero_ref[...])
    grad = own_ref[...].astype(F32) + got_ref[...].astype(F32)
    back, gain = norm_back(unit, inverse, gains_ref[0:1, :], grad)
    d_zero = done_ref[...] + back
    low = d_zero.astype(BF)
    items, variables, height = edge_ref.shape
    pos = d_zero[0:LANES]
    for item in range(1, items):
        pos = pos + d_zero[item * LANES : (item + 1) * LANES]
    width = pos_ref.shape[2]
    for k in range(2):
        pos_ref[k] = pos[:, k * width : (k + 1) * width].astype(BF)
    pos_send[...] = pos_ref[1 - ids_ref[1]]
    pos_keep[...] = pos_ref[ids_ref[1]]
    features = patches_ref.shape[0]
    rows_ref[...] = jnp.zeros_like(rows_ref)
    rows_ref[0:features, :] = nn(patches_ref[...], low)
    rows_ref[features : features + 1, :] = gain
    rows_ref[features + 1 : features + 2, :] = gain_two_ref[...]
    emit_turned(rows_ref[...], ids_ref, embed, hold)
    half = height // PATCH
    row = lax.broadcasted_iota(jnp.int32, (LANES, height), 0)
    lane = lax.broadcasted_iota(jnp.int32, (LANES, height), 1)
    fields_ref[...] = jnp.zeros_like(fields_ref)
    order = feature_order(variables, True)
    for item in range(items):
        d_patches = nt(we_ref[...], low[item * LANES : (item + 1) * LANES])
        high = d_patches.astype(BF)
        rest = (d_patches - high.astype(F32)).astype(BF)
        high, rest = nn(order, high).astype(BF), nn(order, rest).astype(BF)
        for j in range(2):
            total = None
            for a in range(PATCH):
                place = jnp.where(
                    (row // half == j) & (lane == PATCH * (row % half) + a), 1.0, 0.0
                ).astype(BF)
                span = slice(a * 2 * variables, (a + 1) * 2 * variables)
                part = nn(high[span], place) + nn(rest[span], place)
                total = part if total is None else total + part
            for b in range(PATCH):
                block = total[b * variables : (b + 1) * variables]
                column = 2 * j + b - 1
                if column < 0:
                    edge_ref[item] = block.astype(BF)
                else:
                    fields_ref[item, pl.ds(column, variables, stride=cols), :] = block


def down_kernel(act_ref, wd_ref, out_ref):
    width = act_ref.shape[2]
    total = nn(act_ref[0], wd_ref[0:width, :]) + nn(act_ref[1], wd_ref[width:, :])
    out_ref[...] = total.astype(BF)


def pin(xs, after):
    def body(*refs):
        pass

    anywhere = pl.BlockSpec(memory_space=pl.ANY)
    several = isinstance(xs, (list, tuple))
    xs = list(xs) if several else [xs]
    out = pl.pallas_call(
        body,
        out_shape=[pltpu.HBM(x.shape, x.dtype) for x in xs],
        in_specs=[anywhere] * (len(xs) + len(after)),
        out_specs=[anywhere] * len(xs),
        input_output_aliases={k: k for k in range(len(xs))},
        name="pin",
    )(*[pltpu.with_memory_space_constraint(x, pltpu.HBM) for x in xs], *after)
    return out if several else out[0]


def product_of(own, got, b_own, b_got):
    parts, rows, tokens = own.shape
    total = nn(own[...].reshape(parts * rows, tokens), b_own)
    return total + nn(got[...].reshape(parts * rows, tokens), b_got)


def split_dp(ids_ref, hold, send, keep, columns):
    half = hold.shape[0] // 2
    for out, at in ((send, 1 - ids_ref[1]), (keep, ids_ref[1])):
        for k in range(half):
            out[k, :, 0:columns] = hold[at * half + k]


def split_near(ids_ref, hold, send, keep, columns):
    for out, at in ((send, 1 - ids_ref[2]), (keep, ids_ref[2])):
        for k in range(hold.shape[0] // 2):
            out[k, :, 0:columns] = hold[2 * k + at]


def plus(a, b):
    return (a[...].astype(F32) + b[...].astype(F32)).astype(BF)


def grads_ff_kernel(ids_ref, at_own, at_got, pre_own, pre_got, ct_own, ct_got, act_own, act_got,
                    send_a, keep_a, send_b, keep_b, hold, inner):
    parts, rows, total = hold.shape
    columns = total - keep_b.shape[2]
    product = product_of(at_own, at_got, pre_own[...], pre_got[...])
    hold[...] = product.astype(BF).reshape(hold.shape)
    split_dp(ids_ref, hold.at[:, :, 0:columns], send_a, keep_a, columns)
    split_near(ids_ref, hold.at[:, :, columns:], send_b, keep_b, total - columns)
    product = (nn(ct_own[...], act_own[ids_ref[0]]) + nn(ct_got[...], act_got[...])).astype(BF)
    tiles, groups = inner.shape[1], inner.shape[3] // LANES
    for k in range(2):
        for q in range(tiles):
            for g in range(groups):
                inner[k, q, :, g * LANES : (g + 1) * LANES] = product[
                    g * rows : (g + 1) * rows, (k * tiles + q) * LANES : (k * tiles + q + 1) * LANES
                ]
    for q in range(tiles):
        send_a[q, :, columns:] = inner[1 - ids_ref[1], q]
        keep_a[q, :, columns:] = inner[ids_ref[1], q]


def fold_ff_kernel(ids_ref, keep_a, got_a, keep_b, got_b, send_a, left_a, send_b, left_b, hold, hold_b):
    columns = hold.shape[2]
    extra = keep_a.shape[2] - columns
    hold[...] = plus(keep_a.at[:, :, 0:columns], got_a.at[:, :, 0:columns])
    split_near(ids_ref, hold, send_a, left_a, columns)
    for q in range(keep_a.shape[0]):
        total = plus(keep_a.at[q, :, columns:], got_a.at[q, :, columns:])
        at = columns + q % 2 * extra
        for out in (send_a, left_a):
            out[q // 2, :, at : at + extra] = total
    hold_b[...] = plus(keep_b, got_b)
    split_dp(ids_ref, hold_b, send_b, left_b, hold_b.shape[2])


def merge_ff_kernel(ids_ref, keep_a, got_a, keep_b, got_b, send, left, hold):
    columns = hold.shape[2] - keep_b.shape[2]
    extra = keep_a.shape[2] - columns
    hold[:, :, 0:columns] = plus(keep_a.at[:, :, 0:columns], got_a.at[:, :, 0:columns])
    hold[:, :, columns:] = plus(keep_b, got_b)
    far = ids_ref[3]
    width = hold.shape[2]
    send[:, 0:width] = hold[1 - far]
    left[:, 0:width] = hold[far]
    for k in range(2):
        total = plus(keep_a.at[k, :, columns:], got_a.at[k, :, columns:])
        at = width + k * extra
        for out in (send, left):
            out[:, at : at + extra] = total


def grads_oh_kernel(ids_ref, one_own, one_got, mixed_own, mixed_got, two_own, two_got, ct_own, ct_got,
                    send, keep, hold):
    width, features = mixed_own.shape[1], ct_own.shape[0]
    shape3 = hold.shape[:2]
    product = product_of(one_own, one_got, mixed_own[...], mixed_got[...])
    hold[:, :, 0:width] = product.astype(BF).reshape(*shape3, width)
    hold[:, :, width:] = jnp.zeros((*shape3, hold.shape[2] - width), BF)
    product = product_of(
        two_own, two_got, ct_own[...].astype(F32).T.astype(BF), ct_got[...].astype(F32).T.astype(BF)
    )
    hold[:, :, width : width + features] = product.astype(BF).reshape(*shape3, features)
    split_dp(ids_ref, hold, send, keep, hold.shape[2])


def grads_q_kernel(ids_ref, at_own, at_got, b_own, b_got, send_a, keep_a, send_b, keep_b, hold):
    cut, total = keep_a.shape[2], hold.shape[2]
    hold[...] = product_of(at_own, at_got, b_own[...], b_got[...]).astype(BF).reshape(hold.shape)
    split_dp(ids_ref, hold.at[:, :, 0:cut], send_a, keep_a, cut)
    split_near(ids_ref, hold.at[:, :, cut:], send_b, keep_b, total - cut)


def fold_q_kernel(ids_ref, keep_a, got_a, keep_b, got_b, up_keep, up_got, oh_keep, oh_got, embed_own, embed_got,
                  send_a, left_a, send_b, left_b, send_o, left_o, hold_a, hold_b, hold_o, hold_e):
    hold_a[...] = plus(keep_a, got_a)
    split_near(ids_ref, hold_a, send_a, left_a, hold_a.shape[2])
    hold_b[...] = plus(keep_b, got_b)
    columns = hold_b.shape[2]
    split_dp(ids_ref, hold_b, send_b, left_b, columns)
    hold_o[...] = plus(oh_keep, oh_got)
    for out, at in ((send_o, 1 - ids_ref[3]), (left_o, ids_ref[3])):
        for k in range(2):
            out[k] = hold_o[2 * at + k]
    hold_e[...] = plus(embed_own, embed_got)
    width = hold_e.shape[2]
    for out, at in ((send_b, 1 - ids_ref[1]), (left_b, ids_ref[1])):
        for k in range(4):
            start = columns + k % 2 * width
            out[k // 2, :, start : start + width] = hold_e[4 * at + k]
    start = columns + 2 * width
    half = send_b.shape[2] - start
    for k in range(2):
        at = up_keep.shape[1] - (2 - k) * half
        total = plus(up_keep.at[:, at : at + half], up_got.at[:, at : at + half])
        for out in (send_b, left_b):
            out[k, :, start:] = total


def merge_q_kernel(ids_ref, keep_a, got_a, keep_b, got_b, oh_keep, oh_got,
                   send, left, pair_ref, near_ref, embed_both, oh_left, hold, hold_e, hold_o):
    width = embed_both.shape[1]
    half = pair_ref.shape[2] // 2
    first = keep_a.shape[2]
    columns = keep_b.shape[2] - half - 2 * width
    total = hold.shape[2]
    hold[:, :, 0:first] = plus(keep_a, got_a)
    hold[:, :, first:] = plus(keep_b.at[:, :, 0:columns], got_b.at[:, :, 0:columns])
    hold_o[...] = plus(oh_keep, oh_got)
    for k in range(4):
        span = slice(columns + k % 2 * width, columns + (k % 2 + 1) * width)
        hold_e[k] = plus(keep_b.at[k // 2, :, span], got_b.at[k // 2, :, span])
    far, near = ids_ref[3], ids_ref[2]
    for out, at in ((send, 1 - far), (left, far)):
        out[:, 0:total] = hold[at]
        out[:, total:] = hold_e[2 * at + near]
    near_ref[:, 0:width] = hold_e[2 * far + 1 - near]
    near_ref[:, width:] = hold_o[1 - near]
    oh_left[...] = hold_o[near]
    embed_both[...] = hold_e[2 * (1 - far) + 1 - near]
    for k in range(2):
        span = slice(k * half, (k + 1) * half)
        pair_ref[0, :, span] = keep_b[k, :, columns + 2 * width :]
        pair_ref[1, :, span] = got_b[k, :, columns + 2 * width :]


def expand(ids_ref, rows_ref, pair_own, pair_got, out_ref, block):
    rows = rows_ref.shape[0]
    groups = block.shape[0] // rows
    tiles = block.shape[1] // LANES
    for a, b in ((0, 0), (0, 1), (1, 0), (1, 1)):
        source = pair_got if a else pair_own
        for q in range(tiles):
            for g in range(groups):
                at = (q * groups + g) * LANES
                block[g * rows : (g + 1) * rows, q * LANES : (q + 1) * LANES] = source[b, :, at : at + LANES]
        core, dp = (1 - ids_ref[0] if a else ids_ref[0]), (1 - ids_ref[1] if b else ids_ref[1])
        at = pl.multiple_of((core * 2 + dp) * block.shape[1], LANES)
        out_ref[:, pl.ds(at, block.shape[1])] = nn(rows_ref[...], block[...])


def insert_east(cols, fields_ref, east_ref, out_ref):
    variables = east_ref.shape[1]
    out_ref[...] = fields_ref[...]
    for item in range(east_ref.shape[0]):
        out_ref[item, pl.ds(cols - 1, variables, stride=cols), :] = east_ref[item].astype(F32)


def close_kernel(cols, ids_ref, fields_ref, east_ref, pos_ref, pos_got_ref, *refs):
    outs = refs
    if len(refs) > 2:
        (up_ref, up_got_ref, rows_ref, pair_own, pair_got), outs, block = refs[:5], refs[5:-1], refs[-1]
        width = outs[2].shape[1]
        outs[2][...] = up_ref[:, 0:width].astype(F32) + up_got_ref[:, 0:width].astype(F32)
        expand(ids_ref, rows_ref, pair_own, pair_got, outs[3], block)
    insert_east(cols, fields_ref, east_ref, outs[0])
    outs[1][...] = pos_ref[...].astype(F32) + pos_got_ref[...].astype(F32)


def end_kernel(*refs):
    if len(refs) > 3:
        (near_ref, both_ref, oh_ref, keep_ref, got_ref), refs = refs[:5], refs[5:]
        out_ref, head_ref, grad_ref = refs[2:]
        embed_width = both_ref.shape[1]
        both = keep_ref[...].astype(F32) + got_ref[...].astype(F32)
        width = grad_ref.shape[2]
        for c in range(3):
            grad_ref[c] = both[:, c * width : (c + 1) * width]
        total = both[:, 3 * width :] + near_ref[:, 0:embed_width].astype(F32) + both_ref[...].astype(F32)
        both = oh_ref[...].astype(F32) + near_ref[:, embed_width:].astype(F32)
        out_ref[...] = both[:, 0:width]
        head_ref[...] = both[:, width : width + head_ref.shape[1]]
    else:
        total, refs = jnp.sum(refs[0][...].astype(F32), axis=0), refs[1:]
    features = refs[0].shape[1]
    refs[0][...] = total[:, 0:features]
    refs[1][...] = total[:, LANES:].T[features - LANES : features - LANES + 2, :]


def local(
    dataset,
    indices,
    run_count,
    run_mean,
    run_var,
    w_embed,
    pos_embed,
    gains,
    w_qkv,
    w_out,
    w_up,
    w_down,
    w_head,
    cotangent,
):
    items = indices.shape[0]
    variables, height, columns = dataset.shape[1:]
    dp, lon = lax.axis_size("dp"), lax.axis_size("lon")
    everyone = dp * lon
    width = w_embed.shape[1]
    local_width = w_qkv.shape[2]
    heads = local_width // HDIM
    item_tokens = cotangent.shape[1]
    tokens = items * item_tokens
    features = w_embed.shape[0]
    hidden_units = w_up.shape[1]
    scale = 1.0 / math.sqrt(HDIM)
    group, far = heads, lon // heads
    groups = [[group * g + i for i in range(group)] for g in range(far)]
    across = [[i + group * g for g in range(far)] for i in range(group)]
    assert items * HDIM == LANES and item_tokens == LANES and height == LANES and columns == 4
    lon_at, dp_at = lax.axis_index("lon"), lax.axis_index("dp")
    ids = [lon_at % 2, dp_at, lon_at // 2 % 2, lon_at // 4 % 2, *[lon_at // 2 ^ k for k in range(4)], dp_at * lon + lon_at, lax.axis_index("mp")]
    ids = jnp.stack(ids).astype(jnp.int32)
    paired = dp == 2 and lon == 8
    parts, rows = width // (2 * (width // everyone)), width // everyone
    turned_shape = (
        [shape((parts, rows, tokens))] * 2 if paired else [shape((width, tokens))]
    )
    turned_hold = pltpu.VMEM((parts, 2, rows, tokens) if paired else (8, LANES), BF)

    alone = dict(axis_index_groups=groups) if far > 1 else {}

    vmem, smem = pl.BlockSpec(memory_space=pltpu.VMEM), pl.BlockSpec(memory_space=pltpu.SMEM)
    assert dp == 2

    data = dataset.transpose(0, 1, 3, 2).reshape(dataset.shape[0], variables * columns, height)
    fields, edge, moments, _ = call(
        moments_kernel,
        "moments",
        [
            warm((items, variables * columns, height), F32),
            warm((items, variables, height)),
            warm((8, LANES) if paired else (everyone, 8, LANES), F32),
        ],
        indices, data,
        in_specs=[pl.BlockSpec(memory_space=pltpu.SMEM), pl.BlockSpec(memory_space=pl.ANY)],
        scratch=[pltpu.VMEM((LANES, LANES), F32), pltpu.SemaphoreType.DMA((items,))],
    )
    edge = from_behind(edge, "lon", 1)
    if paired:
        row = lax.broadcasted_iota(jnp.int32, moments.shape, 0)
        held = float(items * height * columns)
        for axis, distance in (("lon", 1), ("lon", 2), ("lon", 4), ("dp", 1)):
            got = swap(moments, axis, distance)
            apart = jnp.square(moments[0:1] - got[0:1]) * (0.5 * held)
            moments = jnp.where(row == 0, 0.5 * (moments + got), moments + got + apart)
            held = 2.0 * held
    else:
        moments = lax.all_to_all(moments, ("dp", "lon"), 0, 0)
    wh_turned = w_head.T

    out = call(
        functools.partial(start_kernel, float(items * height * columns), everyone),
        "start",
        [
            *[shape((1, variables), F32)] * 3,
            shape((tokens, width), F32),
            shape((features, tokens)),
            *([warm((2, 3, item_tokens, LANES))] * 4 if paired else [shape((heads, 3, item_tokens, LANES))]),
            *turned_shape,
        ],
        ids, Warm(moments), *[r.reshape(1, variables) for r in (run_count, run_mean, run_var)],
        Warm(fields), Warm(edge), w_embed, pos_embed, gains, w_qkv,
        in_specs=[smem, *[vmem] * 9, pl.BlockSpec(memory_space=pl.ANY)],
        scratch=[
            pltpu.VMEM((LANES, LANES), F32),
            pltpu.VMEM((8, LANES), F32),
            turned_hold,
            pltpu.VMEM(w_qkv.shape, BF),
            pltpu.SemaphoreType.DMA,
            pltpu.VMEM((heads, 3, item_tokens, LANES), BF),
        ],
        flops=2 * tokens * width * (features + 3 * local_width),
    )
    count = 4 if paired else 1
    stats, (hidden_zero, patches), packed = out[:3], out[3:5], out[5 : 5 + count]
    normed_one, token = out[5 + count : -1], out[-1]

    def along(messages):
        return [messages[0], *[swap(messages[k], "lon", 2 * k) for k in range(1, count)]]

    if paired:
        own = along(packed)
    else:
        sent = lax.all_to_all(packed[0], "lon", 0, 0, **alone)
        kv = sent
        if far > 1:
            kv = lax.all_gather(sent, "lon", axis=0, tiled=True, axis_index_groups=across)

    if paired:
        wo_got, normed_got = swap(w_out, "mp", 1), swap(normed_one[1], "lon", 1)
        other = [swap(x, "lon", 1) for x in own]
    if paired:
        attended, kept, token = pair_attend(own, other, items, scale, [token, normed_got])
        attended = along(attended)
    else:
        attended, attended_t, weights_t, token = attend(sent, kv, items, scale, [token])
        attended = [lax.all_to_all(attended, "lon", 0, 0, **alone)]
    anywhere = pl.BlockSpec(memory_space=pl.ANY)
    d_two, d_act, ct_turned, *mine, token = call(
        cotangent_kernel,
        "cotangent",
        [
            shape((tokens, width), F32),
            shape((tokens, hidden_units)),
            shape((features, tokens)),
            *[shape((rows, features))] * paired,
        ],
        ids, cotangent.transpose(0, 2, 1), wh_turned, w_down,
        after=[token],
        scratch=[pltpu.VMEM((everyone, rows, features), BF)] * paired,
        flops=2 * tokens * width * (features + hidden_units),
    )

    if paired:
        ct_got = swap(ct_turned, "lon", 1)
        attended[0] = pin(attended[0], [token])
        attended += [swap(x, "mp", 1) for x in attended]
    if paired:
        branches = [attended[0], *[Warm(x) for x in attended[1:]], w_out, Warm(wo_got)]
    else:
        mixed, branch, token = call(
            project_kernel,
            "project",
            [shape((tokens, local_width)), warm((tokens, width))],
            ids, *attended, w_out,
            after=[token],
            flops=2 * tokens * width * local_width,
        )
        branches = [Warm(branch), Warm(swap(branch, "mp", 1))]
    block = min(512, hidden_units // 2)
    chunks = hidden_units // block
    out = call(
        functools.partial(forward_kernel, count if paired else 0),
        "forward",
        [
            warm((tokens, width)),
            *[shape((tokens, local_width))] * paired,
            shape((tokens, width), F32),
            shape((tokens, hidden_units)),
            shape((2, tokens, hidden_units // 2)),
            shape((tokens, hidden_units // 2)),
            *turned_shape,
        ],
        ids, *branches, Warm(hidden_zero), gains, w_up, d_act,
        after=[token],
        in_specs=[
            smem,
            *([*[vmem] * (len(branches) - 2), anywhere, anywhere] if paired else [vmem] * 2),
            vmem,
            vmem,
            anywhere,
            anywhere,
        ],
        out_specs=[*[vmem] * (1 + paired), *[anywhere] * (4 + len(turned_shape))],
        scratch=[
            *[pltpu.VMEM(x.shape, BF) for x in turned_shape],
            pltpu.VMEM((tokens, width), F32),
            pltpu.VMEM((chunks, width, block), BF),
            pltpu.VMEM((chunks, tokens, block), BF),
            pltpu.VMEM((tokens, hidden_units), BF),
            pltpu.VMEM((2, tokens, hidden_units // 2), BF),
            pltpu.VMEM((tokens, width), BF),
            turned_hold,
            pltpu.SemaphoreType.DMA((2 * chunks,)),
            pltpu.SemaphoreType.DMA((2 + len(turned_shape) + 2 * chunks,)),
            *[
                pltpu.VMEM((2, *w_out.shape), BF),
                pltpu.VMEM((2, tokens, local_width), BF),
                pltpu.SemaphoreType.DMA((2,)),
            ] * paired,
        ],
        limit=32,
        flops=4 * tokens * width * hidden_units,
    )
    d_norm, *out, token = out
    if paired:
        mixed, out = out[0], out[1:]
        mixed_got = swap(mixed, "lon", 1)
    hidden_one, d_pre, activated, act_send = out[:4]
    normed_two = out[4:]
    d_norm_got = swap(d_norm, "mp", 1)
    half = hidden_units // 2
    if paired:
        inner_columns = features // rows * LANES
        first = half - LANES
        out_a = shape((parts // 2, rows, first + inner_columns))
        out_b = shape((parts // 2, rows, hidden_units - first))
        send_a, keep_a, send_b, keep_b, token = call(
            grads_ff_kernel,
            "grads_ff",
            [Warm(out_a), out_a, Warm(out_b), out_b],
            ids, normed_two[0], Warm(swap(normed_two[1], "lon", 1)), d_pre, Warm(swap(d_pre, "lon", 1)),
            ct_turned, Warm(ct_got), activated, Warm(swap(act_send, "lon", 1)),
            after=[token],
            scratch=[
                pltpu.VMEM((parts, rows, hidden_units), BF),
                pltpu.VMEM((2, parts // 2, rows, inner_columns), BF),
            ],
            limit=32,
            flops=2 * tokens * (width + features) * hidden_units,
        )
        got_a, got_b = swap(send_a, "dp", 1), swap(send_b, "lon", 2)
    forward, token = call(
        down_kernel,
        "down",
        [shape((tokens, width))],
        activated, Warm(w_down),
        after=[token, *([mixed_got] if paired else [])],
        flops=2 * tokens * width * hidden_units,
    )

    out = call(
        second_kernel,
        "second",
        [
            shape((tokens, width), F32),
            shape((1, width), F32),
            warm((heads, item_tokens, LANES)),
            *turned_shape,
        ],
        ids, Warm(hidden_one), Warm(d_two), Warm(d_norm), Warm(d_norm_got), gains, Warm(w_out),
        after=[token],
        scratch=[turned_hold],
        flops=2 * tokens * width * local_width,
    )
    d_one, gain_two, d_mixed = out[0], out[1], out[2:3]
    d_one_turned, token = out[3:-1], out[-1]
    if paired:
        d_one_got = swap(d_one_turned[1], "lon", 1)
    if paired:
        chips = [[2 * k + c for k in range(lon // 2)] for c in range(2)]
        d_heads = lax.all_to_all(
            d_mixed[0].reshape(lon // 2, 2, item_tokens, LANES), "lon", 0, 0, axis_index_groups=chips
        )
    else:
        d_heads = lax.all_to_all(d_mixed[0], "lon", 0, 0, **alone)
    forward_got = swap(forward, "mp", 1)
    if paired:
        out_a = shape((2, rows, first + 2 * inner_columns))
        out_b = shape((2, rows, hidden_units - first))
        send_a, keep_a, send_b, keep_b, token = call(
            fold_ff_kernel,
            "fold_ff",
            [out_a, out_a, out_b, out_b],
            ids, keep_a, Warm(got_a), keep_b, Warm(got_b),
            after=[token],
            scratch=[
                pltpu.VMEM((parts // 2, rows, first), BF),
                pltpu.VMEM((parts // 2, rows, hidden_units - first), BF),
            ],
        )
        send_a, send_b = pin([send_a, send_b], [d_heads])
        got_a, got_b = swap(send_a, "lon", 2), swap(send_b, "dp", 1)

    if paired:
        back, cross, token = pair_attend_back(ids, kept, d_heads, items, scale, [token])
        *back, token = call(
            combine_kernel,
            "combine",
            [warm(x.shape) for x in back],
            *back, Warm(swap(pin(cross, [got_a, got_b, forward_got]), "lon", 1)),
            after=[token],
        )
        back = along(back)
    else:
        back, token = attend_back(sent, kv, d_heads, attended_t, weights_t, items, scale, [token])
        if far > 1:
            d_query, d_kv = back
            d_kv = lax.psum_scatter(
                d_kv, "lon", scatter_dimension=0, tiled=True, axis_index_groups=across
            ).astype(BF)
            back = [jnp.concatenate([d_query[:, None], d_kv], axis=1)]
        back = [lax.all_to_all(back[0], "lon", 0, 0, **alone)]
    out = call(
        head_kernel,
        "head",
        [shape((items, features, item_tokens), F32), *turned_shape],
        ids, hidden_one, forward, Warm(forward_got), wh_turned,
        after=[token],
        scratch=[turned_hold],
        flops=2 * tokens * width * features,
    )
    pred, hidden_turned, token = out[0].transpose(0, 2, 1), list(out[1:-1]), out[-1]
    if paired:
        up_send, up_keep, token = call(
            merge_ff_kernel,
            "merge_ff",
            [shape((rows, hidden_units + 4 * inner_columns))] * 2,
            ids, keep_a, Warm(got_a), keep_b, got_b,
            after=[token],
            scratch=[pltpu.VMEM((2, rows, hidden_units), BF)],
        )
    d_qkv, d_norm, token = call(
        functools.partial(third_kernel, count),
        "third",
        [shape((tokens, 3 * local_width)), warm((tokens, width))],
        ids, *[Warm(x) for x in back], Warm(w_qkv),
        after=[token],
        flops=6 * tokens * width * local_width,
    )
    d_norm_got = swap(d_norm, "mp", 1)
    if paired:
        up_send, hidden_turned[1] = pin([up_send, hidden_turned[1]], [token])
        up_got = swap(up_send, "lon", 4)
        wide = local_width + 2 * LANES
        cut = 3 * local_width // 2 + LANES
        first, second = (shape((parts // 2, rows, c)) for c in (cut, 3 * local_width - cut))
        send_a, keep_a, send_b, keep_b, token = call(
            grads_q_kernel,
            "grads_q",
            [Warm(first), first, Warm(second), second],
            ids, normed_one[0], normed_got, d_qkv, Warm(swap(d_qkv, "lon", 1)),
            after=[token],
            scratch=[pltpu.VMEM((parts, rows, 3 * local_width), BF)],
            flops=6 * tokens * width * local_width,
        )
        oh_send, oh_keep, token = call(
            grads_oh_kernel,
            "grads_oh",
            [shape((parts // 2, rows, wide))] * 2,
            ids, d_one_turned[0], Warm(d_one_got), mixed, Warm(mixed_got),
            hidden_turned[0], Warm(swap(hidden_turned[1], "lon", 1)), ct_turned, Warm(ct_got),
            after=[token],
            scratch=[pltpu.VMEM((parts, rows, wide), BF)],
            flops=2 * tokens * width * wide,
        )
        oh_got = swap(oh_send, "dp", 1)
        got_a, got_b = swap(send_a, "dp", 1), swap(send_b, "lon", 2)

    out = call(
        functools.partial(last_kernel, columns),
        "last",
        [
            *[shape((item_tokens, width // 2))] * 2,
            shape((items, variables * columns, height), F32),
            shape((items, variables, height)),
            *([shape((parts, rows, 2 * LANES)), warm((parts, rows, 2 * LANES))] if paired else [shape((width, 2 * LANES))]),
        ],
        ids, Warm(hidden_zero), Warm(d_one), Warm(d_norm), Warm(d_norm_got), gains, gain_two, patches, w_embed,
        after=[token],
        scratch=[
            pltpu.VMEM((2 * LANES, width), F32),
            pltpu.VMEM((2, item_tokens, width // 2), BF),
            pltpu.VMEM((parts, 2, rows, 2 * LANES) if paired else (8, LANES), BF),
        ],
        flops=4 * tokens * width * features,
    )
    pos_send, pos, d_fields, d_edge = out[:4]
    embed, token = out[4:-1], out[-1]
    if not paired:
        east, pos_got = from_behind(d_edge, "lon", -1), swap(pos_send, "dp", 1)
    more, more_outs, more_scratch, rest, rest_outs = [], [], [], [], []
    if paired:
        embed_width = embed[0].shape[2]
        step_a, side = shape((2, rows, cut)), shape((2, rows, wide))
        step_b = shape((2, rows, 3 * local_width - cut + 2 * embed_width + 2 * inner_columns))
        send_a, keep_a, send_b, keep_b, oh_send, oh_keep, token = call(
            fold_q_kernel,
            "fold_q",
            [Warm(step_a), step_a, Warm(step_b), step_b, Warm(side), side],
            ids, keep_a, Warm(got_a), keep_b, Warm(got_b), up_keep, Warm(up_got), oh_keep, Warm(oh_got),
            embed[0], Warm(swap(embed[1], "lon", 1)),
            after=[token],
            scratch=[
                pltpu.VMEM(keep_a.shape, BF),
                pltpu.VMEM(keep_b.shape, BF),
                pltpu.VMEM(oh_keep.shape, BF),
                pltpu.VMEM(embed[0].shape, BF),
            ],
        )
        got_a, got_b, oh_got = swap(send_a, "lon", 2), swap(send_b, "dp", 1), swap(oh_send, "lon", 4)
        east = from_behind(pin(d_edge, [token]), "lon", -1)
        final, block = shape((rows, 3 * local_width + embed_width)), shape((rows, embed_width))
        send, keep, pair, near_send, embed_both, oh_keep, token = call(
            merge_q_kernel,
            "merge_q",
            [
                Warm(final),
                final,
                shape((2, rows, 4 * inner_columns)),
                warm((rows, embed_width + wide)),
                Warm(block),
                shape((rows, wide)),
            ],
            ids, keep_a, Warm(got_a), keep_b, Warm(got_b), oh_keep, Warm(oh_got),
            after=[token, east],
            scratch=[
                pltpu.VMEM((2, rows, 3 * local_width), BF),
                pltpu.VMEM((4, *block.shape), BF),
                pltpu.VMEM((2, rows, wide), BF),
            ],
        )
        pos_got = swap(pin(pos_send, [token]), "dp", 1)
        more = [up_keep, Warm(up_got), mine[0], pair, Warm(swap(pair, "lon", 1))]
        more_outs = [shape((rows, hidden_units), F32)] * 2
        more_scratch = [pltpu.VMEM((features, hidden_units // 4), BF)]
        rest = [
            Warm(swap(near_send, "lon", 2)), Warm(swap(embed_both, "lon", 6)), oh_keep,
            keep, Warm(swap(send, "lon", 4)),
        ]
        rest_outs = [
            shape((rows, local_width), F32),
            shape((rows, features), F32),
            shape((3, rows, local_width), F32),
        ]
    else:
        rest = [lax.all_to_all(embed[0].reshape(everyone, rows, 2 * LANES), ("dp", "lon"), 0, 0)]
    *closed, token = call(
        functools.partial(close_kernel, columns),
        "close",
        [shape(d_fields.shape, F32), shape(pos.shape, F32), *more_outs],
        ids, d_fields, east, pos, Warm(pos_got), *more,
        after=[token],
        scratch=more_scratch,
    )
    *ended, token = call(
        end_kernel,
        "end",
        [shape((rows, features), F32), shape((2, rows), F32), *rest_outs],
        *rest,
        after=[token],
    )
    if paired:
        grad_up, grad_down, (grad_out, grad_head, grad_qkv) = closed[2], closed[3], ended[2:]
    else:
        flat = activated.transpose(1, 0, 2).reshape(tokens, hidden_units)
        grad_up = scatter(nn(normed_two[0], d_pre))
        grad_down = scatter(nn(d_two.T.astype(BF), flat))
        grad_out = scatter(nn(d_one_turned[0], mixed))
        grad_head = scatter(nt(hidden_turned[0], ct_turned))
        grad_qkv = scatter(nn(normed_one[0], d_qkv)).reshape(rows, 3, local_width).transpose(1, 0, 2)
    return (
        pred,
        *[x.reshape(variables) for x in stats],
        closed[0].reshape(items, variables, columns, height).transpose(0, 1, 3, 2),
        ended[0].T,
        closed[1],
        ended[1],
        grad_qkv,
        grad_out.T,
        grad_up,
        grad_down.T,
        grad_head,
    )


def solution(mesh):
    in_specs = (
        P(None, None, None, "lon"),
        P("dp"),
        P(),
        P(),
        P(),
        P(),
        P("lon", None),
        P(),
        P(None, None, "mp"),
        P("mp", None),
        P(None, "mp"),
        P("mp", None),
        P(),
        P("dp", "lon", None),
    )
    out_specs = (
        P("dp", "lon", None),
        P(),
        P(),
        P(),
        P("dp", None, None, "lon"),
        P(None, ("dp", "lon")),
        P("lon", "dp"),
        P(None, ("dp", "lon")),
        P(None, ("dp", "lon"), "mp"),
        P("mp", ("dp", "lon")),
        P(("dp", "lon"), "mp"),
        P("mp", ("dp", "lon")),
        P(("dp", "lon"), None),
    )
    return jax.shard_map(local, mesh=mesh, in_specs=in_specs, out_specs=out_specs, check_vma=False)
```
